256 devices in a mesh: dom: 4 (over x), gx: 16 (over z, y_hi), gy: 4 (over y_lo, core).
Axes of the slice: x: 4, y: 4 (y_hi: 2, y_lo: 2; y = y_hi * 2 + y_lo), z: 8, core: 2. Of those that a mesh axis runs over, the one named last changes fastest.
Arguments:
- state: float32 [9, 32, 128, 1024], P(None, 'dom', 'gx', 'gy'), may hold values from -6 to 6
- source: float32 [6, 128, 1024], P(None, 'gx', 'gy'), may hold values from -6 to 6
- seafloor: int32 [128, 1024], P('gx', 'gy'), may hold values from 1 to 8
- region: int32 [32, 128, 1024], P('dom', 'gx', 'gy'), may hold values from 0 to 15
- lame_lambda: float32 [16], replicated, may hold values from 1 to 2
- shear_mu: float32 [16], replicated, may hold values from 0.3 to 0.6
- buoyancy: float32 [16], replicated, may hold values from 0.5 to 1
Outputs:
- adjoint_state: float32 [9, 32, 128, 1024], P(None, 'dom', 'gx', 'gy')
The draws below stay inside these ranges and needn't reach their ends.
All inputs are finite; a program needn't handle non-finite values.
Results may differ from the reference program's by a relative error of at most 0.00011.
Values sent between devices are 32-bit elements; how exact they have to be, the bound alone decides.
A program may use at most 64 MiB of HBM per device.

```python
import math
import jax
import jax.numpy as jnp

L_DEV = 8
STEPS = 6
REGIONS = 16
LEVELS = 32
NX = 128
NY = 1024


def set_ends(values, rng, least, high):
    shape = values.shape
    index_at = [jax.random.randint(jax.random.fold_in(rng, axis), (), 0, shape[axis]) for axis in range(len(shape))]
    values = values.at[tuple(index_at)].set(least)
    longest = shape.index(max(shape))
    index_at[longest] = (index_at[longest] + 1) % shape[longest]
    return values.at[tuple(index_at)].set(high)


def level_of(stream_key, dims, shards, smallest, largest):
    gain, own = 1.0, jax.random.fold_in(stream_key, 6)
    for position, parts in shards:
        draws = jnp.exp(jax.random.uniform(jax.random.fold_in(own, position), (parts,), jnp.float32, smallest / len(shards), largest / len(shards)))
        gain = gain * jnp.repeat(draws, dims[position] // parts).reshape([-1 if axis == position else 1 for axis in range(len(dims))])
    return gain


def normal_values(stream_key, extent, spread, bound, split=(), kind=jnp.bfloat16):
    values = jax.random.normal(stream_key, extent, jnp.float32) * spread
    if len(split) > 0:
        values = level_of(stream_key, extent, split, -0.22, 0.18) * values
    return jnp.clip(values, min=-bound, max=bound).astype(kind)


def setup_inputs(seed: int = 0) -> dict:
    splits = jax.random.split(jax.random.key(seed), 8)
    state = normal_values(splits[0], (9, LEVELS, NX, NY), 1.0, 6.0, ((1, 4), (2, 16), (3, 4)), jnp.float32)
    source = normal_values(splits[1], (STEPS, NX, NY), 1.0, 6.0, ((1, 16), (2, 4)), jnp.float32)
    seafloor = set_ends(jax.random.randint(splits[2], (NX, NY), 1, L_DEV + 1), jax.random.fold_in(splits[2], 1), 1, L_DEV).astype(jnp.int32)
    region = set_ends(jax.random.randint(splits[3], (LEVELS, NX, NY), 0, REGIONS), jax.random.fold_in(splits[3], 1), 0, REGIONS - 1).astype(jnp.int32)
    lame_lambda = jnp.clip(jnp.exp(jax.random.uniform(splits[4], (REGIONS,), jnp.float32, math.log(1.0), math.log(2.0))), 1.0, 2.0)
    shear_mu = jnp.clip(jnp.exp(jax.random.uniform(splits[5], (REGIONS,), jnp.float32, math.log(0.3), math.log(0.6))), 0.3, 0.6)
    buoyancy = jnp.clip(jnp.exp(jax.random.uniform(splits[6], (REGIONS,), jnp.float32, math.log(0.5), math.log(1.0))), 0.5, 1.0)
    return {"state": state, "source": source, "seafloor": seafloor, "region": region, "lame_lambda": lame_lambda, "shear_mu": shear_mu, "buoyancy": buoyancy}


courant = 0.25


def inner(ext, axis, shift):
    index = [slice(None)] * ext.ndim
    for dim in range(ext.ndim - 3, ext.ndim):
        index[dim] = slice(1, ext.shape[dim] - 1)
    index[axis] = slice(1 + shift, ext.shape[axis] - 1 + shift)
    return ext[tuple(index)]


def central(ext, axis):
    return 0.5 * (inner(ext, axis, 1) - inner(ext, axis, -1))


def reference(state, source, seafloor, region, lame_lambda, shear_mu, buoyancy):
    levels = jnp.arange(LEVELS, dtype=jnp.int32)[:, None, None]
    solid = (levels >= seafloor[None]).astype(jnp.float32)
    lam = lame_lambda[region]
    mu = shear_mu[region] * solid
    buoy = buoyancy[region]
    top = (levels == 0).astype(jnp.float32)
    vx, vy, vz = state[0], state[1], state[2]
    sxx, syy, szz = state[3], state[4], state[5]
    sxy, sxz, syz = state[6] * solid, state[7] * solid, state[8] * solid
    for step in range(STEPS):
        added = top * source[step][None]
        sxx = sxx + added
        syy = syy + added
        szz = szz + added
        pxx, pyy, pzz = jnp.pad(sxx, 1), jnp.pad(syy, 1), jnp.pad(szz, 1)
        pxy, pxz, pyz = jnp.pad(sxy, 1), jnp.pad(sxz, 1), jnp.pad(syz, 1)
        vx = vx - courant * buoy * (central(pxx, -2) + central(pxy, -1) + central(pxz, -3))
        vy = vy - courant * buoy * (central(pxy, -2) + central(pyy, -1) + central(pyz, -3))
        vz = vz - courant * buoy * (central(pxz, -2) + central(pyz, -1) + central(pzz, -3))
        qx, qy, qz = jnp.pad(vx, 1), jnp.pad(vy, 1), jnp.pad(vz, 1)
        exx = central(qx, -2)
        eyy = central(qy, -1)
        ezz = central(qz, -3)
        trace = exx + eyy + ezz
        sxx = sxx - courant * (lam * trace + 2.0 * mu * exx)
        syy = syy - courant * (lam * trace + 2.0 * mu * eyy)
        szz = szz - courant * (lam * trace + 2.0 * mu * ezz)
        sxy = (sxy - courant * mu * (central(qx, -1) + central(qy, -2))) * solid
        sxz = (sxz - courant * mu * (central(qx, -3) + central(qz, -2))) * solid
        syz = (syz - courant * mu * (central(qy, -3) + central(qz, -1))) * solid
    return jnp.stack([vx, vy, vz, sxx, syy, szz, sxy, sxz, syz])
```

```python
import functools

import jax
import jax.numpy as jnp
from jax import lax
from jax.experimental import pallas as pl
from jax.experimental.pallas import tpu as pltpu
from jax.sharding import PartitionSpec as P

STEPS = 6
COURANT = 0.25
REGIONS = 16
BLOCK = 16
WIDE = 12
NEAR = 10
MESH = pl.DeviceIdType.MESH

f32 = jnp.float32


def lane_iota():
    return lax.broadcasted_iota(jnp.int32, (8, 128), 1)


def row_iota():
    return lax.broadcasted_iota(jnp.int32, (8, 128), 0)


def rows(z, x=0):
    return (z + 1) * BLOCK + 8 + x


def column(x):
    return pl.ds(rows(0, x), 8, stride=BLOCK)


def dy(v, lane):
    ahead = pltpu.roll(v, 127, 2)
    behind = pltpu.roll(v, 1, 2)
    ahead = jnp.where(lane == 127, jnp.concatenate([ahead[1:], ahead[:1]], 0), ahead)
    behind = jnp.where(lane == 0, jnp.concatenate([behind[2:], behind[:2]], 0), behind)
    return ahead - behind


def pick(bits, table):
    values = [table[i] for i in range(REGIONS)]
    for bit in bits:
        values = [jnp.where(bit, values[2 * i + 1], values[2 * i]) for i in range(len(values) // 2)]
    return values[0]


def pack(tiles, width, lane):
    out = jnp.zeros((8, 128), f32)
    for k, tile in enumerate(tiles):
        moved = pltpu.roll(tile, 2 * width * k + width, 1)
        out = jnp.where((lane >= 2 * width * k) & (lane < 2 * width * (k + 1)), moved, out)
    return out


def unpack(tile, k, width):
    return pltpu.roll(tile, (128 - (2 * width * k + width)) % 128, 1)


def kernel(
    sizes, state, source, floor, region, lame, shear, buoy, out,
    S, V, L, M, B, SRC, ys, yr, xs0, xr0, zs0, zr0, xs, xr, zs, zr, es, er,
    y_send, y_recv, first_send, first_recv, send_sem, recv_sem,
):
    n_dom, n_gx, n_gy = sizes
    dom, gx, gy = lax.axis_index("dom"), lax.axis_index("gx"), lax.axis_index("gy")
    lane, sub = lane_iota(), row_iota()
    zero = jnp.zeros((8, 128), f32)

    def there(dz, dx, dyy):
        ok = None
        for delta, at, n in ((dz, dom, n_dom), (dx, gx, n_gx), (dyy, gy, n_gy)):
            if delta:
                cond = at > 0 if delta < 0 else at < n - 1
                ok = cond if ok is None else ok & cond
        return ok

    def at(dz, dx, dyy):
        return (dom + dz, gx + dx, gy + dyy)

    sides = (-1, 1)
    y_ways = [(0, 0, -1), (0, 0, 1)]
    x_ways = [(0, -1, 0), (0, 1, 0)]
    z_ways = [(-1, 0, 0), (1, 0, 0)]
    e_ways = [(dz, dx, 0) for dx in sides for dz in sides]
    ways = x_ways + z_ways + e_ways

    barrier = pltpu.get_barrier_semaphore()
    count = jnp.int32(0)
    for way in y_ways + ways:
        ok = there(*way)
        count = count + ok.astype(jnp.int32)

        @pl.when(ok)
        def _(way=way):
            pl.semaphore_signal(barrier, inc=1, device_id=at(*way), device_id_type=MESH)

    for i in range(2):
        @pl.when(jnp.logical_not(there(*y_ways[i])))
        def _(i=i):
            yr[i] = jnp.zeros(yr.shape[1:], f32)

        @pl.when(jnp.logical_not(there(*x_ways[i])))
        def _(i=i):
            xr0[i] = jnp.zeros(xr0.shape[1:], f32)
            for slot in range(2):
                xr[slot, i] = jnp.zeros(xr.shape[2:], f32)

        @pl.when(jnp.logical_not(there(*z_ways[i])))
        def _(i=i):
            zr0[i] = jnp.zeros(zr0.shape[1:], f32)
            for slot in range(2):
                zr[slot, i] = jnp.zeros(zr.shape[2:], f32)

    for i in range(4):
        @pl.when(jnp.logical_not(there(*e_ways[i])))
        def _(i=i):
            for slot in range(2):
                er[slot, i] = zero

    for z in range(8):
        for i, t in ((0, 0), (1, 1)):
            tile = zero
            for f in range(10):
                if f < 9:
                    v = state[f, z, :, 128 * t : 128 * t + 128]
                else:
                    v = region[z, :, 128 * t : 128 * t + 128].astype(f32)
                shift = (WIDE * f + (WIDE if t else 0)) % 128
                v = pltpu.roll(v, shift, 1) if shift else v
                tile = jnp.where((lane >= WIDE * f) & (lane < WIDE * (f + 1)), v, tile)
            ys[i, z] = tile
    for i, t in ((0, 0), (1, 1)):
        tile = zero
        for f in range(STEPS + 1):
            if f < STEPS:
                v = source[f, :, 128 * t : 128 * t + 128]
            else:
                v = floor[:, 128 * t : 128 * t + 128].astype(f32)
            shift = (WIDE * f + (WIDE if t else 0)) % 128
            v = pltpu.roll(v, shift, 1) if shift else v
            tile = jnp.where((lane >= WIDE * f) & (lane < WIDE * (f + 1)), v, tile)
        ys[i, 8] = tile

    pl.semaphore_wait(barrier, count)

    def y_copy(i):
        return pltpu.make_async_remote_copy(
            src_ref=ys.at[i], dst_ref=yr.at[1 - i], send_sem=y_send.at[i], recv_sem=y_recv.at[1 - i],
            device_id=at(*y_ways[i]), device_id_type=MESH)

    for i in range(2):
        @pl.when(there(*y_ways[i]))
        def _(i=i):
            y_copy(i).start()

    for z in range(-1, 9):
        for f in range(3):
            for t in range(3):
                V[f, t, pl.ds(rows(z, -8), 8), :] = zero
    for z in (-1, 8):
        for f in range(3):
            for t in range(3):
                V[f, t, pl.ds(rows(z), 8), :] = zero
    for t in range(3):
        for s in (6, 7):
            SRC[t, pl.ds(8 * s, 8), :] = zero

    def materials(number, seafloor, z, inside):
        bits = [(number & (1 << k)) != 0 for k in range(4)]
        solid = (dom * 8 + z) >= seafloor
        scale = 0.5 * COURANT
        lam = pick(bits, [lame[i] * scale for i in range(REGIONS)])
        mu = jnp.where(solid, pick(bits, [shear[i] * scale for i in range(REGIONS)]), 0.0)
        b = pick(bits, [buoy[i] * scale for i in range(REGIONS)])
        if inside is not None:
            lam, mu, b = (jnp.where(inside, v, 0.0) for v in (lam, mu, b))
        return lam, mu, b, solid

    for t in range(2):
        cut = slice(128 * t, 128 * t + 128)
        seafloor = floor[:, cut]
        for s in range(STEPS):
            SRC[t, pl.ds(8 * s, 8), :] = source[s, :, cut]
        for z in range(8):
            lam, mu, b, solid = materials(region[z, :, cut], seafloor, z, None)
            r = pl.ds(8 * z, 8)
            L[t, r, :], M[t, r, :], B[t, r, :] = lam, mu, b
            for f in range(9):
                v = state[f, z, :, cut]
                if f < 3:
                    V[f, t, pl.ds(rows(z), 8), :] = v
                else:
                    S[f - 3, t, pl.ds(rows(z), 8), :] = jnp.where(solid, v, 0.0) if f >= 6 else v

    for i in range(2):
        @pl.when(there(*y_ways[i]))
        def _(i=i):
            y_copy(1 - i).wait_recv()

    left = lane >= 128 - WIDE
    right = lane < WIDE
    inside = (left & (gy > 0)) | (right & (gy < n_gy - 1))

    def margin(k, f):
        shift_r = (128 - WIDE * f) % 128
        shift_l = (256 - WIDE - WIDE * f) % 128
        a = yr[1, k]
        a = pltpu.roll(a, shift_r, 1) if shift_r else a
        c = yr[0, k]
        c = pltpu.roll(c, shift_l, 1) if shift_l else c
        return jnp.where(left, c, jnp.where(right, a, 0.0))

    seafloor = margin(8, STEPS).astype(jnp.int32)
    for s in range(STEPS):
        SRC[2, pl.ds(8 * s, 8), :] = margin(8, s)
    for z in range(8):
        lam, mu, b, solid = materials(margin(z, 9).astype(jnp.int32), seafloor, z, inside)
        r = pl.ds(8 * z, 8)
        L[2, r, :], M[2, r, :], B[2, r, :] = lam, mu, b
        for f in range(9):
            v = margin(z, f)
            if f < 3:
                V[f, 2, pl.ds(rows(z), 8), :] = v
            else:
                S[f - 3, 2, pl.ds(rows(z), 8), :] = jnp.where(solid, v, 0.0) if f >= 6 else v

    x_fields, z_fields = (0, 3, 4), (2, 4, 5)
    for i, x in ((0, 0), (1, 7)):
        parts = [S[f, :, column(x), :] for f in x_fields]
        parts += [m[:, pl.ds(x, 8, stride=8), :] for m in (L, M)]
        for k, v in enumerate(parts):
            xs0[i, 2 * k : 2 * k + 2] = v[0:2]
        xs0[i, 10] = pack([v[2] for v in parts], WIDE, lane)
        xs0[i, 11:14] = SRC[:, pl.ds(x, 8, stride=8), :]
    for i, z in ((0, 0), (1, 7)):
        parts = [S[f, :, pl.ds(rows(z), 8), :] for f in z_fields]
        parts += [m[:, pl.ds(8 * z, 8), :] for m in (L, M)]
        for k, v in enumerate(parts):
            zs0[i, 2 * k : 2 * k + 2] = v[0:2]
        zs0[i, 10] = pack([v[2] for v in parts], WIDE, lane)

    def first_copy(i):
        way = (x_ways + z_ways)[i]
        src, dst = (xs0, xr0) if i < 2 else (zs0, zr0)
        k = i % 2
        return pltpu.make_async_remote_copy(
            src_ref=src.at[k], dst_ref=dst.at[1 - k], send_sem=first_send.at[i], recv_sem=first_recv.at[i ^ 1],
            device_id=at(*way), device_id_type=MESH)

    for i in range(4):
        @pl.when(there(*ways[i]))
        def _(i=i):
            first_copy(i).start()
    for i in range(4):
        @pl.when(there(*ways[i]))
        def _(i=i):
            first_copy(i ^ 1).wait_recv()

    def opened(buffer, i, k, packed, width):
        return jnp.concatenate([buffer[i, 2 * k : 2 * k + 2], unpack(packed, k, width)[None]], 0)

    for i, x in ((0, -1), (1, 8)):
        packed = xr0[i, 10]
        for k, f in enumerate(x_fields):
            S[f, :, column(x), :] = opened(xr0, i, k, packed, WIDE)
    for i, z in ((0, -1), (1, 8)):
        packed = zr0[i, 10]
        for k, f in enumerate(z_fields):
            S[f, :, pl.ds(rows(z), 8), :] = opened(zr0, i, k, packed, WIDE)

    def copy(i, slot):
        way = ways[i]
        if i < 2:
            src, dst = xs.at[i], xr.at[slot, 1 - i]
            back = i ^ 1
        elif i < 4:
            src, dst = zs.at[i - 2], zr.at[slot, 3 - i]
            back = i ^ 1
        else:
            src, dst = es.at[i - 4], er.at[slot, 7 - i]
            back = 11 - i
        return pltpu.make_async_remote_copy(
            src_ref=src, dst_ref=dst, send_sem=send_sem.at[i], recv_sem=recv_sem.at[slot, back],
            device_id=at(*way), device_id_type=MESH)

    opposite = [1, 0, 3, 2, 7, 6, 5, 4]

    def step(s, carry):
        slot = lax.rem(s, 2)

        @pl.when(dom == 0)
        def _():
            added = SRC[:, pl.ds(pl.multiple_of(8 * s, 8), 8), :]
            for f in range(3):
                S[f, :, pl.ds(rows(0), 8), :] += added
            for i, x in ((0, -1), (1, 8)):
                S[0, :, pl.ds(rows(0, x), 1), :] += xr0[i, 11:14, pl.ds(s, 1), :]

        for z in range(8):
            own = pl.ds(rows(z), 8)
            after, before = pl.ds(rows(z, 1), 8), pl.ds(rows(z, -1), 8)
            above, below = pl.ds(rows(z + 1), 8), pl.ds(rows(z - 1), 8)

            def dx(f):
                return S[f, :, after, :] - S[f, :, before, :]

            def dz(f):
                return S[f, :, above, :] - S[f, :, below, :]

            b = B[:, pl.ds(8 * z, 8), :]
            V[0, :, own, :] -= b * (dx(0) + dy(S[3, :, own, :], lane) + dz(4))
            V[1, :, own, :] -= b * (dx(3) + dy(S[1, :, own, :], lane) + dz(5))
            V[2, :, own, :] -= b * (dx(4) + dy(S[5, :, own, :], lane) + dz(2))

        for i, xx in ((0, (0, 1)), (1, (7, 6))):
            parts = [V[f, :, column(x), :] for x in xx for f in range(3)]
            for k, v in enumerate(parts):
                xs[i, 2 * k : 2 * k + 2] = v[0:2]
            xs[i, 12] = pack([v[2] for v in parts], NEAR, lane)
        for i in range(2):
            @pl.when(there(*ways[i]))
            def _(i=i):
                copy(i, slot).start()
        for i, (dz_, dx_, _) in enumerate(e_ways):
            r = rows(0 if dz_ < 0 else 7, 0 if dx_ < 0 else 7)
            for k, f in enumerate((0, 2)):
                for t in range(3):
                    es[i, pl.ds(3 * k + t, 1), :] = V[f, t, pl.ds(r, 1), :]
        for i in range(4, 8):
            @pl.when(there(*ways[i]))
            def _(i=i):
                copy(i, slot).start()
        for i, zz in ((0, (0, 1)), (1, (7, 6))):
            parts = [V[f, :, pl.ds(rows(z), 8), :] for z in zz for f in range(3)]
            for k, v in enumerate(parts):
                zs[i, 2 * k : 2 * k + 2] = v[0:2]
            zs[i, 12] = pack([v[2] for v in parts], NEAR, lane)
        for i in range(2, 4):
            @pl.when(there(*ways[i]))
            def _(i=i):
                copy(i, slot).start()

        for z in range(8):
            own = pl.ds(rows(z), 8)
            after, before = pl.ds(rows(z, 1), 8), pl.ds(rows(z, -1), 8)
            above, below = pl.ds(rows(z + 1), 8), pl.ds(rows(z - 1), 8)
            v = [V[f, :, own, :] for f in range(3)]
            dxs = [V[f, :, after, :] - V[f, :, before, :] for f in range(3)]
            dzs = [V[f, :, above, :] - V[f, :, below, :] for f in range(3)]
            dys = [dy(v[f], lane) for f in range(3)]
            lam, mu = L[:, pl.ds(8 * z, 8), :], M[:, pl.ds(8 * z, 8), :]
            spread = lam * (dxs[0] + dys[1] + dzs[2])
            mu2 = mu + mu
            S[0, :, own, :] -= spread + mu2 * dxs[0]
            S[1, :, own, :] -= spread + mu2 * dys[1]
            S[2, :, own, :] -= spread + mu2 * dzs[2]
            S[3, :, own, :] -= mu * (dys[0] + dxs[1])
            S[4, :, own, :] -= mu * (dzs[0] + dxs[2])
            S[5, :, own, :] -= mu * (dzs[1] + dys[2])

        for i in (2, 3, 0, 1, 4, 5, 6, 7):
            @pl.when(there(*ways[i]))
            def _(i=i):
                copy(opposite[i], slot).wait_recv()

        for i, x, sign in ((0, 0, -1.0), (1, 7, 1.0)):
            packed = xr[slot, i, 12]
            got = [
                jnp.concatenate([xr[slot, i, 2 * k : 2 * k + 2], unpack(packed, k, NEAR)[None]], 0) for k in range(6)
            ]
            near, far = got[0:3], got[3:6]
            mine = [jnp.concatenate([xs[i, 2 * k : 2 * k + 2], V[k, 2:3, column(x), :]], 0) for k in range(3)]
            lam, mu = L[:, pl.ds(x, 8, stride=8), :], M[:, pl.ds(x, 8, stride=8), :]
            slope = [sign * v for v in near]
            spread = lam * slope[0]
            S[0, :, column(x), :] -= spread + (mu + mu) * slope[0]
            S[1, :, column(x), :] -= spread
            S[2, :, column(x), :] -= spread
            S[3, :, column(x), :] -= mu * slope[1]
            S[4, :, column(x), :] -= mu * slope[2]

            packed = xr0[i, 10]
            lam, mu = opened(xr0, i, 3, packed, WIDE), opened(xr0, i, 4, packed, WIDE)
            dxs = [sign * (far[f] - mine[f]) for f in range(3)]
            dzs = {}
            for k, f in enumerate((0, 2)):
                top = jnp.stack([er[slot, 2 * i, pl.ds(3 * k + t, 1), :] for t in range(3)])
                bottom = jnp.stack([er[slot, 2 * i + 1, pl.ds(3 * k + t, 1), :] for t in range(3)])
                down = jnp.where(sub == 0, top, pltpu.roll(near[f], 1, 1))
                up = jnp.where(sub == 7, bottom, pltpu.roll(near[f], 7, 1))
                dzs[f] = up - down
            trace = dxs[0] + dy(near[1], lane) + dzs[2]
            beyond = column(x + int(sign))
            S[0, :, beyond, :] -= lam * trace + (mu + mu) * dxs[0]
            S[3, :, beyond, :] -= mu * (dy(near[0], lane) + dxs[1])
            S[4, :, beyond, :] -= mu * (dzs[0] + dxs[2])

        for i, z, sign in ((0, 0, -1.0), (1, 7, 1.0)):
            packed = zr[slot, i, 12]
            got = [
                jnp.concatenate([zr[slot, i, 2 * k : 2 * k + 2], unpack(packed, k, NEAR)[None]], 0) for k in range(6)
            ]
            near, far = got[0:3], got[3:6]
            own = pl.ds(rows(z), 8)
            mine = [V[f, :, own, :] for f in range(3)]
            lam, mu = L[:, pl.ds(8 * z, 8), :], M[:, pl.ds(8 * z, 8), :]
            slope = [sign * v for v in near]
            spread = lam * slope[2]
            S[0, :, own, :] -= spread
            S[1, :, own, :] -= spread
            S[2, :, own, :] -= spread + (mu + mu) * slope[2]
            S[4, :, own, :] -= mu * slope[0]
            S[5, :, own, :] -= mu * slope[1]

            packed = zr0[i, 10]
            lam, mu = opened(zr0, i, 3, packed, WIDE), opened(zr0, i, 4, packed, WIDE)
            dzs = [sign * (far[f] - mine[f]) for f in range(3)]
            dxs = {}
            for k, f in enumerate((0, 2)):
                first = jnp.stack([er[slot, i, pl.ds(3 * k + t, 1), :] for t in range(3)])
                last = jnp.stack([er[slot, i + 2, pl.ds(3 * k + t, 1), :] for t in range(3)])
                behind = jnp.where(sub == 0, first, pltpu.roll(near[f], 1, 1))
                ahead = jnp.where(sub == 7, last, pltpu.roll(near[f], 7, 1))
                dxs[f] = ahead - behind
            trace = dxs[0] + dy(near[1], lane) + dzs[2]
            beyond = pl.ds(rows(z + int(sign)), 8)
            S[2, :, beyond, :] -= lam * trace + (mu + mu) * dzs[2]
            S[4, :, beyond, :] -= mu * (dzs[0] + dxs[2])
            S[5, :, beyond, :] -= mu * (dzs[1] + dy(near[2], lane))

        for i in range(8):
            @pl.when(there(*ways[i]))
            def _(i=i):
                copy(i, slot).wait_send()
        return carry

    lax.fori_loop(0, STEPS, step, 0)

    for f in range(9):
        for z in range(8):
            for t in range(2):
                src = V[f, t, pl.ds(rows(z), 8), :] if f < 3 else S[f - 3, t, pl.ds(rows(z), 8), :]
                out[f, z, :, 128 * t : 128 * t + 128] = src

    for i in range(2):
        @pl.when(there(*y_ways[i]))
        def _(i=i):
            y_copy(i).wait_send()
    for i in range(4):
        @pl.when(there(*ways[i]))
        def _(i=i):
            first_copy(i).wait_send()


def solution(mesh):
    sizes = (mesh.shape["dom"], mesh.shape["gx"], mesh.shape["gy"])

    def on_device(state, source, floor, region, lame, shear, buoy):
        vmem = pl.BlockSpec(memory_space=pltpu.VMEM)
        smem = pl.BlockSpec(memory_space=pltpu.SMEM)
        return pl.pallas_call(
            functools.partial(kernel, sizes),
            out_shape=jax.ShapeDtypeStruct(state.shape, f32),
            in_specs=[vmem] * 4 + [smem] * 3,
            out_specs=vmem,
            scratch_shapes=[
                pltpu.VMEM((6, 3, 10 * BLOCK, 128), f32),
                pltpu.VMEM((3, 3, 10 * BLOCK, 128), f32),
                pltpu.VMEM((3, 64, 128), f32),
                pltpu.VMEM((3, 64, 128), f32),
                pltpu.VMEM((3, 64, 128), f32),
                pltpu.VMEM((3, 64, 128), f32),
                pltpu.VMEM((2, 9, 8, 128), f32),
                pltpu.VMEM((2, 9, 8, 128), f32),
                pltpu.VMEM((2, 14, 8, 128), f32),
                pltpu.VMEM((2, 14, 8, 128), f32),
                pltpu.VMEM((2, 11, 8, 128), f32),
                pltpu.VMEM((2, 11, 8, 128), f32),
                pltpu.VMEM((2, 13, 8, 128), f32),
                pltpu.VMEM((2, 2, 13, 8, 128), f32),
                pltpu.VMEM((2, 13, 8, 128), f32),
                pltpu.VMEM((2, 2, 13, 8, 128), f32),
                pltpu.VMEM((4, 8, 128), f32),
                pltpu.VMEM((2, 4, 8, 128), f32),
                pltpu.SemaphoreType.DMA((2,)),
                pltpu.SemaphoreType.DMA((2,)),
                pltpu.SemaphoreType.DMA((4,)),
                pltpu.SemaphoreType.DMA((4,)),
                pltpu.SemaphoreType.DMA((8,)),
                pltpu.SemaphoreType.DMA((2, 8)),
            ],
            compiler_params=pltpu.CompilerParams(
                collective_id=0, has_side_effects=True, vmem_limit_bytes=32 * 1024 * 1024
            ),
        )(state, source, floor, region, lame, shear, buoy)

    return jax.shard_map(
        on_device,
        mesh=mesh,
        in_specs=(
            P(None, "dom", "gx", "gy"),
            P(None, "gx", "gy"),
            P("gx", "gy"),
            P("dom", "gx", "gy"),
            P(),
            P(),
            P(),
        ),
        out_specs=P(None, "dom", "gx", "gy"),
        check_vma=False,
    )
```

```python
import functools

import jax
import jax.numpy as jnp
from jax import lax
from jax.experimental import pallas as pl
from jax.experimental.pallas import tpu as pltpu
from jax.sharding import PartitionSpec as P

STEPS = 6
COURANT = 0.25
REGIONS = 16
BLOCK = 16
WIDE = 12
NEAR = 10
MESH = pl.DeviceIdType.MESH

f32 = jnp.float32


def lane_iota():
    return lax.broadcasted_iota(jnp.int32, (8, 128), 1)


def row_iota():
    return lax.broadcasted_iota(jnp.int32, (8, 128), 0)


def rows(z, x=0):
    return (z + 1) * BLOCK + 8 + x


def column(x):
    return pl.ds(rows(0, x), 8, stride=BLOCK)


def dy(v, lane):
    ahead = pltpu.roll(v, 127, 2)
    behind = pltpu.roll(v, 1, 2)
    ahead = jnp.where(lane == 127, jnp.concatenate([ahead[1:], ahead[:1]], 0), ahead)
    behind = jnp.where(lane == 0, jnp.concatenate([behind[2:], behind[:2]], 0), behind)
    return ahead - behind


def pick(bits, table):
    values = [table[i] for i in range(REGIONS)]
    for bit in bits:
        values = [jnp.where(bit, values[2 * i + 1], values[2 * i]) for i in range(len(values) // 2)]
    return values[0]


def pack(tiles, width, lane):
    out = jnp.zeros((8, 128), f32)
    for k, tile in enumerate(tiles):
        moved = pltpu.roll(tile, 2 * width * k + width, 1)
        out = jnp.where((lane >= 2 * width * k) & (lane < 2 * width * (k + 1)), moved, out)
    return out


def unpack(tile, k, width):
    return pltpu.roll(tile, (128 - (2 * width * k + width)) % 128, 1)


def kernel(
    sizes, state_in, source_in, floor_in, region_in, lame_in, shear_in, buoy_in, out,
    state, source, floor, region, lame, shear, buoy,
    S, V, L, M, B, SRC, LX, MX, LZ, MZ, SX, ys, yr, xs0, xr0, zs0, zr0, ds, dr, xs, xr, zs, zr, es, er,
    in_sem, out_sem, first_send, first_recv, send_sem, recv_sem,
):
    n_dom, n_gx, n_gy = sizes
    dom, gx, gy = lax.axis_index("dom"), lax.axis_index("gx"), lax.axis_index("gy")
    lane, sub = lane_iota(), row_iota()
    zero = jnp.zeros((8, 128), f32)

    loads = [
        pltpu.make_async_copy(src, dst, in_sem.at[i])
        for i, (src, dst) in enumerate((
            (region_in, region), (floor_in, floor), (source_in, source), (state_in, state),
            (lame_in, lame), (shear_in, shear), (buoy_in, buoy)))
    ]
    for load in loads:
        load.start()

    sides = (-1, 1)
    there = [gx > 0, gx < n_gx - 1]
    z_there = [dom > 0, dom < n_dom - 1]

    def at(dz, dx, dyy):
        return (lax.rem(dom + dz + n_dom, n_dom), gx + dx, lax.rem(gy + dyy + n_gy, n_gy))

    def reach(i, then):
        pl.when(there[i])(then)

    barrier = pltpu.get_barrier_semaphore()

    def greet(*way):
        pl.semaphore_signal(barrier, inc=1, device_id=at(*way), device_id_type=MESH)

    for i, dx in enumerate(sides):
        @functools.partial(reach, i)
        def _(dx=dx):
            for way in ((0, dx, 0), (-1, dx, 0), (1, dx, 0), (0, dx, -1), (0, dx, 1)):
                greet(*way)
    for way in [(a, 0, b) for a in (-1, 0, 1) for b in (-1, 0, 1) if a or b]:
        greet(*way)

    for i in range(2):
        @pl.when(jnp.logical_not(there[i]))
        def _(i=i):
            xr0[i] = jnp.zeros(xr0.shape[1:], f32)
            for j in range(2):
                dr[i, j] = zero
            for slot in range(2):
                xr[slot, i] = jnp.zeros(xr.shape[2:], f32)
                for j in range(2):
                    er[slot, i, j] = zero

    for z in range(-1, 9):
        for f in range(3):
            for t in range(3):
                V[f, t, pl.ds(rows(z, -8), 8), :] = zero
    for z in (-1, 8):
        for f in range(3):
            for t in range(3):
                V[f, t, pl.ds(rows(z), 8), :] = zero
    for t in range(3):
        for s in (6, 7):
            SRC[t, pl.ds(8 * s, 8), :] = zero

    for load in loads[:4]:
        load.wait()

    def side_by_side(parts, t, first=None):
        tile = zero if first is None else first
        for k, v in parts:
            shift = (WIDE * k + (WIDE if t else 0)) % 128
            v = pltpu.roll(v, shift, 1) if shift else v
            tile = jnp.where((lane >= WIDE * k) & (lane < WIDE * (k + 1)), v, tile)
        return tile

    def cut(t):
        return slice(128 * t, 128 * t + 128)

    for i in range(2):
        for z in range(8):
            parts = [(f, state[f, z, :, cut(i)]) for f in range(9)] + [(9, region[z, :, cut(i)].astype(f32))]
            ys[i, z] = side_by_side(parts, i)
        parts = [(s, source[s, :, cut(i)]) for s in range(STEPS)] + [(STEPS, floor[:, cut(i)].astype(f32))]
        ys[i, 8] = side_by_side(parts, i)

    def x_first(i):
        return pltpu.make_async_remote_copy(
            src_ref=xs0.at[i], dst_ref=xr0.at[1 - i], send_sem=first_send.at[i], recv_sem=first_recv.at[1 - i],
            device_id=at(0, sides[i], 0), device_id_type=MESH)

    def z_first(i):
        return pltpu.make_async_remote_copy(
            src_ref=zs0.at[i], dst_ref=zr0.at[1 - i], send_sem=first_send.at[2 + i], recv_sem=first_recv.at[3 - i],
            device_id=at(sides[i], 0, 0), device_id_type=MESH)

    def y_first(i):
        return pltpu.make_async_remote_copy(
            src_ref=ys.at[i], dst_ref=yr.at[1 - i], send_sem=first_send.at[4 + i], recv_sem=first_recv.at[5 - i],
            device_id=at(0, 0, sides[i]), device_id_type=MESH)

    def xy_first(i, j):
        k, back = 6 + 2 * i + j, 6 + 2 * (1 - i) + 1 - j
        return pltpu.make_async_remote_copy(
            src_ref=ds.at[i, j], dst_ref=dr.at[1 - i, 1 - j], send_sem=first_send.at[k], recv_sem=first_recv.at[back],
            device_id=at(0, sides[i], sides[j]), device_id_type=MESH)

    def zy_first(i, j):
        k, back = 10 + 2 * i + j, 10 + 2 * (1 - i) + 1 - j
        return pltpu.make_async_remote_copy(
            src_ref=ds.at[2 + i, j], dst_ref=dr.at[3 - i, 1 - j], send_sem=first_send.at[k], recv_sem=first_recv.at[back],
            device_id=at(sides[i], 0, sides[j]), device_id_type=MESH)

    pl.semaphore_wait(barrier, 8 + 5 * (there[0].astype(jnp.int32) + there[1].astype(jnp.int32)))
    for i in range(2):
        y_first(i).start()
    for load in loads[4:]:
        load.wait()

    scale = 0.5 * COURANT
    tables = [[t[k] * scale for k in range(REGIONS)] for t in (lame, shear, buoy)]

    def materials(number, seafloor, z, inside):
        bits = [(number & (1 << k)) != 0 for k in range(4)]
        solid = (dom * 8 + z) >= seafloor
        lam, mu, b = (pick(bits, t) for t in tables)
        mu = jnp.where(solid, mu, 0.0)
        if inside is not None:
            lam, mu, b = (jnp.where(inside, v, 0.0) for v in (lam, mu, b))
        return lam, mu, b, solid

    for t in range(2):
        seafloor = floor[:, cut(t)]
        for s in range(STEPS):
            SRC[t, pl.ds(8 * s, 8), :] = jnp.where(dom == 0, source[s, :, cut(t)], 0.0)
        for z in range(8):
            lam, mu, b, solid = materials(region[z, :, cut(t)], seafloor, z, None)
            r = pl.ds(8 * z, 8)
            L[t, r, :], M[t, r, :], B[t, r, :] = lam, mu, b
            for f in range(9):
                v = state[f, z, :, cut(t)]
                if f < 3:
                    V[f, t, pl.ds(rows(z), 8), :] = v
                else:
                    S[f - 3, t, pl.ds(rows(z), 8), :] = jnp.where(solid, v, 0.0) if f >= 6 else v

    x_fields, z_fields = (0, 3, 4), (2, 4, 5)
    for i, x in ((0, 0), (1, 7)):
        parts = [S[f, 0:2, column(x), :] for f in x_fields]
        parts += [m[0:2, pl.ds(x, 8, stride=8), :] for m in (L, M, SRC)]
        for k, v in enumerate(parts):
            xs0[i, 2 * k : 2 * k + 2] = v
        for j in range(2):
            ds[i, j] = side_by_side([(k, v[j]) for k, v in enumerate(parts)], j)

        @functools.partial(reach, i)
        def _(i=i):
            x_first(i).start()
            for j in range(2):
                xy_first(i, j).start()
    for i, z in ((0, 0), (1, 7)):
        parts = [S[f, 0:2, pl.ds(rows(z), 8), :] for f in z_fields]
        parts += [m[0:2, pl.ds(8 * z, 8), :] for m in (L, M)]
        for k, v in enumerate(parts):
            zs0[i, 2 * k : 2 * k + 2] = v
        z_first(i).start()
        for j in range(2):
            ds[2 + i, j] = side_by_side([(k, v[j]) for k, v in enumerate(parts)], j)
            zy_first(i, j).start()

    left = (lane >= 128 - WIDE) & (gy > 0)
    right = (lane < WIDE) & (gy < n_gy - 1)
    inside = left | right

    def margin(low, high, f):
        shift_r = (128 - WIDE * f) % 128
        shift_l = (256 - WIDE - WIDE * f) % 128
        a = pltpu.roll(high, shift_r, 1) if shift_r else high
        c = pltpu.roll(low, shift_l, 1) if shift_l else low
        return jnp.where(left, c, jnp.where(right, a, 0.0))

    for i in range(2):
        y_first(1 - i).wait_recv()
    seafloor = margin(yr[0, 8], yr[1, 8], STEPS).astype(jnp.int32)
    for s in range(STEPS):
        SRC[2, pl.ds(8 * s, 8), :] = jnp.where(dom == 0, margin(yr[0, 8], yr[1, 8], s), 0.0)
    for z in range(8):
        low, high = yr[0, z], yr[1, z]
        lam, mu, b, solid = materials(margin(low, high, 9).astype(jnp.int32), seafloor, z, inside)
        r = pl.ds(8 * z, 8)
        L[2, r, :], M[2, r, :], B[2, r, :] = lam, mu, b
        for f in range(9):
            v = margin(low, high, f)
            if f < 3:
                V[f, 2, pl.ds(rows(z), 8), :] = v
            else:
                S[f - 3, 2, pl.ds(rows(z), 8), :] = jnp.where(solid, v, 0.0) if f >= 6 else v

    for i in range(2):
        z_first(1 - i).wait_recv()
        for j in range(2):
            zy_first(1 - i, 1 - j).wait_recv()

        @functools.partial(reach, i)
        def _(i=i):
            x_first(1 - i).wait_recv()
            for j in range(2):
                xy_first(1 - i, 1 - j).wait_recv()

    for i, x in ((0, -1), (1, 8)):
        low, high = dr[i, 0], dr[i, 1]
        for k in range(6):
            v = jnp.concatenate([xr0[i, 2 * k : 2 * k + 2], margin(low, high, k)[None]], 0)
            if k < 3:
                S[x_fields[k], :, column(x), :] = v
            else:
                (LX, MX, SX)[k - 3][i] = v
    for i, z in ((0, -1), (1, 8)):
        low, high = dr[2 + i, 0], dr[2 + i, 1]
        for k in range(5):
            v = jnp.concatenate([zr0[i, 2 * k : 2 * k + 2], margin(low, high, k)[None]], 0)
            v = jnp.where(z_there[i], v, 0.0)
            if k < 3:
                S[z_fields[k], :, pl.ds(rows(z), 8), :] = v
            else:
                (LZ, MZ)[k - 3][i] = v

    def x_copy(i, slot, last):
        src, dst = xs.at[i], xr.at[slot, 1 - i]
        if last:
            src, dst = src.at[0:7], dst.at[0:7]
        return pltpu.make_async_remote_copy(
            src_ref=src, dst_ref=dst, send_sem=send_sem.at[i], recv_sem=recv_sem.at[slot, 1 - i],
            device_id=at(0, sides[i], 0), device_id_type=MESH)

    def z_copy(i, slot, last):
        src, dst = zs.at[i], zr.at[slot, 1 - i]
        if last:
            src, dst = src.at[0:7], dst.at[0:7]
        return pltpu.make_async_remote_copy(
            src_ref=src, dst_ref=dst, send_sem=send_sem.at[2 + i], recv_sem=recv_sem.at[slot, 3 - i],
            device_id=at(sides[i], 0, 0), device_id_type=MESH)

    def e_copy(i, j, slot):
        return pltpu.make_async_remote_copy(
            src_ref=es.at[i, j], dst_ref=er.at[slot, 1 - i, 1 - j], send_sem=send_sem.at[4 + 2 * i + j],
            recv_sem=recv_sem.at[slot, 4 + 2 * (1 - i) + 1 - j],
            device_id=at(sides[j], sides[i], 0), device_id_type=MESH)

    def fill(buffer, i, near, far):
        for f, v in enumerate(near):
            buffer[i, 2 * f : 2 * f + 2] = v[0:2]
        buffer[i, 6] = pack([v[2] for v in near + far], NEAR, lane)
        for f, v in enumerate(far):
            buffer[i, 7 + 2 * f : 9 + 2 * f] = v[0:2]

    def opened(buffer, slot, i, k):
        packed = buffer[slot, i, 6]
        start = 2 * k if k < 3 else 2 * k + 1
        return jnp.concatenate([buffer[slot, i, start : start + 2], unpack(packed, k, NEAR)[None]], 0)

    def store(f):
        return pltpu.make_async_copy(state.at[f], out.at[f], out_sem.at[f])

    def step(s, last):
        slot = s % 2 if last else lax.rem(s, 2)

        added = SRC[:, pl.ds(8 * s if last else pl.multiple_of(8 * s, 8), 8), :]
        for f in range(3):
            S[f, :, pl.ds(rows(0), 8), :] += added
        for i, x in ((0, -1), (1, 8)):
            S[0, :, pl.ds(rows(0, x), 1), :] += SX[i, :, pl.ds(s, 1), :]

        for z in range(8):
            own = pl.ds(rows(z), 8)
            after, before = pl.ds(rows(z, 1), 8), pl.ds(rows(z, -1), 8)
            above, below = pl.ds(rows(z + 1), 8), pl.ds(rows(z - 1), 8)

            def dx(f):
                return S[f, :, after, :] - S[f, :, before, :]

            def dz(f):
                return S[f, :, above, :] - S[f, :, below, :]

            b = B[:, pl.ds(8 * z, 8), :]
            V[0, :, own, :] -= b * (dx(0) + dy(S[3, :, own, :], lane) + dz(4))
            V[1, :, own, :] -= b * (dx(3) + dy(S[1, :, own, :], lane) + dz(5))
            V[2, :, own, :] -= b * (dx(4) + dy(S[5, :, own, :], lane) + dz(2))

        for i, (x, inner) in enumerate(((0, 1), (7, 6))):
            fill(xs, i, [V[f, :, column(x), :] for f in range(3)], [V[f, :, column(inner), :] for f in range(3)])

            @functools.partial(reach, i)
            def _(i=i):
                x_copy(i, slot, last).start()
        if not last:
            for i in range(2):
                for j in range(2):
                    r = rows(7 * j, 7 * i)
                    for k, f in enumerate((0, 2)):
                        for t in range(3):
                            es[i, j, pl.ds(3 * k + t, 1), :] = V[f, t, pl.ds(r, 1), :]

                @functools.partial(reach, i)
                def _(i=i):
                    for j in range(2):
                        e_copy(i, j, slot).start()
        for i, (z, inner) in enumerate(((0, 1), (7, 6))):
            fill(zs, i, [V[f, :, pl.ds(rows(z), 8), :] for f in range(3)],
                 [V[f, :, pl.ds(rows(inner), 8), :] for f in range(3)])
            z_copy(i, slot, last).start()

        for z in range(8):
            own = pl.ds(rows(z), 8)
            after, before = pl.ds(rows(z, 1), 8), pl.ds(rows(z, -1), 8)
            above, below = pl.ds(rows(z + 1), 8), pl.ds(rows(z - 1), 8)
            v = [V[f, :, own, :] for f in range(3)]
            dxs = [V[f, :, after, :] - V[f, :, before, :] for f in range(3)]
            dzs = [V[f, :, above, :] - V[f, :, below, :] for f in range(3)]
            dys = [dy(v[f], lane) for f in range(3)]
            lam, mu = L[:, pl.ds(8 * z, 8), :], M[:, pl.ds(8 * z, 8), :]
            spread = lam * (dxs[0] + dys[1] + dzs[2])
            mu2 = mu + mu
            S[0, :, own, :] -= spread + mu2 * dxs[0]
            S[1, :, own, :] -= spread + mu2 * dys[1]
            S[2, :, own, :] -= spread + mu2 * dzs[2]
            S[3, :, own, :] -= mu * (dys[0] + dxs[1])
            S[4, :, own, :] -= mu * (dzs[0] + dxs[2])
            S[5, :, own, :] -= mu * (dzs[1] + dys[2])
            if last:
                for f in range(3):
                    for t in range(2):
                        state[f, z, :, cut(t)] = v[f][t]
        if last:
            for f in range(3):
                store(f).start()

        z_got = []
        for i, z in ((0, 0), (1, 7)):
            z_copy(1 - i, slot, last).wait_recv()
            near = [opened(zr, slot, i, k) for k in range(3)]
            z_got.append(near)
            sign = jnp.where(z_there[i], (-1.0, 1.0)[i], 0.0)
            own = pl.ds(rows(z), 8)
            lam, mu = L[:, pl.ds(8 * z, 8), :], M[:, pl.ds(8 * z, 8), :]
            slope = [sign * v for v in near]
            spread = lam * slope[2]
            S[0, :, own, :] -= spread
            S[1, :, own, :] -= spread
            S[2, :, own, :] -= spread + (mu + mu) * slope[2]
            S[4, :, own, :] -= mu * slope[0]
            S[5, :, own, :] -= mu * slope[1]

        for i in range(2):
            @functools.partial(reach, i)
            def _(i=i):
                x_copy(1 - i, slot, last).wait_recv()
                if not last:
                    for j in range(2):
                        e_copy(1 - i, 1 - j, slot).wait_recv()

        x_got = []
        for i, x, sign in ((0, 0, -1.0), (1, 7, 1.0)):
            near = [opened(xr, slot, i, k) for k in range(3)]
            x_got.append(near)
            lam, mu = L[:, pl.ds(x, 8, stride=8), :], M[:, pl.ds(x, 8, stride=8), :]
            slope = [sign * v for v in near]
            spread = lam * slope[0]
            S[0, :, column(x), :] -= spread + (mu + mu) * slope[0]
            S[1, :, column(x), :] -= spread
            S[2, :, column(x), :] -= spread
            S[3, :, column(x), :] -= mu * slope[1]
            S[4, :, column(x), :] -= mu * slope[2]

        if not last:
            for i, x, sign in ((0, 0, -1.0), (1, 7, 1.0)):
                near, far = x_got[i], [opened(xr, slot, i, k) for k in range(3, 6)]
                lam, mu = LX[i], MX[i]
                dxs = [sign * (far[f] - V[f, :, column(x), :]) for f in range(3)]
                dzs = {}
                for k, f in enumerate((0, 2)):
                    top, bottom = (
                        jnp.where(z_there[j], jnp.stack([er[slot, i, j, pl.ds(3 * k + t, 1), :] for t in range(3)]), 0.0)
                        for j in range(2)
                    )
                    down = jnp.where(sub == 0, top, pltpu.roll(near[f], 1, 1))
                    up = jnp.where(sub == 7, bottom, pltpu.roll(near[f], 7, 1))
                    dzs[f] = up - down
                trace = dxs[0] + dy(near[1], lane) + dzs[2]
                beyond = column(-1 if i == 0 else 8)
                S[0, :, beyond, :] -= lam * trace + (mu + mu) * dxs[0]
                S[3, :, beyond, :] -= mu * (dy(near[0], lane) + dxs[1])
                S[4, :, beyond, :] -= mu * (dzs[0] + dxs[2])
            for i, z, sign in ((0, 0, -1.0), (1, 7, 1.0)):
                near, far = z_got[i], [opened(zr, slot, i, k) for k in range(3, 6)]
                lam, mu = LZ[i], MZ[i]
                dzs = [sign * (far[f] - V[f, :, pl.ds(rows(z), 8), :]) for f in range(3)]
                dxs = {}
                for k, f in enumerate((0, 2)):
                    first, final = (
                        jnp.stack([er[slot, j, i, pl.ds(3 * k + t, 1), :] for t in range(3)]) for j in range(2)
                    )
                    behind = jnp.where(sub == 0, first, pltpu.roll(near[f], 1, 1))
                    ahead = jnp.where(sub == 7, final, pltpu.roll(near[f], 7, 1))
                    dxs[f] = ahead - behind
                trace = dxs[0] + dy(near[1], lane) + dzs[2]
                beyond = pl.ds(rows(-1 if i == 0 else 8), 8)
                S[2, :, beyond, :] -= lam * trace + (mu + mu) * dzs[2]
                S[4, :, beyond, :] -= mu * (dzs[0] + dxs[2])
                S[5, :, beyond, :] -= mu * (dzs[1] + dy(near[2], lane))

        for i in range(2):
            z_copy(i, slot, last).wait_send()

            @functools.partial(reach, i)
            def _(i=i):
                x_copy(i, slot, last).wait_send()
                if not last:
                    for j in range(2):
                        e_copy(i, j, slot).wait_send()

    def body(s, carry):
        step(s, False)
        return carry

    lax.fori_loop(0, STEPS - 1, body, 0)
    step(STEPS - 1, True)

    for f in range(6):
        for z in range(8):
            for t in range(2):
                state[3 + f, z, :, cut(t)] = S[f, t, pl.ds(rows(z), 8), :]
        store(3 + f).start()

    for i in range(2):
        y_first(i).wait_send()
        z_first(i).wait_send()
        for j in range(2):
            zy_first(i, j).wait_send()

        @functools.partial(reach, i)
        def _(i=i):
            x_first(i).wait_send()
            for j in range(2):
                xy_first(i, j).wait_send()
    for f in range(9):
        store(f).wait()


def solution(mesh):
    sizes = (mesh.shape["dom"], mesh.shape["gx"], mesh.shape["gy"])

    def on_device(state, source, floor, region, lame, shear, buoy):
        hbm = pl.BlockSpec(memory_space=pltpu.HBM)
        block, column_tile = (8, 128), (3, 8, 128)
        return pl.pallas_call(
            functools.partial(kernel, sizes),
            out_shape=jax.ShapeDtypeStruct(state.shape, f32),
            in_specs=[hbm] * 7,
            out_specs=hbm,
            scratch_shapes=[
                pltpu.VMEM(state.shape, f32),
                pltpu.VMEM(source.shape, f32),
                pltpu.VMEM(floor.shape, jnp.int32),
                pltpu.VMEM(region.shape, jnp.int32),
                pltpu.SMEM(lame.shape, f32),
                pltpu.SMEM(shear.shape, f32),
                pltpu.SMEM(buoy.shape, f32),
                pltpu.VMEM((6, 3, 10 * BLOCK, 128), f32),
                pltpu.VMEM((3, 3, 10 * BLOCK, 128), f32),
                pltpu.VMEM((3, 64, 128), f32),
                pltpu.VMEM((3, 64, 128), f32),
                pltpu.VMEM((3, 64, 128), f32),
                pltpu.VMEM((3, 64, 128), f32),
                pltpu.VMEM((2,) + column_tile, f32),
                pltpu.VMEM((2,) + column_tile, f32),
                pltpu.VMEM((2,) + column_tile, f32),
                pltpu.VMEM((2,) + column_tile, f32),
                pltpu.VMEM((2,) + column_tile, f32),
                pltpu.VMEM((2, 9) + block, f32),
                pltpu.VMEM((2, 9) + block, f32),
                pltpu.VMEM((2, 12) + block, f32),
                pltpu.VMEM((2, 12) + block, f32),
                pltpu.VMEM((2, 10) + block, f32),
                pltpu.VMEM((2, 10) + block, f32),
                pltpu.VMEM((4, 2) + block, f32),
                pltpu.VMEM((4, 2) + block, f32),
                pltpu.VMEM((2, 13) + block, f32),
                pltpu.VMEM((2, 2, 13) + block, f32),
                pltpu.VMEM((2, 13) + block, f32),
                pltpu.VMEM((2, 2, 13) + block, f32),
                pltpu.VMEM((2, 2) + block, f32),
                pltpu.VMEM((2, 2, 2) + block, f32),
                pltpu.SemaphoreType.DMA((7,)),
                pltpu.SemaphoreType.DMA((9,)),
                pltpu.SemaphoreType.DMA((14,)),
                pltpu.SemaphoreType.DMA((14,)),
                pltpu.SemaphoreType.DMA((8,)),
                pltpu.SemaphoreType.DMA((2, 8)),
            ],
            compiler_params=pltpu.CompilerParams(
                collective_id=0, has_side_effects=True, vmem_limit_bytes=60 * 1024 * 1024
            ),
        )(state, source, floor, region, lame, shear, buoy)

    return jax.shard_map(
        on_device,
        mesh=mesh,
        in_specs=(
            P(None, "dom", "gx", "gy"),
            P(None, "gx", "gy"),
            P("gx", "gy"),
            P("dom", "gx", "gy"),
            P(),
            P(),
            P(),
        ),
        out_specs=P(None, "dom", "gx", "gy"),
        check_vma=False,
    )
```

```python
import functools

import jax
import jax.numpy as jnp
from jax import lax
from jax.experimental import pallas as pl
from jax.experimental.pallas import tpu as pltpu
from jax.sharding import PartitionSpec as P

STEPS = 6
COURANT = 0.25
REGIONS = 16
BLOCK = 16
WIDE = 12
NEAR = 10
MESH = pl.DeviceIdType.MESH

f32 = jnp.float32


def lane_iota():
    return lax.broadcasted_iota(jnp.int32, (8, 128), 1)


def row_iota():
    return lax.broadcasted_iota(jnp.int32, (8, 128), 0)


def rows(z, x=0):
    return (z + 1) * BLOCK + 8 + x


def column(x):
    return pl.ds(rows(0, x), 8, stride=BLOCK)


def dy(v, lane):
    ahead = pltpu.roll(v, 127, 2)
    behind = pltpu.roll(v, 1, 2)
    ahead = jnp.where(lane == 127, jnp.concatenate([ahead[1:], ahead[:1]], 0), ahead)
    behind = jnp.where(lane == 0, jnp.concatenate([behind[2:], behind[:2]], 0), behind)
    return ahead - behind


def pick(bits, table):
    values = [table[i] for i in range(REGIONS)]
    for bit in bits:
        values = [jnp.where(bit, values[2 * i + 1], values[2 * i]) for i in range(len(values) // 2)]
    return values[0]


def pack(tiles, width, lane):
    out = jnp.zeros((8, 128), f32)
    for k, tile in enumerate(tiles):
        moved = pltpu.roll(tile, 2 * width * k + width, 1)
        out = jnp.where((lane >= 2 * width * k) & (lane < 2 * width * (k + 1)), moved, out)
    return out


def unpack(tile, k, width):
    return pltpu.roll(tile, (128 - (2 * width * k + width)) % 128, 1)


def kernel(
    sizes, state_in, source_in, floor_in, region_in, lame_in, shear_in, buoy_in, out,
    state, source, floor, region, lame, shear, buoy,
    S, V, L, M, B, SRC, LX, MX, LZ, MZ, SX, ys, yr, xs0, xr0, zs0, zr0, ds, dr, xs, rr, xr, zs, zr, es, er,
    in_sem, out_sem, first_send, first_recv, send_sem, recv_sem, x_send, x_recv,
):
    n_dom, n_gx, n_gy = sizes
    dom, gx, gy = lax.axis_index("dom"), lax.axis_index("gx"), lax.axis_index("gy")
    lane, sub = lane_iota(), row_iota()
    zero = jnp.zeros((8, 128), f32)

    loads = [
        pltpu.make_async_copy(src, dst, in_sem.at[i])
        for i, (src, dst) in enumerate((
            (region_in, region), (floor_in, floor), (source_in, source), (state_in, state),
            (lame_in, lame), (shear_in, shear), (buoy_in, buoy)))
    ]
    for load in loads:
        load.start()

    sides = (-1, 1)
    there = [gx > 0, gx < n_gx - 1]
    z_there = [dom > 0, dom < n_dom - 1]

    half, other = lax.div(gy, 2), 1 - 2 * lax.rem(gx, 2)
    relay_gy = gy + 2 - 4 * half
    relay_gx = [gx + (1 - half) * other, gx + half * other]
    serves = [relay_gx[1] > 0, relay_gx[0] < n_gx - 1]

    def relay(i):
        return (dom, relay_gx[i], relay_gy)

    def target(i):
        return (dom, relay_gx[1 - i] + sides[i], relay_gy)

    def server(i):
        theirs = gx + sides[i]
        return (dom, theirs + ((1 - half), half)[1 - i] * (1 - 2 * lax.rem(theirs, 2)), relay_gy)

    def at(dz, dx, dyy):
        return (lax.rem(dom + dz + n_dom, n_dom), gx + dx, lax.rem(gy + dyy + n_gy, n_gy))

    def reach(i, then):
        pl.when(there[i])(then)

    barrier = pltpu.get_barrier_semaphore()

    def greet(*way):
        pl.semaphore_signal(barrier, inc=1, device_id=at(*way), device_id_type=MESH)

    for i, dx in enumerate(sides):
        @functools.partial(reach, i)
        def _(dx=dx):
            for way in ((0, dx, 0), (-1, dx, 0), (1, dx, 0), (0, dx, -1), (0, dx, 1)):
                greet(*way)
    for way in [(a, 0, b) for a in (-1, 0, 1) for b in (-1, 0, 1) if a or b]:
        greet(*way)
    for i in range(2):
        @functools.partial(reach, i)
        def _(i=i):
            pl.semaphore_signal(barrier, inc=1, device_id=server(i), device_id_type=MESH)

        @pl.when(serves[i])
        def _(i=i):
            pl.semaphore_signal(barrier, inc=1, device_id=relay(1 - i), device_id_type=MESH)

    for i in range(2):
        @pl.when(jnp.logical_not(there[i]))
        def _(i=i):
            xr0[i] = jnp.zeros(xr0.shape[1:], f32)
            for j in range(2):
                dr[i, j] = zero
            for slot in range(2):
                xr[slot, i] = jnp.zeros(xr.shape[2:], f32)
                for j in range(2):
                    er[slot, i, j] = zero

    for z in range(-1, 9):
        for f in range(3):
            for t in range(3):
                V[f, t, pl.ds(rows(z, -8), 8), :] = zero
    for z in (-1, 8):
        for f in range(3):
            for t in range(3):
                V[f, t, pl.ds(rows(z), 8), :] = zero
    for t in range(3):
        for s in (6, 7):
            SRC[t, pl.ds(8 * s, 8), :] = zero

    for load in loads[:4]:
        load.wait()

    def side_by_side(parts, t, first=None):
        tile = zero if first is None else first
        for k, v in parts:
            shift = (WIDE * k + (WIDE if t else 0)) % 128
            v = pltpu.roll(v, shift, 1) if shift else v
            tile = jnp.where((lane >= WIDE * k) & (lane < WIDE * (k + 1)), v, tile)
        return tile

    def cut(t):
        return slice(128 * t, 128 * t + 128)

    for i in range(2):
        for z in range(8):
            parts = [(f, state[f, z, :, cut(i)]) for f in range(9)] + [(9, region[z, :, cut(i)].astype(f32))]
            ys[i, z] = side_by_side(parts, i)
        parts = [(s, source[s, :, cut(i)]) for s in range(STEPS)] + [(STEPS, floor[:, cut(i)].astype(f32))]
        ys[i, 8] = side_by_side(parts, i)

    def x_first(i):
        return pltpu.make_async_remote_copy(
            src_ref=xs0.at[i], dst_ref=xr0.at[1 - i], send_sem=first_send.at[i], recv_sem=first_recv.at[1 - i],
            device_id=at(0, sides[i], 0), device_id_type=MESH)

    def z_first(i):
        return pltpu.make_async_remote_copy(
            src_ref=zs0.at[i], dst_ref=zr0.at[1 - i], send_sem=first_send.at[2 + i], recv_sem=first_recv.at[3 - i],
            device_id=at(sides[i], 0, 0), device_id_type=MESH)

    def y_first(i):
        return pltpu.make_async_remote_copy(
            src_ref=ys.at[i], dst_ref=yr.at[1 - i], send_sem=first_send.at[4 + i], recv_sem=first_recv.at[5 - i],
            device_id=at(0, 0, sides[i]), device_id_type=MESH)

    def xy_first(i, j):
        k, back = 6 + 2 * i + j, 6 + 2 * (1 - i) + 1 - j
        return pltpu.make_async_remote_copy(
            src_ref=ds.at[i, j], dst_ref=dr.at[1 - i, 1 - j], send_sem=first_send.at[k], recv_sem=first_recv.at[back],
            device_id=at(0, sides[i], sides[j]), device_id_type=MESH)

    def zy_first(i, j):
        k, back = 10 + 2 * i + j, 10 + 2 * (1 - i) + 1 - j
        return pltpu.make_async_remote_copy(
            src_ref=ds.at[2 + i, j], dst_ref=dr.at[3 - i, 1 - j], send_sem=first_send.at[k], recv_sem=first_recv.at[back],
            device_id=at(sides[i], 0, sides[j]), device_id_type=MESH)

    pl.semaphore_wait(barrier,
        8 + sum(6 * there[i].astype(jnp.int32) + serves[i].astype(jnp.int32) for i in range(2)))
    for i in range(2):
        y_first(i).start()
    for load in loads[4:]:
        load.wait()

    scale = 0.5 * COURANT
    tables = [[t[k] * scale for k in range(REGIONS)] for t in (lame, shear, buoy)]

    def materials(number, seafloor, z, inside):
        bits = [(number & (1 << k)) != 0 for k in range(4)]
        solid = (dom * 8 + z) >= seafloor
        lam, mu, b = (pick(bits, t) for t in tables)
        mu = jnp.where(solid, mu, 0.0)
        if inside is not None:
            lam, mu, b = (jnp.where(inside, v, 0.0) for v in (lam, mu, b))
        return lam, mu, b, solid

    for t in range(2):
        seafloor = floor[:, cut(t)]
        for s in range(STEPS):
            SRC[t, pl.ds(8 * s, 8), :] = jnp.where(dom == 0, source[s, :, cut(t)], 0.0)
        for z in range(8):
            lam, mu, b, solid = materials(region[z, :, cut(t)], seafloor, z, None)
            r = pl.ds(8 * z, 8)
            L[t, r, :], M[t, r, :], B[t, r, :] = lam, mu, b
            for f in range(9):
                v = state[f, z, :, cut(t)]
                if f < 3:
                    V[f, t, pl.ds(rows(z), 8), :] = v
                else:
                    S[f - 3, t, pl.ds(rows(z), 8), :] = jnp.where(solid, v, 0.0) if f >= 6 else v

    x_fields, z_fields = (0, 3, 4), (2, 4, 5)
    for i, x in ((0, 0), (1, 7)):
        parts = [S[f, 0:2, column(x), :] for f in x_fields]
        parts += [m[0:2, pl.ds(x, 8, stride=8), :] for m in (L, M, SRC)]
        for k, v in enumerate(parts):
            xs0[i, 2 * k : 2 * k + 2] = v
        for j in range(2):
            ds[i, j] = side_by_side([(k, v[j]) for k, v in enumerate(parts)], j)

        @functools.partial(reach, i)
        def _(i=i):
            x_first(i).start()
            for j in range(2):
                xy_first(i, j).start()
    for i, z in ((0, 0), (1, 7)):
        parts = [S[f, 0:2, pl.ds(rows(z), 8), :] for f in z_fields]
        parts += [m[0:2, pl.ds(8 * z, 8), :] for m in (L, M)]
        for k, v in enumerate(parts):
            zs0[i, 2 * k : 2 * k + 2] = v
        z_first(i).start()
        for j in range(2):
            ds[2 + i, j] = side_by_side([(k, v[j]) for k, v in enumerate(parts)], j)
            zy_first(i, j).start()

    left = (lane >= 128 - WIDE) & (gy > 0)
    right = (lane < WIDE) & (gy < n_gy - 1)
    inside = left | right

    def margin(low, high, f):
        shift_r = (128 - WIDE * f) % 128
        shift_l = (256 - WIDE - WIDE * f) % 128
        a = pltpu.roll(high, shift_r, 1) if shift_r else high
        c = pltpu.roll(low, shift_l, 1) if shift_l else low
        return jnp.where(left, c, jnp.where(right, a, 0.0))

    for i in range(2):
        y_first(1 - i).wait_recv()
    seafloor = margin(yr[0, 8], yr[1, 8], STEPS).astype(jnp.int32)
    for s in range(STEPS):
        SRC[2, pl.ds(8 * s, 8), :] = jnp.where(dom == 0, margin(yr[0, 8], yr[1, 8], s), 0.0)
    for z in range(8):
        low, high = yr[0, z], yr[1, z]
        lam, mu, b, solid = materials(margin(low, high, 9).astype(jnp.int32), seafloor, z, inside)
        r = pl.ds(8 * z, 8)
        L[2, r, :], M[2, r, :], B[2, r, :] = lam, mu, b
        for f in range(9):
            v = margin(low, high, f)
            if f < 3:
                V[f, 2, pl.ds(rows(z), 8), :] = v
            else:
                S[f - 3, 2, pl.ds(rows(z), 8), :] = jnp.where(solid, v, 0.0) if f >= 6 else v

    for i in range(2):
        z_first(1 - i).wait_recv()
        for j in range(2):
            zy_first(1 - i, 1 - j).wait_recv()

        @functools.partial(reach, i)
        def _(i=i):
            x_first(1 - i).wait_recv()
            for j in range(2):
                xy_first(1 - i, 1 - j).wait_recv()

    for i, x in ((0, -1), (1, 8)):
        low, high = dr[i, 0], dr[i, 1]
        for k in range(6):
            v = jnp.concatenate([xr0[i, 2 * k : 2 * k + 2], margin(low, high, k)[None]], 0)
            if k < 3:
                S[x_fields[k], :, column(x), :] = v
            else:
                (LX, MX, SX)[k - 3][i] = v
    for i, z in ((0, -1), (1, 8)):
        low, high = dr[2 + i, 0], dr[2 + i, 1]
        for k in range(5):
            v = jnp.concatenate([zr0[i, 2 * k : 2 * k + 2], margin(low, high, k)[None]], 0)
            v = jnp.where(z_there[i], v, 0.0)
            if k < 3:
                S[z_fields[k], :, pl.ds(rows(z), 8), :] = v
            else:
                (LZ, MZ)[k - 3][i] = v

    def part(ref, p):
        return ref.at[0:7] if p == 0 else ref.at[7:13]

    def x_leave(i, p, s):
        return pltpu.make_async_remote_copy(
            src_ref=part(xs.at[i], p), dst_ref=part(rr.at[s, i], p), send_sem=x_send.at[0, i, p],
            recv_sem=x_recv.at[s, 0, i, p], device_id=relay(i), device_id_type=MESH)

    def x_pass(i, p, s):
        return pltpu.make_async_remote_copy(
            src_ref=part(rr.at[s, i], p), dst_ref=part(xr.at[s % 2 if isinstance(s, int) else lax.rem(s, 2), 1 - i], p), send_sem=x_send.at[1, i, p],
            recv_sem=x_recv.at[s, 1, i, p], device_id=target(i), device_id_type=MESH)

    def z_copy(i, slot, last):
        src, dst = zs.at[i], zr.at[slot, 1 - i]
        if last:
            src, dst = src.at[0:7], dst.at[0:7]
        return pltpu.make_async_remote_copy(
            src_ref=src, dst_ref=dst, send_sem=send_sem.at[2 + i], recv_sem=recv_sem.at[slot, 3 - i],
            device_id=at(sides[i], 0, 0), device_id_type=MESH)

    def e_copy(i, j, slot):
        return pltpu.make_async_remote_copy(
            src_ref=es.at[i, j], dst_ref=er.at[slot, 1 - i, 1 - j], send_sem=send_sem.at[4 + 2 * i + j],
            recv_sem=recv_sem.at[slot, 4 + 2 * (1 - i) + 1 - j],
            device_id=at(sides[j], sides[i], 0), device_id_type=MESH)

    def fill(buffer, i, near, far):
        for f, v in enumerate(near):
            buffer[i, 2 * f : 2 * f + 2] = v[0:2]
        buffer[i, 6] = pack([v[2] for v in near + far], NEAR, lane)
        for f, v in enumerate(far):
            buffer[i, 7 + 2 * f : 9 + 2 * f] = v[0:2]

    def opened(buffer, slot, i, k):
        packed = buffer[slot, i, 6]
        start = 2 * k if k < 3 else 2 * k + 1
        return jnp.concatenate([buffer[slot, i, start : start + 2], unpack(packed, k, NEAR)[None]], 0)

    def store(f):
        return pltpu.make_async_copy(state.at[f], out.at[f], out_sem.at[f])

    def step(s, last):
        slot = s % 2 if last else lax.rem(s, 2)
        parts = (0,) if last else (0, 1)

        added = SRC[:, pl.ds(8 * s if last else pl.multiple_of(8 * s, 8), 8), :]
        for f in range(3):
            S[f, :, pl.ds(rows(0), 8), :] += added
        for i, x in ((0, -1), (1, 8)):
            S[0, :, pl.ds(rows(0, x), 1), :] += SX[i, :, pl.ds(s, 1), :]

        for z in range(8):
            own = pl.ds(rows(z), 8)
            after, before = pl.ds(rows(z, 1), 8), pl.ds(rows(z, -1), 8)
            above, below = pl.ds(rows(z + 1), 8), pl.ds(rows(z - 1), 8)

            def dx(f):
                return S[f, :, after, :] - S[f, :, before, :]

            def dz(f):
                return S[f, :, above, :] - S[f, :, below, :]

            b = B[:, pl.ds(8 * z, 8), :]
            V[0, :, own, :] -= b * (dx(0) + dy(S[3, :, own, :], lane) + dz(4))
            V[1, :, own, :] -= b * (dx(3) + dy(S[1, :, own, :], lane) + dz(5))
            V[2, :, own, :] -= b * (dx(4) + dy(S[5, :, own, :], lane) + dz(2))

        for i, (x, inner) in enumerate(((0, 1), (7, 6))):
            fill(xs, i, [V[f, :, column(x), :] for f in range(3)], [V[f, :, column(inner), :] for f in range(3)])

            @functools.partial(reach, i)
            def _(i=i):
                for p in parts:
                    x_leave(i, p, s).start()
        if not last:
            for i in range(2):
                for j in range(2):
                    r = rows(7 * j, 7 * i)
                    for k, f in enumerate((0, 2)):
                        for t in range(3):
                            es[i, j, pl.ds(3 * k + t, 1), :] = V[f, t, pl.ds(r, 1), :]

                @functools.partial(reach, i)
                def _(i=i):
                    for j in range(2):
                        e_copy(i, j, slot).start()
        for i, (z, inner) in enumerate(((0, 1), (7, 6))):
            fill(zs, i, [V[f, :, pl.ds(rows(z), 8), :] for f in range(3)],
                 [V[f, :, pl.ds(rows(inner), 8), :] for f in range(3)])
            z_copy(i, slot, last).start()

        for z in range(8):
            own = pl.ds(rows(z), 8)
            after, before = pl.ds(rows(z, 1), 8), pl.ds(rows(z, -1), 8)
            above, below = pl.ds(rows(z + 1), 8), pl.ds(rows(z - 1), 8)
            v = [V[f, :, own, :] for f in range(3)]
            dxs = [V[f, :, after, :] - V[f, :, before, :] for f in range(3)]
            dzs = [V[f, :, above, :] - V[f, :, below, :] for f in range(3)]
            dys = [dy(v[f], lane) for f in range(3)]
            lam, mu = L[:, pl.ds(8 * z, 8), :], M[:, pl.ds(8 * z, 8), :]
            spread = lam * (dxs[0] + dys[1] + dzs[2])
            mu2 = mu + mu
            S[0, :, own, :] -= spread + mu2 * dxs[0]
            S[1, :, own, :] -= spread + mu2 * dys[1]
            S[2, :, own, :] -= spread + mu2 * dzs[2]
            S[3, :, own, :] -= mu * (dys[0] + dxs[1])
            S[4, :, own, :] -= mu * (dzs[0] + dxs[2])
            S[5, :, own, :] -= mu * (dzs[1] + dys[2])
            if last:
                for f in range(3):
                    for t in range(2):
                        state[f, z, :, cut(t)] = v[f][t]
        if last:
            for f in range(3):
                store(f).start()

        for p in parts:
            for i in range(2):
                @pl.when(serves[i])
                def _(i=i, p=p):
                    x_leave(i, p, s).wait_recv()
                    x_pass(i, p, s).start()

        z_got = []
        for i, z in ((0, 0), (1, 7)):
            z_copy(1 - i, slot, last).wait_recv()
            near = [opened(zr, slot, i, k) for k in range(3)]
            z_got.append(near)
            sign = jnp.where(z_there[i], (-1.0, 1.0)[i], 0.0)
            own = pl.ds(rows(z), 8)
            lam, mu = L[:, pl.ds(8 * z, 8), :], M[:, pl.ds(8 * z, 8), :]
            slope = [sign * v for v in near]
            spread = lam * slope[2]
            S[0, :, own, :] -= spread
            S[1, :, own, :] -= spread
            S[2, :, own, :] -= spread + (mu + mu) * slope[2]
            S[4, :, own, :] -= mu * slope[0]
            S[5, :, own, :] -= mu * slope[1]

        for i in range(2):
            @functools.partial(reach, i)
            def _(i=i):
                for p in parts:
                    x_pass(1 - i, p, s).wait_recv()
                if not last:
                    for j in range(2):
                        e_copy(1 - i, 1 - j, slot).wait_recv()

        x_got = []
        for i, x, sign in ((0, 0, -1.0), (1, 7, 1.0)):
            near = [opened(xr, slot, i, k) for k in range(3)]
            x_got.append(near)
            lam, mu = L[:, pl.ds(x, 8, stride=8), :], M[:, pl.ds(x, 8, stride=8), :]
            slope = [sign * v for v in near]
            spread = lam * slope[0]
            S[0, :, column(x), :] -= spread + (mu + mu) * slope[0]
            S[1, :, column(x), :] -= spread
            S[2, :, column(x), :] -= spread
            S[3, :, column(x), :] -= mu * slope[1]
            S[4, :, column(x), :] -= mu * slope[2]

        if not last:
            for i, x, sign in ((0, 0, -1.0), (1, 7, 1.0)):
                near, far = x_got[i], [opened(xr, slot, i, k) for k in range(3, 6)]
                lam, mu = LX[i], MX[i]
                dxs = [sign * (far[f] - V[f, :, column(x), :]) for f in range(3)]
                dzs = {}
                for k, f in enumerate((0, 2)):
                    top, bottom = (
                        jnp.where(z_there[j], jnp.stack([er[slot, i, j, pl.ds(3 * k + t, 1), :] for t in range(3)]), 0.0)
                        for j in range(2)
                    )
                    down = jnp.where(sub == 0, top, pltpu.roll(near[f], 1, 1))
                    up = jnp.where(sub == 7, bottom, pltpu.roll(near[f], 7, 1))
                    dzs[f] = up - down
                trace = dxs[0] + dy(near[1], lane) + dzs[2]
                beyond = column(-1 if i == 0 else 8)
                S[0, :, beyond, :] -= lam * trace + (mu + mu) * dxs[0]
                S[3, :, beyond, :] -= mu * (dy(near[0], lane) + dxs[1])
                S[4, :, beyond, :] -= mu * (dzs[0] + dxs[2])
            for i, z, sign in ((0, 0, -1.0), (1, 7, 1.0)):
                near, far = z_got[i], [opened(zr, slot, i, k) for k in range(3, 6)]
                lam, mu = LZ[i], MZ[i]
                dzs = [sign * (far[f] - V[f, :, pl.ds(rows(z), 8), :]) for f in range(3)]
                dxs = {}
                for k, f in enumerate((0, 2)):
                    first, final = (
                        jnp.stack([er[slot, j, i, pl.ds(3 * k + t, 1), :] for t in range(3)]) for j in range(2)
                    )
                    behind = jnp.where(sub == 0, first, pltpu.roll(near[f], 1, 1))
                    ahead = jnp.where(sub == 7, final, pltpu.roll(near[f], 7, 1))
                    dxs[f] = ahead - behind
                trace = dxs[0] + dy(near[1], lane) + dzs[2]
                beyond = pl.ds(rows(-1 if i == 0 else 8), 8)
                S[2, :, beyond, :] -= lam * trace + (mu + mu) * dzs[2]
                S[4, :, beyond, :] -= mu * (dzs[0] + dxs[2])
                S[5, :, beyond, :] -= mu * (dzs[1] + dy(near[2], lane))

        for i in range(2):
            z_copy(i, slot, last).wait_send()

            @functools.partial(reach, i)
            def _(i=i):
                for p in parts:
                    x_leave(i, p, s).wait_send()
                if not last:
                    for j in range(2):
                        e_copy(i, j, slot).wait_send()

            @pl.when(serves[i])
            def _(i=i):
                for p in parts:
                    x_pass(i, p, s).wait_send()

    def body(s, carry):
        step(s, False)
        return carry

    lax.fori_loop(0, STEPS - 1, body, 0)
    step(STEPS - 1, True)

    for f in range(6):
        for z in range(8):
            for t in range(2):
                state[3 + f, z, :, cut(t)] = S[f, t, pl.ds(rows(z), 8), :]
        store(3 + f).start()

    for i in range(2):
        y_first(i).wait_send()
        z_first(i).wait_send()
        for j in range(2):
            zy_first(i, j).wait_send()

        @functools.partial(reach, i)
        def _(i=i):
            x_first(i).wait_send()
            for j in range(2):
                xy_first(i, j).wait_send()
    for f in range(9):
        store(f).wait()


def solution(mesh):
    sizes = (mesh.shape["dom"], mesh.shape["gx"], mesh.shape["gy"])

    def on_device(state, source, floor, region, lame, shear, buoy):
        hbm = pl.BlockSpec(memory_space=pltpu.HBM)
        block, column_tile = (8, 128), (3, 8, 128)
        return pl.pallas_call(
            functools.partial(kernel, sizes),
            out_shape=jax.ShapeDtypeStruct(state.shape, f32),
            in_specs=[hbm] * 7,
            out_specs=hbm,
            scratch_shapes=[
                pltpu.VMEM(state.shape, f32),
                pltpu.VMEM(source.shape, f32),
                pltpu.VMEM(floor.shape, jnp.int32),
                pltpu.VMEM(region.shape, jnp.int32),
                pltpu.SMEM(lame.shape, f32),
                pltpu.SMEM(shear.shape, f32),
                pltpu.SMEM(buoy.shape, f32),
                pltpu.VMEM((6, 3, 10 * BLOCK, 128), f32),
                pltpu.VMEM((3, 3, 10 * BLOCK, 128), f32),
                pltpu.VMEM((3, 64, 128), f32),
                pltpu.VMEM((3, 64, 128), f32),
                pltpu.VMEM((3, 64, 128), f32),
                pltpu.VMEM((3, 64, 128), f32),
                pltpu.VMEM((2,) + column_tile, f32),
                pltpu.VMEM((2,) + column_tile, f32),
                pltpu.VMEM((2,) + column_tile, f32),
                pltpu.VMEM((2,) + column_tile, f32),
                pltpu.VMEM((2,) + column_tile, f32),
                pltpu.VMEM((2, 9) + block, f32),
                pltpu.VMEM((2, 9) + block, f32),
                pltpu.VMEM((2, 12) + block, f32),
                pltpu.VMEM((2, 12) + block, f32),
                pltpu.VMEM((2, 10) + block, f32),
                pltpu.VMEM((2, 10) + block, f32),
                pltpu.VMEM((4, 2) + block, f32),
                pltpu.VMEM((4, 2) + block, f32),
                pltpu.VMEM((2, 13) + block, f32),
                pltpu.VMEM((STEPS, 2, 13) + block, f32),
                pltpu.VMEM((2, 2, 13) + block, f32),
                pltpu.VMEM((2, 13) + block, f32),
                pltpu.VMEM((2, 2, 13) + block, f32),
                pltpu.VMEM((2, 2) + block, f32),
                pltpu.VMEM((2, 2, 2) + block, f32),
                pltpu.SemaphoreType.DMA((7,)),
                pltpu.SemaphoreType.DMA((9,)),
                pltpu.SemaphoreType.DMA((14,)),
                pltpu.SemaphoreType.DMA((14,)),
                pltpu.SemaphoreType.DMA((8,)),
                pltpu.SemaphoreType.DMA((2, 8)),
                pltpu.SemaphoreType.DMA((2, 2, 2)),
                pltpu.SemaphoreType.DMA((STEPS, 2, 2, 2)),
            ],
            compiler_params=pltpu.CompilerParams(
                collective_id=0, has_side_effects=True, vmem_limit_bytes=60 * 1024 * 1024
            ),
        )(state, source, floor, region, lame, shear, buoy)

    return jax.shard_map(
        on_device,
        mesh=mesh,
        in_specs=(
            P(None, "dom", "gx", "gy"),
            P(None, "gx", "gy"),
            P("gx", "gy"),
            P("dom", "gx", "gy"),
            P(),
            P(),
            P(),
        ),
        out_specs=P(None, "dom", "gx", "gy"),
        check_vma=False,
    )
```

```python
import functools

import jax
import jax.numpy as jnp
from jax import lax
from jax.experimental import pallas as pl
from jax.experimental.pallas import tpu as pltpu
from jax.sharding import PartitionSpec as P

STEPS = 6
COURANT = 0.25
REGIONS = 16
BLOCK = 16
WIDE = 12
MIDDLE, LEFT, RIGHT = 0, 1, 2
FIRST_CUT, SECOND_CUT, SEAM = 86, 171 - 128, 64
MESH = pl.DeviceIdType.MESH

f32 = jnp.float32


def rows(z, x=0):
    return (z + 1) * BLOCK + 8 + x


def level(z):
    return pl.ds(rows(z), 8)


def column(x):
    return pl.ds(rows(0, x), 8, stride=BLOCK)


def dy(v):
    return pltpu.roll(v, 127, 1) - pltpu.roll(v, 1, 1)


def pick(bits, table):
    values = list(table)
    for bit in bits:
        values = [jnp.where(bit, values[2 * i + 1], values[2 * i]) for i in range(len(values) // 2)]
    return values[0]


def kernel(
    sizes, state_in, source_in, floor_in, region_in, lame_in, shear_in, buoy_in, out,
    state, source, floor, region, lame, shear, buoy,
    S, V, L, M, B, SRC, LX, MX, SX, LZ, MZ, ys, yr, xa, xra, xb, xrb, za, zra, zb, zrb, ds, dr,
    xs, xr, zs, zr, es, er, in_sem, out_sem, first_send, first_recv, send_sem, recv_sem,
):
    n_dom, n_gx, n_gy = sizes
    dom, gx, gy = lax.axis_index("dom"), lax.axis_index("gx"), lax.axis_index("gy")
    lane = lax.broadcasted_iota(jnp.int32, (8, 128), 1)
    sub = lax.broadcasted_iota(jnp.int32, (8, 128), 0)
    zero = jnp.zeros((8, 128), f32)

    loads = [
        pltpu.make_async_copy(src, dst, in_sem.at[i])
        for i, (src, dst) in enumerate((
            (region_in, region), (floor_in, floor), (source_in, source), (state_in, state),
            (lame_in, lame), (shear_in, shear), (buoy_in, buoy)))
    ]
    for load in loads:
        load.start()

    sides = (-1, 1)
    there = [gx > 0, gx < n_gx - 1]
    z_there = [dom > 0, dom < n_dom - 1]

    def at(dz, dx, dyy):
        return (lax.rem(dom + dz + n_dom, n_dom), gx + dx, lax.rem(gy + dyy + n_gy, n_gy))

    def reach(i, then):
        pl.when(there[i])(then)

    barrier = pltpu.get_barrier_semaphore()

    def greet(*way):
        pl.semaphore_signal(barrier, inc=1, device_id=at(*way), device_id_type=MESH)

    for i, dx in enumerate(sides):
        @functools.partial(reach, i)
        def _(dx=dx):
            for way in ((0, dx, 0), (-1, dx, 0), (1, dx, 0), (0, dx, -1), (0, dx, 1)):
                greet(*way)
    for way in [(a, 0, b) for a in (-1, 0, 1) for b in (-1, 0, 1) if a or b]:
        greet(*way)

    for i in range(2):
        @pl.when(jnp.logical_not(there[i]))
        def _(i=i):
            xra[i] = jnp.zeros(xra.shape[1:], f32)
            xrb[i] = jnp.zeros(xrb.shape[1:], f32)
            for j in range(2):
                dr[i, j] = zero
            for slot in range(2):
                for p in range(3):
                    xr[slot, p, i] = jnp.zeros(xr.shape[3:], f32)
                    for j in range(2):
                        er[slot, p, i, j] = jnp.zeros((2, 128), f32)

    for p in range(3):
        for f in range(3):
            for z in range(-1, 9):
                V[p, f, pl.ds(rows(z, -8), 8), :] = zero
            for z in (-1, 8):
                V[p, f, level(z), :] = zero

    for load in loads[:4]:
        load.wait()

    def side_by_side(parts, t):
        tile = zero
        for k, v in enumerate(parts):
            shift = (WIDE * k + (WIDE if t else 0)) % 128
            v = pltpu.roll(v, shift, 1) if shift else v
            tile = jnp.where((lane >= WIDE * k) & (lane < WIDE * (k + 1)), v, tile)
        return tile

    def cut(t):
        return slice(128 * t, 128 * t + 128)

    for i in range(2):
        for z in range(8):
            ys[i, z] = side_by_side(
                [state[f, z, :, cut(i)] for f in range(9)] + [region[z, :, cut(i)].astype(f32)], i)
        ys[i, 8] = side_by_side([source[s, :, cut(i)] for s in range(STEPS)] + [floor[:, cut(i)].astype(f32)], i)

    def remote(src, dst, send, recv, way):
        return pltpu.make_async_remote_copy(
            src_ref=src, dst_ref=dst, send_sem=send, recv_sem=recv, device_id=at(*way), device_id_type=MESH)

    def first(k, back, src, dst, way):
        return remote(src, dst, first_send.at[k], first_recv.at[back], way)

    def xa_first(i):
        return first(i, 1 - i, xa.at[i], xra.at[1 - i], (0, sides[i], 0))

    def za_first(i):
        return first(2 + i, 3 - i, za.at[i], zra.at[1 - i], (sides[i], 0, 0))

    def y_first(i):
        return first(4 + i, 5 - i, ys.at[i], yr.at[1 - i], (0, 0, sides[i]))

    def xy_first(i, j):
        return first(6 + 2 * i + j, 9 - 2 * i - j, ds.at[i, j], dr.at[1 - i, 1 - j], (0, sides[i], sides[j]))

    def zy_first(i, j):
        return first(10 + 2 * i + j, 13 - 2 * i - j, ds.at[2 + i, j], dr.at[3 - i, 1 - j], (sides[i], 0, sides[j]))

    def xb_first(i):
        return first(14 + i, 15 - i, xb.at[i], xrb.at[1 - i], (0, sides[i], 0))

    def zb_first(i):
        return first(16 + i, 17 - i, zb.at[i], zrb.at[1 - i], (sides[i], 0, 0))

    for load in loads[4:]:
        load.wait()
    scale = 0.5 * COURANT
    tables = [[t[k] * scale for k in range(REGIONS)] for t in (lame, shear, buoy)]

    def materials(number, seafloor, z):
        bits = [(number & (1 << k)) != 0 for k in range(4)]
        solid = (dom * 8 + z) >= seafloor
        lam, mu, b = (pick(bits, t) for t in tables)
        return lam, jnp.where(solid, mu, 0.0), b, solid

    def put(ref, index, pair):
        ref[(MIDDLE, *index)] = jnp.where(lane < SEAM, pair[1], pair[0])
        ref[(LEFT, *index)] = pair[0]
        ref[(RIGHT, *index)] = pair[1]

    def put_margin(ref, index, v):
        ref[(LEFT, *index)] = jnp.where(lane >= 128 - WIDE, v, ref[(LEFT, *index)])
        ref[(RIGHT, *index)] = jnp.where(lane < WIDE, v, ref[(RIGHT, *index)])

    everywhere = slice(None)
    for s in range(STEPS):
        put(SRC, (pl.ds(8 * s, 8), everywhere),
            [jnp.where(dom == 0, source[s, :, cut(t)], 0.0) for t in range(2)])
    for z in range(8):
        made = [materials(region[z, :, cut(t)], floor[:, cut(t)], z) for t in range(2)]
        for k, ref in enumerate((L, M, B)):
            put(ref, (pl.ds(8 * z, 8), everywhere), [m[k] for m in made])
        for f in range(9):
            v = [state[f, z, :, cut(t)] for t in range(2)]
            if f < 3:
                put(V, (f, level(z), everywhere), v)
            else:
                if f >= 6:
                    v = [jnp.where(m[3], w, 0.0) for m, w in zip(made, v)]
                elif z == 0:
                    v = [w + jnp.where(dom == 0, source[0, :, cut(t)], 0.0) for t, w in enumerate(v)]
                put(S, (f - 3, level(z), everywhere), v)

    x_fields, z_fields = (0, 3, 4), (2, 4, 5)
    pair = (LEFT, RIGHT)
    for i, x in ((0, 0), (1, 7)):
        parts = [[S[p, f, column(x), :] for p in pair] for f in x_fields]
        parts += [[m[p, pl.ds(x, 8, stride=8), :] for p in pair] for m in (L, M)]
        parts += [[SRC[p, pl.ds(x, 6, stride=8), :] for p in pair]]
        for k in range(6):
            for t in range(2):
                if k < 3:
                    xa[i, 2 * k + t] = parts[k][t]
                elif k < 5:
                    xb[i, 2 * k + t - 6] = parts[k][t]
                else:
                    xb[i, 2 * k + t - 6] = jnp.concatenate([parts[k][t], jnp.zeros((2, 128), f32)], 0)
        for j in range(2):
            ds[i, j] = side_by_side([v[j] for v in parts[:5]] + [xb[i, 4 + j]], j)
    for i, z in ((0, 0), (1, 7)):
        parts = [[S[p, f, level(z), :] for p in pair] for f in z_fields]
        parts += [[m[p, pl.ds(8 * z, 8), :] for p in pair] for m in (L, M)]
        for k in range(5):
            for t in range(2):
                if k < 3:
                    za[i, 2 * k + t] = parts[k][t]
                else:
                    zb[i, 2 * k + t - 6] = parts[k][t]
        for j in range(2):
            ds[2 + i, j] = side_by_side([v[j] for v in parts], j)

    pl.semaphore_wait(barrier, 8 + 5 * (there[0].astype(jnp.int32) + there[1].astype(jnp.int32)))
    for i in range(2):
        @functools.partial(reach, i)
        def _(i=i):
            xa_first(i).start()
            for j in range(2):
                xy_first(i, j).start()
    for i in range(2):
        y_first(i).start()
        za_first(i).start()
        for j in range(2):
            zy_first(i, j).start()
    for i in range(2):
        @functools.partial(reach, i)
        def _(i=i):
            xb_first(i).start()
        zb_first(i).start()

    left = (lane >= 128 - WIDE) & (gy > 0)
    right = (lane < WIDE) & (gy < n_gy - 1)
    inside = left | right

    def margin(low, high, f):
        shift_r = (128 - WIDE * f) % 128
        shift_l = (256 - WIDE - WIDE * f) % 128
        a = pltpu.roll(high, shift_r, 1) if shift_r else high
        c = pltpu.roll(low, shift_l, 1) if shift_l else low
        return jnp.where(left, c, jnp.where(right, a, 0.0))

    for i in range(2):
        y_first(1 - i).wait_recv()
    low, high = yr[0, 8], yr[1, 8]
    seafloor = margin(low, high, STEPS).astype(jnp.int32)
    first_source = None
    for s in range(STEPS):
        v = jnp.where(dom == 0, margin(low, high, s), 0.0)
        first_source = v if s == 0 else first_source
        put_margin(SRC, (pl.ds(8 * s, 8), everywhere), v)
    for z in range(8):
        low, high = yr[0, z], yr[1, z]
        lam, mu, b, solid = materials(margin(low, high, 9).astype(jnp.int32), seafloor, z)
        for ref, v in ((L, lam), (M, mu), (B, b)):
            put_margin(ref, (pl.ds(8 * z, 8), everywhere), jnp.where(inside, v, 0.0))
        for f in range(9):
            v = margin(low, high, f)
            if f < 3:
                put_margin(V, (f, level(z), everywhere), v)
            else:
                if f >= 6:
                    v = jnp.where(solid, v, 0.0)
                elif z == 0:
                    v = v + first_source
                put_margin(S, (f - 3, level(z), everywhere), v)

    for i in range(2):
        za_first(1 - i).wait_recv()
        for j in range(2):
            zy_first(1 - i, 1 - j).wait_recv()

        @functools.partial(reach, i)
        def _(i=i):
            xa_first(1 - i).wait_recv()
            for j in range(2):
                xy_first(1 - i, 1 - j).wait_recv()

    def three(first_tile, second_tile, edge):
        return (
            jnp.where(lane < SEAM, second_tile, first_tile),
            jnp.where(lane >= 128 - WIDE, edge, first_tile),
            jnp.where(lane < WIDE, edge, second_tile),
        )

    for i, x in ((0, -1), (1, 8)):
        for k, f in enumerate(x_fields):
            tiles = three(xra[i, 2 * k], xra[i, 2 * k + 1], margin(dr[i, 0], dr[i, 1], k))
            for p in range(3):
                S[p, f, column(x), :] = tiles[p]
    for i, z in ((0, -1), (1, 8)):
        for k, f in enumerate(z_fields):
            tiles = three(zra[i, 2 * k], zra[i, 2 * k + 1], margin(dr[2 + i, 0], dr[2 + i, 1], k))
            for p in range(3):
                S[p, f, level(z), :] = jnp.where(z_there[i], tiles[p], 0.0)

    def x_copy(p, i, slot, last):
        src, dst = xs.at[p, i], xr.at[slot, p, 1 - i]
        if last:
            src, dst = src.at[0:3], dst.at[0:3]
        return remote(src, dst, send_sem.at[p, i], recv_sem.at[slot, p, 1 - i], (0, sides[i], 0))

    def z_copy(p, i, slot, last):
        src, dst = zs.at[p, i], zr.at[slot, p, 1 - i]
        if last:
            src, dst = src.at[0:3], dst.at[0:3]
        return remote(src, dst, send_sem.at[p, 2 + i], recv_sem.at[slot, p, 3 - i], (sides[i], 0, 0))

    def e_copy(p, i, j, slot):
        return remote(
            es.at[p, i, j], er.at[slot, p, 1 - i, 1 - j], send_sem.at[p, 4 + 2 * i + j],
            recv_sem.at[slot, p, 7 - 2 * i - j], (sides[j], sides[i], 0))

    def sent(p, slot, last):
        for i in range(2):
            @functools.partial(reach, i)
            def _(i=i):
                x_copy(p, i, slot, last).wait_send()
                if not last:
                    for j in range(2):
                        e_copy(p, i, j, slot).wait_send()
            z_copy(p, i, slot, last).wait_send()

    def move(p, s, slot, begin=False, last=False):
        if not begin:
            at_step = pl.ds(8 * s if last else pl.multiple_of(8 * s, 8), 8)
            added = SRC[p, at_step, :]
            for f in range(3):
                S[p, f, level(0), :] += added
            for i, x in ((0, -1), (1, 8)):
                S[p, 0, pl.ds(rows(0, x), 1), :] += SX[i, p, pl.ds(s, 1), :]
        for z in range(8):
            own = level(z)
            after, before = pl.ds(rows(z, 1), 8), pl.ds(rows(z, -1), 8)
            above, below = level(z + 1), level(z - 1)

            def dx(f):
                return S[p, f, after, :] - S[p, f, before, :]

            def dz(f):
                return S[p, f, above, :] - S[p, f, below, :]

            b = B[p, pl.ds(8 * z, 8), :]
            V[p, 0, own, :] -= b * (dx(0) + dy(S[p, 3, own, :]) + dz(4))
            V[p, 1, own, :] -= b * (dx(3) + dy(S[p, 1, own, :]) + dz(5))
            V[p, 2, own, :] -= b * (dx(4) + dy(S[p, 5, own, :]) + dz(2))

        if not begin:
            sent(p, slot, False)
        for i, (x, inner) in enumerate(((0, 1), (7, 6))):
            for f in range(3):
                xs[p, i, f] = V[p, f, column(x), :]
                if not last:
                    xs[p, i, 3 + f] = V[p, f, column(inner), :]
            if not last:
                for j in range(2):
                    for k, f in enumerate((0, 2)):
                        es[p, i, j, k : k + 1, :] = V[p, f, pl.ds(rows(7 * j, x), 1), :]

            @functools.partial(reach, i)
            def _(i=i):
                x_copy(p, i, slot, last).start()
                if not last:
                    for j in range(2):
                        e_copy(p, i, j, slot).start()
        for i, (z, inner) in enumerate(((0, 1), (7, 6))):
            for f in range(3):
                zs[p, i, f] = V[p, f, level(z), :]
                if not last:
                    zs[p, i, 3 + f] = V[p, f, level(inner), :]
            z_copy(p, i, slot, last).start()

        for z in range(8):
            own = level(z)
            after, before = pl.ds(rows(z, 1), 8), pl.ds(rows(z, -1), 8)
            above, below = level(z + 1), level(z - 1)
            dxs = [V[p, f, after, :] - V[p, f, before, :] for f in range(3)]
            dzs = [V[p, f, above, :] - V[p, f, below, :] for f in range(3)]
            dys = [dy(V[p, f, own, :]) for f in range(3)]
            lam, mu = L[p, pl.ds(8 * z, 8), :], M[p, pl.ds(8 * z, 8), :]
            spread = lam * (dxs[0] + dys[1] + dzs[2])
            mu2 = mu + mu
            S[p, 0, own, :] -= spread + mu2 * dxs[0]
            S[p, 1, own, :] -= spread + mu2 * dys[1]
            S[p, 2, own, :] -= spread + mu2 * dzs[2]
            S[p, 3, own, :] -= mu * (dys[0] + dxs[1])
            S[p, 4, own, :] -= mu * (dzs[0] + dxs[2])
            S[p, 5, own, :] -= mu * (dzs[1] + dys[2])

    def finish(p, slot, last=False):
        for i in range(2):
            z_copy(p, 1 - i, slot, last).wait_recv()
        for i, z in ((0, 0), (1, 7)):
            near = [zr[slot, p, i, f] for f in range(3)]
            own = level(z)
            lam, mu = L[p, pl.ds(8 * z, 8), :], M[p, pl.ds(8 * z, 8), :]
            sign = jnp.where(z_there[i], (-1.0, 1.0)[i], 0.0)
            slope = [sign * v for v in near]
            spread = lam * slope[2]
            S[p, 0, own, :] -= spread
            S[p, 1, own, :] -= spread
            S[p, 2, own, :] -= spread + (mu + mu) * slope[2]
            S[p, 4, own, :] -= mu * slope[0]
            S[p, 5, own, :] -= mu * slope[1]

        for i in range(2):
            @functools.partial(reach, i)
            def _(i=i):
                x_copy(p, 1 - i, slot, last).wait_recv()
                if not last:
                    for j in range(2):
                        e_copy(p, 1 - i, 1 - j, slot).wait_recv()

        for i, x, sign in ((0, 0, -1.0), (1, 7, 1.0)):
            near = [xr[slot, p, i, f] for f in range(3)]
            lam, mu = L[p, pl.ds(x, 8, stride=8), :], M[p, pl.ds(x, 8, stride=8), :]
            slope = [sign * v for v in near]
            spread = lam * slope[0]
            S[p, 0, column(x), :] -= spread + (mu + mu) * slope[0]
            S[p, 1, column(x), :] -= spread
            S[p, 2, column(x), :] -= spread
            S[p, 3, column(x), :] -= mu * slope[1]
            S[p, 4, column(x), :] -= mu * slope[2]

        if last:
            return
        for i, x, sign in ((0, 0, -1.0), (1, 7, 1.0)):
            near, far = [xr[slot, p, i, f] for f in range(3)], [xr[slot, p, i, 3 + f] for f in range(3)]
            lam, mu = LX[i, p], MX[i, p]
            dxs = [sign * (far[f] - V[p, f, column(x), :]) for f in range(3)]
            dzs = {}
            for k, f in enumerate((0, 2)):
                top, bottom = (jnp.where(z_there[j], er[slot, p, i, j, k : k + 1, :], 0.0) for j in range(2))
                down = jnp.where(sub == 0, top, pltpu.roll(near[f], 1, 0))
                up = jnp.where(sub == 7, bottom, pltpu.roll(near[f], 7, 0))
                dzs[f] = up - down
            trace = dxs[0] + dy(near[1]) + dzs[2]
            beyond = column((-1, 8)[i])
            S[p, 0, beyond, :] -= lam * trace + (mu + mu) * dxs[0]
            S[p, 3, beyond, :] -= mu * (dy(near[0]) + dxs[1])
            S[p, 4, beyond, :] -= mu * (dzs[0] + dxs[2])
        for i, z, sign in ((0, 0, -1.0), (1, 7, 1.0)):
            near, far = [zr[slot, p, i, f] for f in range(3)], [zr[slot, p, i, 3 + f] for f in range(3)]
            lam, mu = LZ[i, p], MZ[i, p]
            dzs = [sign * (far[f] - V[p, f, level(z), :]) for f in range(3)]
            dxs = {}
            for k, f in enumerate((0, 2)):
                low, high = (er[slot, p, j, i, k : k + 1, :] for j in range(2))
                behind = jnp.where(sub == 0, low, pltpu.roll(near[f], 1, 0))
                ahead = jnp.where(sub == 7, high, pltpu.roll(near[f], 7, 0))
                dxs[f] = ahead - behind
            trace = dxs[0] + dy(near[1]) + dzs[2]
            beyond = level((-1, 8)[i])
            S[p, 2, beyond, :] -= lam * trace + (mu + mu) * dzs[2]
            S[p, 4, beyond, :] -= mu * (dzs[0] + dxs[2])
            S[p, 5, beyond, :] -= mu * (dzs[1] + dy(near[2]))

    def each_part(then):
        def body(p, carry):
            then(p)
            return carry

        lax.fori_loop(0, 3, body, 0)

    each_part(lambda p: move(p, 0, 0, begin=True))

    for i in range(2):
        zb_first(1 - i).wait_recv()

        @functools.partial(reach, i)
        def _(i=i):
            xb_first(1 - i).wait_recv()
    for i in range(2):
        for k, ref in enumerate((LX, MX, SX)):
            tiles = three(xrb[i, 2 * k], xrb[i, 2 * k + 1], margin(dr[i, 0], dr[i, 1], 3 + k))
            for p in range(3):
                ref[i, p] = tiles[p]
        for k, ref in enumerate((LZ, MZ)):
            tiles = three(zrb[i, 2 * k], zrb[i, 2 * k + 1], margin(dr[2 + i, 0], dr[2 + i, 1], 3 + k))
            for p in range(3):
                ref[i, p] = jnp.where(z_there[i], tiles[p], 0.0)

    def step(s, carry):
        slot = lax.rem(s, 2)

        def turn(p):
            finish(p, 1 - slot)
            move(p, s, slot)

        each_part(turn)
        return carry

    lax.fori_loop(1, STEPS - 1, step, 0)

    end = STEPS - 1

    def final(p):
        finish(p, (end - 1) % 2)
        move(p, end, end % 2, last=True)

    each_part(final)

    def store(f):
        return pltpu.make_async_copy(state.at[f], out.at[f], out_sem.at[f])

    def gather(f, ref, k):
        for z in range(8):
            middle, first_tile, second_tile = (ref[p, k, level(z), :] for p in (MIDDLE, LEFT, RIGHT))
            state[f, z, :, cut(0)] = jnp.where(lane < FIRST_CUT, first_tile, middle)
            state[f, z, :, cut(1)] = jnp.where(lane < SECOND_CUT, middle, second_tile)
        store(f).start()

    for f in range(3):
        gather(f, V, f)
    each_part(lambda p: finish(p, end % 2, last=True))
    for f in range(6):
        gather(3 + f, S, f)

    each_part(lambda p: sent(p, end % 2, True))
    for i in range(2):
        y_first(i).wait_send()
        za_first(i).wait_send()
        zb_first(i).wait_send()
        for j in range(2):
            zy_first(i, j).wait_send()

        @functools.partial(reach, i)
        def _(i=i):
            xa_first(i).wait_send()
            xb_first(i).wait_send()
            for j in range(2):
                xy_first(i, j).wait_send()
    for f in range(9):
        store(f).wait()


def solution(mesh):
    sizes = (mesh.shape["dom"], mesh.shape["gx"], mesh.shape["gy"])

    def on_device(state, source, floor, region, lame, shear, buoy):
        hbm = pl.BlockSpec(memory_space=pltpu.HBM)

        def tiles(*shape):
            return pltpu.VMEM(shape + (8, 128), f32)

        return pl.pallas_call(
            functools.partial(kernel, sizes),
            out_shape=jax.ShapeDtypeStruct(state.shape, f32),
            in_specs=[hbm] * 7,
            out_specs=hbm,
            scratch_shapes=[
                pltpu.VMEM(state.shape, f32),
                pltpu.VMEM(source.shape, f32),
                pltpu.VMEM(floor.shape, jnp.int32),
                pltpu.VMEM(region.shape, jnp.int32),
                pltpu.SMEM(lame.shape, f32),
                pltpu.SMEM(shear.shape, f32),
                pltpu.SMEM(buoy.shape, f32),
                pltpu.VMEM((3, 6, 10 * BLOCK, 128), f32),
                pltpu.VMEM((3, 3, 10 * BLOCK, 128), f32),
                pltpu.VMEM((3, 64, 128), f32),
                pltpu.VMEM((3, 64, 128), f32),
                pltpu.VMEM((3, 64, 128), f32),
                pltpu.VMEM((3, 8 * STEPS, 128), f32),
                tiles(2, 3),
                tiles(2, 3),
                tiles(2, 3),
                tiles(2, 3),
                tiles(2, 3),
                tiles(2, 9),
                tiles(2, 9),
                tiles(2, 6),
                tiles(2, 6),
                tiles(2, 6),
                tiles(2, 6),
                tiles(2, 6),
                tiles(2, 6),
                tiles(2, 4),
                tiles(2, 4),
                tiles(4, 2),
                tiles(4, 2),
                tiles(3, 2, 6),
                tiles(2, 3, 2, 6),
                tiles(3, 2, 6),
                tiles(2, 3, 2, 6),
                pltpu.VMEM((3, 2, 2, 2, 128), f32),
                pltpu.VMEM((2, 3, 2, 2, 2, 128), f32),
                pltpu.SemaphoreType.DMA((7,)),
                pltpu.SemaphoreType.DMA((9,)),
                pltpu.SemaphoreType.DMA((18,)),
                pltpu.SemaphoreType.DMA((18,)),
                pltpu.SemaphoreType.DMA((3, 8)),
                pltpu.SemaphoreType.DMA((2, 3, 8)),
            ],
            compiler_params=pltpu.CompilerParams(
                collective_id=0, has_side_effects=True, vmem_limit_bytes=60 * 1024 * 1024
            ),
        )(state, source, floor, region, lame, shear, buoy)

    return jax.shard_map(
        on_device,
        mesh=mesh,
        in_specs=(
            P(None, "dom", "gx", "gy"),
            P(None, "gx", "gy"),
            P("gx", "gy"),
            P("dom", "gx", "gy"),
            P(),
            P(),
            P(),
        ),
        out_specs=P(None, "dom", "gx", "gy"),
        check_vma=False,
    )
```

```python
import functools

import jax
import jax.numpy as jnp
from jax import lax
from jax.experimental import pallas as pl
from jax.experimental.pallas import tpu as pltpu
from jax.sharding import PartitionSpec as P

STEPS = 6
COURANT = 0.25
REGIONS = 16
BLOCK = 16
WIDE = 12
MIDDLE, LEFT, RIGHT = 0, 1, 2
FIRST_CUT, SECOND_CUT, SEAM = 86, 171 - 128, 64
MESH = pl.DeviceIdType.MESH

f32 = jnp.float32


def rows(z, x=0):
    return (z + 1) * BLOCK + 8 + x


def level(z):
    return pl.ds(rows(z), 8)


def column(x):
    return pl.ds(rows(0, x), 8, stride=BLOCK)


def dy(v):
    return pltpu.roll(v, 127, 1) - pltpu.roll(v, 1, 1)


def pick(bits, table):
    values = list(table)
    for bit in bits:
        values = [jnp.where(bit, values[2 * i + 1], values[2 * i]) for i in range(len(values) // 2)]
    return values[0]


def kernel(
    sizes, state_in, source_in, floor_in, region_in, lame_in, shear_in, buoy_in, out,
    state, source, floor, region, lame, shear, buoy,
    S, V, L, M, B, SRC, LX, MX, SX, LZ, MZ, ys, yr, xa, xra, xb, xrb, za, zra, zb, zrb, ds, dr,
    xs, xr, zs, zr, es, er, in_sem, first_send, first_recv, send_sem, recv_sem,
):
    n_dom, n_gx, n_gy = sizes
    dom, gx, gy = lax.axis_index("dom"), lax.axis_index("gx"), lax.axis_index("gy")
    lane = lax.broadcasted_iota(jnp.int32, (8, 128), 1)
    sub = lax.broadcasted_iota(jnp.int32, (8, 128), 0)
    zero = jnp.zeros((8, 128), f32)

    loads = [
        pltpu.make_async_copy(src, dst, in_sem.at[i])
        for i, (src, dst) in enumerate((
            (region_in, region), (floor_in, floor), (source_in, source), (state_in, state),
            (lame_in, lame), (shear_in, shear), (buoy_in, buoy)))
    ]
    for load in loads:
        load.start()

    sides = (-1, 1)
    there = [gx > 0, gx < n_gx - 1]
    z_there = [dom > 0, dom < n_dom - 1]

    def at(dz, dx, dyy):
        return (lax.rem(dom + dz + n_dom, n_dom), gx + dx, lax.rem(gy + dyy + n_gy, n_gy))

    def reach(i, then):
        pl.when(there[i])(then)

    barrier = pltpu.get_barrier_semaphore()

    def greet(*way):
        pl.semaphore_signal(barrier, inc=1, device_id=at(*way), device_id_type=MESH)

    for i, dx in enumerate(sides):
        @functools.partial(reach, i)
        def _(dx=dx):
            for way in ((0, dx, 0), (-1, dx, 0), (1, dx, 0), (0, dx, -1), (0, dx, 1)):
                greet(*way)
    for way in [(a, 0, b) for a in (-1, 0, 1) for b in (-1, 0, 1) if a or b]:
        greet(*way)

    for i in range(2):
        @pl.when(jnp.logical_not(there[i]))
        def _(i=i):
            xra[i] = jnp.zeros(xra.shape[1:], f32)
            xrb[i] = jnp.zeros(xrb.shape[1:], f32)
            for j in range(2):
                dr[i, j] = zero
            for slot in range(2):
                for p in range(3):
                    xr[slot, p, i] = jnp.zeros(xr.shape[3:], f32)
                    for j in range(2):
                        er[slot, p, i, j] = jnp.zeros((2, 128), f32)

    for p in range(3):
        for f in range(3):
            for z in range(-1, 9):
                V[p, f, pl.ds(rows(z, -8), 8), :] = zero
            for z in (-1, 8):
                V[p, f, level(z), :] = zero

    for load in loads[:4]:
        load.wait()

    def side_by_side(parts, t):
        tile = zero
        for k, v in enumerate(parts):
            shift = (WIDE * k + (WIDE if t else 0)) % 128
            v = pltpu.roll(v, shift, 1) if shift else v
            tile = jnp.where((lane >= WIDE * k) & (lane < WIDE * (k + 1)), v, tile)
        return tile

    def cut(t):
        return slice(128 * t, 128 * t + 128)

    for i in range(2):
        for z in range(8):
            ys[i, z] = side_by_side(
                [state[f, z, :, cut(i)] for f in range(9)] + [region[z, :, cut(i)].astype(f32)], i)
        ys[i, 8] = side_by_side([source[s, :, cut(i)] for s in range(STEPS)] + [floor[:, cut(i)].astype(f32)], i)

    def remote(src, dst, send, recv, way):
        return pltpu.make_async_remote_copy(
            src_ref=src, dst_ref=dst, send_sem=send, recv_sem=recv, device_id=at(*way), device_id_type=MESH)

    def first(k, back, src, dst, way):
        return remote(src, dst, first_send.at[k], first_recv.at[back], way)

    def xa_first(i):
        return first(i, 1 - i, xa.at[i], xra.at[1 - i], (0, sides[i], 0))

    def za_first(i):
        return first(2 + i, 3 - i, za.at[i], zra.at[1 - i], (sides[i], 0, 0))

    def y_first(i):
        return first(4 + i, 5 - i, ys.at[i], yr.at[1 - i], (0, 0, sides[i]))

    def xy_first(i, j):
        return first(6 + 2 * i + j, 9 - 2 * i - j, ds.at[i, j], dr.at[1 - i, 1 - j], (0, sides[i], sides[j]))

    def zy_first(i, j):
        return first(10 + 2 * i + j, 13 - 2 * i - j, ds.at[2 + i, j], dr.at[3 - i, 1 - j], (sides[i], 0, sides[j]))

    def xb_first(i):
        return first(14 + i, 15 - i, xb.at[i], xrb.at[1 - i], (0, sides[i], 0))

    def zb_first(i):
        return first(16 + i, 17 - i, zb.at[i], zrb.at[1 - i], (sides[i], 0, 0))

    for load in loads[4:]:
        load.wait()
    scale = 0.5 * COURANT
    tables = [[t[k] * scale for k in range(REGIONS)] for t in (lame, shear, buoy)]

    def materials(number, seafloor, z):
        bits = [(number & (1 << k)) != 0 for k in range(4)]
        solid = (dom * 8 + z) >= seafloor
        lam, mu, b = (pick(bits, t) for t in tables)
        return lam, jnp.where(solid, mu, 0.0), b, solid

    def put(ref, index, pair):
        ref[(MIDDLE, *index)] = jnp.where(lane < SEAM, pair[1], pair[0])
        ref[(LEFT, *index)] = pair[0]
        ref[(RIGHT, *index)] = pair[1]

    def put_margin(ref, index, v):
        ref[(LEFT, *index)] = jnp.where(lane >= 128 - WIDE, v, ref[(LEFT, *index)])
        ref[(RIGHT, *index)] = jnp.where(lane < WIDE, v, ref[(RIGHT, *index)])

    everywhere = slice(None)
    for s in range(STEPS):
        put(SRC, (pl.ds(8 * s, 8), everywhere),
            [jnp.where(dom == 0, source[s, :, cut(t)], 0.0) for t in range(2)])
    for z in range(8):
        made = [materials(region[z, :, cut(t)], floor[:, cut(t)], z) for t in range(2)]
        for k, ref in enumerate((L, M, B)):
            put(ref, (pl.ds(8 * z, 8), everywhere), [m[k] for m in made])
        for f in range(9):
            v = [state[f, z, :, cut(t)] for t in range(2)]
            if f < 3:
                put(V, (f, level(z), everywhere), v)
            else:
                if f >= 6:
                    v = [jnp.where(m[3], w, 0.0) for m, w in zip(made, v)]
                elif z == 0:
                    v = [w + jnp.where(dom == 0, source[0, :, cut(t)], 0.0) for t, w in enumerate(v)]
                put(S, (f - 3, level(z), everywhere), v)

    x_fields, z_fields = (0, 3, 4), (2, 4, 5)
    pair = (LEFT, RIGHT)
    for i, x in ((0, 0), (1, 7)):
        parts = [[S[p, f, column(x), :] for p in pair] for f in x_fields]
        parts += [[m[p, pl.ds(x, 8, stride=8), :] for p in pair] for m in (L, M)]
        parts += [[SRC[p, pl.ds(x, 6, stride=8), :] for p in pair]]
        for k in range(6):
            for t in range(2):
                if k < 3:
                    xa[i, 2 * k + t] = parts[k][t]
                elif k < 5:
                    xb[i, 2 * k + t - 6] = parts[k][t]
                else:
                    xb[i, 2 * k + t - 6] = jnp.concatenate([parts[k][t], jnp.zeros((2, 128), f32)], 0)
        for j in range(2):
            ds[i, j] = side_by_side([v[j] for v in parts[:5]] + [xb[i, 4 + j]], j)
    for i, z in ((0, 0), (1, 7)):
        parts = [[S[p, f, level(z), :] for p in pair] for f in z_fields]
        parts += [[m[p, pl.ds(8 * z, 8), :] for p in pair] for m in (L, M)]
        for k in range(5):
            for t in range(2):
                if k < 3:
                    za[i, 2 * k + t] = parts[k][t]
                else:
                    zb[i, 2 * k + t - 6] = parts[k][t]
        for j in range(2):
            ds[2 + i, j] = side_by_side([v[j] for v in parts], j)

    pl.semaphore_wait(barrier, 8 + 5 * (there[0].astype(jnp.int32) + there[1].astype(jnp.int32)))
    for i in range(2):
        @functools.partial(reach, i)
        def _(i=i):
            xa_first(i).start()
            for j in range(2):
                xy_first(i, j).start()
    for i in range(2):
        y_first(i).start()
        za_first(i).start()
        for j in range(2):
            zy_first(i, j).start()
    for i in range(2):
        @functools.partial(reach, i)
        def _(i=i):
            xb_first(i).start()
        zb_first(i).start()

    left = (lane >= 128 - WIDE) & (gy > 0)
    right = (lane < WIDE) & (gy < n_gy - 1)
    inside = left | right

    def margin(low, high, f):
        shift_r = (128 - WIDE * f) % 128
        shift_l = (256 - WIDE - WIDE * f) % 128
        a = pltpu.roll(high, shift_r, 1) if shift_r else high
        c = pltpu.roll(low, shift_l, 1) if shift_l else low
        return jnp.where(left, c, jnp.where(right, a, 0.0))

    for i in range(2):
        za_first(1 - i).wait_recv()

        @functools.partial(reach, i)
        def _(i=i):
            xa_first(1 - i).wait_recv()

    def three(first_tile, second_tile, edge):
        return (
            jnp.where(lane < SEAM, second_tile, first_tile),
            jnp.where(lane >= 128 - WIDE, edge, first_tile),
            jnp.where(lane < WIDE, edge, second_tile),
        )

    def border(parts):
        for i, x in ((0, -1), (1, 8)):
            for k, f in enumerate(x_fields):
                edge = zero if parts == (MIDDLE,) else margin(dr[i, 0], dr[i, 1], k)
                tiles = three(xra[i, 2 * k], xra[i, 2 * k + 1], edge)
                for p in parts:
                    S[p, f, column(x), :] = tiles[p]
        for i, z in ((0, -1), (1, 8)):
            for k, f in enumerate(z_fields):
                edge = zero if parts == (MIDDLE,) else margin(dr[2 + i, 0], dr[2 + i, 1], k)
                tiles = three(zra[i, 2 * k], zra[i, 2 * k + 1], edge)
                for p in parts:
                    S[p, f, level(z), :] = jnp.where(z_there[i], tiles[p], 0.0)

    border((MIDDLE,))
    def x_copy(p, i, slot, last):
        src, dst = xs.at[p, i], xr.at[slot, p, 1 - i]
        if last:
            src, dst = src.at[0:3], dst.at[0:3]
        return remote(src, dst, send_sem.at[p, i], recv_sem.at[slot, p, 1 - i], (0, sides[i], 0))

    def z_copy(p, i, slot, last):
        src, dst = zs.at[p, i], zr.at[slot, p, 1 - i]
        if last:
            src, dst = src.at[0:3], dst.at[0:3]
        return remote(src, dst, send_sem.at[p, 2 + i], recv_sem.at[slot, p, 3 - i], (sides[i], 0, 0))

    def e_copy(p, i, j, slot):
        return remote(
            es.at[p, i, j], er.at[slot, p, 1 - i, 1 - j], send_sem.at[p, 4 + 2 * i + j],
            recv_sem.at[slot, p, 7 - 2 * i - j], (sides[j], sides[i], 0))

    def sent(p, slot, last):
        for i in range(2):
            @functools.partial(reach, i)
            def _(i=i):
                x_copy(p, i, slot, last).wait_send()
                if not last:
                    for j in range(2):
                        e_copy(p, i, j, slot).wait_send()
            z_copy(p, i, slot, last).wait_send()

    def move(p, s, slot, begin=False, last=False):
        if not begin:
            at_step = pl.ds(8 * s if last else pl.multiple_of(8 * s, 8), 8)
            added = SRC[p, at_step, :]
            for f in range(3):
                S[p, f, level(0), :] += added
            for i, x in ((0, -1), (1, 8)):
                S[p, 0, pl.ds(rows(0, x), 1), :] += SX[i, p, pl.ds(s, 1), :]
        for z in range(8):
            own = level(z)
            after, before = pl.ds(rows(z, 1), 8), pl.ds(rows(z, -1), 8)
            above, below = level(z + 1), level(z - 1)

            def dx(f):
                return S[p, f, after, :] - S[p, f, before, :]

            def dz(f):
                return S[p, f, above, :] - S[p, f, below, :]

            b = B[p, pl.ds(8 * z, 8), :]
            V[p, 0, own, :] -= b * (dx(0) + dy(S[p, 3, own, :]) + dz(4))
            V[p, 1, own, :] -= b * (dx(3) + dy(S[p, 1, own, :]) + dz(5))
            V[p, 2, own, :] -= b * (dx(4) + dy(S[p, 5, own, :]) + dz(2))

        if not begin:
            sent(p, slot, False)
        for i, (x, inner) in enumerate(((0, 1), (7, 6))):
            for f in range(3):
                xs[p, i, f] = V[p, f, column(x), :]
                if not last:
                    xs[p, i, 3 + f] = V[p, f, column(inner), :]
            if not last:
                for j in range(2):
                    for k, f in enumerate((0, 2)):
                        es[p, i, j, k : k + 1, :] = V[p, f, pl.ds(rows(7 * j, x), 1), :]

            @functools.partial(reach, i)
            def _(i=i):
                if not last:
                    for j in range(2):
                        e_copy(p, i, j, slot).start()
                x_copy(p, i, slot, last).start()
        for i, (z, inner) in enumerate(((0, 1), (7, 6))):
            for f in range(3):
                zs[p, i, f] = V[p, f, level(z), :]
                if not last:
                    zs[p, i, 3 + f] = V[p, f, level(inner), :]
            z_copy(p, i, slot, last).start()

        for z in range(8):
            own = level(z)
            after, before = pl.ds(rows(z, 1), 8), pl.ds(rows(z, -1), 8)
            above, below = level(z + 1), level(z - 1)
            dxs = [V[p, f, after, :] - V[p, f, before, :] for f in range(3)]
            dzs = [V[p, f, above, :] - V[p, f, below, :] for f in range(3)]
            dys = [dy(V[p, f, own, :]) for f in range(3)]
            lam, mu = L[p, pl.ds(8 * z, 8), :], M[p, pl.ds(8 * z, 8), :]
            spread = lam * (dxs[0] + dys[1] + dzs[2])
            mu2 = mu + mu
            S[p, 0, own, :] -= spread + mu2 * dxs[0]
            S[p, 1, own, :] -= spread + mu2 * dys[1]
            S[p, 2, own, :] -= spread + mu2 * dzs[2]
            S[p, 3, own, :] -= mu * (dys[0] + dxs[1])
            S[p, 4, own, :] -= mu * (dzs[0] + dxs[2])
            S[p, 5, own, :] -= mu * (dzs[1] + dys[2])

    def finish(p, slot, last=False):
        for i in range(2):
            z_copy(p, 1 - i, slot, last).wait_recv()
        for i, z in ((0, 0), (1, 7)):
            near = [zr[slot, p, i, f] for f in range(3)]
            own = level(z)
            lam, mu = L[p, pl.ds(8 * z, 8), :], M[p, pl.ds(8 * z, 8), :]
            sign = jnp.where(z_there[i], (-1.0, 1.0)[i], 0.0)
            slope = [sign * v for v in near]
            spread = lam * slope[2]
            S[p, 0, own, :] -= spread
            S[p, 1, own, :] -= spread
            S[p, 2, own, :] -= spread + (mu + mu) * slope[2]
            S[p, 4, own, :] -= mu * slope[0]
            S[p, 5, own, :] -= mu * slope[1]

        for i in range(2):
            @functools.partial(reach, i)
            def _(i=i):
                x_copy(p, 1 - i, slot, last).wait_recv()
                if not last:
                    for j in range(2):
                        e_copy(p, 1 - i, 1 - j, slot).wait_recv()

        for i, x, sign in ((0, 0, -1.0), (1, 7, 1.0)):
            near = [xr[slot, p, i, f] for f in range(3)]
            lam, mu = L[p, pl.ds(x, 8, stride=8), :], M[p, pl.ds(x, 8, stride=8), :]
            slope = [sign * v for v in near]
            spread = lam * slope[0]
            S[p, 0, column(x), :] -= spread + (mu + mu) * slope[0]
            S[p, 1, column(x), :] -= spread
            S[p, 2, column(x), :] -= spread
            S[p, 3, column(x), :] -= mu * slope[1]
            S[p, 4, column(x), :] -= mu * slope[2]

        if last:
            return
        for i, x, sign in ((0, 0, -1.0), (1, 7, 1.0)):
            near, far = [xr[slot, p, i, f] for f in range(3)], [xr[slot, p, i, 3 + f] for f in range(3)]
            lam, mu = LX[i, p], MX[i, p]
            dxs = [sign * (far[f] - V[p, f, column(x), :]) for f in range(3)]
            dzs = {}
            for k, f in enumerate((0, 2)):
                top, bottom = (jnp.where(z_there[j], er[slot, p, i, j, k : k + 1, :], 0.0) for j in range(2))
                down = jnp.where(sub == 0, top, pltpu.roll(near[f], 1, 0))
                up = jnp.where(sub == 7, bottom, pltpu.roll(near[f], 7, 0))
                dzs[f] = up - down
            trace = dxs[0] + dy(near[1]) + dzs[2]
            beyond = column((-1, 8)[i])
            S[p, 0, beyond, :] -= lam * trace + (mu + mu) * dxs[0]
            S[p, 3, beyond, :] -= mu * (dy(near[0]) + dxs[1])
            S[p, 4, beyond, :] -= mu * (dzs[0] + dxs[2])
        for i, z, sign in ((0, 0, -1.0), (1, 7, 1.0)):
            near, far = [zr[slot, p, i, f] for f in range(3)], [zr[slot, p, i, 3 + f] for f in range(3)]
            lam, mu = LZ[i, p], MZ[i, p]
            dzs = [sign * (far[f] - V[p, f, level(z), :]) for f in range(3)]
            dxs = {}
            for k, f in enumerate((0, 2)):
                low, high = (er[slot, p, j, i, k : k + 1, :] for j in range(2))
                behind = jnp.where(sub == 0, low, pltpu.roll(near[f], 1, 0))
                ahead = jnp.where(sub == 7, high, pltpu.roll(near[f], 7, 0))
                dxs[f] = ahead - behind
            trace = dxs[0] + dy(near[1]) + dzs[2]
            beyond = level((-1, 8)[i])
            S[p, 2, beyond, :] -= lam * trace + (mu + mu) * dzs[2]
            S[p, 4, beyond, :] -= mu * (dzs[0] + dxs[2])
            S[p, 5, beyond, :] -= mu * (dzs[1] + dy(near[2]))

    def each_part(then):
        def body(p, carry):
            then(p)
            return carry

        lax.fori_loop(0, 3, body, 0)

    move(MIDDLE, 0, 0, begin=True)

    for i in range(2):
        y_first(1 - i).wait_recv()
    low, high = yr[0, 8], yr[1, 8]
    seafloor = margin(low, high, STEPS).astype(jnp.int32)
    first_source = None
    for s in range(STEPS):
        v = jnp.where(dom == 0, margin(low, high, s), 0.0)
        first_source = v if s == 0 else first_source
        put_margin(SRC, (pl.ds(8 * s, 8), everywhere), v)
    for z in range(8):
        low, high = yr[0, z], yr[1, z]
        lam, mu, b, solid = materials(margin(low, high, 9).astype(jnp.int32), seafloor, z)
        for ref, v in ((L, lam), (M, mu), (B, b)):
            put_margin(ref, (pl.ds(8 * z, 8), everywhere), jnp.where(inside, v, 0.0))
        for f in range(9):
            v = margin(low, high, f)
            if f < 3:
                put_margin(V, (f, level(z), everywhere), v)
            else:
                if f >= 6:
                    v = jnp.where(solid, v, 0.0)
                elif z == 0:
                    v = v + first_source
                put_margin(S, (f - 3, level(z), everywhere), v)

    for i in range(2):
        for j in range(2):
            zy_first(1 - i, 1 - j).wait_recv()

        @functools.partial(reach, i)
        def _(i=i):
            for j in range(2):
                xy_first(1 - i, 1 - j).wait_recv()
    border((LEFT, RIGHT))

    def begin(p, carry):
        move(p, 0, 0, begin=True)
        return carry

    lax.fori_loop(1, 3, begin, 0)

    for i in range(2):
        zb_first(1 - i).wait_recv()

        @functools.partial(reach, i)
        def _(i=i):
            xb_first(1 - i).wait_recv()
    for i in range(2):
        for k, ref in enumerate((LX, MX, SX)):
            tiles = three(xrb[i, 2 * k], xrb[i, 2 * k + 1], margin(dr[i, 0], dr[i, 1], 3 + k))
            for p in range(3):
                ref[i, p] = tiles[p]
        for k, ref in enumerate((LZ, MZ)):
            tiles = three(zrb[i, 2 * k], zrb[i, 2 * k + 1], margin(dr[2 + i, 0], dr[2 + i, 1], 3 + k))
            for p in range(3):
                ref[i, p] = jnp.where(z_there[i], tiles[p], 0.0)

    def step(s, carry):
        slot = lax.rem(s, 2)

        def turn(p):
            finish(p, 1 - slot)
            move(p, s, slot)

        each_part(turn)
        return carry

    lax.fori_loop(1, STEPS - 1, step, 0)

    end = STEPS - 1

    def final(p):
        finish(p, (end - 1) % 2)
        move(p, end, end % 2, last=True)

    each_part(final)

    def gather(f, ref, k):
        for z in range(8):
            middle, first_tile, second_tile = (ref[p, k, level(z), :] for p in (MIDDLE, LEFT, RIGHT))
            out[f, z, :, cut(0)] = jnp.where(lane < FIRST_CUT, first_tile, middle)
            out[f, z, :, cut(1)] = jnp.where(lane < SECOND_CUT, middle, second_tile)

    for f in range(3):
        gather(f, V, f)
    each_part(lambda p: finish(p, end % 2, last=True))
    for f in range(6):
        gather(3 + f, S, f)

    each_part(lambda p: sent(p, end % 2, True))
    for i in range(2):
        y_first(i).wait_send()
        za_first(i).wait_send()
        zb_first(i).wait_send()
        for j in range(2):
            zy_first(i, j).wait_send()

        @functools.partial(reach, i)
        def _(i=i):
            xa_first(i).wait_send()
            xb_first(i).wait_send()
            for j in range(2):
                xy_first(i, j).wait_send()


def solution(mesh):
    sizes = (mesh.shape["dom"], mesh.shape["gx"], mesh.shape["gy"])

    def on_device(state, source, floor, region, lame, shear, buoy):
        hbm = pl.BlockSpec(memory_space=pltpu.HBM)

        def tiles(*shape):
            return pltpu.VMEM(shape + (8, 128), f32)

        return pl.pallas_call(
            functools.partial(kernel, sizes),
            out_shape=jax.ShapeDtypeStruct(state.shape, f32),
            in_specs=[hbm] * 7,
            out_specs=pl.BlockSpec(memory_space=pltpu.VMEM),
            scratch_shapes=[
                pltpu.VMEM(state.shape, f32),
                pltpu.VMEM(source.shape, f32),
                pltpu.VMEM(floor.shape, jnp.int32),
                pltpu.VMEM(region.shape, jnp.int32),
                pltpu.SMEM(lame.shape, f32),
                pltpu.SMEM(shear.shape, f32),
                pltpu.SMEM(buoy.shape, f32),
                pltpu.VMEM((3, 6, 10 * BLOCK, 128), f32),
                pltpu.VMEM((3, 3, 10 * BLOCK, 128), f32),
                pltpu.VMEM((3, 64, 128), f32),
                pltpu.VMEM((3, 64, 128), f32),
                pltpu.VMEM((3, 64, 128), f32),
                pltpu.VMEM((3, 8 * STEPS, 128), f32),
                tiles(2, 3),
                tiles(2, 3),
                tiles(2, 3),
                tiles(2, 3),
                tiles(2, 3),
                tiles(2, 9),
                tiles(2, 9),
                tiles(2, 6),
                tiles(2, 6),
                tiles(2, 6),
                tiles(2, 6),
                tiles(2, 6),
                tiles(2, 6),
                tiles(2, 4),
                tiles(2, 4),
                tiles(4, 2),
                tiles(4, 2),
                tiles(3, 2, 6),
                tiles(2, 3, 2, 6),
                tiles(3, 2, 6),
                tiles(2, 3, 2, 6),
                pltpu.VMEM((3, 2, 2, 2, 128), f32),
                pltpu.VMEM((2, 3, 2, 2, 2, 128), f32),
                pltpu.SemaphoreType.DMA((7,)),
                pltpu.SemaphoreType.DMA((18,)),
                pltpu.SemaphoreType.DMA((18,)),
                pltpu.SemaphoreType.DMA((3, 8)),
                pltpu.SemaphoreType.DMA((2, 3, 8)),
            ],
            compiler_params=pltpu.CompilerParams(
                collective_id=0, has_side_effects=True, vmem_limit_bytes=32 * 1024 * 1024
            ),
        )(*(
            pltpu.with_memory_space_constraint(v, pltpu.HBM)
            for v in (state, source, floor, region, lame, shear, buoy)
        ))

    return jax.shard_map(
        on_device,
        mesh=mesh,
        in_specs=(
            P(None, "dom", "gx", "gy"),
            P(None, "gx", "gy"),
            P("gx", "gy"),
            P("dom", "gx", "gy"),
            P(),
            P(),
            P(),
        ),
        out_specs=P(None, "dom", "gx", "gy"),
        check_vma=False,
    )
```

```python
import functools

import jax
import jax.numpy as jnp
from jax import lax
from jax.experimental import pallas as pl
from jax.experimental.pallas import tpu as pltpu
from jax.sharding import PartitionSpec as P

STEPS = 6
COURANT = 0.25
REGIONS = 16
NEED = 106
SPARE = 128 - NEED
BLOCK = 16
WIDE = 12
MIDDLE, LEFT, RIGHT = 0, 1, 2
FIRST_CUT, SECOND_CUT, SEAM = 86, 171 - 128, 64
MESH = pl.DeviceIdType.MESH

f32 = jnp.float32


def rows(z, x=0):
    return (z + 1) * BLOCK + 8 + x


def level(z):
    return pl.ds(rows(z), 8)


def column(x):
    return pl.ds(rows(0, x), 8, stride=BLOCK)


def dy(v):
    return pltpu.roll(v, 127, 1) - pltpu.roll(v, 1, 1)


def pick(bits, table):
    values = list(table)
    for bit in bits:
        values = [jnp.where(bit, values[2 * i + 1], values[2 * i]) for i in range(len(values) // 2)]
    return values[0]


def kernel(
    sizes, state_in, source_in, floor_in, region_in, lame_in, shear_in, buoy_in, out,
    state, source, floor, region, lame, shear, buoy,
    S, V, L, M, B, SRC, LX, MX, SX, LZ, MZ, ys, yr, xa, xra, xb, xrb, za, zra, zb, zrb, ds, dr,
    xs, xr, zs, zr, es, er, in_sem, first_send, first_recv, send_sem, recv_sem,
):
    n_dom, n_gx, n_gy = sizes
    dom, gx, gy = lax.axis_index("dom"), lax.axis_index("gx"), lax.axis_index("gy")
    lane = lax.broadcasted_iota(jnp.int32, (8, 128), 1)
    sub = lax.broadcasted_iota(jnp.int32, (8, 128), 0)
    zero = jnp.zeros((8, 128), f32)

    loads = [
        pltpu.make_async_copy(src, dst, in_sem.at[i])
        for i, (src, dst) in enumerate((
            (region_in, region), (floor_in, floor), (source_in, source), (state_in, state),
            (lame_in, lame), (shear_in, shear), (buoy_in, buoy)))
    ]
    for load in loads:
        load.start()

    sides = (-1, 1)
    there = [gx > 0, gx < n_gx - 1]
    z_there = [dom > 0, dom < n_dom - 1]

    def at(dz, dx, dyy):
        return (lax.rem(dom + dz + n_dom, n_dom), gx + dx, lax.rem(gy + dyy + n_gy, n_gy))

    def reach(i, then):
        pl.when(there[i])(then)

    barrier = pltpu.get_barrier_semaphore()

    def greet(*way):
        pl.semaphore_signal(barrier, inc=1, device_id=at(*way), device_id_type=MESH)

    for i, dx in enumerate(sides):
        @functools.partial(reach, i)
        def _(dx=dx):
            for way in ((0, dx, 0), (-1, dx, 0), (1, dx, 0), (0, dx, -1), (0, dx, 1)):
                greet(*way)
    for way in [(a, 0, b) for a in (-1, 0, 1) for b in (-1, 0, 1) if a or b]:
        greet(*way)

    for i in range(2):
        @pl.when(jnp.logical_not(there[i]))
        def _(i=i):
            xra[i] = jnp.zeros(xra.shape[1:], f32)
            xrb[i] = jnp.zeros(xrb.shape[1:], f32)
            for j in range(2):
                dr[i, j] = zero
            for slot in range(2):
                for p in range(3):
                    xr[slot, p, i] = jnp.zeros(xr.shape[3:], f32)
                    for j in range(2):
                        er[slot, p, i, j] = jnp.zeros((2, 128), f32)

    for p in range(3):
        for f in range(3):
            for z in range(-1, 9):
                V[p, f, pl.ds(rows(z, -8), 8), :] = zero
            for z in (-1, 8):
                V[p, f, level(z), :] = zero

    for load in loads[:4]:
        load.wait()

    def side_by_side(parts, t):
        tile = zero
        for k, v in enumerate(parts):
            shift = (WIDE * k + (WIDE if t else 0)) % 128
            v = pltpu.roll(v, shift, 1) if shift else v
            tile = jnp.where((lane >= WIDE * k) & (lane < WIDE * (k + 1)), v, tile)
        return tile

    def cut(t):
        return slice(128 * t, 128 * t + 128)

    for i in range(2):
        for z in range(8):
            ys[i, z] = side_by_side(
                [state[f, z, :, cut(i)] for f in range(9)] + [region[z, :, cut(i)].astype(f32)], i)
        ys[i, 8] = side_by_side([source[s, :, cut(i)] for s in range(STEPS)] + [floor[:, cut(i)].astype(f32)], i)

    def remote(src, dst, send, recv, way):
        return pltpu.make_async_remote_copy(
            src_ref=src, dst_ref=dst, send_sem=send, recv_sem=recv, device_id=at(*way), device_id_type=MESH)

    def first(k, back, src, dst, way):
        return remote(src, dst, first_send.at[k], first_recv.at[back], way)

    def xa_first(i):
        return first(i, 1 - i, xa.at[i], xra.at[1 - i], (0, sides[i], 0))

    def za_first(i):
        return first(2 + i, 3 - i, za.at[i], zra.at[1 - i], (sides[i], 0, 0))

    def y_first(i):
        return first(4 + i, 5 - i, ys.at[i], yr.at[1 - i], (0, 0, sides[i]))

    def xy_first(i, j):
        return first(6 + 2 * i + j, 9 - 2 * i - j, ds.at[i, j], dr.at[1 - i, 1 - j], (0, sides[i], sides[j]))

    def zy_first(i, j):
        return first(10 + 2 * i + j, 13 - 2 * i - j, ds.at[2 + i, j], dr.at[3 - i, 1 - j], (sides[i], 0, sides[j]))

    def xb_first(i):
        return first(14 + i, 15 - i, xb.at[i], xrb.at[1 - i], (0, sides[i], 0))

    def zb_first(i):
        return first(16 + i, 17 - i, zb.at[i], zrb.at[1 - i], (sides[i], 0, 0))

    for load in loads[4:]:
        load.wait()
    scale = 0.5 * COURANT
    tables = [[t[k] * scale for k in range(REGIONS)] for t in (lame, shear, buoy)]

    def materials(number, seafloor, z):
        bits = [(number & (1 << k)) != 0 for k in range(4)]
        solid = (dom * 8 + z) >= seafloor
        lam, mu, b = (pick(bits, t) for t in tables)
        return lam, jnp.where(solid, mu, 0.0), b, solid

    def put(ref, index, pair):
        ref[(MIDDLE, *index)] = jnp.where(lane < SEAM, pair[1], pair[0])
        ref[(LEFT, *index)] = pair[0]
        ref[(RIGHT, *index)] = pair[1]

    def put_margin(ref, index, v):
        ref[(LEFT, *index)] = jnp.where(lane >= 128 - WIDE, v, ref[(LEFT, *index)])
        ref[(RIGHT, *index)] = jnp.where(lane < WIDE, v, ref[(RIGHT, *index)])

    everywhere = slice(None)
    for s in range(STEPS):
        put(SRC, (pl.ds(8 * s, 8), everywhere),
            [jnp.where(dom == 0, source[s, :, cut(t)], 0.0) for t in range(2)])
    for z in range(8):
        made = [materials(region[z, :, cut(t)], floor[:, cut(t)], z) for t in range(2)]
        for k, ref in enumerate((L, M, B)):
            put(ref, (pl.ds(8 * z, 8), everywhere), [m[k] for m in made])
        for f in range(9):
            v = [state[f, z, :, cut(t)] for t in range(2)]
            if f < 3:
                put(V, (f, level(z), everywhere), v)
            else:
                if f >= 6:
                    v = [jnp.where(m[3], w, 0.0) for m, w in zip(made, v)]
                elif z == 0:
                    v = [w + jnp.where(dom == 0, source[0, :, cut(t)], 0.0) for t, w in enumerate(v)]
                put(S, (f - 3, level(z), everywhere), v)

    x_fields, z_fields = (0, 3, 4), (2, 4, 5)
    pair = (LEFT, RIGHT)
    for i, x in ((0, 0), (1, 7)):
        parts = [[S[p, f, column(x), :] for p in pair] for f in x_fields]
        parts += [[m[p, pl.ds(x, 8, stride=8), :] for p in pair] for m in (L, M)]
        parts += [[SRC[p, pl.ds(x, 6, stride=8), :] for p in pair]]
        for k in range(6):
            for t in range(2):
                if k < 3:
                    xa[i, 2 * k + t] = parts[k][t]
                elif k < 5:
                    xb[i, 2 * k + t - 6] = parts[k][t]
                else:
                    xb[i, 2 * k + t - 6] = jnp.concatenate([parts[k][t], jnp.zeros((2, 128), f32)], 0)
        for j in range(2):
            ds[i, j] = side_by_side([v[j] for v in parts[:5]] + [xb[i, 4 + j]], j)
    for i, z in ((0, 0), (1, 7)):
        parts = [[S[p, f, level(z), :] for p in pair] for f in z_fields]
        parts += [[m[p, pl.ds(8 * z, 8), :] for p in pair] for m in (L, M)]
        for k in range(5):
            for t in range(2):
                if k < 3:
                    za[i, 2 * k + t] = parts[k][t]
                else:
                    zb[i, 2 * k + t - 6] = parts[k][t]
        for j in range(2):
            ds[2 + i, j] = side_by_side([v[j] for v in parts], j)

    pl.semaphore_wait(barrier, 8 + 5 * (there[0].astype(jnp.int32) + there[1].astype(jnp.int32)))
    for i in range(2):
        @functools.partial(reach, i)
        def _(i=i):
            xa_first(i).start()
            for j in range(2):
                xy_first(i, j).start()
    for i in range(2):
        y_first(i).start()
        za_first(i).start()
        for j in range(2):
            zy_first(i, j).start()
    for i in range(2):
        @functools.partial(reach, i)
        def _(i=i):
            xb_first(i).start()
        zb_first(i).start()

    left = (lane >= 128 - WIDE) & (gy > 0)
    right = (lane < WIDE) & (gy < n_gy - 1)
    inside = left | right

    def margin(low, high, f):
        shift_r = (128 - WIDE * f) % 128
        shift_l = (256 - WIDE - WIDE * f) % 128
        a = pltpu.roll(high, shift_r, 1) if shift_r else high
        c = pltpu.roll(low, shift_l, 1) if shift_l else low
        return jnp.where(left, c, jnp.where(right, a, 0.0))

    for i in range(2):
        za_first(1 - i).wait_recv()

        @functools.partial(reach, i)
        def _(i=i):
            xa_first(1 - i).wait_recv()

    def three(first_tile, second_tile, edge):
        return (
            jnp.where(lane < SEAM, second_tile, first_tile),
            jnp.where(lane >= 128 - WIDE, edge, first_tile),
            jnp.where(lane < WIDE, edge, second_tile),
        )

    def border(parts):
        for i, x in ((0, -1), (1, 8)):
            for k, f in enumerate(x_fields):
                edge = zero if parts == (MIDDLE,) else margin(dr[i, 0], dr[i, 1], k)
                tiles = three(xra[i, 2 * k], xra[i, 2 * k + 1], edge)
                for p in parts:
                    S[p, f, column(x), :] = tiles[p]
        for i, z in ((0, -1), (1, 8)):
            for k, f in enumerate(z_fields):
                edge = zero if parts == (MIDDLE,) else margin(dr[2 + i, 0], dr[2 + i, 1], k)
                tiles = three(zra[i, 2 * k], zra[i, 2 * k + 1], edge)
                for p in parts:
                    S[p, f, level(z), :] = jnp.where(z_there[i], tiles[p], 0.0)

    border((MIDDLE,))
    def place(p):
        return (lane + (52 - 42 * p)) & 127

    def squeeze(where, row, k, sixth):
        return jnp.where(where < NEED, row, pltpu.roll(sixth, NEED - SPARE * k, 1))

    def restore(where, tiles):
        sixth = pltpu.roll(tiles[4], 5 * SPARE, 1)
        for k in range(4):
            sixth = jnp.where((where >= SPARE * k) & (where < SPARE * (k + 1)), pltpu.roll(tiles[k], SPARE * (k + 1), 1), sixth)
        return sixth

    def x_copy(p, i, slot, last):
        src, dst = xs.at[p, i], xr.at[slot, p, 1 - i]
        if last:
            src, dst = src.at[0:3], dst.at[0:3]
        return remote(src, dst, send_sem.at[p, i], recv_sem.at[slot, p, 1 - i], (0, sides[i], 0))

    def z_copy(p, i, slot, last):
        src, dst = zs.at[p, i], zr.at[slot, p, 1 - i]
        if last:
            src, dst = src.at[0:3], dst.at[0:3]
        return remote(src, dst, send_sem.at[p, 2 + i], recv_sem.at[slot, p, 3 - i], (sides[i], 0, 0))

    def e_copy(p, i, j, slot):
        return remote(
            es.at[p, i, j], er.at[slot, p, 1 - i, 1 - j], send_sem.at[p, 4 + 2 * i + j],
            recv_sem.at[slot, p, 7 - 2 * i - j], (sides[j], sides[i], 0))

    def sent(p, slot, last):
        for i in range(2):
            @functools.partial(reach, i)
            def _(i=i):
                x_copy(p, i, slot, last).wait_send()
                if not last:
                    for j in range(2):
                        e_copy(p, i, j, slot).wait_send()
            z_copy(p, i, slot, last).wait_send()

    def move(p, s, slot, begin=False, last=False):
        if not begin:
            at_step = pl.ds(8 * s if last else pl.multiple_of(8 * s, 8), 8)
            added = SRC[p, at_step, :]
            for f in range(3):
                S[p, f, level(0), :] += added
            for i, x in ((0, -1), (1, 8)):
                S[p, 0, pl.ds(rows(0, x), 1), :] += SX[i, p, pl.ds(s, 1), :]
        for z in range(8):
            own = level(z)
            after, before = pl.ds(rows(z, 1), 8), pl.ds(rows(z, -1), 8)
            above, below = level(z + 1), level(z - 1)

            def dx(f):
                return S[p, f, after, :] - S[p, f, before, :]

            def dz(f):
                return S[p, f, above, :] - S[p, f, below, :]

            b = B[p, pl.ds(8 * z, 8), :]
            V[p, 0, own, :] -= b * (dx(0) + dy(S[p, 3, own, :]) + dz(4))
            V[p, 1, own, :] -= b * (dx(3) + dy(S[p, 1, own, :]) + dz(5))
            V[p, 2, own, :] -= b * (dx(4) + dy(S[p, 5, own, :]) + dz(2))

        if not begin:
            sent(p, slot, False)
        where = place(p)
        for i, (x, inner) in enumerate(((0, 1), (7, 6))):
            near = [V[p, f, column(x), :] for f in range(3)]
            if last:
                for f in range(3):
                    xs[p, i, f] = near[f]
            else:
                far = [V[p, f, column(inner), :] for f in range(3)]
                for k, row in enumerate(near + [far[0], far[2]]):
                    xs[p, i, k] = squeeze(where, row, k, far[1])
            if not last:
                for j in range(2):
                    for k, f in enumerate((0, 2)):
                        es[p, i, j, k : k + 1, :] = V[p, f, pl.ds(rows(7 * j, x), 1), :]

            @functools.partial(reach, i)
            def _(i=i):
                if not last:
                    for j in range(2):
                        e_copy(p, i, j, slot).start()
                x_copy(p, i, slot, last).start()
        for i, (z, inner) in enumerate(((0, 1), (7, 6))):
            for f in range(3):
                zs[p, i, f] = V[p, f, level(z), :]
                if not last:
                    zs[p, i, 3 + f] = V[p, f, level(inner), :]
            z_copy(p, i, slot, last).start()

        for z in range(8):
            own = level(z)
            after, before = pl.ds(rows(z, 1), 8), pl.ds(rows(z, -1), 8)
            above, below = level(z + 1), level(z - 1)
            dxs = [V[p, f, after, :] - V[p, f, before, :] for f in range(3)]
            dzs = [V[p, f, above, :] - V[p, f, below, :] for f in range(3)]
            dys = [dy(V[p, f, own, :]) for f in range(3)]
            lam, mu = L[p, pl.ds(8 * z, 8), :], M[p, pl.ds(8 * z, 8), :]
            spread = lam * (dxs[0] + dys[1] + dzs[2])
            mu2 = mu + mu
            S[p, 0, own, :] -= spread + mu2 * dxs[0]
            S[p, 1, own, :] -= spread + mu2 * dys[1]
            S[p, 2, own, :] -= spread + mu2 * dzs[2]
            S[p, 3, own, :] -= mu * (dys[0] + dxs[1])
            S[p, 4, own, :] -= mu * (dzs[0] + dxs[2])
            S[p, 5, own, :] -= mu * (dzs[1] + dys[2])

    def finish(p, slot, last=False):
        for i in range(2):
            z_copy(p, 1 - i, slot, last).wait_recv()
        for i, z in ((0, 0), (1, 7)):
            near = [zr[slot, p, i, f] for f in range(3)]
            own = level(z)
            lam, mu = L[p, pl.ds(8 * z, 8), :], M[p, pl.ds(8 * z, 8), :]
            sign = jnp.where(z_there[i], (-1.0, 1.0)[i], 0.0)
            slope = [sign * v for v in near]
            spread = lam * slope[2]
            S[p, 0, own, :] -= spread
            S[p, 1, own, :] -= spread
            S[p, 2, own, :] -= spread + (mu + mu) * slope[2]
            S[p, 4, own, :] -= mu * slope[0]
            S[p, 5, own, :] -= mu * slope[1]

        for i in range(2):
            @functools.partial(reach, i)
            def _(i=i):
                x_copy(p, 1 - i, slot, last).wait_recv()
                if not last:
                    for j in range(2):
                        e_copy(p, 1 - i, 1 - j, slot).wait_recv()

        for i, x, sign in ((0, 0, -1.0), (1, 7, 1.0)):
            near = [xr[slot, p, i, f] for f in range(3)]
            lam, mu = L[p, pl.ds(x, 8, stride=8), :], M[p, pl.ds(x, 8, stride=8), :]
            slope = [sign * v for v in near]
            spread = lam * slope[0]
            S[p, 0, column(x), :] -= spread + (mu + mu) * slope[0]
            S[p, 1, column(x), :] -= spread
            S[p, 2, column(x), :] -= spread
            S[p, 3, column(x), :] -= mu * slope[1]
            S[p, 4, column(x), :] -= mu * slope[2]

        if last:
            return
        where = place(p)
        for i, x, sign in ((0, 0, -1.0), (1, 7, 1.0)):
            got = [xr[slot, p, i, k] for k in range(5)]
            near, far = got[0:3], (got[3], restore(where, got), got[4])
            lam, mu = LX[i, p], MX[i, p]
            dxs = [sign * (far[f] - V[p, f, column(x), :]) for f in range(3)]
            dzs = {}
            for k, f in enumerate((0, 2)):
                top, bottom = (jnp.where(z_there[j], er[slot, p, i, j, k : k + 1, :], 0.0) for j in range(2))
                down = jnp.where(sub == 0, top, pltpu.roll(near[f], 1, 0))
                up = jnp.where(sub == 7, bottom, pltpu.roll(near[f], 7, 0))
                dzs[f] = up - down
            trace = dxs[0] + dy(near[1]) + dzs[2]
            beyond = column((-1, 8)[i])
            S[p, 0, beyond, :] -= lam * trace + (mu + mu) * dxs[0]
            S[p, 3, beyond, :] -= mu * (dy(near[0]) + dxs[1])
            S[p, 4, beyond, :] -= mu * (dzs[0] + dxs[2])
        for i, z, sign in ((0, 0, -1.0), (1, 7, 1.0)):
            near, far = [zr[slot, p, i, f] for f in range(3)], [zr[slot, p, i, 3 + f] for f in range(3)]
            lam, mu = LZ[i, p], MZ[i, p]
            dzs = [sign * (far[f] - V[p, f, level(z), :]) for f in range(3)]
            dxs = {}
            for k, f in enumerate((0, 2)):
                low, high = (er[slot, p, j, i, k : k + 1, :] for j in range(2))
                behind = jnp.where(sub == 0, low, pltpu.roll(near[f], 1, 0))
                ahead = jnp.where(sub == 7, high, pltpu.roll(near[f], 7, 0))
                dxs[f] = ahead - behind
            trace = dxs[0] + dy(near[1]) + dzs[2]
            beyond = level((-1, 8)[i])
            S[p, 2, beyond, :] -= lam * trace + (mu + mu) * dzs[2]
            S[p, 4, beyond, :] -= mu * (dzs[0] + dxs[2])
            S[p, 5, beyond, :] -= mu * (dzs[1] + dy(near[2]))

    def each_part(then):
        def body(p, carry):
            then(p)
            return carry

        lax.fori_loop(0, 3, body, 0)

    move(MIDDLE, 0, 0, begin=True)

    for i in range(2):
        y_first(1 - i).wait_recv()
    low, high = yr[0, 8], yr[1, 8]
    seafloor = margin(low, high, STEPS).astype(jnp.int32)
    first_source = None
    for s in range(STEPS):
        v = jnp.where(dom == 0, margin(low, high, s), 0.0)
        first_source = v if s == 0 else first_source
        put_margin(SRC, (pl.ds(8 * s, 8), everywhere), v)
    for z in range(8):
        low, high = yr[0, z], yr[1, z]
        lam, mu, b, solid = materials(margin(low, high, 9).astype(jnp.int32), seafloor, z)
        for ref, v in ((L, lam), (M, mu), (B, b)):
            put_margin(ref, (pl.ds(8 * z, 8), everywhere), jnp.where(inside, v, 0.0))
        for f in range(9):
            v = margin(low, high, f)
            if f < 3:
                put_margin(V, (f, level(z), everywhere), v)
            else:
                if f >= 6:
                    v = jnp.where(solid, v, 0.0)
                elif z == 0:
                    v = v + first_source
                put_margin(S, (f - 3, level(z), everywhere), v)

    for i in range(2):
        for j in range(2):
            zy_first(1 - i, 1 - j).wait_recv()

        @functools.partial(reach, i)
        def _(i=i):
            for j in range(2):
                xy_first(1 - i, 1 - j).wait_recv()
    border((LEFT, RIGHT))

    def begin(p, carry):
        move(p, 0, 0, begin=True)
        return carry

    lax.fori_loop(1, 3, begin, 0)

    for i in range(2):
        zb_first(1 - i).wait_recv()

        @functools.partial(reach, i)
        def _(i=i):
            xb_first(1 - i).wait_recv()
    for i in range(2):
        for k, ref in enumerate((LX, MX, SX)):
            tiles = three(xrb[i, 2 * k], xrb[i, 2 * k + 1], margin(dr[i, 0], dr[i, 1], 3 + k))
            for p in range(3):
                ref[i, p] = tiles[p]
        for k, ref in enumerate((LZ, MZ)):
            tiles = three(zrb[i, 2 * k], zrb[i, 2 * k + 1], margin(dr[2 + i, 0], dr[2 + i, 1], 3 + k))
            for p in range(3):
                ref[i, p] = jnp.where(z_there[i], tiles[p], 0.0)

    def step(s, carry):
        slot = lax.rem(s, 2)

        def turn(p):
            finish(p, 1 - slot)
            move(p, s, slot)

        each_part(turn)
        return carry

    lax.fori_loop(1, STEPS - 1, step, 0)

    end = STEPS - 1

    def final(p):
        finish(p, (end - 1) % 2)
        move(p, end, end % 2, last=True)

    each_part(final)

    def gather(f, ref, k):
        for z in range(8):
            middle, first_tile, second_tile = (ref[p, k, level(z), :] for p in (MIDDLE, LEFT, RIGHT))
            out[f, z, :, cut(0)] = jnp.where(lane < FIRST_CUT, first_tile, middle)
            out[f, z, :, cut(1)] = jnp.where(lane < SECOND_CUT, middle, second_tile)

    for f in range(3):
        gather(f, V, f)
    each_part(lambda p: finish(p, end % 2, last=True))
    for f in range(6):
        gather(3 + f, S, f)

    each_part(lambda p: sent(p, end % 2, True))
    for i in range(2):
        y_first(i).wait_send()
        za_first(i).wait_send()
        zb_first(i).wait_send()
        for j in range(2):
            zy_first(i, j).wait_send()

        @functools.partial(reach, i)
        def _(i=i):
            xa_first(i).wait_send()
            xb_first(i).wait_send()
            for j in range(2):
                xy_first(i, j).wait_send()


def solution(mesh):
    sizes = (mesh.shape["dom"], mesh.shape["gx"], mesh.shape["gy"])

    def on_device(state, source, floor, region, lame, shear, buoy):
        hbm = pl.BlockSpec(memory_space=pltpu.HBM)

        def tiles(*shape):
            return pltpu.VMEM(shape + (8, 128), f32)

        return pl.pallas_call(
            functools.partial(kernel, sizes),
            out_shape=jax.ShapeDtypeStruct(state.shape, f32),
            in_specs=[hbm] * 7,
            out_specs=pl.BlockSpec(memory_space=pltpu.VMEM),
            scratch_shapes=[
                pltpu.VMEM(state.shape, f32),
                pltpu.VMEM(source.shape, f32),
                pltpu.VMEM(floor.shape, jnp.int32),
                pltpu.VMEM(region.shape, jnp.int32),
                pltpu.SMEM(lame.shape, f32),
                pltpu.SMEM(shear.shape, f32),
                pltpu.SMEM(buoy.shape, f32),
                pltpu.VMEM((3, 6, 10 * BLOCK, 128), f32),
                pltpu.VMEM((3, 3, 10 * BLOCK, 128), f32),
                pltpu.VMEM((3, 64, 128), f32),
                pltpu.VMEM((3, 64, 128), f32),
                pltpu.VMEM((3, 64, 128), f32),
                pltpu.VMEM((3, 8 * STEPS, 128), f32),
                tiles(2, 3),
                tiles(2, 3),
                tiles(2, 3),
                tiles(2, 3),
                tiles(2, 3),
                tiles(2, 9),
                tiles(2, 9),
                tiles(2, 6),
                tiles(2, 6),
                tiles(2, 6),
                tiles(2, 6),
                tiles(2, 6),
                tiles(2, 6),
                tiles(2, 4),
                tiles(2, 4),
                tiles(4, 2),
                tiles(4, 2),
                tiles(3, 2, 5),
                tiles(2, 3, 2, 5),
                tiles(3, 2, 6),
                tiles(2, 3, 2, 6),
                pltpu.VMEM((3, 2, 2, 2, 128), f32),
                pltpu.VMEM((2, 3, 2, 2, 2, 128), f32),
                pltpu.SemaphoreType.DMA((7,)),
                pltpu.SemaphoreType.DMA((18,)),
                pltpu.SemaphoreType.DMA((18,)),
                pltpu.SemaphoreType.DMA((3, 8)),
                pltpu.SemaphoreType.DMA((2, 3, 8)),
            ],
            compiler_params=pltpu.CompilerParams(
                collective_id=0, has_side_effects=True, vmem_limit_bytes=32 * 1024 * 1024
            ),
        )(*(
            pltpu.with_memory_space_constraint(v, pltpu.HBM)
            for v in (state, source, floor, region, lame, shear, buoy)
        ))

    return jax.shard_map(
        on_device,
        mesh=mesh,
        in_specs=(
            P(None, "dom", "gx", "gy"),
            P(None, "gx", "gy"),
            P("gx", "gy"),
            P("dom", "gx", "gy"),
            P(),
            P(),
            P(),
        ),
        out_specs=P(None, "dom", "gx", "gy"),
        check_vma=False,
    )
```

```python
import functools

import jax
import jax.numpy as jnp
from jax import lax
from jax.experimental import pallas as pl
from jax.experimental.pallas import tpu as pltpu
from jax.sharding import PartitionSpec as P

STEPS = 6
COURANT = 0.25
REGIONS = 16
BLOCK = 16
WIDE = 12
MIDDLE, LEFT, RIGHT = 0, 1, 2
FIRST_CUT, SECOND_CUT, SEAM = 86, 171 - 128, 64
MESH = pl.DeviceIdType.MESH

f32 = jnp.float32


def rows(z, x=0):
    return (z + 1) * BLOCK + 8 + x


def level(z):
    return pl.ds(rows(z), 8)


def column(x):
    return pl.ds(rows(0, x), 8, stride=BLOCK)


def dy(v):
    return pltpu.roll(v, 127, 1) - pltpu.roll(v, 1, 1)


def pick(bits, table):
    values = list(table)
    for bit in bits:
        values = [jnp.where(bit, values[2 * i + 1], values[2 * i]) for i in range(len(values) // 2)]
    return values[0]


def kernel(
    sizes, state_in, source_in, floor_in, region_in, lame_in, shear_in, buoy_in, out,
    state, source, floor, region, lame, shear, buoy,
    S, V, L, M, B, SRC, LX, MX, SX, LZ, MZ, OX, OZ, XR0, ZR0, YR, XR, ZR,
    in_sem, x_send, z_send, x_first_recv, z_first_recv, y_recv, x_recv, z_recv,
):
    n_dom, n_gx, n_gy = sizes
    dom, gx, gy = lax.axis_index("dom"), lax.axis_index("gx"), lax.axis_index("gy")
    lane = lax.broadcasted_iota(jnp.int32, (8, 128), 1)
    sub = lax.broadcasted_iota(jnp.int32, (8, 128), 0)
    zero = jnp.zeros((8, 128), f32)

    loads = [
        pltpu.make_async_copy(src, dst, in_sem.at[i])
        for i, (src, dst) in enumerate((
            (region_in, region), (floor_in, floor), (source_in, source), (state_in, state),
            (lame_in, lame), (shear_in, shear), (buoy_in, buoy)))
    ]
    for load in loads:
        load.start()

    sides = (-1, 1)
    there = [gx > 0, gx < n_gx - 1]
    z_there = [dom > 0, dom < n_dom - 1]

    doms = [dom, jnp.where(dom == n_dom - 1, 0, dom + 1), jnp.where(dom == 0, n_dom - 1, dom - 1)]
    gxs = [gx, gx + 1, gx - 1]
    gys = [gy, jnp.where(gy == n_gy - 1, 0, gy + 1), jnp.where(gy == 0, n_gy - 1, gy - 1)]

    def at(dz, dx, dyy):
        return (doms[dz], gxs[dx], gys[dyy])

    def reach(i, then):
        pl.when(there[i])(then)

    barrier = pltpu.get_barrier_semaphore()

    def greet(*way):
        pl.semaphore_signal(barrier, inc=1, device_id=at(*way), device_id_type=MESH)

    for i, dx in enumerate(sides):
        @functools.partial(reach, i)
        def _(dx=dx):
            for way in ((0, dx, 0), (-1, dx, 0), (1, dx, 0), (0, dx, -1), (0, dx, 1)):
                greet(*way)
    for way in [(a, 0, b) for a in (-1, 0, 1) for b in (-1, 0, 1) if a or b]:
        greet(*way)

    for i in range(2):
        @pl.when(jnp.logical_not(there[i]))
        def _(i=i):
            XR0[i] = jnp.zeros(XR0.shape[1:], f32)
            for slot in range(2):
                for p in range(3):
                    XR[slot, p, i] = jnp.zeros(XR.shape[3:], f32)

    for p in range(3):
        for f in range(3):
            for z in range(-1, 9):
                V[p, f, pl.ds(rows(z, -8), 8), :] = zero
            for z in (-1, 8):
                V[p, f, level(z), :] = zero

    for load in loads[:4]:
        load.wait()

    def side_by_side(parts, t):
        tile = zero
        for k, v in enumerate(parts):
            shift = (WIDE * k + (WIDE if t else 0)) % 128
            v = pltpu.roll(v, shift, 1) if shift else v
            tile = jnp.where((lane >= WIDE * k) & (lane < WIDE * (k + 1)), v, tile)
        return tile

    def cut(t):
        return slice(128 * t, 128 * t + 128)

    for i in range(2):
        for z in range(8):
            OZ[i, 111 + z] = side_by_side(
                [state[f, z, :, cut(i)] for f in range(9)] + [region[z, :, cut(i)].astype(f32)], i)
        OZ[i, 119] = side_by_side([source[s, :, cut(i)] for s in range(STEPS)] + [floor[:, cut(i)].astype(f32)], i)

    def remote(src, dst, send, recv, way):
        return pltpu.make_async_remote_copy(
            src_ref=src, dst_ref=dst, send_sem=send, recv_sem=recv, device_id=at(*way), device_id_type=MESH)

    def xa_first(i):
        return remote(OX.at[i, 0:6], XR0.at[1 - i, 0:6], x_send.at[i], x_first_recv.at[0, 1 - i], (0, sides[i], 0))

    def xy_first(i, j):
        return remote(
            OX.at[i, 6 + j], XR0.at[1 - i, 7 - j], x_send.at[i], x_first_recv.at[0, 1 - i], (0, sides[i], sides[j]))

    def xb_first(i):
        return remote(OX.at[i, 8:14], XR0.at[1 - i, 8:14], x_send.at[i], x_first_recv.at[1, 1 - i], (0, sides[i], 0))

    def za_first(i):
        return remote(OZ.at[i, 0:6], ZR0.at[1 - i, 0:6], z_send.at[i], z_first_recv.at[0], (sides[i], 0, 0))

    def zy_first(i, j):
        return remote(
            OZ.at[i, 6 + j], ZR0.at[1 - i, 7 - j], z_send.at[i], z_first_recv.at[0], (sides[i], 0, sides[j]))

    def zb_first(i):
        return remote(OZ.at[i, 8:12], ZR0.at[1 - i, 8:12], z_send.at[i], z_first_recv.at[1], (sides[i], 0, 0))

    def y_first(i):
        return remote(OZ.at[i, 111:120], YR.at[1 - i], z_send.at[i], y_recv.at[0], (0, 0, sides[i]))

    def arrived(ref, sem):
        pltpu.make_async_copy(ref, ref, sem).wait()

    for load in loads[4:]:
        load.wait()
    scale = 0.5 * COURANT
    tables = [[t[k] * scale for k in range(REGIONS)] for t in (lame, shear, buoy)]

    def materials(number, seafloor, z):
        bits = [(number & (1 << k)) != 0 for k in range(4)]
        solid = (dom * 8 + z) >= seafloor
        lam, mu, b = (pick(bits, t) for t in tables)
        return lam, jnp.where(solid, mu, 0.0), b, solid

    def put(ref, index, pair):
        ref[(MIDDLE, *index)] = jnp.where(lane < SEAM, pair[1], pair[0])
        ref[(LEFT, *index)] = pair[0]
        ref[(RIGHT, *index)] = pair[1]

    def put_margin(ref, index, v):
        ref[(LEFT, *index)] = jnp.where(lane >= 128 - WIDE, v, ref[(LEFT, *index)])
        ref[(RIGHT, *index)] = jnp.where(lane < WIDE, v, ref[(RIGHT, *index)])

    everywhere = slice(None)
    for s in range(STEPS):
        put(SRC, (pl.ds(8 * s, 8), everywhere),
            [jnp.where(dom == 0, source[s, :, cut(t)], 0.0) for t in range(2)])
    for z in range(8):
        made = [materials(region[z, :, cut(t)], floor[:, cut(t)], z) for t in range(2)]
        for k, ref in enumerate((L, M, B)):
            put(ref, (pl.ds(8 * z, 8), everywhere), [m[k] for m in made])
        for f in range(9):
            v = [state[f, z, :, cut(t)] for t in range(2)]
            if f < 3:
                put(V, (f, level(z), everywhere), v)
            else:
                if f >= 6:
                    v = [jnp.where(m[3], w, 0.0) for m, w in zip(made, v)]
                elif z == 0:
                    v = [w + jnp.where(dom == 0, source[0, :, cut(t)], 0.0) for t, w in enumerate(v)]
                put(S, (f - 3, level(z), everywhere), v)

    x_fields, z_fields = (0, 3, 4), (2, 4, 5)
    pair = (LEFT, RIGHT)
    for i, x in ((0, 0), (1, 7)):
        parts = [[S[p, f, column(x), :] for p in pair] for f in x_fields]
        parts += [[m[p, pl.ds(x, 8, stride=8), :] for p in pair] for m in (L, M)]
        parts += [[
            jnp.concatenate([SRC[p, pl.ds(x, STEPS, stride=8), :], jnp.zeros((8 - STEPS, 128), f32)], 0) for p in pair]]
        for k in range(6):
            for t in range(2):
                OX[i, 2 * k + t + (0 if k < 3 else 2)] = parts[k][t]
        for j in range(2):
            OX[i, 6 + j] = side_by_side([v[j] for v in parts], j)
    for i, z in ((0, 0), (1, 7)):
        parts = [[S[p, f, level(z), :] for p in pair] for f in z_fields]
        parts += [[m[p, pl.ds(8 * z, 8), :] for p in pair] for m in (L, M)]
        for k in range(5):
            for t in range(2):
                OZ[i, 2 * k + t + (0 if k < 3 else 2)] = parts[k][t]
        for j in range(2):
            OZ[i, 6 + j] = side_by_side([v[j] for v in parts], j)

    pl.semaphore_wait(barrier, 8 + 5 * (there[0].astype(jnp.int32) + there[1].astype(jnp.int32)))
    for i in range(2):
        @functools.partial(reach, i)
        def _(i=i):
            xa_first(i).start()
            for j in range(2):
                xy_first(i, j).start()
    for i in range(2):
        y_first(i).start()
        za_first(i).start()
        for j in range(2):
            zy_first(i, j).start()
    for i in range(2):
        @functools.partial(reach, i)
        def _(i=i):
            xb_first(i).start()
        zb_first(i).start()

    left = (lane >= 128 - WIDE) & (gy > 0)
    right = (lane < WIDE) & (gy < n_gy - 1)
    inside = left | right

    def margin(low, high, f):
        shift_r = (128 - WIDE * f) % 128
        shift_l = (256 - WIDE - WIDE * f) % 128
        a = pltpu.roll(high, shift_r, 1) if shift_r else high
        c = pltpu.roll(low, shift_l, 1) if shift_l else low
        return jnp.where(left, c, jnp.where(right, a, 0.0))

    arrived(ZR0.at[:, 0:8], z_first_recv.at[0])
    for i in range(2):
        @functools.partial(reach, i)
        def _(i=i):
            arrived(XR0.at[i, 0:8], x_first_recv.at[0, i])

    def three(first_tile, second_tile, edge):
        return (
            jnp.where(lane < SEAM, second_tile, first_tile),
            jnp.where(lane >= 128 - WIDE, edge, first_tile),
            jnp.where(lane < WIDE, edge, second_tile),
        )

    def border(parts):
        for i, x in ((0, -1), (1, 8)):
            for k, f in enumerate(x_fields):
                edge = zero if parts == (MIDDLE,) else margin(XR0[i, 6], XR0[i, 7], k)
                tiles = three(XR0[i, 2 * k], XR0[i, 2 * k + 1], edge)
                for p in parts:
                    S[p, f, column(x), :] = tiles[p]
        for i, z in ((0, -1), (1, 8)):
            for k, f in enumerate(z_fields):
                edge = zero if parts == (MIDDLE,) else margin(ZR0[i, 6], ZR0[i, 7], k)
                tiles = three(ZR0[i, 2 * k], ZR0[i, 2 * k + 1], edge)
                for p in parts:
                    S[p, f, level(z), :] = jnp.where(z_there[i], tiles[p], 0.0)

    border((MIDDLE,))
    def x_base(p, s, last):
        return 14 + 24 * s + (3 * p if last else 8 * p)

    def z_base(p, s, last):
        return 12 + 18 * s + (3 * p if last else 6 * p)

    def x_copy(p, i, s, slot, last):
        n = 3 if last else 6
        return remote(
            OX.at[i, pl.ds(x_base(p, s, last), n)], XR.at[slot, p, 1 - i, 0:n], x_send.at[i], x_recv.at[slot, p, 1 - i],
            (0, sides[i], 0))

    def e_copy(p, i, j, s, slot):
        return remote(
            OX.at[i, x_base(p, s, False) + 6 + j], XR.at[slot, p, 1 - i, 7 - j], x_send.at[i],
            x_recv.at[slot, p, 1 - i], (sides[j], sides[i], 0))

    def z_copy(p, i, s, slot, last):
        n = 3 if last else 6
        return remote(
            OZ.at[i, pl.ds(z_base(p, s, last), n)], ZR.at[slot, p, 1 - i, 0:n], z_send.at[i], z_recv.at[slot, p],
            (sides[i], 0, 0))

    def move(p, s, slot, begin=False, last=False):
        if not begin:
            at_step = pl.ds(8 * s if last else pl.multiple_of(8 * s, 8), 8)
            added = SRC[p, at_step, :]
            for f in range(3):
                S[p, f, level(0), :] += added
            for i, x in ((0, -1), (1, 8)):
                S[p, 0, pl.ds(rows(0, x), 1), :] += SX[i, p, pl.ds(s, 1), :]
        for z in range(8):
            own = level(z)
            after, before = pl.ds(rows(z, 1), 8), pl.ds(rows(z, -1), 8)
            above, below = level(z + 1), level(z - 1)

            def dx(f):
                return S[p, f, after, :] - S[p, f, before, :]

            def dz(f):
                return S[p, f, above, :] - S[p, f, below, :]

            b = B[p, pl.ds(8 * z, 8), :]
            V[p, 0, own, :] -= b * (dx(0) + dy(S[p, 3, own, :]) + dz(4))
            V[p, 1, own, :] -= b * (dx(3) + dy(S[p, 1, own, :]) + dz(5))
            V[p, 2, own, :] -= b * (dx(4) + dy(S[p, 5, own, :]) + dz(2))

        base = x_base(p, s, last)
        for i, (x, inner) in enumerate(((0, 1), (7, 6))):
            for f in range(3):
                OX[i, base + f] = V[p, f, column(x), :]
                if not last:
                    OX[i, base + 3 + f] = V[p, f, column(inner), :]
            if not last:
                for j in range(2):
                    for k, f in enumerate((0, 2)):
                        OX[i, base + 6 + j, k : k + 1, :] = V[p, f, pl.ds(rows(7 * j, x), 1), :]

            @functools.partial(reach, i)
            def _(i=i):
                if not last:
                    for j in range(2):
                        e_copy(p, i, j, s, slot).start()
                x_copy(p, i, s, slot, last).start()
        base = z_base(p, s, last)
        for i, (z, inner) in enumerate(((0, 1), (7, 6))):
            for f in range(3):
                OZ[i, base + f] = V[p, f, level(z), :]
                if not last:
                    OZ[i, base + 3 + f] = V[p, f, level(inner), :]
            z_copy(p, i, s, slot, last).start()

        for z in range(8):
            own = level(z)
            after, before = pl.ds(rows(z, 1), 8), pl.ds(rows(z, -1), 8)
            above, below = level(z + 1), level(z - 1)
            dxs = [V[p, f, after, :] - V[p, f, before, :] for f in range(3)]
            dzs = [V[p, f, above, :] - V[p, f, below, :] for f in range(3)]
            dys = [dy(V[p, f, own, :]) for f in range(3)]
            lam, mu = L[p, pl.ds(8 * z, 8), :], M[p, pl.ds(8 * z, 8), :]
            spread = lam * (dxs[0] + dys[1] + dzs[2])
            mu2 = mu + mu
            S[p, 0, own, :] -= spread + mu2 * dxs[0]
            S[p, 1, own, :] -= spread + mu2 * dys[1]
            S[p, 2, own, :] -= spread + mu2 * dzs[2]
            S[p, 3, own, :] -= mu * (dys[0] + dxs[1])
            S[p, 4, own, :] -= mu * (dzs[0] + dxs[2])
            S[p, 5, own, :] -= mu * (dzs[1] + dys[2])

    def finish(p, slot, last=False):
        arrived(ZR.at[slot, p, :, 0:3] if last else ZR.at[slot, p], z_recv.at[slot, p])
        for i, z in ((0, 0), (1, 7)):
            near = [ZR[slot, p, i, f] for f in range(3)]
            own = level(z)
            lam, mu = L[p, pl.ds(8 * z, 8), :], M[p, pl.ds(8 * z, 8), :]
            sign = jnp.where(z_there[i], (-1.0, 1.0)[i], 0.0)
            slope = [sign * v for v in near]
            spread = lam * slope[2]
            S[p, 0, own, :] -= spread
            S[p, 1, own, :] -= spread
            S[p, 2, own, :] -= spread + (mu + mu) * slope[2]
            S[p, 4, own, :] -= mu * slope[0]
            S[p, 5, own, :] -= mu * slope[1]

        for i in range(2):
            @functools.partial(reach, i)
            def _(i=i):
                arrived(XR.at[slot, p, i, 0:3] if last else XR.at[slot, p, i], x_recv.at[slot, p, i])

        for i, x, sign in ((0, 0, -1.0), (1, 7, 1.0)):
            near = [XR[slot, p, i, f] for f in range(3)]
            lam, mu = L[p, pl.ds(x, 8, stride=8), :], M[p, pl.ds(x, 8, stride=8), :]
            slope = [sign * v for v in near]
            spread = lam * slope[0]
            S[p, 0, column(x), :] -= spread + (mu + mu) * slope[0]
            S[p, 1, column(x), :] -= spread
            S[p, 2, column(x), :] -= spread
            S[p, 3, column(x), :] -= mu * slope[1]
            S[p, 4, column(x), :] -= mu * slope[2]

        if last:
            return
        for i, x, sign in ((0, 0, -1.0), (1, 7, 1.0)):
            near, far = [XR[slot, p, i, f] for f in range(3)], [XR[slot, p, i, 3 + f] for f in range(3)]
            lam, mu = LX[i, p], MX[i, p]
            dxs = [sign * (far[f] - V[p, f, column(x), :]) for f in range(3)]
            dzs = {}
            for k, f in enumerate((0, 2)):
                top, bottom = (jnp.where(z_there[j], XR[slot, p, i, 6 + j, k : k + 1, :], 0.0) for j in range(2))
                down = jnp.where(sub == 0, top, pltpu.roll(near[f], 1, 0))
                up = jnp.where(sub == 7, bottom, pltpu.roll(near[f], 7, 0))
                dzs[f] = up - down
            trace = dxs[0] + dy(near[1]) + dzs[2]
            beyond = column((-1, 8)[i])
            S[p, 0, beyond, :] -= lam * trace + (mu + mu) * dxs[0]
            S[p, 3, beyond, :] -= mu * (dy(near[0]) + dxs[1])
            S[p, 4, beyond, :] -= mu * (dzs[0] + dxs[2])
        for i, z, sign in ((0, 0, -1.0), (1, 7, 1.0)):
            near, far = [ZR[slot, p, i, f] for f in range(3)], [ZR[slot, p, i, 3 + f] for f in range(3)]
            lam, mu = LZ[i, p], MZ[i, p]
            dzs = [sign * (far[f] - V[p, f, level(z), :]) for f in range(3)]
            dxs = {}
            for k, f in enumerate((0, 2)):
                low, high = (XR[slot, p, j, 6 + i, k : k + 1, :] for j in range(2))
                behind = jnp.where(sub == 0, low, pltpu.roll(near[f], 1, 0))
                ahead = jnp.where(sub == 7, high, pltpu.roll(near[f], 7, 0))
                dxs[f] = ahead - behind
            trace = dxs[0] + dy(near[1]) + dzs[2]
            beyond = level((-1, 8)[i])
            S[p, 2, beyond, :] -= lam * trace + (mu + mu) * dzs[2]
            S[p, 4, beyond, :] -= mu * (dzs[0] + dxs[2])
            S[p, 5, beyond, :] -= mu * (dzs[1] + dy(near[2]))

    def each_part(then):
        def body(p, carry):
            then(p)
            return carry

        lax.fori_loop(0, 3, body, 0)

    move(MIDDLE, 0, 0, begin=True)

    arrived(YR, y_recv.at[0])
    low, high = YR[0, 8], YR[1, 8]
    seafloor = margin(low, high, STEPS).astype(jnp.int32)
    first_source = None
    for s in range(STEPS):
        v = jnp.where(dom == 0, margin(low, high, s), 0.0)
        first_source = v if s == 0 else first_source
        put_margin(SRC, (pl.ds(8 * s, 8), everywhere), v)
    for z in range(8):
        low, high = YR[0, z], YR[1, z]
        lam, mu, b, solid = materials(margin(low, high, 9).astype(jnp.int32), seafloor, z)
        for ref, v in ((L, lam), (M, mu), (B, b)):
            put_margin(ref, (pl.ds(8 * z, 8), everywhere), jnp.where(inside, v, 0.0))
        for f in range(9):
            v = margin(low, high, f)
            if f < 3:
                put_margin(V, (f, level(z), everywhere), v)
            else:
                if f >= 6:
                    v = jnp.where(solid, v, 0.0)
                elif z == 0:
                    v = v + first_source
                put_margin(S, (f - 3, level(z), everywhere), v)

    border((LEFT, RIGHT))

    def begin(p, carry):
        move(p, 0, 0, begin=True)
        return carry

    lax.fori_loop(1, 3, begin, 0)

    arrived(ZR0.at[:, 8:12], z_first_recv.at[1])
    for i in range(2):
        @functools.partial(reach, i)
        def _(i=i):
            arrived(XR0.at[i, 8:14], x_first_recv.at[1, i])
    for i in range(2):
        for k, ref in enumerate((LX, MX, SX)):
            tiles = three(XR0[i, 8 + 2 * k], XR0[i, 9 + 2 * k], margin(XR0[i, 6], XR0[i, 7], 3 + k))
            for p in range(3):
                ref[i, p] = tiles[p]
        for k, ref in enumerate((LZ, MZ)):
            tiles = three(ZR0[i, 8 + 2 * k], ZR0[i, 9 + 2 * k], margin(ZR0[i, 6], ZR0[i, 7], 3 + k))
            for p in range(3):
                ref[i, p] = jnp.where(z_there[i], tiles[p], 0.0)

    def step(s, carry):
        slot = lax.rem(s, 2)

        def turn(p):
            finish(p, 1 - slot)
            move(p, s, slot)

        each_part(turn)
        return carry

    lax.fori_loop(1, STEPS - 1, step, 0)

    end = STEPS - 1

    def final(p):
        finish(p, (end - 1) % 2)
        move(p, end, end % 2, last=True)

    each_part(final)

    def gather(f, ref, k):
        for z in range(8):
            middle, first_tile, second_tile = (ref[p, k, level(z), :] for p in (MIDDLE, LEFT, RIGHT))
            out[f, z, :, cut(0)] = jnp.where(lane < FIRST_CUT, first_tile, middle)
            out[f, z, :, cut(1)] = jnp.where(lane < SECOND_CUT, middle, second_tile)

    for f in range(3):
        gather(f, V, f)
    each_part(lambda p: finish(p, end % 2, last=True))
    for f in range(6):
        gather(3 + f, S, f)

    for i in range(2):
        arrived(OZ.at[i], z_send.at[i])

        @functools.partial(reach, i)
        def _(i=i):
            arrived(OX.at[i], x_send.at[i])


def solution(mesh):
    sizes = (mesh.shape["dom"], mesh.shape["gx"], mesh.shape["gy"])

    def on_device(state, source, floor, region, lame, shear, buoy):
        hbm = pl.BlockSpec(memory_space=pltpu.HBM)

        def tiles(*shape):
            return pltpu.VMEM(shape + (8, 128), f32)

        return pl.pallas_call(
            functools.partial(kernel, sizes),
            out_shape=jax.ShapeDtypeStruct(state.shape, f32),
            in_specs=[hbm] * 7,
            out_specs=pl.BlockSpec(memory_space=pltpu.VMEM),
            scratch_shapes=[
                pltpu.VMEM(state.shape, f32),
                pltpu.VMEM(source.shape, f32),
                pltpu.VMEM(floor.shape, jnp.int32),
                pltpu.VMEM(region.shape, jnp.int32),
                pltpu.SMEM(lame.shape, f32),
                pltpu.SMEM(shear.shape, f32),
                pltpu.SMEM(buoy.shape, f32),
                pltpu.VMEM((3, 6, 10 * BLOCK, 128), f32),
                pltpu.VMEM((3, 3, 10 * BLOCK, 128), f32),
                pltpu.VMEM((3, 64, 128), f32),
                pltpu.VMEM((3, 64, 128), f32),
                pltpu.VMEM((3, 64, 128), f32),
                pltpu.VMEM((3, 8 * STEPS, 128), f32),
                tiles(2, 3),
                tiles(2, 3),
                tiles(2, 3),
                tiles(2, 3),
                tiles(2, 3),
                tiles(2, 143),
                tiles(2, 120),
                tiles(2, 14),
                tiles(2, 12),
                tiles(2, 9),
                tiles(2, 3, 2, 8),
                tiles(2, 3, 2, 6),
                pltpu.SemaphoreType.DMA((7,)),
                pltpu.SemaphoreType.DMA((2,)),
                pltpu.SemaphoreType.DMA((2,)),
                pltpu.SemaphoreType.DMA((2, 2)),
                pltpu.SemaphoreType.DMA((2,)),
                pltpu.SemaphoreType.DMA((1,)),
                pltpu.SemaphoreType.DMA((2, 3, 2)),
                pltpu.SemaphoreType.DMA((2, 3)),
            ],
            compiler_params=pltpu.CompilerParams(
                collective_id=0, has_side_effects=True, vmem_limit_bytes=32 * 1024 * 1024
            ),
        )(*(
            pltpu.with_memory_space_constraint(v, pltpu.HBM)
            for v in (state, source, floor, region, lame, shear, buoy)
        ))

    return jax.shard_map(
        on_device,
        mesh=mesh,
        in_specs=(
            P(None, "dom", "gx", "gy"),
            P(None, "gx", "gy"),
            P("gx", "gy"),
            P("dom", "gx", "gy"),
            P(),
            P(),
            P(),
        ),
        out_specs=P(None, "dom", "gx", "gy"),
        check_vma=False,
    )
```

```python
import functools

import jax
import jax.numpy as jnp
from jax import lax
from jax.experimental import pallas as pl
from jax.experimental.pallas import tpu as pltpu
from jax.sharding import PartitionSpec as P

STEPS = 6
COURANT = 0.25
REGIONS = 16
BLOCK = 16
WIDE = 12
MIDDLE, LEFT, RIGHT = 0, 1, 2
FIRST_CUT, SECOND_CUT, SEAM = 86, 171 - 128, 64
MESH = pl.DeviceIdType.MESH

f32 = jnp.float32


def rows(z, x=0):
    return (z + 1) * BLOCK + 8 + x


def level(z):
    return pl.ds(rows(z), 8)


def column(x):
    return pl.ds(rows(0, x), 8, stride=BLOCK)


def dy(v):
    return pltpu.roll(v, 127, 1) - pltpu.roll(v, 1, 1)


def pick(bits, table):
    values = list(table)
    for bit in bits:
        values = [jnp.where(bit, values[2 * i + 1], values[2 * i]) for i in range(len(values) // 2)]
    return values[0]


def kernel(
    sizes, state_in, source_in, floor_in, region_in, lame_in, shear_in, buoy_in, out,
    state, source, floor, region, lame, shear, buoy,
    S, V, L, M, B, SRC, LX, MX, SX, LZ, MZ, OX, OZ, OE, XR0, ZR0, YR, XR, ZR, ER,
    in_sem, x_send, z_send, e_send, x_first_recv, z_first_recv, y_recv, x_recv, z_recv, e_recv,
):
    n_dom, n_gx, n_gy = sizes
    dom, gx, gy = lax.axis_index("dom"), lax.axis_index("gx"), lax.axis_index("gy")
    lane = lax.broadcasted_iota(jnp.int32, (8, 128), 1)
    sub = lax.broadcasted_iota(jnp.int32, (8, 128), 0)
    zero = jnp.zeros((8, 128), f32)

    loads = [
        pltpu.make_async_copy(src, dst, in_sem.at[i])
        for i, (src, dst) in enumerate((
            (region_in, region), (floor_in, floor), (source_in, source), (state_in, state),
            (lame_in, lame), (shear_in, shear), (buoy_in, buoy)))
    ]
    for load in loads:
        load.start()

    sides = (-1, 1)
    there = [gx > 0, gx < n_gx - 1]
    z_there = [dom > 0, dom < n_dom - 1]

    doms = [dom, jnp.where(dom == n_dom - 1, 0, dom + 1), jnp.where(dom == 0, n_dom - 1, dom - 1)]
    gxs = [gx, gx + 1, gx - 1]
    gys = [gy, jnp.where(gy == n_gy - 1, 0, gy + 1), jnp.where(gy == 0, n_gy - 1, gy - 1)]

    def at(dz, dx, dyy):
        return (doms[dz], gxs[dx], gys[dyy])

    def reach(i, then):
        pl.when(there[i])(then)

    barrier = pltpu.get_barrier_semaphore()

    def greet(*way):
        pl.semaphore_signal(barrier, inc=1, device_id=at(*way), device_id_type=MESH)

    for i, dx in enumerate(sides):
        @functools.partial(reach, i)
        def _(dx=dx):
            for way in ((0, dx, 0), (-1, dx, 0), (1, dx, 0), (0, dx, -1), (0, dx, 1)):
                greet(*way)
    for way in [(a, 0, b) for a in (-1, 0, 1) for b in (-1, 0, 1) if a or b]:
        greet(*way)

    for i in range(2):
        @pl.when(jnp.logical_not(there[i]))
        def _(i=i):
            XR0[i] = jnp.zeros(XR0.shape[1:], f32)
            for slot in range(2):
                for p in range(3):
                    XR[slot, p, i] = jnp.zeros(XR.shape[3:], f32)
                    ER[slot, p, i] = jnp.zeros(ER.shape[3:], f32)

    for p in range(3):
        for f in range(3):
            for z in range(-1, 9):
                V[p, f, pl.ds(rows(z, -8), 8), :] = zero
            for z in (-1, 8):
                V[p, f, level(z), :] = zero

    for load in loads[:4]:
        load.wait()

    def side_by_side(parts, t):
        tile = zero
        for k, v in enumerate(parts):
            shift = (WIDE * k + (WIDE if t else 0)) % 128
            v = pltpu.roll(v, shift, 1) if shift else v
            tile = jnp.where((lane >= WIDE * k) & (lane < WIDE * (k + 1)), v, tile)
        return tile

    def cut(t):
        return slice(128 * t, 128 * t + 128)

    for i in range(2):
        for z in range(8):
            OZ[i, 111 + z] = side_by_side(
                [state[f, z, :, cut(i)] for f in range(9)] + [region[z, :, cut(i)].astype(f32)], i)
        OZ[i, 119] = side_by_side([source[s, :, cut(i)] for s in range(STEPS)] + [floor[:, cut(i)].astype(f32)], i)

    def remote(src, dst, send, recv, way):
        return pltpu.make_async_remote_copy(
            src_ref=src, dst_ref=dst, send_sem=send, recv_sem=recv, device_id=at(*way), device_id_type=MESH)

    def xa_first(i):
        return remote(OX.at[i, 0:6], XR0.at[1 - i, 0:6], x_send.at[i], x_first_recv.at[0, 1 - i], (0, sides[i], 0))

    def xy_first(i, j):
        return remote(
            OX.at[i, 6 + j], XR0.at[1 - i, 7 - j], x_send.at[i], x_first_recv.at[0, 1 - i], (0, sides[i], sides[j]))

    def xb_first(i):
        return remote(OX.at[i, 8:14], XR0.at[1 - i, 8:14], x_send.at[i], x_first_recv.at[1, 1 - i], (0, sides[i], 0))

    def za_first(i):
        return remote(OZ.at[i, 0:6], ZR0.at[1 - i, 0:6], z_send.at[i], z_first_recv.at[0], (sides[i], 0, 0))

    def zy_first(i, j):
        return remote(
            OZ.at[i, 6 + j], ZR0.at[1 - i, 7 - j], z_send.at[i], z_first_recv.at[0], (sides[i], 0, sides[j]))

    def zb_first(i):
        return remote(OZ.at[i, 8:12], ZR0.at[1 - i, 8:12], z_send.at[i], z_first_recv.at[1], (sides[i], 0, 0))

    def y_first(i):
        return remote(OZ.at[i, 111:120], YR.at[1 - i], z_send.at[i], y_recv.at[0], (0, 0, sides[i]))

    def arrived(ref, sem):
        pltpu.make_async_copy(ref, ref, sem).wait()

    for load in loads[4:]:
        load.wait()
    scale = 0.5 * COURANT
    tables = [[t[k] * scale for k in range(REGIONS)] for t in (lame, shear, buoy)]

    def materials(number, seafloor, z):
        bits = [(number & (1 << k)) != 0 for k in range(4)]
        solid = (dom * 8 + z) >= seafloor
        lam, mu, b = (pick(bits, t) for t in tables)
        return lam, jnp.where(solid, mu, 0.0), b, solid

    def put(ref, index, pair):
        ref[(MIDDLE, *index)] = jnp.where(lane < SEAM, pair[1], pair[0])
        ref[(LEFT, *index)] = pair[0]
        ref[(RIGHT, *index)] = pair[1]

    def put_margin(ref, index, v):
        ref[(LEFT, *index)] = jnp.where(lane >= 128 - WIDE, v, ref[(LEFT, *index)])
        ref[(RIGHT, *index)] = jnp.where(lane < WIDE, v, ref[(RIGHT, *index)])

    everywhere = slice(None)
    for s in range(STEPS):
        put(SRC, (pl.ds(8 * s, 8), everywhere),
            [jnp.where(dom == 0, source[s, :, cut(t)], 0.0) for t in range(2)])
    for z in range(8):
        made = [materials(region[z, :, cut(t)], floor[:, cut(t)], z) for t in range(2)]
        for k, ref in enumerate((L, M, B)):
            put(ref, (pl.ds(8 * z, 8), everywhere), [m[k] for m in made])
        for f in range(9):
            v = [state[f, z, :, cut(t)] for t in range(2)]
            if f < 3:
                put(V, (f, level(z), everywhere), v)
            else:
                if f >= 6:
                    v = [jnp.where(m[3], w, 0.0) for m, w in zip(made, v)]
                elif z == 0:
                    v = [w + jnp.where(dom == 0, source[0, :, cut(t)], 0.0) for t, w in enumerate(v)]
                put(S, (f - 3, level(z), everywhere), v)

    x_fields, z_fields = (0, 3, 4), (2, 4, 5)
    pair = (LEFT, RIGHT)
    for i, x in ((0, 0), (1, 7)):
        parts = [[S[p, f, column(x), :] for p in pair] for f in x_fields]
        parts += [[m[p, pl.ds(x, 8, stride=8), :] for p in pair] for m in (L, M)]
        parts += [[
            jnp.concatenate([SRC[p, pl.ds(x, STEPS, stride=8), :], jnp.zeros((8 - STEPS, 128), f32)], 0) for p in pair]]
        for k in range(6):
            for t in range(2):
                OX[i, 2 * k + t + (0 if k < 3 else 2)] = parts[k][t]
        for j in range(2):
            OX[i, 6 + j] = side_by_side([v[j] for v in parts], j)
    for i, z in ((0, 0), (1, 7)):
        parts = [[S[p, f, level(z), :] for p in pair] for f in z_fields]
        parts += [[m[p, pl.ds(8 * z, 8), :] for p in pair] for m in (L, M)]
        for k in range(5):
            for t in range(2):
                OZ[i, 2 * k + t + (0 if k < 3 else 2)] = parts[k][t]
        for j in range(2):
            OZ[i, 6 + j] = side_by_side([v[j] for v in parts], j)

    pl.semaphore_wait(barrier, 8 + 5 * (there[0].astype(jnp.int32) + there[1].astype(jnp.int32)))
    for i in range(2):
        @functools.partial(reach, i)
        def _(i=i):
            xa_first(i).start()
            for j in range(2):
                xy_first(i, j).start()
    for i in range(2):
        y_first(i).start()
        za_first(i).start()
        for j in range(2):
            zy_first(i, j).start()
    for i in range(2):
        @functools.partial(reach, i)
        def _(i=i):
            xb_first(i).start()
        zb_first(i).start()

    left = (lane >= 128 - WIDE) & (gy > 0)
    right = (lane < WIDE) & (gy < n_gy - 1)
    inside = left | right

    def margin(low, high, f):
        shift_r = (128 - WIDE * f) % 128
        shift_l = (256 - WIDE - WIDE * f) % 128
        a = pltpu.roll(high, shift_r, 1) if shift_r else high
        c = pltpu.roll(low, shift_l, 1) if shift_l else low
        return jnp.where(left, c, jnp.where(right, a, 0.0))

    arrived(ZR0.at[:, 0:8], z_first_recv.at[0])
    for i in range(2):
        @functools.partial(reach, i)
        def _(i=i):
            arrived(XR0.at[i, 0:8], x_first_recv.at[0, i])

    def three(first_tile, second_tile, edge):
        return (
            jnp.where(lane < SEAM, second_tile, first_tile),
            jnp.where(lane >= 128 - WIDE, edge, first_tile),
            jnp.where(lane < WIDE, edge, second_tile),
        )

    def border(parts):
        for i, x in ((0, -1), (1, 8)):
            for k, f in enumerate(x_fields):
                edge = zero if parts == (MIDDLE,) else margin(XR0[i, 6], XR0[i, 7], k)
                tiles = three(XR0[i, 2 * k], XR0[i, 2 * k + 1], edge)
                for p in parts:
                    S[p, f, column(x), :] = tiles[p]
        for i, z in ((0, -1), (1, 8)):
            for k, f in enumerate(z_fields):
                edge = zero if parts == (MIDDLE,) else margin(ZR0[i, 6], ZR0[i, 7], k)
                tiles = three(ZR0[i, 2 * k], ZR0[i, 2 * k + 1], edge)
                for p in parts:
                    S[p, f, level(z), :] = jnp.where(z_there[i], tiles[p], 0.0)

    border((MIDDLE,))
    def x_base(p, s, last):
        return 14 + 18 * s + (3 * p if last else 6 * p)

    def z_base(p, s, last):
        return 12 + 18 * s + (3 * p if last else 6 * p)

    def x_copy(p, i, s, slot, last):
        n = 3 if last else 6
        return remote(
            OX.at[i, pl.ds(x_base(p, s, last), n)], XR.at[slot, p, 1 - i, 0:n], x_send.at[i], x_recv.at[slot, p, 1 - i],
            (0, sides[i], 0))

    def e_copy(p, i, j, s, slot):
        return remote(
            OE.at[i, 3 * s + p, j], ER.at[slot, p, 1 - i, 1 - j], e_send.at[i],
            e_recv.at[slot, p, 1 - i], (sides[j], sides[i], 0))

    def z_copy(p, i, s, slot, last):
        n = 3 if last else 6
        return remote(
            OZ.at[i, pl.ds(z_base(p, s, last), n)], ZR.at[slot, p, 1 - i, 0:n], z_send.at[i], z_recv.at[slot, p],
            (sides[i], 0, 0))

    def move(p, s, slot, begin=False, last=False):
        if not begin:
            at_step = pl.ds(8 * s if last else pl.multiple_of(8 * s, 8), 8)
            added = SRC[p, at_step, :]
            for f in range(3):
                S[p, f, level(0), :] += added
            for i, x in ((0, -1), (1, 8)):
                S[p, 0, pl.ds(rows(0, x), 1), :] += SX[i, p, pl.ds(s, 1), :]

        def accelerate(z):
            own = level(z)
            after, before = pl.ds(rows(z, 1), 8), pl.ds(rows(z, -1), 8)
            above, below = level(z + 1), level(z - 1)

            def dx(f):
                return S[p, f, after, :] - S[p, f, before, :]

            def dz(f):
                return S[p, f, above, :] - S[p, f, below, :]

            b = B[p, pl.ds(8 * z, 8), :]
            V[p, 0, own, :] -= b * (dx(0) + dy(S[p, 3, own, :]) + dz(4))
            V[p, 1, own, :] -= b * (dx(3) + dy(S[p, 1, own, :]) + dz(5))
            V[p, 2, own, :] -= b * (dx(4) + dy(S[p, 5, own, :]) + dz(2))

        for z in (0, 7):
            accelerate(z)
        if not last:
            for i, x in ((0, 0), (1, 7)):
                for j in range(2):
                    for k, f in enumerate((0, 2)):
                        OE[i, 3 * s + p, j, k : k + 1, :] = V[p, f, pl.ds(rows(7 * j, x), 1), :]

                @functools.partial(reach, i)
                def _(i=i):
                    for j in range(2):
                        e_copy(p, i, j, s, slot).start()
        for z in range(1, 7):
            accelerate(z)
        base = x_base(p, s, last)
        for i, (x, inner) in enumerate(((0, 1), (7, 6))):
            for f in range(3):
                OX[i, base + f] = V[p, f, column(x), :]
                if not last:
                    OX[i, base + 3 + f] = V[p, f, column(inner), :]

            @functools.partial(reach, i)
            def _(i=i):
                x_copy(p, i, s, slot, last).start()
        base = z_base(p, s, last)
        for i, (z, inner) in enumerate(((0, 1), (7, 6))):
            for f in range(3):
                OZ[i, base + f] = V[p, f, level(z), :]
                if not last:
                    OZ[i, base + 3 + f] = V[p, f, level(inner), :]
            z_copy(p, i, s, slot, last).start()

        for z in range(8):
            own = level(z)
            after, before = pl.ds(rows(z, 1), 8), pl.ds(rows(z, -1), 8)
            above, below = level(z + 1), level(z - 1)
            dxs = [V[p, f, after, :] - V[p, f, before, :] for f in range(3)]
            dzs = [V[p, f, above, :] - V[p, f, below, :] for f in range(3)]
            dys = [dy(V[p, f, own, :]) for f in range(3)]
            lam, mu = L[p, pl.ds(8 * z, 8), :], M[p, pl.ds(8 * z, 8), :]
            spread = lam * (dxs[0] + dys[1] + dzs[2])
            mu2 = mu + mu
            S[p, 0, own, :] -= spread + mu2 * dxs[0]
            S[p, 1, own, :] -= spread + mu2 * dys[1]
            S[p, 2, own, :] -= spread + mu2 * dzs[2]
            S[p, 3, own, :] -= mu * (dys[0] + dxs[1])
            S[p, 4, own, :] -= mu * (dzs[0] + dxs[2])
            S[p, 5, own, :] -= mu * (dzs[1] + dys[2])

    def finish(p, slot, last=False):
        arrived(ZR.at[slot, p, :, 0:3] if last else ZR.at[slot, p], z_recv.at[slot, p])
        for i, z in ((0, 0), (1, 7)):
            near = [ZR[slot, p, i, f] for f in range(3)]
            own = level(z)
            lam, mu = L[p, pl.ds(8 * z, 8), :], M[p, pl.ds(8 * z, 8), :]
            sign = jnp.where(z_there[i], (-1.0, 1.0)[i], 0.0)
            slope = [sign * v for v in near]
            spread = lam * slope[2]
            S[p, 0, own, :] -= spread
            S[p, 1, own, :] -= spread
            S[p, 2, own, :] -= spread + (mu + mu) * slope[2]
            S[p, 4, own, :] -= mu * slope[0]
            S[p, 5, own, :] -= mu * slope[1]

        for i in range(2):
            @functools.partial(reach, i)
            def _(i=i):
                arrived(XR.at[slot, p, i, 0:3] if last else XR.at[slot, p, i], x_recv.at[slot, p, i])
                if not last:
                    arrived(ER.at[slot, p, i], e_recv.at[slot, p, i])

        for i, x, sign in ((0, 0, -1.0), (1, 7, 1.0)):
            near = [XR[slot, p, i, f] for f in range(3)]
            lam, mu = L[p, pl.ds(x, 8, stride=8), :], M[p, pl.ds(x, 8, stride=8), :]
            slope = [sign * v for v in near]
            spread = lam * slope[0]
            S[p, 0, column(x), :] -= spread + (mu + mu) * slope[0]
            S[p, 1, column(x), :] -= spread
            S[p, 2, column(x), :] -= spread
            S[p, 3, column(x), :] -= mu * slope[1]
            S[p, 4, column(x), :] -= mu * slope[2]

        if last:
            return
        for i, x, sign in ((0, 0, -1.0), (1, 7, 1.0)):
            near, far = [XR[slot, p, i, f] for f in range(3)], [XR[slot, p, i, 3 + f] for f in range(3)]
            lam, mu = LX[i, p], MX[i, p]
            dxs = [sign * (far[f] - V[p, f, column(x), :]) for f in range(3)]
            dzs = {}
            for k, f in enumerate((0, 2)):
                top, bottom = (jnp.where(z_there[j], ER[slot, p, i, j, k : k + 1, :], 0.0) for j in range(2))
                down = jnp.where(sub == 0, top, pltpu.roll(near[f], 1, 0))
                up = jnp.where(sub == 7, bottom, pltpu.roll(near[f], 7, 0))
                dzs[f] = up - down
            trace = dxs[0] + dy(near[1]) + dzs[2]
            beyond = column((-1, 8)[i])
            S[p, 0, beyond, :] -= lam * trace + (mu + mu) * dxs[0]
            S[p, 3, beyond, :] -= mu * (dy(near[0]) + dxs[1])
            S[p, 4, beyond, :] -= mu * (dzs[0] + dxs[2])
        for i, z, sign in ((0, 0, -1.0), (1, 7, 1.0)):
            near, far = [ZR[slot, p, i, f] for f in range(3)], [ZR[slot, p, i, 3 + f] for f in range(3)]
            lam, mu = LZ[i, p], MZ[i, p]
            dzs = [sign * (far[f] - V[p, f, level(z), :]) for f in range(3)]
            dxs = {}
            for k, f in enumerate((0, 2)):
                low, high = (ER[slot, p, j, i, k : k + 1, :] for j in range(2))
                behind = jnp.where(sub == 0, low, pltpu.roll(near[f], 1, 0))
                ahead = jnp.where(sub == 7, high, pltpu.roll(near[f], 7, 0))
                dxs[f] = ahead - behind
            trace = dxs[0] + dy(near[1]) + dzs[2]
            beyond = level((-1, 8)[i])
            S[p, 2, beyond, :] -= lam * trace + (mu + mu) * dzs[2]
            S[p, 4, beyond, :] -= mu * (dzs[0] + dxs[2])
            S[p, 5, beyond, :] -= mu * (dzs[1] + dy(near[2]))

    def each_part(then):
        def body(p, carry):
            then(p)
            return carry

        lax.fori_loop(0, 3, body, 0)

    move(MIDDLE, 0, 0, begin=True)

    arrived(YR, y_recv.at[0])
    low, high = YR[0, 8], YR[1, 8]
    seafloor = margin(low, high, STEPS).astype(jnp.int32)
    first_source = None
    for s in range(STEPS):
        v = jnp.where(dom == 0, margin(low, high, s), 0.0)
        first_source = v if s == 0 else first_source
        put_margin(SRC, (pl.ds(8 * s, 8), everywhere), v)
    for z in range(8):
        low, high = YR[0, z], YR[1, z]
        lam, mu, b, solid = materials(margin(low, high, 9).astype(jnp.int32), seafloor, z)
        for ref, v in ((L, lam), (M, mu), (B, b)):
            put_margin(ref, (pl.ds(8 * z, 8), everywhere), jnp.where(inside, v, 0.0))
        for f in range(9):
            v = margin(low, high, f)
            if f < 3:
                put_margin(V, (f, level(z), everywhere), v)
            else:
                if f >= 6:
                    v = jnp.where(solid, v, 0.0)
                elif z == 0:
                    v = v + first_source
                put_margin(S, (f - 3, level(z), everywhere), v)

    border((LEFT, RIGHT))

    def begin(p, carry):
        move(p, 0, 0, begin=True)
        return carry

    lax.fori_loop(1, 3, begin, 0)

    arrived(ZR0.at[:, 8:12], z_first_recv.at[1])
    for i in range(2):
        @functools.partial(reach, i)
        def _(i=i):
            arrived(XR0.at[i, 8:14], x_first_recv.at[1, i])
    for i in range(2):
        for k, ref in enumerate((LX, MX, SX)):
            tiles = three(XR0[i, 8 + 2 * k], XR0[i, 9 + 2 * k], margin(XR0[i, 6], XR0[i, 7], 3 + k))
            for p in range(3):
                ref[i, p] = tiles[p]
        for k, ref in enumerate((LZ, MZ)):
            tiles = three(ZR0[i, 8 + 2 * k], ZR0[i, 9 + 2 * k], margin(ZR0[i, 6], ZR0[i, 7], 3 + k))
            for p in range(3):
                ref[i, p] = jnp.where(z_there[i], tiles[p], 0.0)

    def step(s, carry):
        slot = lax.rem(s, 2)

        def turn(p):
            finish(p, 1 - slot)
            move(p, s, slot)

        each_part(turn)
        return carry

    lax.fori_loop(1, STEPS - 1, step, 0)

    end = STEPS - 1

    def final(p):
        finish(p, (end - 1) % 2)
        move(p, end, end % 2, last=True)

    each_part(final)

    def gather(f, ref, k):
        for z in range(8):
            middle, first_tile, second_tile = (ref[p, k, level(z), :] for p in (MIDDLE, LEFT, RIGHT))
            out[f, z, :, cut(0)] = jnp.where(lane < FIRST_CUT, first_tile, middle)
            out[f, z, :, cut(1)] = jnp.where(lane < SECOND_CUT, middle, second_tile)

    for f in range(3):
        gather(f, V, f)
    each_part(lambda p: finish(p, end % 2, last=True))
    for f in range(6):
        gather(3 + f, S, f)

    for i in range(2):
        arrived(OZ.at[i], z_send.at[i])

        @functools.partial(reach, i)
        def _(i=i):
            arrived(OX.at[i], x_send.at[i])
            arrived(OE.at[i], e_send.at[i])


def solution(mesh):
    sizes = (mesh.shape["dom"], mesh.shape["gx"], mesh.shape["gy"])

    def on_device(state, source, floor, region, lame, shear, buoy):
        hbm = pl.BlockSpec(memory_space=pltpu.HBM)

        def tiles(*shape):
            return pltpu.VMEM(shape + (8, 128), f32)

        return pl.pallas_call(
            functools.partial(kernel, sizes),
            out_shape=jax.ShapeDtypeStruct(state.shape, f32),
            in_specs=[hbm] * 7,
            out_specs=pl.BlockSpec(memory_space=pltpu.VMEM),
            scratch_shapes=[
                pltpu.VMEM(state.shape, f32),
                pltpu.VMEM(source.shape, f32),
                pltpu.VMEM(floor.shape, jnp.int32),
                pltpu.VMEM(region.shape, jnp.int32),
                pltpu.SMEM(lame.shape, f32),
                pltpu.SMEM(shear.shape, f32),
                pltpu.SMEM(buoy.shape, f32),
                pltpu.VMEM((3, 6, 10 * BLOCK, 128), f32),
                pltpu.VMEM((3, 3, 10 * BLOCK, 128), f32),
                pltpu.VMEM((3, 64, 128), f32),
                pltpu.VMEM((3, 64, 128), f32),
                pltpu.VMEM((3, 64, 128), f32),
                pltpu.VMEM((3, 8 * STEPS, 128), f32),
                tiles(2, 3),
                tiles(2, 3),
                tiles(2, 3),
                tiles(2, 3),
                tiles(2, 3),
                tiles(2, 113),
                tiles(2, 120),
                pltpu.VMEM((2, 3 * STEPS - 3, 2, 2, 128), f32),
                tiles(2, 14),
                tiles(2, 12),
                tiles(2, 9),
                tiles(2, 3, 2, 6),
                tiles(2, 3, 2, 6),
                pltpu.VMEM((2, 3, 2, 2, 2, 128), f32),
                pltpu.SemaphoreType.DMA((7,)),
                pltpu.SemaphoreType.DMA((2,)),
                pltpu.SemaphoreType.DMA((2,)),
                pltpu.SemaphoreType.DMA((2,)),
                pltpu.SemaphoreType.DMA((2, 2)),
                pltpu.SemaphoreType.DMA((2,)),
                pltpu.SemaphoreType.DMA((1,)),
                pltpu.SemaphoreType.DMA((2, 3, 2)),
                pltpu.SemaphoreType.DMA((2, 3)),
                pltpu.SemaphoreType.DMA((2, 3, 2)),
            ],
            compiler_params=pltpu.CompilerParams(
                collective_id=0, has_side_effects=True, vmem_limit_bytes=32 * 1024 * 1024
            ),
        )(*(
            pltpu.with_memory_space_constraint(v, pltpu.HBM)
            for v in (state, source, floor, region, lame, shear, buoy)
        ))

    return jax.shard_map(
        on_device,
        mesh=mesh,
        in_specs=(
            P(None, "dom", "gx", "gy"),
            P(None, "gx", "gy"),
            P("gx", "gy"),
            P("dom", "gx", "gy"),
            P(),
            P(),
            P(),
        ),
        out_specs=P(None, "dom", "gx", "gy"),
        check_vma=False,
    )
```

```python
import functools

import jax
import jax.numpy as jnp
from jax import lax
from jax.experimental import pallas as pl
from jax.experimental.pallas import tpu as pltpu
from jax.sharding import PartitionSpec as P

STEPS = 6
COURANT = 0.25
REGIONS = 16
BLOCK = 16
WIDE = 12
NEAR = 10
LEFT, RIGHT = 0, 1
PARTS = 2
MESH = pl.DeviceIdType.MESH

f32 = jnp.float32


def rows(z, x=0):
    return (z + 1) * BLOCK + 8 + x


def level(z):
    return pl.ds(rows(z), 8)


def column(x):
    return pl.ds(rows(0, x), 8, stride=BLOCK)


def dy(v):
    lane = lax.broadcasted_iota(jnp.int32, (8, 128), 1)
    ahead, behind = pltpu.roll(v, 127, 2), pltpu.roll(v, 1, 2)
    ahead = jnp.where(lane == 127, jnp.concatenate([ahead[1:], ahead[:1]], 0), ahead)
    behind = jnp.where(lane == 0, jnp.concatenate([behind[1:], behind[:1]], 0), behind)
    return ahead - behind


def pick(bits, table):
    values = list(table)
    for bit in bits:
        values = [jnp.where(bit, values[2 * i + 1], values[2 * i]) for i in range(len(values) // 2)]
    return values[0]


def kernel(
    sizes, state_in, source_in, floor_in, region_in, lame_in, shear_in, buoy_in, out,
    state, source, floor, region, lame, shear, buoy,
    S, V, L, M, B, SRC, LX, MX, SX, LZ, MZ, OX, OZ, OE, XR0, ZR0, YR, XR, ZR, ER,
    in_sem, x_send, z_send, e_send, x_first_recv, z_first_recv, y_recv, x_recv, z_recv, e_recv,
):
    n_dom, n_gx, n_gy = sizes
    dom, gx, gy = lax.axis_index("dom"), lax.axis_index("gx"), lax.axis_index("gy")
    lane = lax.broadcasted_iota(jnp.int32, (8, 128), 1)
    sub = lax.broadcasted_iota(jnp.int32, (8, 128), 0)
    zero = jnp.zeros((8, 128), f32)

    loads = [
        pltpu.make_async_copy(src, dst, in_sem.at[i])
        for i, (src, dst) in enumerate((
            (region_in, region), (floor_in, floor), (source_in, source), (state_in, state),
            (lame_in, lame), (shear_in, shear), (buoy_in, buoy)))
    ]
    for load in loads:
        load.start()

    sides = (-1, 1)
    there = [gx > 0, gx < n_gx - 1]
    z_there = [dom > 0, dom < n_dom - 1]

    doms = [dom, jnp.where(dom == n_dom - 1, 0, dom + 1), jnp.where(dom == 0, n_dom - 1, dom - 1)]
    gxs = [gx, gx + 1, gx - 1]
    gys = [gy, jnp.where(gy == n_gy - 1, 0, gy + 1), jnp.where(gy == 0, n_gy - 1, gy - 1)]

    def at(dz, dx, dyy):
        return (doms[dz], gxs[dx], gys[dyy])

    def reach(i, then):
        pl.when(there[i])(then)

    barrier = pltpu.get_barrier_semaphore()

    def greet(*way):
        pl.semaphore_signal(barrier, inc=1, device_id=at(*way), device_id_type=MESH)

    for i, dx in enumerate(sides):
        @functools.partial(reach, i)
        def _(dx=dx):
            for way in ((0, dx, 0), (-1, dx, 0), (1, dx, 0), (0, dx, -1), (0, dx, 1)):
                greet(*way)
    for way in [(a, 0, b) for a in (-1, 0, 1) for b in (-1, 0, 1) if a or b]:
        greet(*way)

    for i in range(2):
        @pl.when(jnp.logical_not(there[i]))
        def _(i=i):
            XR0[i] = jnp.zeros(XR0.shape[1:], f32)
            for slot in range(2):
                for p in range(PARTS):
                    XR[slot, p, i] = jnp.zeros(XR.shape[3:], f32)
                    ER[slot, p, i] = jnp.zeros(ER.shape[3:], f32)

    for p in range(PARTS):
        for f in range(3):
            for t in range(2):
                for z in range(-1, 9):
                    V[p, f, t, pl.ds(rows(z, -8), 8), :] = zero
                for z in (-1, 8):
                    V[p, f, t, level(z), :] = zero

    for load in loads[:4]:
        load.wait()

    def side_by_side(parts, t):
        tile = zero
        for k, v in enumerate(parts):
            shift = (WIDE * k + (WIDE if t else 0)) % 128
            v = pltpu.roll(v, shift, 1) if shift else v
            tile = jnp.where((lane >= WIDE * k) & (lane < WIDE * (k + 1)), v, tile)
        return tile

    def cut(t):
        return slice(128 * t, 128 * t + 128)

    for i in range(2):
        for z in range(8):
            OZ[i, 90 + z] = side_by_side(
                [state[f, z, :, cut(i)] for f in range(9)] + [region[z, :, cut(i)].astype(f32)], i)
        OZ[i, 98] = side_by_side([source[s, :, cut(i)] for s in range(STEPS)] + [floor[:, cut(i)].astype(f32)], i)

    def remote(src, dst, send, recv, way):
        return pltpu.make_async_remote_copy(
            src_ref=src, dst_ref=dst, send_sem=send, recv_sem=recv, device_id=at(*way), device_id_type=MESH)

    def xa_first(i):
        return remote(OX.at[i, 0:6], XR0.at[1 - i, 0:6], x_send.at[i], x_first_recv.at[0, 1 - i], (0, sides[i], 0))

    def xy_first(i, j):
        return remote(
            OX.at[i, 6 + j], XR0.at[1 - i, 7 - j], x_send.at[i], x_first_recv.at[0, 1 - i], (0, sides[i], sides[j]))

    def xb_first(i):
        return remote(OX.at[i, 8:14], XR0.at[1 - i, 8:14], x_send.at[i], x_first_recv.at[1, 1 - i], (0, sides[i], 0))

    def za_first(i):
        return remote(OZ.at[i, 0:6], ZR0.at[1 - i, 0:6], z_send.at[i], z_first_recv.at[0], (sides[i], 0, 0))

    def zy_first(i, j):
        return remote(
            OZ.at[i, 6 + j], ZR0.at[1 - i, 7 - j], z_send.at[i], z_first_recv.at[0], (sides[i], 0, sides[j]))

    def zb_first(i):
        return remote(OZ.at[i, 8:12], ZR0.at[1 - i, 8:12], z_send.at[i], z_first_recv.at[1], (sides[i], 0, 0))

    def y_first(i):
        return remote(OZ.at[i, 90:99], YR.at[1 - i], z_send.at[i], y_recv.at[0], (0, 0, sides[i]))

    def arrived(ref, sem):
        pltpu.make_async_copy(ref, ref, sem).wait()

    for load in loads[4:]:
        load.wait()
    scale = 0.5 * COURANT
    tables = [[t[k] * scale for k in range(REGIONS)] for t in (lame, shear, buoy)]

    def materials(number, seafloor, z):
        bits = [(number & (1 << k)) != 0 for k in range(4)]
        solid = (dom * 8 + z) >= seafloor
        lam, mu, b = (pick(bits, t) for t in tables)
        return lam, jnp.where(solid, mu, 0.0), b, solid

    def put(ref, index, pair):
        at_f, at_rows = index
        ref[(LEFT, *at_f, 0, at_rows)] = pair[0]
        ref[(RIGHT, *at_f, 0, at_rows)] = pair[1]
        ref[(LEFT, *at_f, 1, at_rows)] = jnp.where(lane < WIDE, pair[1], 0.0)
        ref[(RIGHT, *at_f, 1, at_rows)] = jnp.where(lane >= 128 - WIDE, pair[0], 0.0)

    def put_margin(ref, index, v):
        at_f, at_rows = index
        ref[(LEFT, *at_f, 1, at_rows)] = jnp.where(lane >= 128 - WIDE, v, ref[(LEFT, *at_f, 1, at_rows)])
        ref[(RIGHT, *at_f, 1, at_rows)] = jnp.where(lane < WIDE, v, ref[(RIGHT, *at_f, 1, at_rows)])

    for s in range(STEPS):
        put(SRC, ((), pl.ds(8 * s, 8)),
            [jnp.where(dom == 0, source[s, :, cut(t)], 0.0) for t in range(2)])
    for z in range(8):
        made = [materials(region[z, :, cut(t)], floor[:, cut(t)], z) for t in range(2)]
        for k, ref in enumerate((L, M, B)):
            put(ref, ((), pl.ds(8 * z, 8)), [m[k] for m in made])
        for f in range(9):
            v = [state[f, z, :, cut(t)] for t in range(2)]
            if f < 3:
                put(V, ((f,), level(z)), v)
            else:
                if f >= 6:
                    v = [jnp.where(m[3], w, 0.0) for m, w in zip(made, v)]
                elif z == 0:
                    v = [w + jnp.where(dom == 0, source[0, :, cut(t)], 0.0) for t, w in enumerate(v)]
                put(S, ((f - 3,), level(z)), v)

    x_fields, z_fields = (0, 3, 4), (2, 4, 5)
    pair = (LEFT, RIGHT)
    for i, x in ((0, 0), (1, 7)):
        parts = [[S[p, f, 0, column(x), :] for p in pair] for f in x_fields]
        parts += [[m[p, 0, pl.ds(x, 8, stride=8), :] for p in pair] for m in (L, M)]
        parts += [[
            jnp.concatenate([SRC[p, 0, pl.ds(x, STEPS, stride=8), :], jnp.zeros((8 - STEPS, 128), f32)], 0) for p in pair]]
        for k in range(6):
            for t in range(2):
                OX[i, 2 * k + t + (0 if k < 3 else 2)] = parts[k][t]
        for j in range(2):
            OX[i, 6 + j] = side_by_side([v[j] for v in parts], j)
    for i, z in ((0, 0), (1, 7)):
        parts = [[S[p, f, 0, level(z), :] for p in pair] for f in z_fields]
        parts += [[m[p, 0, pl.ds(8 * z, 8), :] for p in pair] for m in (L, M)]
        for k in range(5):
            for t in range(2):
                OZ[i, 2 * k + t + (0 if k < 3 else 2)] = parts[k][t]
        for j in range(2):
            OZ[i, 6 + j] = side_by_side([v[j] for v in parts], j)

    pl.semaphore_wait(barrier, 8 + 5 * (there[0].astype(jnp.int32) + there[1].astype(jnp.int32)))
    for i in range(2):
        @functools.partial(reach, i)
        def _(i=i):
            xa_first(i).start()
            for j in range(2):
                xy_first(i, j).start()
    for i in range(2):
        y_first(i).start()
        za_first(i).start()
        for j in range(2):
            zy_first(i, j).start()
    for i in range(2):
        @functools.partial(reach, i)
        def _(i=i):
            xb_first(i).start()
        zb_first(i).start()

    left = (lane >= 128 - WIDE) & (gy > 0)
    right = (lane < WIDE) & (gy < n_gy - 1)
    inside = left | right

    def margin(low, high, f):
        shift_r = (128 - WIDE * f) % 128
        shift_l = (256 - WIDE - WIDE * f) % 128
        a = pltpu.roll(high, shift_r, 1) if shift_r else high
        c = pltpu.roll(low, shift_l, 1) if shift_l else low
        return jnp.where(left, c, jnp.where(right, a, 0.0))

    def both(first_tile, second_tile, edge):
        return (
            jnp.stack([first_tile, jnp.where(lane < WIDE, second_tile, edge)]),
            jnp.stack([second_tile, jnp.where(lane >= 128 - WIDE, first_tile, edge)]),
        )

    def border():
        for i, x in ((0, -1), (1, 8)):
            for k, f in enumerate(x_fields):
                tiles = both(XR0[i, 2 * k], XR0[i, 2 * k + 1], margin(XR0[i, 6], XR0[i, 7], k))
                for p in range(PARTS):
                    S[p, f, :, column(x), :] = tiles[p]
        for i, z in ((0, -1), (1, 8)):
            for k, f in enumerate(z_fields):
                tiles = both(ZR0[i, 2 * k], ZR0[i, 2 * k + 1], margin(ZR0[i, 6], ZR0[i, 7], k))
                for p in range(PARTS):
                    S[p, f, :, level(z), :] = jnp.where(z_there[i], tiles[p], 0.0)

    def pack(tiles):
        out = zero
        for k, tile in enumerate(tiles):
            moved = pltpu.roll(tile, 2 * NEAR * k + NEAR, 1)
            out = jnp.where((lane >= 2 * NEAR * k) & (lane < 2 * NEAR * (k + 1)), moved, out)
        return out

    def fill(buffer, base, near, far):
        for f in range(3):
            buffer[base + f] = near[f][0]
            if far:
                buffer[base + 4 + f] = far[f][0]
        buffer[base + 3] = pack([v[1] for v in near + far])

    def opened(buffer, k):
        packed = pltpu.roll(buffer[3], (128 - 2 * NEAR * k - NEAR) % 128, 1)
        return jnp.stack([buffer[k if k < 3 else k + 1], packed])

    def x_base(p, s, last):
        return 14 + 14 * s + (4 * p if last else 7 * p)

    def z_base(p, s, last):
        return 12 + 14 * s + (4 * p if last else 7 * p)

    def x_copy(p, i, s, slot, last):
        n = 4 if last else 7
        return remote(
            OX.at[i, pl.ds(x_base(p, s, last), n)], XR.at[slot, p, 1 - i, 0:n], x_send.at[i], x_recv.at[slot, p, 1 - i],
            (0, sides[i], 0))

    def e_copy(p, i, j, s, slot):
        return remote(
            OE.at[i, 2 * s + p, j], ER.at[slot, p, 1 - i, 1 - j], e_send.at[i],
            e_recv.at[slot, p, 1 - i], (sides[j], sides[i], 0))

    def z_copy(p, i, s, slot, last):
        n = 4 if last else 7
        return remote(
            OZ.at[i, pl.ds(z_base(p, s, last), n)], ZR.at[slot, p, 1 - i, 0:n], z_send.at[i], z_recv.at[slot, p],
            (sides[i], 0, 0))

    def move(p, s, slot, begin=False, last=False):
        if not begin:
            at_step = pl.ds(8 * s if last else pl.multiple_of(8 * s, 8), 8)
            added = SRC[p, :, at_step, :]
            for f in range(3):
                S[p, f, :, level(0), :] += added
            for i, x in ((0, -1), (1, 8)):
                S[p, 0, :, pl.ds(rows(0, x), 1), :] += SX[i, p, :, pl.ds(s, 1), :]

        def accelerate(z):
            own = level(z)
            after, before = pl.ds(rows(z, 1), 8), pl.ds(rows(z, -1), 8)
            above, below = level(z + 1), level(z - 1)

            def dx(f):
                return S[p, f, :, after, :] - S[p, f, :, before, :]

            def dz(f):
                return S[p, f, :, above, :] - S[p, f, :, below, :]

            b = B[p, :, pl.ds(8 * z, 8), :]
            V[p, 0, :, own, :] -= b * (dx(0) + dy(S[p, 3, :, own, :]) + dz(4))
            V[p, 1, :, own, :] -= b * (dx(3) + dy(S[p, 1, :, own, :]) + dz(5))
            V[p, 2, :, own, :] -= b * (dx(4) + dy(S[p, 5, :, own, :]) + dz(2))

        for z in (0, 7):
            accelerate(z)
        if not last:
            for i, x in ((0, 0), (1, 7)):
                for j in range(2):
                    for k, f in enumerate((0, 2)):
                        for t in range(2):
                            OE[i, 2 * s + p, j, pl.ds(2 * k + t, 1), :] = V[p, f, t, pl.ds(rows(7 * j, x), 1), :]

                @functools.partial(reach, i)
                def _(i=i):
                    for j in range(2):
                        e_copy(p, i, j, s, slot).start()
        for z in range(1, 7):
            accelerate(z)
        base = x_base(p, s, last)
        for i, (x, inner) in enumerate(((0, 1), (7, 6))):
            fill(OX.at[i], base, [V[p, f, :, column(x), :] for f in range(3)],
                 [] if last else [V[p, f, :, column(inner), :] for f in range(3)])

            @functools.partial(reach, i)
            def _(i=i):
                x_copy(p, i, s, slot, last).start()
        base = z_base(p, s, last)
        for i, (z, inner) in enumerate(((0, 1), (7, 6))):
            fill(OZ.at[i], base, [V[p, f, :, level(z), :] for f in range(3)],
                 [] if last else [V[p, f, :, level(inner), :] for f in range(3)])
            z_copy(p, i, s, slot, last).start()

        for z in range(8):
            own = level(z)
            after, before = pl.ds(rows(z, 1), 8), pl.ds(rows(z, -1), 8)
            above, below = level(z + 1), level(z - 1)
            dxs = [V[p, f, :, after, :] - V[p, f, :, before, :] for f in range(3)]
            dzs = [V[p, f, :, above, :] - V[p, f, :, below, :] for f in range(3)]
            dys = [dy(V[p, f, :, own, :]) for f in range(3)]
            lam, mu = L[p, :, pl.ds(8 * z, 8), :], M[p, :, pl.ds(8 * z, 8), :]
            spread = lam * (dxs[0] + dys[1] + dzs[2])
            mu2 = mu + mu
            S[p, 0, :, own, :] -= spread + mu2 * dxs[0]
            S[p, 1, :, own, :] -= spread + mu2 * dys[1]
            S[p, 2, :, own, :] -= spread + mu2 * dzs[2]
            S[p, 3, :, own, :] -= mu * (dys[0] + dxs[1])
            S[p, 4, :, own, :] -= mu * (dzs[0] + dxs[2])
            S[p, 5, :, own, :] -= mu * (dzs[1] + dys[2])

    def edge_row(slot, p, i, j, k):
        return jnp.stack([ER[slot, p, i, j, pl.ds(2 * k + t, 1), :] for t in range(2)])

    def finish(p, slot, last=False):
        arrived(ZR.at[slot, p, :, 0:4] if last else ZR.at[slot, p], z_recv.at[slot, p])
        for i, z in ((0, 0), (1, 7)):
            near = [opened(ZR.at[slot, p, i], f) for f in range(3)]
            own = level(z)
            lam, mu = L[p, :, pl.ds(8 * z, 8), :], M[p, :, pl.ds(8 * z, 8), :]
            sign = jnp.where(z_there[i], (-1.0, 1.0)[i], 0.0)
            slope = [sign * v for v in near]
            spread = lam * slope[2]
            S[p, 0, :, own, :] -= spread
            S[p, 1, :, own, :] -= spread
            S[p, 2, :, own, :] -= spread + (mu + mu) * slope[2]
            S[p, 4, :, own, :] -= mu * slope[0]
            S[p, 5, :, own, :] -= mu * slope[1]

        for i in range(2):
            @functools.partial(reach, i)
            def _(i=i):
                arrived(XR.at[slot, p, i, 0:4] if last else XR.at[slot, p, i], x_recv.at[slot, p, i])
                if not last:
                    arrived(ER.at[slot, p, i], e_recv.at[slot, p, i])

        for i, x, sign in ((0, 0, -1.0), (1, 7, 1.0)):
            near = [opened(XR.at[slot, p, i], f) for f in range(3)]
            lam, mu = L[p, :, pl.ds(x, 8, stride=8), :], M[p, :, pl.ds(x, 8, stride=8), :]
            slope = [sign * v for v in near]
            spread = lam * slope[0]
            S[p, 0, :, column(x), :] -= spread + (mu + mu) * slope[0]
            S[p, 1, :, column(x), :] -= spread
            S[p, 2, :, column(x), :] -= spread
            S[p, 3, :, column(x), :] -= mu * slope[1]
            S[p, 4, :, column(x), :] -= mu * slope[2]

        if last:
            return
        for i, x, sign in ((0, 0, -1.0), (1, 7, 1.0)):
            got = [opened(XR.at[slot, p, i], k) for k in range(6)]
            near, far = got[:3], got[3:]
            lam, mu = LX[i, p], MX[i, p]
            dxs = [sign * (far[f] - V[p, f, :, column(x), :]) for f in range(3)]
            dzs = {}
            for k, f in enumerate((0, 2)):
                top, bottom = (jnp.where(z_there[j], edge_row(slot, p, i, j, k), 0.0) for j in range(2))
                down = jnp.where(sub == 0, top, pltpu.roll(near[f], 1, 1))
                up = jnp.where(sub == 7, bottom, pltpu.roll(near[f], 7, 1))
                dzs[f] = up - down
            trace = dxs[0] + dy(near[1]) + dzs[2]
            beyond = column((-1, 8)[i])
            S[p, 0, :, beyond, :] -= lam * trace + (mu + mu) * dxs[0]
            S[p, 3, :, beyond, :] -= mu * (dy(near[0]) + dxs[1])
            S[p, 4, :, beyond, :] -= mu * (dzs[0] + dxs[2])
        for i, z, sign in ((0, 0, -1.0), (1, 7, 1.0)):
            got = [opened(ZR.at[slot, p, i], k) for k in range(6)]
            near, far = got[:3], got[3:]
            lam, mu = LZ[i, p], MZ[i, p]
            dzs = [sign * (far[f] - V[p, f, :, level(z), :]) for f in range(3)]
            dxs = {}
            for k, f in enumerate((0, 2)):
                low, high = (edge_row(slot, p, j, i, k) for j in range(2))
                behind = jnp.where(sub == 0, low, pltpu.roll(near[f], 1, 1))
                ahead = jnp.where(sub == 7, high, pltpu.roll(near[f], 7, 1))
                dxs[f] = ahead - behind
            trace = dxs[0] + dy(near[1]) + dzs[2]
            beyond = level((-1, 8)[i])
            S[p, 2, :, beyond, :] -= lam * trace + (mu + mu) * dzs[2]
            S[p, 4, :, beyond, :] -= mu * (dzs[0] + dxs[2])
            S[p, 5, :, beyond, :] -= mu * (dzs[1] + dy(near[2]))

    def each_part(then):
        def body(p, carry):
            then(p)
            return carry

        lax.fori_loop(0, PARTS, body, 0)

    arrived(YR, y_recv.at[0])
    low, high = YR[0, 8], YR[1, 8]
    seafloor = margin(low, high, STEPS).astype(jnp.int32)
    first_source = None
    for s in range(STEPS):
        v = jnp.where(dom == 0, margin(low, high, s), 0.0)
        first_source = v if s == 0 else first_source
        put_margin(SRC, ((), pl.ds(8 * s, 8)), v)
    for z in range(8):
        low, high = YR[0, z], YR[1, z]
        lam, mu, b, solid = materials(margin(low, high, 9).astype(jnp.int32), seafloor, z)
        for ref, v in ((L, lam), (M, mu), (B, b)):
            put_margin(ref, ((), pl.ds(8 * z, 8)), jnp.where(inside, v, 0.0))
        for f in range(9):
            v = margin(low, high, f)
            if f < 3:
                put_margin(V, ((f,), level(z)), v)
            else:
                if f >= 6:
                    v = jnp.where(solid, v, 0.0)
                elif z == 0:
                    v = v + first_source
                put_margin(S, ((f - 3,), level(z)), v)

    arrived(ZR0.at[:, 0:8], z_first_recv.at[0])
    for i in range(2):
        @functools.partial(reach, i)
        def _(i=i):
            arrived(XR0.at[i, 0:8], x_first_recv.at[0, i])
    border()

    each_part(lambda p: move(p, 0, 0, begin=True))

    arrived(ZR0.at[:, 8:12], z_first_recv.at[1])
    for i in range(2):
        @functools.partial(reach, i)
        def _(i=i):
            arrived(XR0.at[i, 8:14], x_first_recv.at[1, i])
    for i in range(2):
        for k, ref in enumerate((LX, MX, SX)):
            tiles = both(XR0[i, 8 + 2 * k], XR0[i, 9 + 2 * k], margin(XR0[i, 6], XR0[i, 7], 3 + k))
            for p in range(PARTS):
                ref[i, p] = tiles[p]
        for k, ref in enumerate((LZ, MZ)):
            tiles = both(ZR0[i, 8 + 2 * k], ZR0[i, 9 + 2 * k], margin(ZR0[i, 6], ZR0[i, 7], 3 + k))
            for p in range(PARTS):
                ref[i, p] = jnp.where(z_there[i], tiles[p], 0.0)

    def step(s, carry):
        slot = lax.rem(s, 2)

        def turn(p):
            finish(p, 1 - slot)
            move(p, s, slot)

        each_part(turn)
        return carry

    lax.fori_loop(1, STEPS - 1, step, 0)

    end = STEPS - 1

    def final(p):
        finish(p, (end - 1) % 2)
        move(p, end, end % 2, last=True)

    each_part(final)

    def gather(f, ref, k):
        for z in range(8):
            for p in range(PARTS):
                out[f, z, :, cut(p)] = ref[p, k, 0, level(z), :]

    for f in range(3):
        gather(f, V, f)
    each_part(lambda p: finish(p, end % 2, last=True))
    for f in range(6):
        gather(3 + f, S, f)

    for i in range(2):
        arrived(OZ.at[i], z_send.at[i])

        @functools.partial(reach, i)
        def _(i=i):
            arrived(OX.at[i], x_send.at[i])
            arrived(OE.at[i], e_send.at[i])


def solution(mesh):
    sizes = (mesh.shape["dom"], mesh.shape["gx"], mesh.shape["gy"])

    def on_device(state, source, floor, region, lame, shear, buoy):
        hbm = pl.BlockSpec(memory_space=pltpu.HBM)

        def tiles(*shape):
            return pltpu.VMEM(shape + (8, 128), f32)

        return pl.pallas_call(
            functools.partial(kernel, sizes),
            out_shape=jax.ShapeDtypeStruct(state.shape, f32),
            in_specs=[hbm] * 7,
            out_specs=pl.BlockSpec(memory_space=pltpu.VMEM),
            scratch_shapes=[
                pltpu.VMEM(state.shape, f32),
                pltpu.VMEM(source.shape, f32),
                pltpu.VMEM(floor.shape, jnp.int32),
                pltpu.VMEM(region.shape, jnp.int32),
                pltpu.SMEM(lame.shape, f32),
                pltpu.SMEM(shear.shape, f32),
                pltpu.SMEM(buoy.shape, f32),
                pltpu.VMEM((PARTS, 6, 2, 10 * BLOCK, 128), f32),
                pltpu.VMEM((PARTS, 3, 2, 10 * BLOCK, 128), f32),
                pltpu.VMEM((PARTS, 2, 64, 128), f32),
                pltpu.VMEM((PARTS, 2, 64, 128), f32),
                pltpu.VMEM((PARTS, 2, 64, 128), f32),
                pltpu.VMEM((PARTS, 2, 8 * STEPS, 128), f32),
                tiles(2, PARTS, 2),
                tiles(2, PARTS, 2),
                tiles(2, PARTS, 2),
                tiles(2, PARTS, 2),
                tiles(2, PARTS, 2),
                tiles(2, 92),
                tiles(2, 99),
                pltpu.VMEM((2, PARTS * (STEPS - 1), 2, 4, 128), f32),
                tiles(2, 14),
                tiles(2, 12),
                tiles(2, 9),
                tiles(2, PARTS, 2, 7),
                tiles(2, PARTS, 2, 7),
                pltpu.VMEM((2, PARTS, 2, 2, 4, 128), f32),
                pltpu.SemaphoreType.DMA((7,)),
                pltpu.SemaphoreType.DMA((2,)),
                pltpu.SemaphoreType.DMA((2,)),
                pltpu.SemaphoreType.DMA((2,)),
                pltpu.SemaphoreType.DMA((2, 2)),
                pltpu.SemaphoreType.DMA((2,)),
                pltpu.SemaphoreType.DMA((1,)),
                pltpu.SemaphoreType.DMA((2, PARTS, 2)),
                pltpu.SemaphoreType.DMA((2, PARTS)),
                pltpu.SemaphoreType.DMA((2, PARTS, 2)),
            ],
            compiler_params=pltpu.CompilerParams(
                collective_id=0, has_side_effects=True, vmem_limit_bytes=32 * 1024 * 1024
            ),
        )(*(
            pltpu.with_memory_space_constraint(v, pltpu.HBM)
            for v in (state, source, floor, region, lame, shear, buoy)
        ))

    return jax.shard_map(
        on_device,
        mesh=mesh,
        in_specs=(
            P(None, "dom", "gx", "gy"),
            P(None, "gx", "gy"),
            P("gx", "gy"),
            P("dom", "gx", "gy"),
            P(),
            P(),
            P(),
        ),
        out_specs=P(None, "dom", "gx", "gy"),
        check_vma=False,
    )
```

```python
import functools

import jax
import jax.numpy as jnp
from jax import lax
from jax.experimental import pallas as pl
from jax.experimental.pallas import tpu as pltpu
from jax.sharding import PartitionSpec as P

STEPS = 6
COURANT = 0.25
REGIONS = 16
BLOCK = 16
WIDE = 12
MIDDLE, LEFT, RIGHT = 0, 1, 2
FIRST_CUT, SECOND_CUT, SEAM = 86, 171 - 128, 64
MESH = pl.DeviceIdType.MESH

f32 = jnp.float32


def rows(z, x=0):
    return (z + 1) * BLOCK + 8 + x


def level(z):
    return pl.ds(rows(z), 8)


def column(x):
    return pl.ds(rows(0, x), 8, stride=BLOCK)


def dy(v):
    return pltpu.roll(v, 127, 1) - pltpu.roll(v, 1, 1)


def pick(bits, table):
    values = list(table)
    for bit in bits:
        values = [jnp.where(bit, values[2 * i + 1], values[2 * i]) for i in range(len(values) // 2)]
    return values[0]


def kernel(
    sizes, state_in, source_in, floor_in, region_in, lame_in, shear_in, buoy_in, out,
    state, source, floor, region, lame, shear, buoy,
    S, V, L, M, B, SRC, LX, MX, SX, LZ, MZ, OX, OZ, OE, XR0, ZR0, YR, XR, ZR, ER,
    in_sem, x_send, z_send, e_send, x_first_recv, z_first_recv, y_recv, x_recv, z_recv, e_recv,
):
    n_dom, n_gx, n_gy = sizes
    dom, gx, gy = lax.axis_index("dom"), lax.axis_index("gx"), lax.axis_index("gy")
    lane = lax.broadcasted_iota(jnp.int32, (8, 128), 1)
    sub = lax.broadcasted_iota(jnp.int32, (8, 128), 0)
    zero = jnp.zeros((8, 128), f32)

    loads = [
        pltpu.make_async_copy(src, dst, in_sem.at[i])
        for i, (src, dst) in enumerate((
            (region_in, region), (floor_in, floor), (source_in, source), (state_in, state),
            (lame_in, lame), (shear_in, shear), (buoy_in, buoy)))
    ]
    for load in loads:
        load.start()

    sides = (-1, 1)
    there = [gx > 0, gx < n_gx - 1]
    z_there = [dom > 0, dom < n_dom - 1]

    doms = [dom, jnp.where(dom == n_dom - 1, 0, dom + 1), jnp.where(dom == 0, n_dom - 1, dom - 1)]
    gxs = [gx, gx + 1, gx - 1]
    gys = [gy, jnp.where(gy == n_gy - 1, 0, gy + 1), jnp.where(gy == 0, n_gy - 1, gy - 1)]

    def at(dz, dx, dyy):
        return (doms[dz], gxs[dx], gys[dyy])

    def reach(i, then):
        pl.when(there[i])(then)

    barrier = pltpu.get_barrier_semaphore()

    def greet(*way):
        pl.semaphore_signal(barrier, inc=1, device_id=at(*way), device_id_type=MESH)

    for i, dx in enumerate(sides):
        @functools.partial(reach, i)
        def _(dx=dx):
            for way in ((0, dx, 0), (-1, dx, 0), (1, dx, 0), (0, dx, -1), (0, dx, 1)):
                greet(*way)
    for way in [(a, 0, b) for a in (-1, 0, 1) for b in (-1, 0, 1) if a or b]:
        greet(*way)

    for i in range(2):
        @pl.when(jnp.logical_not(there[i]))
        def _(i=i):
            XR0[i] = jnp.zeros(XR0.shape[1:], f32)
            for slot in range(2):
                for p in range(3):
                    XR[slot, p, i] = jnp.zeros(XR.shape[3:], f32)
                    ER[slot, p, i] = jnp.zeros(ER.shape[3:], f32)

    for p in range(3):
        for f in range(3):
            for z in range(-1, 9):
                V[p, f, pl.ds(rows(z, -8), 8), :] = zero
            for z in (-1, 8):
                V[p, f, level(z), :] = zero

    for load in loads[:4]:
        load.wait()

    def side_by_side(parts, t):
        tile = zero
        for k, v in enumerate(parts):
            shift = (WIDE * k + (WIDE if t else 0)) % 128
            v = pltpu.roll(v, shift, 1) if shift else v
            tile = jnp.where((lane >= WIDE * k) & (lane < WIDE * (k + 1)), v, tile)
        return tile

    def cut(t):
        return slice(128 * t, 128 * t + 128)

    def remote(src, dst, send, recv, way):
        return pltpu.make_async_remote_copy(
            src_ref=src, dst_ref=dst, send_sem=send, recv_sem=recv, device_id=at(*way), device_id_type=MESH)

    def xa_first(i):
        return remote(OX.at[i, 0:6], XR0.at[1 - i, 0:6], x_send.at[i], x_first_recv.at[0, 1 - i], (0, sides[i], 0))

    def xy_first(i, j):
        return remote(
            OX.at[i, 6 + j], XR0.at[1 - i, 7 - j], x_send.at[i], x_first_recv.at[2, 1 - i], (0, sides[i], sides[j]))

    def xb_first(i):
        return remote(OX.at[i, 8:14], XR0.at[1 - i, 8:14], x_send.at[i], x_first_recv.at[1, 1 - i], (0, sides[i], 0))

    def za_first(i):
        return remote(OZ.at[i, 0:6], ZR0.at[1 - i, 0:6], z_send.at[i], z_first_recv.at[0], (sides[i], 0, 0))

    def zy_first(i, j):
        return remote(
            OZ.at[i, 6 + j], ZR0.at[1 - i, 7 - j], z_send.at[i], z_first_recv.at[2], (sides[i], 0, sides[j]))

    def zb_first(i):
        return remote(OZ.at[i, 8:12], ZR0.at[1 - i, 8:12], z_send.at[i], z_first_recv.at[1], (sides[i], 0, 0))

    def y_first(i):
        return remote(OZ.at[i, 111:120], YR.at[1 - i], z_send.at[i], y_recv.at[0], (0, 0, sides[i]))

    def arrived(ref, sem):
        pltpu.make_async_copy(ref, ref, sem).wait()

    def put(ref, index, pair):
        ref[(MIDDLE, *index)] = jnp.where(lane < SEAM, pair[1], pair[0])
        ref[(LEFT, *index)] = pair[0]
        ref[(RIGHT, *index)] = pair[1]

    def put_margin(ref, index, v):
        ref[(LEFT, *index)] = jnp.where(lane >= 128 - WIDE, v, ref[(LEFT, *index)])
        ref[(RIGHT, *index)] = jnp.where(lane < WIDE, v, ref[(RIGHT, *index)])

    everywhere = slice(None)
    for z in range(8):
        solid = [(dom * 8 + z) >= floor[:, cut(t)] for t in range(2)]
        for f in range(6):
            v = [state[3 + f, z, :, cut(t)] for t in range(2)]
            if f >= 3:
                v = [jnp.where(m, w, 0.0) for m, w in zip(solid, v)]
            elif z == 0:
                v = [w + jnp.where(dom == 0, source[0, :, cut(t)], 0.0) for t, w in enumerate(v)]
            put(S, (f, level(z), everywhere), v)
    x_fields, z_fields = (0, 3, 4), (2, 4, 5)
    pair = (LEFT, RIGHT)
    for i, at_edge in enumerate((0, 7)):
        for k in range(3):
            for t in range(2):
                OX[i, 2 * k + t] = S[pair[t], x_fields[k], column(at_edge), :]
                OZ[i, 2 * k + t] = S[pair[t], z_fields[k], level(at_edge), :]
    for i in range(2):
        for z in range(8):
            OZ[i, 111 + z] = side_by_side(
                [state[f, z, :, cut(i)] for f in range(9)] + [region[z, :, cut(i)].astype(f32)], i)
        OZ[i, 119] = side_by_side([source[s, :, cut(i)] for s in range(STEPS)] + [floor[:, cut(i)].astype(f32)], i)

    pl.semaphore_wait(barrier, 8 + 5 * (there[0].astype(jnp.int32) + there[1].astype(jnp.int32)))
    for i in range(2):
        @functools.partial(reach, i)
        def _(i=i):
            xa_first(i).start()
    for i in range(2):
        za_first(i).start()
        y_first(i).start()

    for load in loads[4:]:
        load.wait()
    scale = 0.5 * COURANT
    tables = [[t[k] * scale for k in range(REGIONS)] for t in (lame, shear, buoy)]

    def materials(number, seafloor, z):
        bits = [(number & (1 << k)) != 0 for k in range(4)]
        solid = (dom * 8 + z) >= seafloor
        lam, mu, b = (pick(bits, t) for t in tables)
        return lam, jnp.where(solid, mu, 0.0), b, solid

    for s in range(STEPS):
        put(SRC, (pl.ds(8 * s, 8), everywhere),
            [jnp.where(dom == 0, source[s, :, cut(t)], 0.0) for t in range(2)])
    for z in range(8):
        made = [materials(region[z, :, cut(t)], floor[:, cut(t)], z) for t in range(2)]
        for k, ref in enumerate((L, M, B)):
            put(ref, (pl.ds(8 * z, 8), everywhere), [m[k] for m in made])
        for f in range(3):
            put(V, (f, level(z), everywhere), [state[f, z, :, cut(t)] for t in range(2)])

    for i, x in ((0, 0), (1, 7)):
        parts = [[OX[i, 2 * k + t] for t in range(2)] for k in range(3)]
        parts += [[m[p, pl.ds(x, 8, stride=8), :] for p in pair] for m in (L, M)]
        parts += [[
            jnp.concatenate([SRC[p, pl.ds(x, STEPS, stride=8), :], jnp.zeros((8 - STEPS, 128), f32)], 0) for p in pair]]
        for k in range(3, 6):
            for t in range(2):
                OX[i, 2 * k + t + 2] = parts[k][t]
        for j in range(2):
            OX[i, 6 + j] = side_by_side([v[j] for v in parts], j)

        @functools.partial(reach, i)
        def _(i=i):
            for j in range(2):
                xy_first(i, j).start()
            xb_first(i).start()
    for i, z in ((0, 0), (1, 7)):
        parts = [[OZ[i, 2 * k + t] for t in range(2)] for k in range(3)]
        parts += [[m[p, pl.ds(8 * z, 8), :] for p in pair] for m in (L, M)]
        for k in range(3, 5):
            for t in range(2):
                OZ[i, 2 * k + t + 2] = parts[k][t]
        for j in range(2):
            OZ[i, 6 + j] = side_by_side([v[j] for v in parts], j)
            zy_first(i, j).start()
        zb_first(i).start()

    left = (lane >= 128 - WIDE) & (gy > 0)
    right = (lane < WIDE) & (gy < n_gy - 1)
    inside = left | right

    def margin(low, high, f):
        shift_r = (128 - WIDE * f) % 128
        shift_l = (256 - WIDE - WIDE * f) % 128
        a = pltpu.roll(high, shift_r, 1) if shift_r else high
        c = pltpu.roll(low, shift_l, 1) if shift_l else low
        return jnp.where(left, c, jnp.where(right, a, 0.0))

    arrived(ZR0.at[:, 0:6], z_first_recv.at[0])
    for i in range(2):
        @functools.partial(reach, i)
        def _(i=i):
            arrived(XR0.at[i, 0:6], x_first_recv.at[0, i])

    def three(first_tile, second_tile, edge):
        return (
            jnp.where(lane < SEAM, second_tile, first_tile),
            jnp.where(lane >= 128 - WIDE, edge, first_tile),
            jnp.where(lane < WIDE, edge, second_tile),
        )

    def border(parts):
        for i, x in ((0, -1), (1, 8)):
            for k, f in enumerate(x_fields):
                edge = zero if parts == (MIDDLE,) else margin(XR0[i, 6], XR0[i, 7], k)
                tiles = three(XR0[i, 2 * k], XR0[i, 2 * k + 1], edge)
                for p in parts:
                    S[p, f, column(x), :] = tiles[p]
        for i, z in ((0, -1), (1, 8)):
            for k, f in enumerate(z_fields):
                edge = zero if parts == (MIDDLE,) else margin(ZR0[i, 6], ZR0[i, 7], k)
                tiles = three(ZR0[i, 2 * k], ZR0[i, 2 * k + 1], edge)
                for p in parts:
                    S[p, f, level(z), :] = jnp.where(z_there[i], tiles[p], 0.0)

    border((MIDDLE,))
    def x_base(p, s, last):
        return 14 + 18 * s + (3 * p if last else 6 * p)

    def z_base(p, s, last):
        return 12 + 18 * s + (3 * p if last else 6 * p)

    def x_copy(p, i, s, slot, last):
        n = 3 if last else 6
        return remote(
            OX.at[i, pl.ds(x_base(p, s, last), n)], XR.at[slot, p, 1 - i, 0:n], x_send.at[i], x_recv.at[slot, p, 1 - i],
            (0, sides[i], 0))

    def e_copy(p, i, j, s, slot):
        return remote(
            OE.at[i, 3 * s + p, j], ER.at[slot, p, 1 - i, 1 - j], e_send.at[i],
            e_recv.at[slot, p, 1 - i], (sides[j], sides[i], 0))

    def z_copy(p, i, s, slot, last):
        n = 3 if last else 6
        return remote(
            OZ.at[i, pl.ds(z_base(p, s, last), n)], ZR.at[slot, p, 1 - i, 0:n], z_send.at[i], z_recv.at[slot, p],
            (sides[i], 0, 0))

    def move(p, s, slot, last=False):
        def accelerate(z):
            own = level(z)
            after, before = pl.ds(rows(z, 1), 8), pl.ds(rows(z, -1), 8)
            above, below = level(z + 1), level(z - 1)

            def dx(f):
                return S[p, f, after, :] - S[p, f, before, :]

            def dz(f):
                return S[p, f, above, :] - S[p, f, below, :]

            b = B[p, pl.ds(8 * z, 8), :]
            V[p, 0, own, :] -= b * (dx(0) + dy(S[p, 3, own, :]) + dz(4))
            V[p, 1, own, :] -= b * (dx(3) + dy(S[p, 1, own, :]) + dz(5))
            V[p, 2, own, :] -= b * (dx(4) + dy(S[p, 5, own, :]) + dz(2))

        for z in (0, 7):
            accelerate(z)
        if not last:
            for i, x in ((0, 0), (1, 7)):
                for j in range(2):
                    for k, f in enumerate((0, 2)):
                        OE[i, 3 * s + p, j, k : k + 1, :] = V[p, f, pl.ds(rows(7 * j, x), 1), :]

                @functools.partial(reach, i)
                def _(i=i):
                    for j in range(2):
                        e_copy(p, i, j, s, slot).start()
        for z in range(1, 7):
            accelerate(z)
        base = x_base(p, s, last)
        for i, (x, inner) in enumerate(((0, 1), (7, 6))):
            for f in range(3):
                OX[i, base + f] = V[p, f, column(x), :]
                if not last:
                    OX[i, base + 3 + f] = V[p, f, column(inner), :]

            @functools.partial(reach, i)
            def _(i=i):
                x_copy(p, i, s, slot, last).start()
        base = z_base(p, s, last)
        for i, (z, inner) in enumerate(((0, 1), (7, 6))):
            for f in range(3):
                OZ[i, base + f] = V[p, f, level(z), :]
                if not last:
                    OZ[i, base + 3 + f] = V[p, f, level(inner), :]
            z_copy(p, i, s, slot, last).start()

        for z in range(8):
            own = level(z)
            after, before = pl.ds(rows(z, 1), 8), pl.ds(rows(z, -1), 8)
            above, below = level(z + 1), level(z - 1)
            dxs = [V[p, f, after, :] - V[p, f, before, :] for f in range(3)]
            dzs = [V[p, f, above, :] - V[p, f, below, :] for f in range(3)]
            dys = [dy(V[p, f, own, :]) for f in range(3)]
            lam, mu = L[p, pl.ds(8 * z, 8), :], M[p, pl.ds(8 * z, 8), :]
            spread = lam * (dxs[0] + dys[1] + dzs[2])
            mu2 = mu + mu
            S[p, 0, own, :] -= spread + mu2 * dxs[0]
            S[p, 1, own, :] -= spread + mu2 * dys[1]
            S[p, 2, own, :] -= spread + mu2 * dzs[2]
            S[p, 3, own, :] -= mu * (dys[0] + dxs[1])
            S[p, 4, own, :] -= mu * (dzs[0] + dxs[2])
            S[p, 5, own, :] -= mu * (dzs[1] + dys[2])

    def finish(p, slot, then=None):
        last = then is None
        if not last:
            added = SRC[p, pl.ds(8 * then if isinstance(then, int) else pl.multiple_of(8 * then, 8), 8), :]
            for f in range(3):
                S[p, f, level(0), :] += added
            for i, x in ((0, -1), (1, 8)):
                S[p, 0, pl.ds(rows(0, x), 1), :] += SX[i, p, pl.ds(then, 1), :]
        arrived(ZR.at[slot, p, :, 0:3] if last else ZR.at[slot, p], z_recv.at[slot, p])
        for i, z in ((0, 0), (1, 7)):
            near = [ZR[slot, p, i, f] for f in range(3)]
            own = level(z)
            lam, mu = L[p, pl.ds(8 * z, 8), :], M[p, pl.ds(8 * z, 8), :]
            sign = jnp.where(z_there[i], (-1.0, 1.0)[i], 0.0)
            slope = [sign * v for v in near]
            spread = lam * slope[2]
            S[p, 0, own, :] -= spread
            S[p, 1, own, :] -= spread
            S[p, 2, own, :] -= spread + (mu + mu) * slope[2]
            S[p, 4, own, :] -= mu * slope[0]
            S[p, 5, own, :] -= mu * slope[1]

        for i in range(2):
            @functools.partial(reach, i)
            def _(i=i):
                arrived(XR.at[slot, p, i, 0:3] if last else XR.at[slot, p, i], x_recv.at[slot, p, i])

        for i, x, sign in ((0, 0, -1.0), (1, 7, 1.0)):
            near = [XR[slot, p, i, f] for f in range(3)]
            lam, mu = L[p, pl.ds(x, 8, stride=8), :], M[p, pl.ds(x, 8, stride=8), :]
            slope = [sign * v for v in near]
            spread = lam * slope[0]
            S[p, 0, column(x), :] -= spread + (mu + mu) * slope[0]
            S[p, 1, column(x), :] -= spread
            S[p, 2, column(x), :] -= spread
            S[p, 3, column(x), :] -= mu * slope[1]
            S[p, 4, column(x), :] -= mu * slope[2]

        if last:
            return
        for i, x, sign in ((0, 0, -1.0), (1, 7, 1.0)):
            near, far = [XR[slot, p, i, f] for f in range(3)], [XR[slot, p, i, 3 + f] for f in range(3)]
            lam, mu = LX[i, p], MX[i, p]
            dxs = [sign * (far[f] - V[p, f, column(x), :]) for f in range(3)]
            dzs = {}
            for f in (0, 2):
                up, down = pltpu.roll(near[f], 7, 0), pltpu.roll(near[f], 1, 0)
                dzs[f] = jnp.where(sub == 7, 0.0, up) - jnp.where(sub == 0, 0.0, down)
            trace = dxs[0] + dy(near[1]) + dzs[2]
            beyond = column((-1, 8)[i])
            S[p, 0, beyond, :] -= lam * trace + (mu + mu) * dxs[0]
            S[p, 3, beyond, :] -= mu * (dy(near[0]) + dxs[1])
            S[p, 4, beyond, :] -= mu * (dzs[0] + dxs[2])
        for i, z, sign in ((0, 0, -1.0), (1, 7, 1.0)):
            near, far = [ZR[slot, p, i, f] for f in range(3)], [ZR[slot, p, i, 3 + f] for f in range(3)]
            lam, mu = LZ[i, p], MZ[i, p]
            dzs = [sign * (far[f] - V[p, f, level(z), :]) for f in range(3)]
            dxs = {}
            for f in (0, 2):
                ahead, behind = pltpu.roll(near[f], 7, 0), pltpu.roll(near[f], 1, 0)
                dxs[f] = jnp.where(sub == 7, 0.0, ahead) - jnp.where(sub == 0, 0.0, behind)
            trace = dxs[0] + dy(near[1]) + dzs[2]
            beyond = level((-1, 8)[i])
            S[p, 2, beyond, :] -= lam * trace + (mu + mu) * dzs[2]
            S[p, 4, beyond, :] -= mu * (dzs[0] + dxs[2])
            S[p, 5, beyond, :] -= mu * (dzs[1] + dy(near[2]))

        for i in range(2):
            @functools.partial(reach, i)
            def _(i=i):
                arrived(ER.at[slot, p, i], e_recv.at[slot, p, i])
        for i, x in ((0, 0), (1, 7)):
            for j, z in ((0, 0), (1, 7)):
                edge_x, edge_z = (ER[slot, p, i, j, k : k + 1, :] for k in range(2))
                sign = jnp.where(z_there[j], (-1.0, 1.0)[j], 0.0)
                outer = pl.ds(rows(z, (-1, 8)[i]), 1)
                at_z, at_x = slice(z, z + 1), slice(x, x + 1)
                S[p, 0, outer, :] -= LX[i, p, at_z, :] * (sign * edge_z)
                S[p, 4, outer, :] -= MX[i, p, at_z, :] * (sign * edge_x)
                outer = pl.ds(rows((-1, 8)[j], x), 1)
                S[p, 2, outer, :] -= LZ[j, p, at_x, :] * (sides[i] * edge_x)
                S[p, 4, outer, :] -= MZ[j, p, at_x, :] * (sides[i] * edge_z)

    def each_part(then):
        def body(p, carry):
            then(p)
            return carry

        lax.fori_loop(0, 3, body, 0)

    move(MIDDLE, 0, 0)

    arrived(YR, y_recv.at[0])
    low, high = YR[0, 8], YR[1, 8]
    seafloor = margin(low, high, STEPS).astype(jnp.int32)
    first_source = None
    for s in range(STEPS):
        v = jnp.where(dom == 0, margin(low, high, s), 0.0)
        first_source = v if s == 0 else first_source
        put_margin(SRC, (pl.ds(8 * s, 8), everywhere), v)
    for z in range(8):
        low, high = YR[0, z], YR[1, z]
        lam, mu, b, solid = materials(margin(low, high, 9).astype(jnp.int32), seafloor, z)
        for ref, v in ((L, lam), (M, mu), (B, b)):
            put_margin(ref, (pl.ds(8 * z, 8), everywhere), jnp.where(inside, v, 0.0))
        for f in range(9):
            v = margin(low, high, f)
            if f < 3:
                put_margin(V, (f, level(z), everywhere), v)
            else:
                if f >= 6:
                    v = jnp.where(solid, v, 0.0)
                elif z == 0:
                    v = v + first_source
                put_margin(S, (f - 3, level(z), everywhere), v)

    arrived(ZR0.at[:, 6:8], z_first_recv.at[2])
    for i in range(2):
        @functools.partial(reach, i)
        def _(i=i):
            arrived(XR0.at[i, 6:8], x_first_recv.at[2, i])
    border((LEFT, RIGHT))

    def begin(p, carry):
        move(p, 0, 0)
        return carry

    lax.fori_loop(1, 3, begin, 0)

    arrived(ZR0.at[:, 8:12], z_first_recv.at[1])
    for i in range(2):
        @functools.partial(reach, i)
        def _(i=i):
            arrived(XR0.at[i, 8:14], x_first_recv.at[1, i])
    for i in range(2):
        for k, ref in enumerate((LX, MX, SX)):
            tiles = three(XR0[i, 8 + 2 * k], XR0[i, 9 + 2 * k], margin(XR0[i, 6], XR0[i, 7], 3 + k))
            for p in range(3):
                ref[i, p] = tiles[p]
        for k, ref in enumerate((LZ, MZ)):
            tiles = three(ZR0[i, 8 + 2 * k], ZR0[i, 9 + 2 * k], margin(ZR0[i, 6], ZR0[i, 7], 3 + k))
            for p in range(3):
                ref[i, p] = jnp.where(z_there[i], tiles[p], 0.0)

    def step(s, carry):
        slot = lax.rem(s, 2)

        def turn(p):
            finish(p, 1 - slot, s)
            move(p, s, slot)

        each_part(turn)
        return carry

    lax.fori_loop(1, STEPS - 1, step, 0)

    end = STEPS - 1

    def final(p):
        finish(p, (end - 1) % 2, end)
        move(p, end, end % 2, last=True)

    each_part(final)

    def gather(f, ref, k):
        for z in range(8):
            middle, first_tile, second_tile = (ref[p, k, level(z), :] for p in (MIDDLE, LEFT, RIGHT))
            out[f, z, :, cut(0)] = jnp.where(lane < FIRST_CUT, first_tile, middle)
            out[f, z, :, cut(1)] = jnp.where(lane < SECOND_CUT, middle, second_tile)

    for f in range(3):
        gather(f, V, f)
    each_part(lambda p: finish(p, end % 2))
    for f in range(6):
        gather(3 + f, S, f)

    for i in range(2):
        arrived(OZ.at[i], z_send.at[i])

        @functools.partial(reach, i)
        def _(i=i):
            arrived(OX.at[i], x_send.at[i])
            arrived(OE.at[i], e_send.at[i])


def solution(mesh):
    sizes = (mesh.shape["dom"], mesh.shape["gx"], mesh.shape["gy"])

    def on_device(state, source, floor, region, lame, shear, buoy):
        hbm = pl.BlockSpec(memory_space=pltpu.HBM)

        def tiles(*shape):
            return pltpu.VMEM(shape + (8, 128), f32)

        return pl.pallas_call(
            functools.partial(kernel, sizes),
            out_shape=jax.ShapeDtypeStruct(state.shape, f32),
            in_specs=[hbm] * 7,
            out_specs=pl.BlockSpec(memory_space=pltpu.VMEM),
            scratch_shapes=[
                pltpu.VMEM(state.shape, f32),
                pltpu.VMEM(source.shape, f32),
                pltpu.VMEM(floor.shape, jnp.int32),
                pltpu.VMEM(region.shape, jnp.int32),
                pltpu.SMEM(lame.shape, f32),
                pltpu.SMEM(shear.shape, f32),
                pltpu.SMEM(buoy.shape, f32),
                pltpu.VMEM((3, 6, 10 * BLOCK, 128), f32),
                pltpu.VMEM((3, 3, 10 * BLOCK, 128), f32),
                pltpu.VMEM((3, 64, 128), f32),
                pltpu.VMEM((3, 64, 128), f32),
                pltpu.VMEM((3, 64, 128), f32),
                pltpu.VMEM((3, 8 * STEPS, 128), f32),
                tiles(2, 3),
                tiles(2, 3),
                tiles(2, 3),
                tiles(2, 3),
                tiles(2, 3),
                tiles(2, 113),
                tiles(2, 120),
                pltpu.VMEM((2, 3 * STEPS - 3, 2, 2, 128), f32),
                tiles(2, 14),
                tiles(2, 12),
                tiles(2, 9),
                tiles(2, 3, 2, 6),
                tiles(2, 3, 2, 6),
                pltpu.VMEM((2, 3, 2, 2, 2, 128), f32),
                pltpu.SemaphoreType.DMA((7,)),
                pltpu.SemaphoreType.DMA((2,)),
                pltpu.SemaphoreType.DMA((2,)),
                pltpu.SemaphoreType.DMA((2,)),
                pltpu.SemaphoreType.DMA((3, 2)),
                pltpu.SemaphoreType.DMA((3,)),
                pltpu.SemaphoreType.DMA((1,)),
                pltpu.SemaphoreType.DMA((2, 3, 2)),
                pltpu.SemaphoreType.DMA((2, 3)),
                pltpu.SemaphoreType.DMA((2, 3, 2)),
            ],
            compiler_params=pltpu.CompilerParams(
                collective_id=0, has_side_effects=True, vmem_limit_bytes=32 * 1024 * 1024
            ),
        )(*(
            pltpu.with_memory_space_constraint(v, pltpu.HBM)
            for v in (state, source, floor, region, lame, shear, buoy)
        ))

    return jax.shard_map(
        on_device,
        mesh=mesh,
        in_specs=(
            P(None, "dom", "gx", "gy"),
            P(None, "gx", "gy"),
            P("gx", "gy"),
            P("dom", "gx", "gy"),
            P(),
            P(),
            P(),
        ),
        out_specs=P(None, "dom", "gx", "gy"),
        check_vma=False,
    )
```

```python
import functools

import jax
import jax.numpy as jnp
from jax import lax
from jax.experimental import pallas as pl
from jax.experimental.pallas import tpu as pltpu
from jax.sharding import PartitionSpec as P

STEPS = 6
COURANT = 0.25
REGIONS = 16
BLOCK = 16
WIDE = 12
MIDDLE, LEFT, RIGHT = 0, 1, 2
FIRST_CUT, SECOND_CUT, SEAM = 86, 171 - 128, 64
MESH = pl.DeviceIdType.MESH

f32 = jnp.float32


def rows(z, x=0):
    return (z + 1) * BLOCK + 8 + x


def level(z):
    return pl.ds(rows(z), 8)


def column(x):
    return pl.ds(rows(0, x), 8, stride=BLOCK)


def dy(v):
    return pltpu.roll(v, 127, 1) - pltpu.roll(v, 1, 1)


def pick(bits, table):
    values = list(table)
    for bit in bits:
        values = [jnp.where(bit, values[2 * i + 1], values[2 * i]) for i in range(len(values) // 2)]
    return values[0]


def kernel(
    sizes, state_in, source_in, floor_in, region_in, lame_in, shear_in, buoy_in, out,
    state, source, floor, region, lame, shear, buoy,
    S, V, L, M, B, SRC, LX, MX, SX, LZ, MZ, OX, OZ, OE, XR0, ZR0, YR, XR, ZR, ER,
    in_sem, x_first_send, x_send, z_send, e_send, x_first_recv, z_first_recv, y_recv, x_recv, z_recv, e_recv,
):
    n_dom, n_gx, n_gy = sizes
    dom, gx, gy = lax.axis_index("dom"), lax.axis_index("gx"), lax.axis_index("gy")
    lane = lax.broadcasted_iota(jnp.int32, (8, 128), 1)
    sub = lax.broadcasted_iota(jnp.int32, (8, 128), 0)
    zero = jnp.zeros((8, 128), f32)

    loads = [
        pltpu.make_async_copy(src, dst, in_sem.at[i])
        for i, (src, dst) in enumerate((
            (region_in, region), (floor_in, floor), (source_in, source), (state_in, state),
            (lame_in, lame), (shear_in, shear), (buoy_in, buoy)))
    ]
    for load in loads:
        load.start()

    sides = (-1, 1)
    there = [gx > 0, gx < n_gx - 1]
    z_there = [dom > 0, dom < n_dom - 1]

    doms = [dom, jnp.where(dom == n_dom - 1, 0, dom + 1), jnp.where(dom == 0, n_dom - 1, dom - 1)]
    gxs = [gx, gx + 1, gx - 1]
    gys = [gy, jnp.where(gy == n_gy - 1, 0, gy + 1), jnp.where(gy == 0, n_gy - 1, gy - 1)]

    def at(dz, dx, dyy):
        return (doms[dz], gxs[dx], gys[dyy])

    def reach(i, then):
        pl.when(there[i])(then)

    barrier = pltpu.get_barrier_semaphore()

    def greet(*way):
        pl.semaphore_signal(barrier, inc=1, device_id=at(*way), device_id_type=MESH)

    for i, dx in enumerate(sides):
        @functools.partial(reach, i)
        def _(dx=dx):
            for way in ((0, dx, 0), (-1, dx, 0), (1, dx, 0), (0, dx, -1), (0, dx, 1)):
                greet(*way)
    for way in [(a, 0, b) for a in (-1, 0, 1) for b in (-1, 0, 1) if a or b]:
        greet(*way)

    for i in range(2):
        @pl.when(jnp.logical_not(there[i]))
        def _(i=i):
            XR0[i] = jnp.zeros(XR0.shape[1:], f32)
            for slot in range(2):
                for p in range(3):
                    XR[slot, p, i] = jnp.zeros(XR.shape[3:], f32)
                    ER[slot, p, i] = jnp.zeros(ER.shape[3:], f32)

    for p in range(3):
        for f in range(3):
            for z in range(-1, 9):
                V[p, f, pl.ds(rows(z, -8), 8), :] = zero
            for z in (-1, 8):
                V[p, f, level(z), :] = zero

    for load in loads[:4]:
        load.wait()

    def side_by_side(parts, t):
        tile = zero
        for k, v in enumerate(parts):
            shift = (WIDE * k + (WIDE if t else 0)) % 128
            v = pltpu.roll(v, shift, 1) if shift else v
            tile = jnp.where((lane >= WIDE * k) & (lane < WIDE * (k + 1)), v, tile)
        return tile

    def cut(t):
        return slice(128 * t, 128 * t + 128)

    def remote(src, dst, send, recv, way):
        return pltpu.make_async_remote_copy(
            src_ref=src, dst_ref=dst, send_sem=send, recv_sem=recv, device_id=at(*way), device_id_type=MESH)

    def xa_first(i):
        return remote(OX.at[i, 0:6], XR0.at[1 - i, 0:6], x_first_send.at[i], x_first_recv.at[0, 1 - i], (0, sides[i], 0))

    def xy_first(i, j):
        return remote(
            OX.at[i, 6 + j], XR0.at[1 - i, 7 - j], x_first_send.at[i], x_first_recv.at[2, 1 - i], (0, sides[i], sides[j]))

    def xb_first(i):
        return remote(OX.at[i, 8:14], XR0.at[1 - i, 8:14], x_first_send.at[i], x_first_recv.at[1, 1 - i], (0, sides[i], 0))

    def za_first(i):
        return remote(OZ.at[i, 0:6], ZR0.at[1 - i, 0:6], z_send.at[i], z_first_recv.at[0], (sides[i], 0, 0))

    def zy_first(i, j):
        return remote(
            OZ.at[i, 6 + j], ZR0.at[1 - i, 7 - j], z_send.at[i], z_first_recv.at[2], (sides[i], 0, sides[j]))

    def zb_first(i):
        return remote(OZ.at[i, 8:12], ZR0.at[1 - i, 8:12], z_send.at[i], z_first_recv.at[1], (sides[i], 0, 0))

    def y_first(i):
        return remote(OZ.at[i, 111:120], YR.at[1 - i], z_send.at[i], y_recv.at[0], (0, 0, sides[i]))

    def arrived(ref, sem):
        pltpu.make_async_copy(ref, ref, sem).wait()

    def put(ref, index, pair):
        ref[(MIDDLE, *index)] = jnp.where(lane < SEAM, pair[1], pair[0])
        ref[(LEFT, *index)] = pair[0]
        ref[(RIGHT, *index)] = pair[1]

    def put_margin(ref, index, v):
        ref[(LEFT, *index)] = jnp.where(lane >= 128 - WIDE, v, ref[(LEFT, *index)])
        ref[(RIGHT, *index)] = jnp.where(lane < WIDE, v, ref[(RIGHT, *index)])

    everywhere = slice(None)
    for z in range(8):
        solid = [(dom * 8 + z) >= floor[:, cut(t)] for t in range(2)]
        for f in range(6):
            v = [state[3 + f, z, :, cut(t)] for t in range(2)]
            if f >= 3:
                v = [jnp.where(m, w, 0.0) for m, w in zip(solid, v)]
            elif z == 0:
                v = [w + jnp.where(dom == 0, source[0, :, cut(t)], 0.0) for t, w in enumerate(v)]
            put(S, (f, level(z), everywhere), v)
    x_fields, z_fields = (0, 3, 4), (2, 4, 5)
    pair = (LEFT, RIGHT)
    for i, at_edge in enumerate((0, 7)):
        for k in range(3):
            for t in range(2):
                OX[i, 2 * k + t] = S[pair[t], x_fields[k], column(at_edge), :]
                OZ[i, 2 * k + t] = S[pair[t], z_fields[k], level(at_edge), :]
    for i in range(2):
        for z in range(8):
            OZ[i, 111 + z] = side_by_side(
                [state[f, z, :, cut(i)] for f in range(9)] + [region[z, :, cut(i)].astype(f32)], i)
        OZ[i, 119] = side_by_side([source[s, :, cut(i)] for s in range(STEPS)] + [floor[:, cut(i)].astype(f32)], i)

    pl.semaphore_wait(barrier, 8 + 5 * (there[0].astype(jnp.int32) + there[1].astype(jnp.int32)))
    for i in range(2):
        @functools.partial(reach, i)
        def _(i=i):
            xa_first(i).start()
    for i in range(2):
        za_first(i).start()
        y_first(i).start()

    for load in loads[4:]:
        load.wait()
    scale = 0.5 * COURANT
    tables = [[t[k] * scale for k in range(REGIONS)] for t in (lame, shear, buoy)]

    def materials(number, seafloor, z):
        bits = [(number & (1 << k)) != 0 for k in range(4)]
        solid = (dom * 8 + z) >= seafloor
        lam, mu, b = (pick(bits, t) for t in tables)
        return lam, jnp.where(solid, mu, 0.0), b, solid

    for s in range(STEPS):
        put(SRC, (pl.ds(8 * s, 8), everywhere),
            [jnp.where(dom == 0, source[s, :, cut(t)], 0.0) for t in range(2)])
    for z in range(8):
        made = [materials(region[z, :, cut(t)], floor[:, cut(t)], z) for t in range(2)]
        for k, ref in enumerate((L, M, B)):
            put(ref, (pl.ds(8 * z, 8), everywhere), [m[k] for m in made])
        for f in range(3):
            put(V, (f, level(z), everywhere), [state[f, z, :, cut(t)] for t in range(2)])

    for i, x in ((0, 0), (1, 7)):
        parts = [[OX[i, 2 * k + t] for t in range(2)] for k in range(3)]
        parts += [[m[p, pl.ds(x, 8, stride=8), :] for p in pair] for m in (L, M)]
        parts += [[
            jnp.concatenate([SRC[p, pl.ds(x, STEPS, stride=8), :], jnp.zeros((8 - STEPS, 128), f32)], 0) for p in pair]]
        for k in range(3, 6):
            for t in range(2):
                OX[i, 2 * k + t + 2] = parts[k][t]
        for j in range(2):
            OX[i, 6 + j] = side_by_side([v[j] for v in parts], j)

        @functools.partial(reach, i)
        def _(i=i):
            for j in range(2):
                xy_first(i, j).start()
            xb_first(i).start()
    for i, z in ((0, 0), (1, 7)):
        parts = [[OZ[i, 2 * k + t] for t in range(2)] for k in range(3)]
        parts += [[m[p, pl.ds(8 * z, 8), :] for p in pair] for m in (L, M)]
        for k in range(3, 5):
            for t in range(2):
                OZ[i, 2 * k + t + 2] = parts[k][t]
        for j in range(2):
            OZ[i, 6 + j] = side_by_side([v[j] for v in parts], j)
            zy_first(i, j).start()
        zb_first(i).start()

    left = (lane >= 128 - WIDE) & (gy > 0)
    right = (lane < WIDE) & (gy < n_gy - 1)
    inside = left | right

    def margin(low, high, f):
        shift_r = (128 - WIDE * f) % 128
        shift_l = (256 - WIDE - WIDE * f) % 128
        a = pltpu.roll(high, shift_r, 1) if shift_r else high
        c = pltpu.roll(low, shift_l, 1) if shift_l else low
        return jnp.where(left, c, jnp.where(right, a, 0.0))

    arrived(ZR0.at[:, 0:6], z_first_recv.at[0])
    for i in range(2):
        @functools.partial(reach, i)
        def _(i=i):
            arrived(XR0.at[i, 0:6], x_first_recv.at[0, i])

    def three(first_tile, second_tile, edge):
        return (
            jnp.where(lane < SEAM, second_tile, first_tile),
            jnp.where(lane >= 128 - WIDE, edge, first_tile),
            jnp.where(lane < WIDE, edge, second_tile),
        )

    def border(parts):
        for i, x in ((0, -1), (1, 8)):
            for k, f in enumerate(x_fields):
                edge = zero if parts == (MIDDLE,) else margin(XR0[i, 6], XR0[i, 7], k)
                tiles = three(XR0[i, 2 * k], XR0[i, 2 * k + 1], edge)
                for p in parts:
                    S[p, f, column(x), :] = tiles[p]
        for i, z in ((0, -1), (1, 8)):
            for k, f in enumerate(z_fields):
                edge = zero if parts == (MIDDLE,) else margin(ZR0[i, 6], ZR0[i, 7], k)
                tiles = three(ZR0[i, 2 * k], ZR0[i, 2 * k + 1], edge)
                for p in parts:
                    S[p, f, level(z), :] = jnp.where(z_there[i], tiles[p], 0.0)

    border((MIDDLE,))
    def x_base(p, s, last):
        return 14 + 18 * s + (3 * p if last else 6 * p)

    def z_base(p, s, last):
        return 12 + 18 * s + (3 * p if last else 6 * p)

    def x_copy(p, i, s, slot, last):
        n = 3 if last else 6
        return remote(
            OX.at[i, pl.ds(x_base(p, s, last), n)], XR.at[slot, p, 1 - i, 0:n], x_send.at[i], x_recv.at[slot, p, 1 - i],
            (0, sides[i], 0))

    def e_copy(p, i, j, s, slot):
        return remote(
            OE.at[i, 3 * s + p, j], ER.at[slot, p, 1 - i, 1 - j], e_send.at[i],
            e_recv.at[slot, p, 1 - i], (sides[j], sides[i], 0))

    def z_copy(p, i, s, slot, last):
        n = 3 if last else 6
        return remote(
            OZ.at[i, pl.ds(z_base(p, s, last), n)], ZR.at[slot, p, 1 - i, 0:n], z_send.at[i], z_recv.at[slot, p],
            (sides[i], 0, 0))

    def move(p, s, slot, first=False, last=False):
        def accelerate(z):
            own = level(z)
            after, before = pl.ds(rows(z, 1), 8), pl.ds(rows(z, -1), 8)
            above, below = level(z + 1), level(z - 1)

            def dx(f):
                return S[p, f, after, :] - S[p, f, before, :]

            def dz(f):
                return S[p, f, above, :] - S[p, f, below, :]

            b = B[p, pl.ds(8 * z, 8), :]
            V[p, 0, own, :] -= b * (dx(0) + dy(S[p, 3, own, :]) + dz(4))
            V[p, 1, own, :] -= b * (dx(3) + dy(S[p, 1, own, :]) + dz(5))
            V[p, 2, own, :] -= b * (dx(4) + dy(S[p, 5, own, :]) + dz(2))

        for z in (0, 7):
            accelerate(z)
        if not last:
            for i, x in ((0, 0), (1, 7)):
                for j in range(2):
                    for k, f in enumerate((0, 2)):
                        OE[i, 3 * s + p, j, k : k + 1, :] = V[p, f, pl.ds(rows(7 * j, x), 1), :]

                @functools.partial(reach, i)
                def _(i=i):
                    for j in range(2):
                        e_copy(p, i, j, s, slot).start()
        for z in range(1, 7):
            accelerate(z)
        base = x_base(p, s, last)
        for i, (x, inner) in enumerate(((0, 1), (7, 6))):
            for f in range(3):
                OX[i, base + f] = V[p, f, column(x), :]
                if not last:
                    OX[i, base + 3 + f] = V[p, f, column(inner), :]

            @functools.partial(reach, i)
            def _(i=i):
                if not (first or last):
                    arrived(OX.at[i, 0:6], x_send.at[i])
                x_copy(p, i, s, slot, last).start()
        base = z_base(p, s, last)
        for i, (z, inner) in enumerate(((0, 1), (7, 6))):
            for f in range(3):
                OZ[i, base + f] = V[p, f, level(z), :]
                if not last:
                    OZ[i, base + 3 + f] = V[p, f, level(inner), :]
            z_copy(p, i, s, slot, last).start()

        for z in range(8):
            own = level(z)
            after, before = pl.ds(rows(z, 1), 8), pl.ds(rows(z, -1), 8)
            above, below = level(z + 1), level(z - 1)
            dxs = [V[p, f, after, :] - V[p, f, before, :] for f in range(3)]
            dzs = [V[p, f, above, :] - V[p, f, below, :] for f in range(3)]
            dys = [dy(V[p, f, own, :]) for f in range(3)]
            lam, mu = L[p, pl.ds(8 * z, 8), :], M[p, pl.ds(8 * z, 8), :]
            spread = lam * (dxs[0] + dys[1] + dzs[2])
            mu2 = mu + mu
            S[p, 0, own, :] -= spread + mu2 * dxs[0]
            S[p, 1, own, :] -= spread + mu2 * dys[1]
            S[p, 2, own, :] -= spread + mu2 * dzs[2]
            S[p, 3, own, :] -= mu * (dys[0] + dxs[1])
            S[p, 4, own, :] -= mu * (dzs[0] + dxs[2])
            S[p, 5, own, :] -= mu * (dzs[1] + dys[2])

    def finish(p, slot, then=None):
        last = then is None
        if not last:
            added = SRC[p, pl.ds(8 * then if isinstance(then, int) else pl.multiple_of(8 * then, 8), 8), :]
            for f in range(3):
                S[p, f, level(0), :] += added
            for i, x in ((0, -1), (1, 8)):
                S[p, 0, pl.ds(rows(0, x), 1), :] += SX[i, p, pl.ds(then, 1), :]
        arrived(ZR.at[slot, p, :, 0:3] if last else ZR.at[slot, p], z_recv.at[slot, p])
        for i, z in ((0, 0), (1, 7)):
            near = [ZR[slot, p, i, f] for f in range(3)]
            own = level(z)
            lam, mu = L[p, pl.ds(8 * z, 8), :], M[p, pl.ds(8 * z, 8), :]
            sign = jnp.where(z_there[i], (-1.0, 1.0)[i], 0.0)
            slope = [sign * v for v in near]
            spread = lam * slope[2]
            S[p, 0, own, :] -= spread
            S[p, 1, own, :] -= spread
            S[p, 2, own, :] -= spread + (mu + mu) * slope[2]
            S[p, 4, own, :] -= mu * slope[0]
            S[p, 5, own, :] -= mu * slope[1]

        for i in range(2):
            @functools.partial(reach, i)
            def _(i=i):
                arrived(XR.at[slot, p, i, 0:3] if last else XR.at[slot, p, i], x_recv.at[slot, p, i])

        for i, x, sign in ((0, 0, -1.0), (1, 7, 1.0)):
            near = [XR[slot, p, i, f] for f in range(3)]
            lam, mu = L[p, pl.ds(x, 8, stride=8), :], M[p, pl.ds(x, 8, stride=8), :]
            slope = [sign * v for v in near]
            spread = lam * slope[0]
            S[p, 0, column(x), :] -= spread + (mu + mu) * slope[0]
            S[p, 1, column(x), :] -= spread
            S[p, 2, column(x), :] -= spread
            S[p, 3, column(x), :] -= mu * slope[1]
            S[p, 4, column(x), :] -= mu * slope[2]

        if last:
            return
        for i, x, sign in ((0, 0, -1.0), (1, 7, 1.0)):
            near, far = [XR[slot, p, i, f] for f in range(3)], [XR[slot, p, i, 3 + f] for f in range(3)]
            lam, mu = LX[i, p], MX[i, p]
            dxs = [sign * (far[f] - V[p, f, column(x), :]) for f in range(3)]
            dzs = {}
            for f in (0, 2):
                up, down = pltpu.roll(near[f], 7, 0), pltpu.roll(near[f], 1, 0)
                dzs[f] = jnp.where(sub == 7, 0.0, up) - jnp.where(sub == 0, 0.0, down)
            trace = dxs[0] + dy(near[1]) + dzs[2]
            beyond = column((-1, 8)[i])
            S[p, 0, beyond, :] -= lam * trace + (mu + mu) * dxs[0]
            S[p, 3, beyond, :] -= mu * (dy(near[0]) + dxs[1])
            S[p, 4, beyond, :] -= mu * (dzs[0] + dxs[2])
        for i, z, sign in ((0, 0, -1.0), (1, 7, 1.0)):
            near, far = [ZR[slot, p, i, f] for f in range(3)], [ZR[slot, p, i, 3 + f] for f in range(3)]
            lam, mu = LZ[i, p], MZ[i, p]
            dzs = [sign * (far[f] - V[p, f, level(z), :]) for f in range(3)]
            dxs = {}
            for f in (0, 2):
                ahead, behind = pltpu.roll(near[f], 7, 0), pltpu.roll(near[f], 1, 0)
                dxs[f] = jnp.where(sub == 7, 0.0, ahead) - jnp.where(sub == 0, 0.0, behind)
            trace = dxs[0] + dy(near[1]) + dzs[2]
            beyond = level((-1, 8)[i])
            S[p, 2, beyond, :] -= lam * trace + (mu + mu) * dzs[2]
            S[p, 4, beyond, :] -= mu * (dzs[0] + dxs[2])
            S[p, 5, beyond, :] -= mu * (dzs[1] + dy(near[2]))

        for i in range(2):
            @functools.partial(reach, i)
            def _(i=i):
                arrived(ER.at[slot, p, i], e_recv.at[slot, p, i])
        for i, x in ((0, 0), (1, 7)):
            for j, z in ((0, 0), (1, 7)):
                edge_x, edge_z = (ER[slot, p, i, j, k : k + 1, :] for k in range(2))
                sign = jnp.where(z_there[j], (-1.0, 1.0)[j], 0.0)
                outer = pl.ds(rows(z, (-1, 8)[i]), 1)
                at_z, at_x = slice(z, z + 1), slice(x, x + 1)
                S[p, 0, outer, :] -= LX[i, p, at_z, :] * (sign * edge_z)
                S[p, 4, outer, :] -= MX[i, p, at_z, :] * (sign * edge_x)
                outer = pl.ds(rows((-1, 8)[j], x), 1)
                S[p, 2, outer, :] -= LZ[j, p, at_x, :] * (sides[i] * edge_x)
                S[p, 4, outer, :] -= MZ[j, p, at_x, :] * (sides[i] * edge_z)

    def each_part(then):
        def body(p, carry):
            then(p)
            return carry

        lax.fori_loop(0, 3, body, 0)

    move(MIDDLE, 0, 0, first=True)

    arrived(YR, y_recv.at[0])
    low, high = YR[0, 8], YR[1, 8]
    seafloor = margin(low, high, STEPS).astype(jnp.int32)
    first_source = None
    for s in range(STEPS):
        v = jnp.where(dom == 0, margin(low, high, s), 0.0)
        first_source = v if s == 0 else first_source
        put_margin(SRC, (pl.ds(8 * s, 8), everywhere), v)
    for z in range(8):
        low, high = YR[0, z], YR[1, z]
        lam, mu, b, solid = materials(margin(low, high, 9).astype(jnp.int32), seafloor, z)
        for ref, v in ((L, lam), (M, mu), (B, b)):
            put_margin(ref, (pl.ds(8 * z, 8), everywhere), jnp.where(inside, v, 0.0))
        for f in range(9):
            v = margin(low, high, f)
            if f < 3:
                put_margin(V, (f, level(z), everywhere), v)
            else:
                if f >= 6:
                    v = jnp.where(solid, v, 0.0)
                elif z == 0:
                    v = v + first_source
                put_margin(S, (f - 3, level(z), everywhere), v)

    arrived(ZR0.at[:, 6:8], z_first_recv.at[2])
    for i in range(2):
        @functools.partial(reach, i)
        def _(i=i):
            arrived(XR0.at[i, 6:8], x_first_recv.at[2, i])
    border((LEFT, RIGHT))

    def begin(p, carry):
        move(p, 0, 0)
        return carry

    lax.fori_loop(1, 3, begin, 0)

    arrived(ZR0.at[:, 8:12], z_first_recv.at[1])
    for i in range(2):
        @functools.partial(reach, i)
        def _(i=i):
            arrived(XR0.at[i, 8:14], x_first_recv.at[1, i])
    for i in range(2):
        for k, ref in enumerate((LX, MX, SX)):
            tiles = three(XR0[i, 8 + 2 * k], XR0[i, 9 + 2 * k], margin(XR0[i, 6], XR0[i, 7], 3 + k))
            for p in range(3):
                ref[i, p] = tiles[p]
        for k, ref in enumerate((LZ, MZ)):
            tiles = three(ZR0[i, 8 + 2 * k], ZR0[i, 9 + 2 * k], margin(ZR0[i, 6], ZR0[i, 7], 3 + k))
            for p in range(3):
                ref[i, p] = jnp.where(z_there[i], tiles[p], 0.0)

    def step(s, carry):
        slot = lax.rem(s, 2)

        def turn(p):
            finish(p, 1 - slot, s)
            move(p, s, slot)

        each_part(turn)
        return carry

    lax.fori_loop(1, STEPS - 1, step, 0)

    end = STEPS - 1

    def final(p):
        finish(p, (end - 1) % 2, end)
        move(p, end, end % 2, last=True)

    each_part(final)

    def gather(f, ref, k):
        for z in range(8):
            middle, first_tile, second_tile = (ref[p, k, level(z), :] for p in (MIDDLE, LEFT, RIGHT))
            out[f, z, :, cut(0)] = jnp.where(lane < FIRST_CUT, first_tile, middle)
            out[f, z, :, cut(1)] = jnp.where(lane < SECOND_CUT, middle, second_tile)

    for f in range(3):
        gather(f, V, f)
    each_part(lambda p: finish(p, end % 2))
    for f in range(6):
        gather(3 + f, S, f)

    for i in range(2):
        arrived(OZ.at[i], z_send.at[i])

        @functools.partial(reach, i)
        def _(i=i):
            arrived(OX.at[i, 0:14], x_first_send.at[i])
            arrived(OX.at[i, 98:113], x_send.at[i])
            arrived(OE.at[i], e_send.at[i])


def solution(mesh):
    sizes = (mesh.shape["dom"], mesh.shape["gx"], mesh.shape["gy"])

    def on_device(state, source, floor, region, lame, shear, buoy):
        hbm = pl.BlockSpec(memory_space=pltpu.HBM)

        def tiles(*shape):
            return pltpu.VMEM(shape + (8, 128), f32)

        return pl.pallas_call(
            functools.partial(kernel, sizes),
            out_shape=jax.ShapeDtypeStruct(state.shape, f32),
            in_specs=[hbm] * 7,
            out_specs=pl.BlockSpec(memory_space=pltpu.VMEM),
            scratch_shapes=[
                pltpu.VMEM(state.shape, f32),
                pltpu.VMEM(source.shape, f32),
                pltpu.VMEM(floor.shape, jnp.int32),
                pltpu.VMEM(region.shape, jnp.int32),
                pltpu.SMEM(lame.shape, f32),
                pltpu.SMEM(shear.shape, f32),
                pltpu.SMEM(buoy.shape, f32),
                pltpu.VMEM((3, 6, 10 * BLOCK, 128), f32),
                pltpu.VMEM((3, 3, 10 * BLOCK, 128), f32),
                pltpu.VMEM((3, 64, 128), f32),
                pltpu.VMEM((3, 64, 128), f32),
                pltpu.VMEM((3, 64, 128), f32),
                pltpu.VMEM((3, 8 * STEPS, 128), f32),
                tiles(2, 3),
                tiles(2, 3),
                tiles(2, 3),
                tiles(2, 3),
                tiles(2, 3),
                tiles(2, 113),
                tiles(2, 120),
                pltpu.VMEM((2, 3 * STEPS - 3, 2, 2, 128), f32),
                tiles(2, 14),
                tiles(2, 12),
                tiles(2, 9),
                tiles(2, 3, 2, 6),
                tiles(2, 3, 2, 6),
                pltpu.VMEM((2, 3, 2, 2, 2, 128), f32),
                pltpu.SemaphoreType.DMA((7,)),
                pltpu.SemaphoreType.DMA((2,)),
                pltpu.SemaphoreType.DMA((2,)),
                pltpu.SemaphoreType.DMA((2,)),
                pltpu.SemaphoreType.DMA((2,)),
                pltpu.SemaphoreType.DMA((3, 2)),
                pltpu.SemaphoreType.DMA((3,)),
                pltpu.SemaphoreType.DMA((1,)),
                pltpu.SemaphoreType.DMA((2, 3, 2)),
                pltpu.SemaphoreType.DMA((2, 3)),
                pltpu.SemaphoreType.DMA((2, 3, 2)),
            ],
            compiler_params=pltpu.CompilerParams(
                collective_id=0, has_side_effects=True, vmem_limit_bytes=32 * 1024 * 1024
            ),
        )(*(
            pltpu.with_memory_space_constraint(v, pltpu.HBM)
            for v in (state, source, floor, region, lame, shear, buoy)
        ))

    return jax.shard_map(
        on_device,
        mesh=mesh,
        in_specs=(
            P(None, "dom", "gx", "gy"),
            P(None, "gx", "gy"),
            P("gx", "gy"),
            P("dom", "gx", "gy"),
            P(),
            P(),
            P(),
        ),
        out_specs=P(None, "dom", "gx", "gy"),
        check_vma=False,
    )
```

```python
import functools

import jax
import jax.numpy as jnp
from jax import lax
from jax.experimental import pallas as pl
from jax.experimental.pallas import tpu as pltpu
from jax.sharding import PartitionSpec as P

STEPS = 6
COURANT = 0.25
REGIONS = 16
BLOCK = 16
WIDE = 12
MIDDLE, LEFT, RIGHT = 0, 1, 2
FIRST_CUT, SECOND_CUT, SEAM = 86, 171 - 128, 64
MESH = pl.DeviceIdType.MESH

f32 = jnp.float32


def rows(z, x=0):
    return (z + 1) * BLOCK + 8 + x


def level(z):
    return pl.ds(rows(z), 8)


def column(x):
    return pl.ds(rows(0, x), 8, stride=BLOCK)


def dy(v):
    return pltpu.roll(v, 127, 1) - pltpu.roll(v, 1, 1)


def pick(bits, table):
    values = list(table)
    for bit in bits:
        values = [jnp.where(bit, values[2 * i + 1], values[2 * i]) for i in range(len(values) // 2)]
    return values[0]


def kernel(
    sizes, state_in, source_in, floor_in, region_in, lame_in, shear_in, buoy_in, out,
    state, source, floor, region, lame, shear, buoy,
    S, V, L, M, B, SRC, LX, MX, SX, LZ, MZ, OX, OZ, OE, XR0, ZR0, YR, XR, ZR, ER,
    in_sem, x_send, z_send, e_send, x_first_recv, z_first_recv, y_recv, x_recv, z_recv, e_recv,
):
    n_dom, n_gx, n_gy = sizes
    dom, gx, gy = lax.axis_index("dom"), lax.axis_index("gx"), lax.axis_index("gy")
    lane = lax.broadcasted_iota(jnp.int32, (8, 128), 1)
    sub = lax.broadcasted_iota(jnp.int32, (8, 128), 0)
    zero = jnp.zeros((8, 128), f32)

    loads = [
        pltpu.make_async_copy(src, dst, in_sem.at[i])
        for i, (src, dst) in enumerate((
            (region_in, region), (floor_in, floor), (source_in, source), (state_in, state),
            (lame_in, lame), (shear_in, shear), (buoy_in, buoy)))
    ]
    for load in loads:
        load.start()

    sides = (-1, 1)
    there = [gx > 0, gx < n_gx - 1]
    z_there = [dom > 0, dom < n_dom - 1]

    doms = [dom, jnp.where(dom == n_dom - 1, 0, dom + 1), jnp.where(dom == 0, n_dom - 1, dom - 1)]
    gxs = [gx, gx + 1, gx - 1]
    gys = [gy, jnp.where(gy == n_gy - 1, 0, gy + 1), jnp.where(gy == 0, n_gy - 1, gy - 1)]

    def at(dz, dx, dyy):
        return (doms[dz], gxs[dx], gys[dyy])

    def reach(i, then):
        pl.when(there[i])(then)

    barrier = pltpu.get_barrier_semaphore()

    def greet(*way):
        pl.semaphore_signal(barrier, inc=1, device_id=at(*way), device_id_type=MESH)

    for i, dx in enumerate(sides):
        @functools.partial(reach, i)
        def _(dx=dx):
            for way in ((0, dx, 0), (-1, dx, 0), (1, dx, 0), (0, dx, -1), (0, dx, 1)):
                greet(*way)
    for way in [(a, 0, b) for a in (-1, 0, 1) for b in (-1, 0, 1) if a or b]:
        greet(*way)

    for i in range(2):
        @pl.when(jnp.logical_not(there[i]))
        def _(i=i):
            XR0[i] = jnp.zeros(XR0.shape[1:], f32)
            for slot in range(2):
                for p in range(3):
                    XR[slot, p, i] = jnp.zeros(XR.shape[3:], f32)
                    ER[slot, p, i] = jnp.zeros(ER.shape[3:], f32)

    for p in range(3):
        for f in range(3):
            for z in range(-1, 9):
                V[p, f, pl.ds(rows(z, -8), 8), :] = zero
            for z in (-1, 8):
                V[p, f, level(z), :] = zero

    for load in loads[:4]:
        load.wait()

    def side_by_side(parts, t):
        tile = zero
        for k, v in enumerate(parts):
            shift = (WIDE * k + (WIDE if t else 0)) % 128
            v = pltpu.roll(v, shift, 1) if shift else v
            tile = jnp.where((lane >= WIDE * k) & (lane < WIDE * (k + 1)), v, tile)
        return tile

    def cut(t):
        return slice(128 * t, 128 * t + 128)

    def remote(src, dst, send, recv, way):
        return pltpu.make_async_remote_copy(
            src_ref=src, dst_ref=dst, send_sem=send, recv_sem=recv, device_id=at(*way), device_id_type=MESH)

    def xa_first(i):
        return remote(OX.at[i, 0:6], XR0.at[1 - i, 0:6], x_send.at[i], x_first_recv.at[0, 1 - i], (0, sides[i], 0))

    def xy_first(i, j):
        return remote(
            OX.at[i, 6 + j], XR0.at[1 - i, 7 - j], x_send.at[i], x_first_recv.at[2, 1 - i], (0, sides[i], sides[j]))

    def xb_first(i):
        return remote(OX.at[i, 8:14], XR0.at[1 - i, 8:14], x_send.at[i], x_first_recv.at[1, 1 - i], (0, sides[i], 0))

    def za_first(i):
        return remote(OZ.at[i, 0:6], ZR0.at[1 - i, 0:6], z_send.at[i], z_first_recv.at[0], (sides[i], 0, 0))

    def zy_first(i, j):
        return remote(
            OZ.at[i, 6 + j], ZR0.at[1 - i, 7 - j], z_send.at[i], z_first_recv.at[2], (sides[i], 0, sides[j]))

    def zb_first(i):
        return remote(OZ.at[i, 8:12], ZR0.at[1 - i, 8:12], z_send.at[i], z_first_recv.at[1], (sides[i], 0, 0))

    def y_first(i):
        return remote(OZ.at[i, 111:120], YR.at[1 - i], z_send.at[i], y_recv.at[0], (0, 0, sides[i]))

    def arrived(ref, sem):
        pltpu.make_async_copy(ref, ref, sem).wait()

    def put(ref, index, pair):
        ref[(MIDDLE, *index)] = jnp.where(lane < SEAM, pair[1], pair[0])
        ref[(LEFT, *index)] = pair[0]
        ref[(RIGHT, *index)] = pair[1]

    def put_margin(ref, index, v):
        ref[(LEFT, *index)] = jnp.where(lane >= 128 - WIDE, v, ref[(LEFT, *index)])
        ref[(RIGHT, *index)] = jnp.where(lane < WIDE, v, ref[(RIGHT, *index)])

    everywhere = slice(None)
    for z in range(8):
        solid = [(dom * 8 + z) >= floor[:, cut(t)] for t in range(2)]
        for f in range(6):
            v = [state[3 + f, z, :, cut(t)] for t in range(2)]
            if f >= 3:
                v = [jnp.where(m, w, 0.0) for m, w in zip(solid, v)]
            elif z == 0:
                v = [w + jnp.where(dom == 0, source[0, :, cut(t)], 0.0) for t, w in enumerate(v)]
            put(S, (f, level(z), everywhere), v)
    x_fields, z_fields = (0, 3, 4), (2, 4, 5)
    pair = (LEFT, RIGHT)
    for i, at_edge in enumerate((0, 7)):
        for k in range(3):
            for t in range(2):
                OX[i, 2 * k + t] = S[pair[t], x_fields[k], column(at_edge), :]
                OZ[i, 2 * k + t] = S[pair[t], z_fields[k], level(at_edge), :]
    for i in range(2):
        for z in range(8):
            OZ[i, 111 + z] = side_by_side(
                [state[f, z, :, cut(i)] for f in range(9)] + [region[z, :, cut(i)].astype(f32)], i)
        OZ[i, 119] = side_by_side([source[s, :, cut(i)] for s in range(STEPS)] + [floor[:, cut(i)].astype(f32)], i)

    pl.semaphore_wait(barrier, 8 + 5 * (there[0].astype(jnp.int32) + there[1].astype(jnp.int32)))
    for i in range(2):
        @functools.partial(reach, i)
        def _(i=i):
            xa_first(i).start()
    for i in range(2):
        za_first(i).start()
        y_first(i).start()

    for load in loads[4:]:
        load.wait()
    scale = 0.5 * COURANT
    tables = [[t[k] * scale for k in range(REGIONS)] for t in (lame, shear, buoy)]

    def materials(number, seafloor, z):
        bits = [(number & (1 << k)) != 0 for k in range(4)]
        solid = (dom * 8 + z) >= seafloor
        lam, mu, b = (pick(bits, t) for t in tables)
        return lam, jnp.where(solid, mu, 0.0), b, solid

    for s in range(STEPS):
        put(SRC, (pl.ds(8 * s, 8), everywhere),
            [jnp.where(dom == 0, source[s, :, cut(t)], 0.0) for t in range(2)])
    for z in range(8):
        made = [materials(region[z, :, cut(t)], floor[:, cut(t)], z) for t in range(2)]
        for k, ref in enumerate((L, M, B)):
            put(ref, (pl.ds(8 * z, 8), everywhere), [m[k] for m in made])
        for f in range(3):
            put(V, (f, level(z), everywhere), [state[f, z, :, cut(t)] for t in range(2)])

    for i, x in ((0, 0), (1, 7)):
        parts = [[OX[i, 2 * k + t] for t in range(2)] for k in range(3)]
        parts += [[m[p, pl.ds(x, 8, stride=8), :] for p in pair] for m in (L, M)]
        parts += [[
            jnp.concatenate([SRC[p, pl.ds(x, STEPS, stride=8), :], jnp.zeros((8 - STEPS, 128), f32)], 0) for p in pair]]
        for k in range(3, 6):
            for t in range(2):
                OX[i, 2 * k + t + 2] = parts[k][t]
        for j in range(2):
            OX[i, 6 + j] = side_by_side([v[j] for v in parts], j)

        @functools.partial(reach, i)
        def _(i=i):
            for j in range(2):
                xy_first(i, j).start()
            xb_first(i).start()
    for i, z in ((0, 0), (1, 7)):
        parts = [[OZ[i, 2 * k + t] for t in range(2)] for k in range(3)]
        parts += [[m[p, pl.ds(8 * z, 8), :] for p in pair] for m in (L, M)]
        for k in range(3, 5):
            for t in range(2):
                OZ[i, 2 * k + t + 2] = parts[k][t]
        for j in range(2):
            OZ[i, 6 + j] = side_by_side([v[j] for v in parts], j)
            zy_first(i, j).start()
        zb_first(i).start()

    left = (lane >= 128 - WIDE) & (gy > 0)
    right = (lane < WIDE) & (gy < n_gy - 1)
    inside = left | right

    def margin(low, high, f):
        shift_r = (128 - WIDE * f) % 128
        shift_l = (256 - WIDE - WIDE * f) % 128
        a = pltpu.roll(high, shift_r, 1) if shift_r else high
        c = pltpu.roll(low, shift_l, 1) if shift_l else low
        return jnp.where(left, c, jnp.where(right, a, 0.0))

    arrived(ZR0.at[:, 0:6], z_first_recv.at[0])
    for i in range(2):
        @functools.partial(reach, i)
        def _(i=i):
            arrived(XR0.at[i, 0:6], x_first_recv.at[0, i])

    def three(first_tile, second_tile, edge):
        return (
            jnp.where(lane < SEAM, second_tile, first_tile),
            jnp.where(lane >= 128 - WIDE, edge, first_tile),
            jnp.where(lane < WIDE, edge, second_tile),
        )

    def border(parts):
        for i, x in ((0, -1), (1, 8)):
            for k, f in enumerate(x_fields):
                edge = zero if parts == (MIDDLE,) else margin(XR0[i, 6], XR0[i, 7], k)
                tiles = three(XR0[i, 2 * k], XR0[i, 2 * k + 1], edge)
                for p in parts:
                    S[p, f, column(x), :] = tiles[p]
        for i, z in ((0, -1), (1, 8)):
            for k, f in enumerate(z_fields):
                edge = zero if parts == (MIDDLE,) else margin(ZR0[i, 6], ZR0[i, 7], k)
                tiles = three(ZR0[i, 2 * k], ZR0[i, 2 * k + 1], edge)
                for p in parts:
                    S[p, f, level(z), :] = jnp.where(z_there[i], tiles[p], 0.0)

    border((MIDDLE,))
    def x_base(p, s, last):
        return 14 + 18 * s + (3 * p if last else 6 * p)

    def z_base(p, s, last):
        return 12 + 18 * s + (3 * p if last else 6 * p)

    def x_copy(p, i, s, slot, last):
        n = 3 if last else 6
        return remote(
            OX.at[i, pl.ds(x_base(p, s, last), n)], XR.at[slot, p, 1 - i, 0:n], x_send.at[i], x_recv.at[slot, p, 1 - i],
            (0, sides[i], 0))

    def e_copy(p, i, j, s, slot):
        return remote(
            OE.at[i, 3 * s + p, j], ER.at[slot, p, 1 - i, 1 - j], e_send.at[i],
            e_recv.at[slot, p, 1 - i], (sides[j], sides[i], 0))

    def z_copy(p, i, s, slot, last):
        n = 3 if last else 6
        return remote(
            OZ.at[i, pl.ds(z_base(p, s, last), n)], ZR.at[slot, p, 1 - i, 0:n], z_send.at[i], z_recv.at[slot, p],
            (sides[i], 0, 0))

    def move(p, s, slot, last=False):
        def accelerate(levels):
            moved = []
            for z in levels:
                own = level(z)
                after, before = pl.ds(rows(z, 1), 8), pl.ds(rows(z, -1), 8)
                above, below = level(z + 1), level(z - 1)

                def dx(f):
                    return S[p, f, after, :] - S[p, f, before, :]

                def dz(f):
                    return S[p, f, above, :] - S[p, f, below, :]

                b = B[p, pl.ds(8 * z, 8), :]
                moved.append((0, own, V[p, 0, own, :] - b * (dx(0) + dy(S[p, 3, own, :]) + dz(4))))
                moved.append((1, own, V[p, 1, own, :] - b * (dx(3) + dy(S[p, 1, own, :]) + dz(5))))
                moved.append((2, own, V[p, 2, own, :] - b * (dx(4) + dy(S[p, 5, own, :]) + dz(2))))
            for f, own, v in moved:
                V[p, f, own, :] = v

        accelerate((0, 7))
        if not last:
            for i, x in ((0, 0), (1, 7)):
                for j in range(2):
                    for k, f in enumerate((0, 2)):
                        OE[i, 3 * s + p, j, k : k + 1, :] = V[p, f, pl.ds(rows(7 * j, x), 1), :]

                @functools.partial(reach, i)
                def _(i=i):
                    for j in range(2):
                        e_copy(p, i, j, s, slot).start()
        accelerate((1, 2, 3))
        accelerate((4, 5, 6))
        base = x_base(p, s, last)
        for i, (x, inner) in enumerate(((0, 1), (7, 6))):
            for k, v in enumerate([V[p, f, column(c), :] for c in ((x,) if last else (x, inner)) for f in range(3)]):
                OX[i, base + k] = v

            @functools.partial(reach, i)
            def _(i=i):
                x_copy(p, i, s, slot, last).start()
        base = z_base(p, s, last)
        for i, (z, inner) in enumerate(((0, 1), (7, 6))):
            for f in range(3):
                OZ[i, base + f] = V[p, f, level(z), :]
                if not last:
                    OZ[i, base + 3 + f] = V[p, f, level(inner), :]
            z_copy(p, i, s, slot, last).start()

        later = []
        for z in range(8):
            own = level(z)
            after, before = pl.ds(rows(z, 1), 8), pl.ds(rows(z, -1), 8)
            above, below = level(z + 1), level(z - 1)
            dxs = [V[p, f, after, :] - V[p, f, before, :] for f in range(3)]
            dzs = [V[p, f, above, :] - V[p, f, below, :] for f in range(3)]
            dys = [dy(V[p, f, own, :]) for f in range(3)]
            lam, mu = L[p, pl.ds(8 * z, 8), :], M[p, pl.ds(8 * z, 8), :]
            spread = lam * (dxs[0] + dys[1] + dzs[2])
            mu2 = mu + mu
            change = (
                spread + mu2 * dxs[0], spread + mu2 * dys[1], spread + mu2 * dzs[2],
                mu * (dys[0] + dxs[1]), mu * (dzs[0] + dxs[2]), mu * (dzs[1] + dys[2]))
            later += [(f, own, S[p, f, own, :] - change[f]) for f in range(6)]
            if z % 2:
                write(p, later)
                later = []

    def write(p, results):
        for f, at_rows, v in results:
            S[p, f, at_rows, :] = v

    def finish(p, slot, then=None):
        last = then is None
        if not last:
            added = SRC[p, pl.ds(8 * then if isinstance(then, int) else pl.multiple_of(8 * then, 8), 8), :]
            results = [(f, level(0), S[p, f, level(0), :] + added) for f in range(3)]
            for i, x in ((0, -1), (1, 8)):
                outer = pl.ds(rows(0, x), 1)
                results.append((0, outer, S[p, 0, outer, :] + SX[i, p, pl.ds(then, 1), :]))
            write(p, results)
        arrived(ZR.at[slot, p, :, 0:3] if last else ZR.at[slot, p], z_recv.at[slot, p])
        results = []
        for i, z in ((0, 0), (1, 7)):
            near = [ZR[slot, p, i, f] for f in range(3)]
            own = level(z)
            lam, mu = L[p, pl.ds(8 * z, 8), :], M[p, pl.ds(8 * z, 8), :]
            sign = jnp.where(z_there[i], (-1.0, 1.0)[i], 0.0)
            slope = [sign * v for v in near]
            spread = lam * slope[2]
            results.append((0, own, S[p, 0, own, :] - (spread)))
            results.append((1, own, S[p, 1, own, :] - (spread)))
            results.append((2, own, S[p, 2, own, :] - (spread + (mu + mu) * slope[2])))
            results.append((4, own, S[p, 4, own, :] - (mu * slope[0])))
            results.append((5, own, S[p, 5, own, :] - (mu * slope[1])))
        write(p, results)

        for i in range(2):
            @functools.partial(reach, i)
            def _(i=i):
                arrived(XR.at[slot, p, i, 0:3] if last else XR.at[slot, p, i], x_recv.at[slot, p, i])

        results = []
        for i, x, sign in ((0, 0, -1.0), (1, 7, 1.0)):
            near = [XR[slot, p, i, f] for f in range(3)]
            lam, mu = L[p, pl.ds(x, 8, stride=8), :], M[p, pl.ds(x, 8, stride=8), :]
            slope = [sign * v for v in near]
            spread = lam * slope[0]
            results.append((0, column(x), S[p, 0, column(x), :] - (spread + (mu + mu) * slope[0])))
            results.append((1, column(x), S[p, 1, column(x), :] - (spread)))
            results.append((2, column(x), S[p, 2, column(x), :] - (spread)))
            results.append((3, column(x), S[p, 3, column(x), :] - (mu * slope[1])))
            results.append((4, column(x), S[p, 4, column(x), :] - (mu * slope[2])))

        if last:
            write(p, results)
            return
        for i, x, sign in ((0, 0, -1.0), (1, 7, 1.0)):
            near, far = [XR[slot, p, i, f] for f in range(3)], [XR[slot, p, i, 3 + f] for f in range(3)]
            lam, mu = LX[i, p], MX[i, p]
            dxs = [sign * (far[f] - V[p, f, column(x), :]) for f in range(3)]
            dzs = {}
            for f in (0, 2):
                up, down = pltpu.roll(near[f], 7, 0), pltpu.roll(near[f], 1, 0)
                dzs[f] = jnp.where(sub == 7, 0.0, up) - jnp.where(sub == 0, 0.0, down)
            trace = dxs[0] + dy(near[1]) + dzs[2]
            beyond = column((-1, 8)[i])
            results.append((0, beyond, S[p, 0, beyond, :] - (lam * trace + (mu + mu) * dxs[0])))
            results.append((3, beyond, S[p, 3, beyond, :] - (mu * (dy(near[0]) + dxs[1]))))
            results.append((4, beyond, S[p, 4, beyond, :] - (mu * (dzs[0] + dxs[2]))))
        for i, z, sign in ((0, 0, -1.0), (1, 7, 1.0)):
            near, far = [ZR[slot, p, i, f] for f in range(3)], [ZR[slot, p, i, 3 + f] for f in range(3)]
            lam, mu = LZ[i, p], MZ[i, p]
            dzs = [sign * (far[f] - V[p, f, level(z), :]) for f in range(3)]
            dxs = {}
            for f in (0, 2):
                ahead, behind = pltpu.roll(near[f], 7, 0), pltpu.roll(near[f], 1, 0)
                dxs[f] = jnp.where(sub == 7, 0.0, ahead) - jnp.where(sub == 0, 0.0, behind)
            trace = dxs[0] + dy(near[1]) + dzs[2]
            beyond = level((-1, 8)[i])
            results.append((2, beyond, S[p, 2, beyond, :] - (lam * trace + (mu + mu) * dzs[2])))
            results.append((4, beyond, S[p, 4, beyond, :] - (mu * (dzs[0] + dxs[2]))))
            results.append((5, beyond, S[p, 5, beyond, :] - (mu * (dzs[1] + dy(near[2])))))

        write(p, results)

        for i in range(2):
            @functools.partial(reach, i)
            def _(i=i):
                arrived(ER.at[slot, p, i], e_recv.at[slot, p, i])
        results = []
        for i, x in ((0, 0), (1, 7)):
            for j, z in ((0, 0), (1, 7)):
                edge_x, edge_z = (ER[slot, p, i, j, k : k + 1, :] for k in range(2))
                sign = jnp.where(z_there[j], (-1.0, 1.0)[j], 0.0)
                outer = pl.ds(rows(z, (-1, 8)[i]), 1)
                at_z, at_x = slice(z, z + 1), slice(x, x + 1)
                results.append((0, outer, S[p, 0, outer, :] - (LX[i, p, at_z, :] * (sign * edge_z))))
                results.append((4, outer, S[p, 4, outer, :] - (MX[i, p, at_z, :] * (sign * edge_x))))
                outer = pl.ds(rows((-1, 8)[j], x), 1)
                results.append((2, outer, S[p, 2, outer, :] - (LZ[j, p, at_x, :] * (sides[i] * edge_x))))
                results.append((4, outer, S[p, 4, outer, :] - (MZ[j, p, at_x, :] * (sides[i] * edge_z))))
        write(p, results)

    def each_part(then):
        for p in range(3):
            then(p)

    move(MIDDLE, 0, 0)

    arrived(YR, y_recv.at[0])
    low, high = YR[0, 8], YR[1, 8]
    seafloor = margin(low, high, STEPS).astype(jnp.int32)
    first_source = None
    for s in range(STEPS):
        v = jnp.where(dom == 0, margin(low, high, s), 0.0)
        first_source = v if s == 0 else first_source
        put_margin(SRC, (pl.ds(8 * s, 8), everywhere), v)
    for z in range(8):
        low, high = YR[0, z], YR[1, z]
        lam, mu, b, solid = materials(margin(low, high, 9).astype(jnp.int32), seafloor, z)
        for ref, v in ((L, lam), (M, mu), (B, b)):
            put_margin(ref, (pl.ds(8 * z, 8), everywhere), jnp.where(inside, v, 0.0))
        for f in range(9):
            v = margin(low, high, f)
            if f < 3:
                put_margin(V, (f, level(z), everywhere), v)
            else:
                if f >= 6:
                    v = jnp.where(solid, v, 0.0)
                elif z == 0:
                    v = v + first_source
                put_margin(S, (f - 3, level(z), everywhere), v)

    arrived(ZR0.at[:, 6:8], z_first_recv.at[2])
    for i in range(2):
        @functools.partial(reach, i)
        def _(i=i):
            arrived(XR0.at[i, 6:8], x_first_recv.at[2, i])
    border((LEFT, RIGHT))

    move(LEFT, 0, 0)
    move(RIGHT, 0, 0)

    arrived(ZR0.at[:, 8:12], z_first_recv.at[1])
    for i in range(2):
        @functools.partial(reach, i)
        def _(i=i):
            arrived(XR0.at[i, 8:14], x_first_recv.at[1, i])
    for i in range(2):
        for k, ref in enumerate((LX, MX, SX)):
            tiles = three(XR0[i, 8 + 2 * k], XR0[i, 9 + 2 * k], margin(XR0[i, 6], XR0[i, 7], 3 + k))
            for p in range(3):
                ref[i, p] = tiles[p]
        for k, ref in enumerate((LZ, MZ)):
            tiles = three(ZR0[i, 8 + 2 * k], ZR0[i, 9 + 2 * k], margin(ZR0[i, 6], ZR0[i, 7], 3 + k))
            for p in range(3):
                ref[i, p] = jnp.where(z_there[i], tiles[p], 0.0)

    def step(s, carry):
        slot = lax.rem(s, 2)

        def turn(p):
            finish(p, 1 - slot, s)
            move(p, s, slot)

        each_part(turn)
        return carry

    lax.fori_loop(1, STEPS - 1, step, 0)

    end = STEPS - 1

    def final(p):
        finish(p, (end - 1) % 2, end)
        move(p, end, end % 2, last=True)

    each_part(final)

    def gather(f, ref, k):
        for z in range(8):
            middle, first_tile, second_tile = (ref[p, k, level(z), :] for p in (MIDDLE, LEFT, RIGHT))
            out[f, z, :, cut(0)] = jnp.where(lane < FIRST_CUT, first_tile, middle)
            out[f, z, :, cut(1)] = jnp.where(lane < SECOND_CUT, middle, second_tile)

    for f in range(3):
        gather(f, V, f)
    each_part(lambda p: finish(p, end % 2))
    for f in range(6):
        gather(3 + f, S, f)

    for i in range(2):
        arrived(OZ.at[i], z_send.at[i])

        @functools.partial(reach, i)
        def _(i=i):
            arrived(OX.at[i], x_send.at[i])
            arrived(OE.at[i], e_send.at[i])


def solution(mesh):
    sizes = (mesh.shape["dom"], mesh.shape["gx"], mesh.shape["gy"])

    def on_device(state, source, floor, region, lame, shear, buoy):
        hbm = pl.BlockSpec(memory_space=pltpu.HBM)

        def tiles(*shape):
            return pltpu.VMEM(shape + (8, 128), f32)

        return pl.pallas_call(
            functools.partial(kernel, sizes),
            out_shape=jax.ShapeDtypeStruct(state.shape, f32),
            in_specs=[hbm] * 7,
            out_specs=pl.BlockSpec(memory_space=pltpu.VMEM),
            scratch_shapes=[
                pltpu.VMEM(state.shape, f32),
                pltpu.VMEM(source.shape, f32),
                pltpu.VMEM(floor.shape, jnp.int32),
                pltpu.VMEM(region.shape, jnp.int32),
                pltpu.SMEM(lame.shape, f32),
                pltpu.SMEM(shear.shape, f32),
                pltpu.SMEM(buoy.shape, f32),
                pltpu.VMEM((3, 6, 10 * BLOCK, 128), f32),
                pltpu.VMEM((3, 3, 10 * BLOCK, 128), f32),
                pltpu.VMEM((3, 64, 128), f32),
                pltpu.VMEM((3, 64, 128), f32),
                pltpu.VMEM((3, 64, 128), f32),
                pltpu.VMEM((3, 8 * STEPS, 128), f32),
                tiles(2, 3),
                tiles(2, 3),
                tiles(2, 3),
                tiles(2, 3),
                tiles(2, 3),
                tiles(2, 113),
                tiles(2, 120),
                pltpu.VMEM((2, 3 * STEPS - 3, 2, 2, 128), f32),
                tiles(2, 14),
                tiles(2, 12),
                tiles(2, 9),
                tiles(2, 3, 2, 6),
                tiles(2, 3, 2, 6),
                pltpu.VMEM((2, 3, 2, 2, 2, 128), f32),
                pltpu.SemaphoreType.DMA((7,)),
                pltpu.SemaphoreType.DMA((2,)),
                pltpu.SemaphoreType.DMA((2,)),
                pltpu.SemaphoreType.DMA((2,)),
                pltpu.SemaphoreType.DMA((3, 2)),
                pltpu.SemaphoreType.DMA((3,)),
                pltpu.SemaphoreType.DMA((1,)),
                pltpu.SemaphoreType.DMA((2, 3, 2)),
                pltpu.SemaphoreType.DMA((2, 3)),
                pltpu.SemaphoreType.DMA((2, 3, 2)),
            ],
            compiler_params=pltpu.CompilerParams(
                collective_id=0, has_side_effects=True, vmem_limit_bytes=32 * 1024 * 1024
            ),
        )(*(
            pltpu.with_memory_space_constraint(v, pltpu.HBM)
            for v in (state, source, floor, region, lame, shear, buoy)
        ))

    return jax.shard_map(
        on_device,
        mesh=mesh,
        in_specs=(
            P(None, "dom", "gx", "gy"),
            P(None, "gx", "gy"),
            P("gx", "gy"),
            P("dom", "gx", "gy"),
            P(),
            P(),
            P(),
        ),
        out_specs=P(None, "dom", "gx", "gy"),
        check_vma=False,
    )
```

```python
import functools

import jax
import jax.numpy as jnp
from jax import lax
from jax.experimental import pallas as pl
from jax.experimental.pallas import tpu as pltpu
from jax.sharding import PartitionSpec as P

STEPS = 6
COURANT = 0.25
REGIONS = 16
BLOCK = 16
WIDE = 12
MIDDLE, LEFT, RIGHT = 0, 1, 2
FIRST_CUT, SECOND_CUT, SEAM = 86, 171 - 128, 64
MESH = pl.DeviceIdType.MESH

f32 = jnp.float32


def rows(z, x=0):
    return (z + 1) * BLOCK + 8 + x


def level(z):
    return pl.ds(rows(z), 8)


def column(x):
    return pl.ds(rows(0, x), 8, stride=BLOCK)


def dy(v):
    return pltpu.roll(v, 127, 1) - pltpu.roll(v, 1, 1)


def pick(bits, table):
    values = list(table)
    for bit in bits:
        values = [jnp.where(bit, values[2 * i + 1], values[2 * i]) for i in range(len(values) // 2)]
    return values[0]


def kernel(
    sizes, state_in, source_in, floor_in, region_in, lame_in, shear_in, buoy_in, out,
    state, source, floor, region, lame, shear, buoy,
    S, V, L, M, B, SRC, LX, MX, SX, LZ, MZ, OX, OZ, OE, XR0, ZR0, YR, XR, ZR, ER,
    in_sem, x_send, z_send, e_send, x_first_recv, z_first_recv, y_recv, x_recv, z_recv, e_recv,
):
    n_dom, n_gx, n_gy = sizes
    dom, gx, gy = lax.axis_index("dom"), lax.axis_index("gx"), lax.axis_index("gy")
    lane = lax.broadcasted_iota(jnp.int32, (8, 128), 1)
    sub = lax.broadcasted_iota(jnp.int32, (8, 128), 0)
    zero = jnp.zeros((8, 128), f32)

    loads = [
        pltpu.make_async_copy(src, dst, in_sem.at[i])
        for i, (src, dst) in enumerate((
            (region_in, region), (floor_in, floor), (source_in, source), (state_in, state),
            (lame_in, lame), (shear_in, shear), (buoy_in, buoy)))
    ]
    for load in loads:
        load.start()

    sides = (-1, 1)
    there = [gx > 0, gx < n_gx - 1]
    z_there = [dom > 0, dom < n_dom - 1]

    doms = [dom, jnp.where(dom == n_dom - 1, 0, dom + 1), jnp.where(dom == 0, n_dom - 1, dom - 1)]
    gxs = [gx, gx + 1, gx - 1]
    gys = [gy, jnp.where(gy == n_gy - 1, 0, gy + 1), jnp.where(gy == 0, n_gy - 1, gy - 1)]

    def at(dz, dx, dyy):
        return (doms[dz], gxs[dx], gys[dyy])

    def reach(i, then):
        pl.when(there[i])(then)

    barrier = pltpu.get_barrier_semaphore()

    def greet(*way):
        pl.semaphore_signal(barrier, inc=1, device_id=at(*way), device_id_type=MESH)

    for i, dx in enumerate(sides):
        @functools.partial(reach, i)
        def _(dx=dx):
            for way in ((0, dx, 0), (-1, dx, 0), (1, dx, 0), (0, dx, -1), (0, dx, 1)):
                greet(*way)
    for way in [(a, 0, b) for a in (-1, 0, 1) for b in (-1, 0, 1) if a or b]:
        greet(*way)

    for i in range(2):
        @pl.when(jnp.logical_not(there[i]))
        def _(i=i):
            XR0[i] = jnp.zeros(XR0.shape[1:], f32)
            for slot in range(2):
                for p in range(3):
                    XR[slot, p, i] = jnp.zeros(XR.shape[3:], f32)
                    ER[slot, p, i] = jnp.zeros(ER.shape[3:], f32)

    for p in range(3):
        for f in range(3):
            for z in range(-1, 9):
                V[p, f, pl.ds(rows(z, -8), 8), :] = zero
            for z in (-1, 8):
                V[p, f, level(z), :] = zero

    for load in loads[:4]:
        load.wait()

    def side_by_side(parts, t):
        tile = zero
        for k, v in enumerate(parts):
            shift = (WIDE * k + (WIDE if t else 0)) % 128
            v = pltpu.roll(v, shift, 1) if shift else v
            tile = jnp.where((lane >= WIDE * k) & (lane < WIDE * (k + 1)), v, tile)
        return tile

    def cut(t):
        return slice(128 * t, 128 * t + 128)

    def remote(src, dst, send, recv, way):
        return pltpu.make_async_remote_copy(
            src_ref=src, dst_ref=dst, send_sem=send, recv_sem=recv, device_id=at(*way), device_id_type=MESH)

    def xa_first(i):
        return remote(OX.at[i, 0:6], XR0.at[1 - i, 0:6], x_send.at[i], x_first_recv.at[0, 1 - i], (0, sides[i], 0))

    def xy_first(i, j):
        return remote(
            OX.at[i, 6 + j], XR0.at[1 - i, 7 - j], x_send.at[i], x_first_recv.at[2, 1 - i], (0, sides[i], sides[j]))

    def xb_first(i):
        return remote(OX.at[i, 8:14], XR0.at[1 - i, 8:14], x_send.at[i], x_first_recv.at[1, 1 - i], (0, sides[i], 0))

    def za_first(i):
        return remote(OZ.at[i, 0:6], ZR0.at[1 - i, 0:6], z_send.at[i], z_first_recv.at[0], (sides[i], 0, 0))

    def zy_first(i, j):
        return remote(
            OZ.at[i, 6 + j], ZR0.at[1 - i, 7 - j], z_send.at[i], z_first_recv.at[2], (sides[i], 0, sides[j]))

    def zb_first(i):
        return remote(OZ.at[i, 8:12], ZR0.at[1 - i, 8:12], z_send.at[i], z_first_recv.at[1], (sides[i], 0, 0))

    def y_first(i):
        return remote(OZ.at[i, 111:120], YR.at[1 - i], z_send.at[i], y_recv.at[0], (0, 0, sides[i]))

    def arrived(ref, sem):
        pltpu.make_async_copy(ref, ref, sem).wait()

    def put(ref, index, pair):
        ref[(MIDDLE, *index)] = jnp.where(lane < SEAM, pair[1], pair[0])
        ref[(LEFT, *index)] = pair[0]
        ref[(RIGHT, *index)] = pair[1]

    def put_margin(ref, index, v):
        ref[(LEFT, *index)] = jnp.where(lane >= 128 - WIDE, v, ref[(LEFT, *index)])
        ref[(RIGHT, *index)] = jnp.where(lane < WIDE, v, ref[(RIGHT, *index)])

    everywhere = slice(None)
    for z in range(8):
        solid = [(dom * 8 + z) >= floor[:, cut(t)] for t in range(2)]
        for f in range(6):
            v = [state[3 + f, z, :, cut(t)] for t in range(2)]
            if f >= 3:
                v = [jnp.where(m, w, 0.0) for m, w in zip(solid, v)]
            elif z == 0:
                v = [w + jnp.where(dom == 0, source[0, :, cut(t)], 0.0) for t, w in enumerate(v)]
            put(S, (f, level(z), everywhere), v)
    x_fields, z_fields = (0, 3, 4), (2, 4, 5)
    pair = (LEFT, RIGHT)
    for i, at_edge in enumerate((0, 7)):
        for k in range(3):
            for t in range(2):
                OX[i, 2 * k + t] = S[pair[t], x_fields[k], column(at_edge), :]
                OZ[i, 2 * k + t] = S[pair[t], z_fields[k], level(at_edge), :]
    for i in range(2):
        for z in range(8):
            OZ[i, 111 + z] = side_by_side(
                [state[f, z, :, cut(i)] for f in range(9)] + [region[z, :, cut(i)].astype(f32)], i)
        OZ[i, 119] = side_by_side([source[s, :, cut(i)] for s in range(STEPS)] + [floor[:, cut(i)].astype(f32)], i)

    pl.semaphore_wait(barrier, 8 + 5 * (there[0].astype(jnp.int32) + there[1].astype(jnp.int32)))
    for i in range(2):
        @functools.partial(reach, i)
        def _(i=i):
            xa_first(i).start()
    for i in range(2):
        za_first(i).start()
        y_first(i).start()

    for load in loads[4:]:
        load.wait()
    scale = 0.5 * COURANT
    tables = [[t[k] * scale for k in range(REGIONS)] for t in (lame, shear, buoy)]

    def materials(number, seafloor, z):
        bits = [(number & (1 << k)) != 0 for k in range(4)]
        solid = (dom * 8 + z) >= seafloor
        lam, mu, b = (pick(bits, t) for t in tables)
        return lam, jnp.where(solid, mu, 0.0), b, solid

    for s in range(STEPS):
        put(SRC, (pl.ds(8 * s, 8), everywhere),
            [jnp.where(dom == 0, source[s, :, cut(t)], 0.0) for t in range(2)])
    for z in range(8):
        made = [materials(region[z, :, cut(t)], floor[:, cut(t)], z) for t in range(2)]
        for k, ref in enumerate((L, M, B)):
            put(ref, (pl.ds(8 * z, 8), everywhere), [m[k] for m in made])
        for f in range(3):
            put(V, (f, level(z), everywhere), [state[f, z, :, cut(t)] for t in range(2)])

    for i, x in ((0, 0), (1, 7)):
        parts = [[OX[i, 2 * k + t] for t in range(2)] for k in range(3)]
        parts += [[m[p, pl.ds(x, 8, stride=8), :] for p in pair] for m in (L, M)]
        parts += [[
            jnp.concatenate([SRC[p, pl.ds(x, STEPS, stride=8), :], jnp.zeros((8 - STEPS, 128), f32)], 0) for p in pair]]
        for k in range(3, 6):
            for t in range(2):
                OX[i, 2 * k + t + 2] = parts[k][t]
        for j in range(2):
            OX[i, 6 + j] = side_by_side([v[j] for v in parts], j)

        @functools.partial(reach, i)
        def _(i=i):
            for j in range(2):
                xy_first(i, j).start()
            xb_first(i).start()
    for i, z in ((0, 0), (1, 7)):
        parts = [[OZ[i, 2 * k + t] for t in range(2)] for k in range(3)]
        parts += [[m[p, pl.ds(8 * z, 8), :] for p in pair] for m in (L, M)]
        for k in range(3, 5):
            for t in range(2):
                OZ[i, 2 * k + t + 2] = parts[k][t]
        for j in range(2):
            OZ[i, 6 + j] = side_by_side([v[j] for v in parts], j)
            zy_first(i, j).start()
        zb_first(i).start()

    left = (lane >= 128 - WIDE) & (gy > 0)
    right = (lane < WIDE) & (gy < n_gy - 1)
    inside = left | right

    def margin(low, high, f):
        shift_r = (128 - WIDE * f) % 128
        shift_l = (256 - WIDE - WIDE * f) % 128
        a = pltpu.roll(high, shift_r, 1) if shift_r else high
        c = pltpu.roll(low, shift_l, 1) if shift_l else low
        return jnp.where(left, c, jnp.where(right, a, 0.0))

    arrived(ZR0.at[:, 0:6], z_first_recv.at[0])
    for i in range(2):
        @functools.partial(reach, i)
        def _(i=i):
            arrived(XR0.at[i, 0:6], x_first_recv.at[0, i])

    def three(first_tile, second_tile, edge):
        return (
            jnp.where(lane < SEAM, second_tile, first_tile),
            jnp.where(lane >= 128 - WIDE, edge, first_tile),
            jnp.where(lane < WIDE, edge, second_tile),
        )

    def border(parts):
        for i, x in ((0, -1), (1, 8)):
            for k, f in enumerate(x_fields):
                edge = zero if parts == (MIDDLE,) else margin(XR0[i, 6], XR0[i, 7], k)
                tiles = three(XR0[i, 2 * k], XR0[i, 2 * k + 1], edge)
                for p in parts:
                    S[p, f, column(x), :] = tiles[p]
        for i, z in ((0, -1), (1, 8)):
            for k, f in enumerate(z_fields):
                edge = zero if parts == (MIDDLE,) else margin(ZR0[i, 6], ZR0[i, 7], k)
                tiles = three(ZR0[i, 2 * k], ZR0[i, 2 * k + 1], edge)
                for p in parts:
                    S[p, f, level(z), :] = jnp.where(z_there[i], tiles[p], 0.0)

    border((MIDDLE,))
    def x_base(p, s, last):
        return 14 + 18 * s + (3 * p if last else 6 * p)

    def z_base(p, s, last):
        return 12 + 18 * s + (3 * p if last else 6 * p)

    def x_copy(p, i, half, s, slot, last):
        return remote(
            OX.at[i, pl.ds(x_base(p, s, last) + 3 * half, 3)], XR.at[slot, p, 1 - i, 3 * half : 3 * half + 3],
            x_send.at[i], x_recv.at[slot, p, 1 - i], (0, sides[i], 0))

    def e_copy(p, i, j, s, slot):
        return remote(
            OE.at[i, 3 * s + p, j], ER.at[slot, p, 1 - i, 1 - j], e_send.at[i],
            e_recv.at[slot, p, 1 - i], (sides[j], sides[i], 0))

    def z_copy(p, i, half, s, slot, last):
        return remote(
            OZ.at[i, pl.ds(z_base(p, s, last) + 3 * half, 3)], ZR.at[slot, p, 1 - i, 3 * half : 3 * half + 3],
            z_send.at[i], z_recv.at[slot, p], (sides[i], 0, 0))

    def move(p, s, slot, last=False):
        def accelerate(levels):
            moved = []
            for z in levels:
                own = level(z)
                after, before = pl.ds(rows(z, 1), 8), pl.ds(rows(z, -1), 8)
                above, below = level(z + 1), level(z - 1)

                def dx(f):
                    return S[p, f, after, :] - S[p, f, before, :]

                def dz(f):
                    return S[p, f, above, :] - S[p, f, below, :]

                b = B[p, pl.ds(8 * z, 8), :]
                moved.append((0, own, V[p, 0, own, :] - b * (dx(0) + dy(S[p, 3, own, :]) + dz(4))))
                moved.append((1, own, V[p, 1, own, :] - b * (dx(3) + dy(S[p, 1, own, :]) + dz(5))))
                moved.append((2, own, V[p, 2, own, :] - b * (dx(4) + dy(S[p, 5, own, :]) + dz(2))))
            for f, own, v in moved:
                V[p, f, own, :] = v

        accelerate((0, 7))
        if not last:
            for i, x in ((0, 0), (1, 7)):
                for j in range(2):
                    for k, f in enumerate((0, 2)):
                        OE[i, 3 * s + p, j, k : k + 1, :] = V[p, f, pl.ds(rows(7 * j, x), 1), :]

                @functools.partial(reach, i)
                def _(i=i):
                    for j in range(2):
                        e_copy(p, i, j, s, slot).start()
        accelerate((1, 2, 3))
        accelerate((4, 5, 6))
        base = x_base(p, s, last)
        for i, (x, inner) in enumerate(((0, 1), (7, 6))):
            for k, v in enumerate([V[p, f, column(c), :] for c in ((x,) if last else (x, inner)) for f in range(3)]):
                OX[i, base + k] = v

            @functools.partial(reach, i)
            def _(i=i):
                for half in (0,) if last else (0, 1):
                    x_copy(p, i, half, s, slot, last).start()
        base = z_base(p, s, last)
        for i, (z, inner) in enumerate(((0, 1), (7, 6))):
            for f in range(3):
                OZ[i, base + f] = V[p, f, level(z), :]
                if not last:
                    OZ[i, base + 3 + f] = V[p, f, level(inner), :]
            for half in (0,) if last else (0, 1):
                z_copy(p, i, half, s, slot, last).start()

        later = []
        for z in range(8):
            own = level(z)
            after, before = pl.ds(rows(z, 1), 8), pl.ds(rows(z, -1), 8)
            above, below = level(z + 1), level(z - 1)
            dxs = [V[p, f, after, :] - V[p, f, before, :] for f in range(3)]
            dzs = [V[p, f, above, :] - V[p, f, below, :] for f in range(3)]
            dys = [dy(V[p, f, own, :]) for f in range(3)]
            lam, mu = L[p, pl.ds(8 * z, 8), :], M[p, pl.ds(8 * z, 8), :]
            spread = lam * (dxs[0] + dys[1] + dzs[2])
            mu2 = mu + mu
            change = (
                spread + mu2 * dxs[0], spread + mu2 * dys[1], spread + mu2 * dzs[2],
                mu * (dys[0] + dxs[1]), mu * (dzs[0] + dxs[2]), mu * (dzs[1] + dys[2]))
            later += [(f, own, S[p, f, own, :] - change[f]) for f in range(6)]
            if z % 2:
                write(p, later)
                later = []

    def write(p, results):
        for f, at_rows, v in results:
            S[p, f, at_rows, :] = v

    def finish(p, slot, then=None):
        last = then is None
        if not last:
            added = SRC[p, pl.ds(8 * then if isinstance(then, int) else pl.multiple_of(8 * then, 8), 8), :]
            results = [(f, level(0), S[p, f, level(0), :] + added) for f in range(3)]
            for i, x in ((0, -1), (1, 8)):
                outer = pl.ds(rows(0, x), 1)
                results.append((0, outer, S[p, 0, outer, :] + SX[i, p, pl.ds(then, 1), :]))
            write(p, results)
        arrived(ZR.at[slot, p, :, 0:3] if last else ZR.at[slot, p], z_recv.at[slot, p])
        results = []
        for i, z in ((0, 0), (1, 7)):
            near = [ZR[slot, p, i, f] for f in range(3)]
            own = level(z)
            lam, mu = L[p, pl.ds(8 * z, 8), :], M[p, pl.ds(8 * z, 8), :]
            sign = jnp.where(z_there[i], (-1.0, 1.0)[i], 0.0)
            slope = [sign * v for v in near]
            spread = lam * slope[2]
            results.append((0, own, S[p, 0, own, :] - (spread)))
            results.append((1, own, S[p, 1, own, :] - (spread)))
            results.append((2, own, S[p, 2, own, :] - (spread + (mu + mu) * slope[2])))
            results.append((4, own, S[p, 4, own, :] - (mu * slope[0])))
            results.append((5, own, S[p, 5, own, :] - (mu * slope[1])))
        write(p, results)

        for i in range(2):
            @functools.partial(reach, i)
            def _(i=i):
                arrived(XR.at[slot, p, i, 0:3] if last else XR.at[slot, p, i], x_recv.at[slot, p, i])

        results = []
        for i, x, sign in ((0, 0, -1.0), (1, 7, 1.0)):
            near = [XR[slot, p, i, f] for f in range(3)]
            lam, mu = L[p, pl.ds(x, 8, stride=8), :], M[p, pl.ds(x, 8, stride=8), :]
            slope = [sign * v for v in near]
            spread = lam * slope[0]
            results.append((0, column(x), S[p, 0, column(x), :] - (spread + (mu + mu) * slope[0])))
            results.append((1, column(x), S[p, 1, column(x), :] - (spread)))
            results.append((2, column(x), S[p, 2, column(x), :] - (spread)))
            results.append((3, column(x), S[p, 3, column(x), :] - (mu * slope[1])))
            results.append((4, column(x), S[p, 4, column(x), :] - (mu * slope[2])))

        if last:
            write(p, results)
            return
        for i, x, sign in ((0, 0, -1.0), (1, 7, 1.0)):
            near, far = [XR[slot, p, i, f] for f in range(3)], [XR[slot, p, i, 3 + f] for f in range(3)]
            lam, mu = LX[i, p], MX[i, p]
            dxs = [sign * (far[f] - V[p, f, column(x), :]) for f in range(3)]
            dzs = {}
            for f in (0, 2):
                up, down = pltpu.roll(near[f], 7, 0), pltpu.roll(near[f], 1, 0)
                dzs[f] = jnp.where(sub == 7, 0.0, up) - jnp.where(sub == 0, 0.0, down)
            trace = dxs[0] + dy(near[1]) + dzs[2]
            beyond = column((-1, 8)[i])
            results.append((0, beyond, S[p, 0, beyond, :] - (lam * trace + (mu + mu) * dxs[0])))
            results.append((3, beyond, S[p, 3, beyond, :] - (mu * (dy(near[0]) + dxs[1]))))
            results.append((4, beyond, S[p, 4, beyond, :] - (mu * (dzs[0] + dxs[2]))))
        for i, z, sign in ((0, 0, -1.0), (1, 7, 1.0)):
            near, far = [ZR[slot, p, i, f] for f in range(3)], [ZR[slot, p, i, 3 + f] for f in range(3)]
            lam, mu = LZ[i, p], MZ[i, p]
            dzs = [sign * (far[f] - V[p, f, level(z), :]) for f in range(3)]
            dxs = {}
            for f in (0, 2):
                ahead, behind = pltpu.roll(near[f], 7, 0), pltpu.roll(near[f], 1, 0)
                dxs[f] = jnp.where(sub == 7, 0.0, ahead) - jnp.where(sub == 0, 0.0, behind)
            trace = dxs[0] + dy(near[1]) + dzs[2]
            beyond = level((-1, 8)[i])
            results.append((2, beyond, S[p, 2, beyond, :] - (lam * trace + (mu + mu) * dzs[2])))
            results.append((4, beyond, S[p, 4, beyond, :] - (mu * (dzs[0] + dxs[2]))))
            results.append((5, beyond, S[p, 5, beyond, :] - (mu * (dzs[1] + dy(near[2])))))

        write(p, results)

        for i in range(2):
            @functools.partial(reach, i)
            def _(i=i):
                arrived(ER.at[slot, p, i], e_recv.at[slot, p, i])
        results = []
        for i, x in ((0, 0), (1, 7)):
            for j, z in ((0, 0), (1, 7)):
                edge_x, edge_z = (ER[slot, p, i, j, k : k + 1, :] for k in range(2))
                sign = jnp.where(z_there[j], (-1.0, 1.0)[j], 0.0)
                outer = pl.ds(rows(z, (-1, 8)[i]), 1)
                at_z, at_x = slice(z, z + 1), slice(x, x + 1)
                results.append((0, outer, S[p, 0, outer, :] - (LX[i, p, at_z, :] * (sign * edge_z))))
                results.append((4, outer, S[p, 4, outer, :] - (MX[i, p, at_z, :] * (sign * edge_x))))
                outer = pl.ds(rows((-1, 8)[j], x), 1)
                results.append((2, outer, S[p, 2, outer, :] - (LZ[j, p, at_x, :] * (sides[i] * edge_x))))
                results.append((4, outer, S[p, 4, outer, :] - (MZ[j, p, at_x, :] * (sides[i] * edge_z))))
        write(p, results)

    def each_part(then):
        for p in range(3):
            then(p)

    move(MIDDLE, 0, 0)

    arrived(YR, y_recv.at[0])
    low, high = YR[0, 8], YR[1, 8]
    seafloor = margin(low, high, STEPS).astype(jnp.int32)
    first_source = None
    for s in range(STEPS):
        v = jnp.where(dom == 0, margin(low, high, s), 0.0)
        first_source = v if s == 0 else first_source
        put_margin(SRC, (pl.ds(8 * s, 8), everywhere), v)
    for z in range(8):
        low, high = YR[0, z], YR[1, z]
        lam, mu, b, solid = materials(margin(low, high, 9).astype(jnp.int32), seafloor, z)
        for ref, v in ((L, lam), (M, mu), (B, b)):
            put_margin(ref, (pl.ds(8 * z, 8), everywhere), jnp.where(inside, v, 0.0))
        for f in range(9):
            v = margin(low, high, f)
            if f < 3:
                put_margin(V, (f, level(z), everywhere), v)
            else:
                if f >= 6:
                    v = jnp.where(solid, v, 0.0)
                elif z == 0:
                    v = v + first_source
                put_margin(S, (f - 3, level(z), everywhere), v)

    arrived(ZR0.at[:, 6:8], z_first_recv.at[2])
    for i in range(2):
        @functools.partial(reach, i)
        def _(i=i):
            arrived(XR0.at[i, 6:8], x_first_recv.at[2, i])
    border((LEFT, RIGHT))

    move(LEFT, 0, 0)
    move(RIGHT, 0, 0)

    arrived(ZR0.at[:, 8:12], z_first_recv.at[1])
    for i in range(2):
        @functools.partial(reach, i)
        def _(i=i):
            arrived(XR0.at[i, 8:14], x_first_recv.at[1, i])
    for i in range(2):
        for k, ref in enumerate((LX, MX, SX)):
            tiles = three(XR0[i, 8 + 2 * k], XR0[i, 9 + 2 * k], margin(XR0[i, 6], XR0[i, 7], 3 + k))
            for p in range(3):
                ref[i, p] = tiles[p]
        for k, ref in enumerate((LZ, MZ)):
            tiles = three(ZR0[i, 8 + 2 * k], ZR0[i, 9 + 2 * k], margin(ZR0[i, 6], ZR0[i, 7], 3 + k))
            for p in range(3):
                ref[i, p] = jnp.where(z_there[i], tiles[p], 0.0)

    def step(s, carry):
        slot = lax.rem(s, 2)

        def turn(p):
            finish(p, 1 - slot, s)
            move(p, s, slot)

        each_part(turn)
        return carry

    lax.fori_loop(1, STEPS - 1, step, 0)

    end = STEPS - 1

    def final(p):
        finish(p, (end - 1) % 2, end)
        move(p, end, end % 2, last=True)

    each_part(final)

    def gather(f, ref, k):
        for z in range(8):
            middle, first_tile, second_tile = (ref[p, k, level(z), :] for p in (MIDDLE, LEFT, RIGHT))
            out[f, z, :, cut(0)] = jnp.where(lane < FIRST_CUT, first_tile, middle)
            out[f, z, :, cut(1)] = jnp.where(lane < SECOND_CUT, middle, second_tile)

    for f in range(3):
        gather(f, V, f)
    each_part(lambda p: finish(p, end % 2))
    for f in range(6):
        gather(3 + f, S, f)

    for i in range(2):
        arrived(OZ.at[i], z_send.at[i])

        @functools.partial(reach, i)
        def _(i=i):
            arrived(OX.at[i], x_send.at[i])
            arrived(OE.at[i], e_send.at[i])


def solution(mesh):
    sizes = (mesh.shape["dom"], mesh.shape["gx"], mesh.shape["gy"])

    def on_device(state, source, floor, region, lame, shear, buoy):
        hbm = pl.BlockSpec(memory_space=pltpu.HBM)

        def tiles(*shape):
            return pltpu.VMEM(shape + (8, 128), f32)

        return pl.pallas_call(
            functools.partial(kernel, sizes),
            out_shape=jax.ShapeDtypeStruct(state.shape, f32),
            in_specs=[hbm] * 7,
            out_specs=pl.BlockSpec(memory_space=pltpu.VMEM),
            scratch_shapes=[
                pltpu.VMEM(state.shape, f32),
                pltpu.VMEM(source.shape, f32),
                pltpu.VMEM(floor.shape, jnp.int32),
                pltpu.VMEM(region.shape, jnp.int32),
                pltpu.SMEM(lame.shape, f32),
                pltpu.SMEM(shear.shape, f32),
                pltpu.SMEM(buoy.shape, f32),
                pltpu.VMEM((3, 6, 10 * BLOCK, 128), f32),
                pltpu.VMEM((3, 3, 10 * BLOCK, 128), f32),
                pltpu.VMEM((3, 64, 128), f32),
                pltpu.VMEM((3, 64, 128), f32),
                pltpu.VMEM((3, 64, 128), f32),
                pltpu.VMEM((3, 8 * STEPS, 128), f32),
                tiles(2, 3),
                tiles(2, 3),
                tiles(2, 3),
                tiles(2, 3),
                tiles(2, 3),
                tiles(2, 113),
                tiles(2, 120),
                pltpu.VMEM((2, 3 * STEPS - 3, 2, 2, 128), f32),
                tiles(2, 14),
                tiles(2, 12),
                tiles(2, 9),
                tiles(2, 3, 2, 6),
                tiles(2, 3, 2, 6),
                pltpu.VMEM((2, 3, 2, 2, 2, 128), f32),
                pltpu.SemaphoreType.DMA((7,)),
                pltpu.SemaphoreType.DMA((2,)),
                pltpu.SemaphoreType.DMA((2,)),
                pltpu.SemaphoreType.DMA((2,)),
                pltpu.SemaphoreType.DMA((3, 2)),
                pltpu.SemaphoreType.DMA((3,)),
                pltpu.SemaphoreType.DMA((1,)),
                pltpu.SemaphoreType.DMA((2, 3, 2)),
                pltpu.SemaphoreType.DMA((2, 3)),
                pltpu.SemaphoreType.DMA((2, 3, 2)),
            ],
            compiler_params=pltpu.CompilerParams(
                collective_id=0, has_side_effects=True, vmem_limit_bytes=32 * 1024 * 1024
            ),
        )(*(
            pltpu.with_memory_space_constraint(v, pltpu.HBM)
            for v in (state, source, floor, region, lame, shear, buoy)
        ))

    return jax.shard_map(
        on_device,
        mesh=mesh,
        in_specs=(
            P(None, "dom", "gx", "gy"),
            P(None, "gx", "gy"),
            P("gx", "gy"),
            P("dom", "gx", "gy"),
            P(),
            P(),
            P(),
        ),
        out_specs=P(None, "dom", "gx", "gy"),
        check_vma=False,
    )
```

```python
import functools

import jax
import jax.numpy as jnp
from jax import lax
from jax.experimental import pallas as pl
from jax.experimental.pallas import tpu as pltpu
from jax.sharding import PartitionSpec as P

STEPS = 6
COURANT = 0.25
REGIONS = 16
BLOCK = 16
WIDE = 12
MIDDLE, LEFT, RIGHT = 0, 1, 2
FIRST_CUT, SECOND_CUT, SEAM = 86, 171 - 128, 64
MESH = pl.DeviceIdType.MESH

f32 = jnp.float32


def rows(z, x=0):
    return (z + 1) * BLOCK + 8 + x


def level(z):
    return pl.ds(rows(z), 8)


def column(x):
    return pl.ds(rows(0, x), 8, stride=BLOCK)


def dy(v):
    return pltpu.roll(v, 127, 1) - pltpu.roll(v, 1, 1)


def pick(bits, table):
    values = list(table)
    for bit in bits:
        values = [jnp.where(bit, values[2 * i + 1], values[2 * i]) for i in range(len(values) // 2)]
    return values[0]


def kernel(
    sizes, state_in, source_in, floor_in, region_in, lame_in, shear_in, buoy_in, out,
    state, source, floor, region, lame, shear, buoy,
    S, V, L, M, B, SRC, LX, MX, SX, LZ, MZ, OX, OZ, OE, XR0, ZR0, YR, XR, ZR, ER,
    in_sem, x_send, z_send, e_send, x_first_recv, z_first_recv, y_recv, x_recv, z_recv, e_recv,
):
    n_dom, n_gx, n_gy = sizes
    dom, gx, gy = lax.axis_index("dom"), lax.axis_index("gx"), lax.axis_index("gy")
    lane = lax.broadcasted_iota(jnp.int32, (8, 128), 1)
    sub = lax.broadcasted_iota(jnp.int32, (8, 128), 0)
    zero = jnp.zeros((8, 128), f32)

    loads = [
        pltpu.make_async_copy(src, dst, in_sem.at[i])
        for i, (src, dst) in enumerate((
            (region_in, region), (floor_in, floor), (source_in, source), (state_in, state),
            (lame_in, lame), (shear_in, shear), (buoy_in, buoy)))
    ]
    for load in loads:
        load.start()

    sides = (-1, 1)
    there = [gx > 0, gx < n_gx - 1]
    z_there = [dom > 0, dom < n_dom - 1]

    doms = [dom, jnp.where(dom == n_dom - 1, 0, dom + 1), jnp.where(dom == 0, n_dom - 1, dom - 1)]
    gxs = [gx, gx + 1, gx - 1]
    gys = [gy, jnp.where(gy == n_gy - 1, 0, gy + 1), jnp.where(gy == 0, n_gy - 1, gy - 1)]

    def at(dz, dx, dyy):
        return (doms[dz], gxs[dx], gys[dyy])

    odd = lax.rem(gx, 2) == 1
    long_way = [there[0] & jnp.logical_not(odd), there[1] & odd]
    short_way = [there[0] & odd, there[1] & jnp.logical_not(odd)]

    def launch(then):
        for way in (long_way, short_way):
            for i in range(2):
                @pl.when(way[i])
                def _(i=i):
                    then(i)

    def reach(i, then):
        pl.when(there[i])(then)

    barrier = pltpu.get_barrier_semaphore()

    def greet(*way):
        pl.semaphore_signal(barrier, inc=1, device_id=at(*way), device_id_type=MESH)

    for i, dx in enumerate(sides):
        @functools.partial(reach, i)
        def _(dx=dx):
            for way in ((0, dx, 0), (-1, dx, 0), (1, dx, 0), (0, dx, -1), (0, dx, 1)):
                greet(*way)
    for way in [(a, 0, b) for a in (-1, 0, 1) for b in (-1, 0, 1) if a or b]:
        greet(*way)

    for i in range(2):
        @pl.when(jnp.logical_not(there[i]))
        def _(i=i):
            XR0[i] = jnp.zeros(XR0.shape[1:], f32)
            for slot in range(2):
                for p in range(3):
                    XR[slot, p, i] = jnp.zeros(XR.shape[3:], f32)
                    ER[slot, p, i] = jnp.zeros(ER.shape[3:], f32)

    for p in range(3):
        for f in range(3):
            for z in range(-1, 9):
                V[p, f, pl.ds(rows(z, -8), 8), :] = zero
            for z in (-1, 8):
                V[p, f, level(z), :] = zero

    for load in loads[:4]:
        load.wait()

    def side_by_side(parts, t):
        tile = zero
        for k, v in enumerate(parts):
            shift = (WIDE * k + (WIDE if t else 0)) % 128
            v = pltpu.roll(v, shift, 1) if shift else v
            tile = jnp.where((lane >= WIDE * k) & (lane < WIDE * (k + 1)), v, tile)
        return tile

    def cut(t):
        return slice(128 * t, 128 * t + 128)

    def remote(src, dst, send, recv, way):
        return pltpu.make_async_remote_copy(
            src_ref=src, dst_ref=dst, send_sem=send, recv_sem=recv, device_id=at(*way), device_id_type=MESH)

    def xa_first(i):
        return remote(OX.at[i, 0:6], XR0.at[1 - i, 0:6], x_send.at[i], x_first_recv.at[0, 1 - i], (0, sides[i], 0))

    def xy_first(i, j):
        return remote(
            OX.at[i, 6 + j], XR0.at[1 - i, 7 - j], x_send.at[i], x_first_recv.at[2, 1 - i], (0, sides[i], sides[j]))

    def xb_first(i):
        return remote(OX.at[i, 8:14], XR0.at[1 - i, 8:14], x_send.at[i], x_first_recv.at[1, 1 - i], (0, sides[i], 0))

    def za_first(i):
        return remote(OZ.at[i, 0:6], ZR0.at[1 - i, 0:6], z_send.at[i], z_first_recv.at[0], (sides[i], 0, 0))

    def zy_first(i, j):
        return remote(
            OZ.at[i, 6 + j], ZR0.at[1 - i, 7 - j], z_send.at[i], z_first_recv.at[2], (sides[i], 0, sides[j]))

    def zb_first(i):
        return remote(OZ.at[i, 8:12], ZR0.at[1 - i, 8:12], z_send.at[i], z_first_recv.at[1], (sides[i], 0, 0))

    def y_first(i):
        return remote(OZ.at[i, 111:120], YR.at[1 - i], z_send.at[i], y_recv.at[0], (0, 0, sides[i]))

    def arrived(ref, sem):
        pltpu.make_async_copy(ref, ref, sem).wait()

    def put(ref, index, pair):
        ref[(MIDDLE, *index)] = jnp.where(lane < SEAM, pair[1], pair[0])
        ref[(LEFT, *index)] = pair[0]
        ref[(RIGHT, *index)] = pair[1]

    def put_margin(ref, index, v):
        ref[(LEFT, *index)] = jnp.where(lane >= 128 - WIDE, v, ref[(LEFT, *index)])
        ref[(RIGHT, *index)] = jnp.where(lane < WIDE, v, ref[(RIGHT, *index)])

    everywhere = slice(None)
    for z in range(8):
        solid = [(dom * 8 + z) >= floor[:, cut(t)] for t in range(2)]
        for f in range(6):
            v = [state[3 + f, z, :, cut(t)] for t in range(2)]
            if f >= 3:
                v = [jnp.where(m, w, 0.0) for m, w in zip(solid, v)]
            elif z == 0:
                v = [w + jnp.where(dom == 0, source[0, :, cut(t)], 0.0) for t, w in enumerate(v)]
            put(S, (f, level(z), everywhere), v)
    x_fields, z_fields = (0, 3, 4), (2, 4, 5)
    pair = (LEFT, RIGHT)
    for i, at_edge in enumerate((0, 7)):
        for k in range(3):
            for t in range(2):
                OX[i, 2 * k + t] = S[pair[t], x_fields[k], column(at_edge), :]
                OZ[i, 2 * k + t] = S[pair[t], z_fields[k], level(at_edge), :]
    for i in range(2):
        for z in range(8):
            OZ[i, 111 + z] = side_by_side(
                [state[f, z, :, cut(i)] for f in range(9)] + [region[z, :, cut(i)].astype(f32)], i)
        OZ[i, 119] = side_by_side([source[s, :, cut(i)] for s in range(STEPS)] + [floor[:, cut(i)].astype(f32)], i)

    pl.semaphore_wait(barrier, 8 + 5 * (there[0].astype(jnp.int32) + there[1].astype(jnp.int32)))
    @launch
    def _(i):
        xa_first(i).start()

    for i in range(2):
        za_first(i).start()
        y_first(i).start()

    for load in loads[4:]:
        load.wait()
    scale = 0.5 * COURANT
    tables = [[t[k] * scale for k in range(REGIONS)] for t in (lame, shear, buoy)]

    def materials(number, seafloor, z):
        bits = [(number & (1 << k)) != 0 for k in range(4)]
        solid = (dom * 8 + z) >= seafloor
        lam, mu, b = (pick(bits, t) for t in tables)
        return lam, jnp.where(solid, mu, 0.0), b, solid

    for s in range(STEPS):
        put(SRC, (pl.ds(8 * s, 8), everywhere),
            [jnp.where(dom == 0, source[s, :, cut(t)], 0.0) for t in range(2)])
    for z in range(8):
        made = [materials(region[z, :, cut(t)], floor[:, cut(t)], z) for t in range(2)]
        for k, ref in enumerate((L, M, B)):
            put(ref, (pl.ds(8 * z, 8), everywhere), [m[k] for m in made])
        for f in range(3):
            put(V, (f, level(z), everywhere), [state[f, z, :, cut(t)] for t in range(2)])

    for i, x in ((0, 0), (1, 7)):
        parts = [[OX[i, 2 * k + t] for t in range(2)] for k in range(3)]
        parts += [[m[p, pl.ds(x, 8, stride=8), :] for p in pair] for m in (L, M)]
        parts += [[
            jnp.concatenate([SRC[p, pl.ds(x, STEPS, stride=8), :], jnp.zeros((8 - STEPS, 128), f32)], 0) for p in pair]]
        for k in range(3, 6):
            for t in range(2):
                OX[i, 2 * k + t + 2] = parts[k][t]
        for j in range(2):
            OX[i, 6 + j] = side_by_side([v[j] for v in parts], j)

        @functools.partial(reach, i)
        def _(i=i):
            for j in range(2):
                xy_first(i, j).start()
    for i, z in ((0, 0), (1, 7)):
        parts = [[OZ[i, 2 * k + t] for t in range(2)] for k in range(3)]
        parts += [[m[p, pl.ds(8 * z, 8), :] for p in pair] for m in (L, M)]
        for k in range(3, 5):
            for t in range(2):
                OZ[i, 2 * k + t + 2] = parts[k][t]
        for j in range(2):
            OZ[i, 6 + j] = side_by_side([v[j] for v in parts], j)
            zy_first(i, j).start()

    left = (lane >= 128 - WIDE) & (gy > 0)
    right = (lane < WIDE) & (gy < n_gy - 1)
    inside = left | right

    def margin(low, high, f):
        shift_r = (128 - WIDE * f) % 128
        shift_l = (256 - WIDE - WIDE * f) % 128
        a = pltpu.roll(high, shift_r, 1) if shift_r else high
        c = pltpu.roll(low, shift_l, 1) if shift_l else low
        return jnp.where(left, c, jnp.where(right, a, 0.0))

    arrived(ZR0.at[:, 0:6], z_first_recv.at[0])
    for i in range(2):
        @functools.partial(reach, i)
        def _(i=i):
            arrived(XR0.at[i, 0:6], x_first_recv.at[0, i])

    def three(first_tile, second_tile, edge):
        return (
            jnp.where(lane < SEAM, second_tile, first_tile),
            jnp.where(lane >= 128 - WIDE, edge, first_tile),
            jnp.where(lane < WIDE, edge, second_tile),
        )

    def border(parts):
        for i, x in ((0, -1), (1, 8)):
            for k, f in enumerate(x_fields):
                edge = zero if parts == (MIDDLE,) else margin(XR0[i, 6], XR0[i, 7], k)
                tiles = three(XR0[i, 2 * k], XR0[i, 2 * k + 1], edge)
                for p in parts:
                    S[p, f, column(x), :] = tiles[p]
        for i, z in ((0, -1), (1, 8)):
            for k, f in enumerate(z_fields):
                edge = zero if parts == (MIDDLE,) else margin(ZR0[i, 6], ZR0[i, 7], k)
                tiles = three(ZR0[i, 2 * k], ZR0[i, 2 * k + 1], edge)
                for p in parts:
                    S[p, f, level(z), :] = jnp.where(z_there[i], tiles[p], 0.0)

    @launch
    def _(i):
        xb_first(i).start()

    for i in range(2):
        zb_first(i).start()
    border((MIDDLE,))
    def x_base(p, s, last):
        return 14 + 18 * s + (3 * p if last else 6 * p)

    def z_base(p, s, last):
        return 12 + 18 * s + (3 * p if last else 6 * p)

    def x_copy(p, i, s, slot, last):
        n = 3 if last else 6
        return remote(
            OX.at[i, pl.ds(x_base(p, s, last), n)], XR.at[slot, p, 1 - i, 0:n], x_send.at[i], x_recv.at[slot, p, 1 - i],
            (0, sides[i], 0))

    def e_copy(p, i, j, s, slot):
        return remote(
            OE.at[i, 3 * s + p, j], ER.at[slot, p, 1 - i, 1 - j], e_send.at[i],
            e_recv.at[slot, p, 1 - i], (sides[j], sides[i], 0))

    def z_copy(p, i, s, slot, last):
        n = 3 if last else 6
        return remote(
            OZ.at[i, pl.ds(z_base(p, s, last), n)], ZR.at[slot, p, 1 - i, 0:n], z_send.at[i], z_recv.at[slot, p],
            (sides[i], 0, 0))

    def move(p, s, slot, last=False):
        def accelerate(levels):
            moved = []
            for z in levels:
                own = level(z)
                after, before = pl.ds(rows(z, 1), 8), pl.ds(rows(z, -1), 8)
                above, below = level(z + 1), level(z - 1)

                def dx(f):
                    return S[p, f, after, :] - S[p, f, before, :]

                def dz(f):
                    return S[p, f, above, :] - S[p, f, below, :]

                b = B[p, pl.ds(8 * z, 8), :]
                moved.append((0, own, V[p, 0, own, :] - b * (dx(0) + dy(S[p, 3, own, :]) + dz(4))))
                moved.append((1, own, V[p, 1, own, :] - b * (dx(3) + dy(S[p, 1, own, :]) + dz(5))))
                moved.append((2, own, V[p, 2, own, :] - b * (dx(4) + dy(S[p, 5, own, :]) + dz(2))))
            for f, own, v in moved:
                V[p, f, own, :] = v

        accelerate((0, 7))
        if not last:
            for i, x in ((0, 0), (1, 7)):
                for j in range(2):
                    for k, f in enumerate((0, 2)):
                        OE[i, 3 * s + p, j, k : k + 1, :] = V[p, f, pl.ds(rows(7 * j, x), 1), :]


            @launch
            def _(i):
                for j in range(2):
                    e_copy(p, i, j, s, slot).start()

        accelerate((1, 2, 3))
        accelerate((4, 5, 6))
        base = x_base(p, s, last)
        for i, (x, inner) in enumerate(((0, 1), (7, 6))):
            for k, v in enumerate([V[p, f, column(c), :] for c in ((x,) if last else (x, inner)) for f in range(3)]):
                OX[i, base + k] = v

        @launch
        def _(i):
            x_copy(p, i, s, slot, last).start()

        base = z_base(p, s, last)
        for i, (z, inner) in enumerate(((0, 1), (7, 6))):
            for f in range(3):
                OZ[i, base + f] = V[p, f, level(z), :]
                if not last:
                    OZ[i, base + 3 + f] = V[p, f, level(inner), :]
            z_copy(p, i, s, slot, last).start()

        later = []
        for z in range(8):
            own = level(z)
            after, before = pl.ds(rows(z, 1), 8), pl.ds(rows(z, -1), 8)
            above, below = level(z + 1), level(z - 1)
            dxs = [V[p, f, after, :] - V[p, f, before, :] for f in range(3)]
            dzs = [V[p, f, above, :] - V[p, f, below, :] for f in range(3)]
            dys = [dy(V[p, f, own, :]) for f in range(3)]
            lam, mu = L[p, pl.ds(8 * z, 8), :], M[p, pl.ds(8 * z, 8), :]
            spread = lam * (dxs[0] + dys[1] + dzs[2])
            mu2 = mu + mu
            change = (
                spread + mu2 * dxs[0], spread + mu2 * dys[1], spread + mu2 * dzs[2],
                mu * (dys[0] + dxs[1]), mu * (dzs[0] + dxs[2]), mu * (dzs[1] + dys[2]))
            later += [(f, own, S[p, f, own, :] - change[f]) for f in range(6)]
            if z % 2:
                write(p, later)
                later = []

    def write(p, results):
        for f, at_rows, v in results:
            S[p, f, at_rows, :] = v

    def finish(p, slot, then=None):
        last = then is None
        if not last:
            added = SRC[p, pl.ds(8 * then if isinstance(then, int) else pl.multiple_of(8 * then, 8), 8), :]
            results = [(f, level(0), S[p, f, level(0), :] + added) for f in range(3)]
            for i, x in ((0, -1), (1, 8)):
                outer = pl.ds(rows(0, x), 1)
                results.append((0, outer, S[p, 0, outer, :] + SX[i, p, pl.ds(then, 1), :]))
            write(p, results)
        arrived(ZR.at[slot, p, :, 0:3] if last else ZR.at[slot, p], z_recv.at[slot, p])
        results = []
        for i, z in ((0, 0), (1, 7)):
            near = [ZR[slot, p, i, f] for f in range(3)]
            own = level(z)
            lam, mu = L[p, pl.ds(8 * z, 8), :], M[p, pl.ds(8 * z, 8), :]
            sign = jnp.where(z_there[i], (-1.0, 1.0)[i], 0.0)
            slope = [sign * v for v in near]
            spread = lam * slope[2]
            results.append((0, own, S[p, 0, own, :] - (spread)))
            results.append((1, own, S[p, 1, own, :] - (spread)))
            results.append((2, own, S[p, 2, own, :] - (spread + (mu + mu) * slope[2])))
            results.append((4, own, S[p, 4, own, :] - (mu * slope[0])))
            results.append((5, own, S[p, 5, own, :] - (mu * slope[1])))
        write(p, results)

        for i in range(2):
            @functools.partial(reach, i)
            def _(i=i):
                arrived(XR.at[slot, p, i, 0:3] if last else XR.at[slot, p, i], x_recv.at[slot, p, i])

        results = []
        for i, x, sign in ((0, 0, -1.0), (1, 7, 1.0)):
            near = [XR[slot, p, i, f] for f in range(3)]
            lam, mu = L[p, pl.ds(x, 8, stride=8), :], M[p, pl.ds(x, 8, stride=8), :]
            slope = [sign * v for v in near]
            spread = lam * slope[0]
            results.append((0, column(x), S[p, 0, column(x), :] - (spread + (mu + mu) * slope[0])))
            results.append((1, column(x), S[p, 1, column(x), :] - (spread)))
            results.append((2, column(x), S[p, 2, column(x), :] - (spread)))
            results.append((3, column(x), S[p, 3, column(x), :] - (mu * slope[1])))
            results.append((4, column(x), S[p, 4, column(x), :] - (mu * slope[2])))

        if last:
            write(p, results)
            return
        for i, x, sign in ((0, 0, -1.0), (1, 7, 1.0)):
            near, far = [XR[slot, p, i, f] for f in range(3)], [XR[slot, p, i, 3 + f] for f in range(3)]
            lam, mu = LX[i, p], MX[i, p]
            dxs = [sign * (far[f] - V[p, f, column(x), :]) for f in range(3)]
            dzs = {}
            for f in (0, 2):
                up, down = pltpu.roll(near[f], 7, 0), pltpu.roll(near[f], 1, 0)
                dzs[f] = jnp.where(sub == 7, 0.0, up) - jnp.where(sub == 0, 0.0, down)
            trace = dxs[0] + dy(near[1]) + dzs[2]
            beyond = column((-1, 8)[i])
            results.append((0, beyond, S[p, 0, beyond, :] - (lam * trace + (mu + mu) * dxs[0])))
            results.append((3, beyond, S[p, 3, beyond, :] - (mu * (dy(near[0]) + dxs[1]))))
            results.append((4, beyond, S[p, 4, beyond, :] - (mu * (dzs[0] + dxs[2]))))
        for i, z, sign in ((0, 0, -1.0), (1, 7, 1.0)):
            near, far = [ZR[slot, p, i, f] for f in range(3)], [ZR[slot, p, i, 3 + f] for f in range(3)]
            lam, mu = LZ[i, p], MZ[i, p]
            dzs = [sign * (far[f] - V[p, f, level(z), :]) for f in range(3)]
            dxs = {}
            for f in (0, 2):
                ahead, behind = pltpu.roll(near[f], 7, 0), pltpu.roll(near[f], 1, 0)
                dxs[f] = jnp.where(sub == 7, 0.0, ahead) - jnp.where(sub == 0, 0.0, behind)
            trace = dxs[0] + dy(near[1]) + dzs[2]
            beyond = level((-1, 8)[i])
            results.append((2, beyond, S[p, 2, beyond, :] - (lam * trace + (mu + mu) * dzs[2])))
            results.append((4, beyond, S[p, 4, beyond, :] - (mu * (dzs[0] + dxs[2]))))
            results.append((5, beyond, S[p, 5, beyond, :] - (mu * (dzs[1] + dy(near[2])))))

        write(p, results)

        for i in range(2):
            @functools.partial(reach, i)
            def _(i=i):
                arrived(ER.at[slot, p, i], e_recv.at[slot, p, i])
        results = []
        for i, x in ((0, 0), (1, 7)):
            for j, z in ((0, 0), (1, 7)):
                edge_x, edge_z = (ER[slot, p, i, j, k : k + 1, :] for k in range(2))
                sign = jnp.where(z_there[j], (-1.0, 1.0)[j], 0.0)
                outer = pl.ds(rows(z, (-1, 8)[i]), 1)
                at_z, at_x = slice(z, z + 1), slice(x, x + 1)
                results.append((0, outer, S[p, 0, outer, :] - (LX[i, p, at_z, :] * (sign * edge_z))))
                results.append((4, outer, S[p, 4, outer, :] - (MX[i, p, at_z, :] * (sign * edge_x))))
                outer = pl.ds(rows((-1, 8)[j], x), 1)
                results.append((2, outer, S[p, 2, outer, :] - (LZ[j, p, at_x, :] * (sides[i] * edge_x))))
                results.append((4, outer, S[p, 4, outer, :] - (MZ[j, p, at_x, :] * (sides[i] * edge_z))))
        write(p, results)

    def each_part(then):
        for p in range(3):
            then(p)

    move(MIDDLE, 0, 0)

    arrived(YR, y_recv.at[0])
    low, high = YR[0, 8], YR[1, 8]
    seafloor = margin(low, high, STEPS).astype(jnp.int32)
    first_source = None
    for s in range(STEPS):
        v = jnp.where(dom == 0, margin(low, high, s), 0.0)
        first_source = v if s == 0 else first_source
        put_margin(SRC, (pl.ds(8 * s, 8), everywhere), v)
    for z in range(8):
        low, high = YR[0, z], YR[1, z]
        lam, mu, b, solid = materials(margin(low, high, 9).astype(jnp.int32), seafloor, z)
        for ref, v in ((L, lam), (M, mu), (B, b)):
            put_margin(ref, (pl.ds(8 * z, 8), everywhere), jnp.where(inside, v, 0.0))
        for f in range(9):
            v = margin(low, high, f)
            if f < 3:
                put_margin(V, (f, level(z), everywhere), v)
            else:
                if f >= 6:
                    v = jnp.where(solid, v, 0.0)
                elif z == 0:
                    v = v + first_source
                put_margin(S, (f - 3, level(z), everywhere), v)

    arrived(ZR0.at[:, 6:8], z_first_recv.at[2])
    for i in range(2):
        @functools.partial(reach, i)
        def _(i=i):
            arrived(XR0.at[i, 6:8], x_first_recv.at[2, i])
    border((LEFT, RIGHT))

    move(LEFT, 0, 0)
    move(RIGHT, 0, 0)

    arrived(ZR0.at[:, 8:12], z_first_recv.at[1])
    for i in range(2):
        @functools.partial(reach, i)
        def _(i=i):
            arrived(XR0.at[i, 8:14], x_first_recv.at[1, i])
    for i in range(2):
        for k, ref in enumerate((LX, MX, SX)):
            tiles = three(XR0[i, 8 + 2 * k], XR0[i, 9 + 2 * k], margin(XR0[i, 6], XR0[i, 7], 3 + k))
            for p in range(3):
                ref[i, p] = tiles[p]
        for k, ref in enumerate((LZ, MZ)):
            tiles = three(ZR0[i, 8 + 2 * k], ZR0[i, 9 + 2 * k], margin(ZR0[i, 6], ZR0[i, 7], 3 + k))
            for p in range(3):
                ref[i, p] = jnp.where(z_there[i], tiles[p], 0.0)

    def step(s, carry):
        slot = lax.rem(s, 2)

        def turn(p):
            finish(p, 1 - slot, s)
            move(p, s, slot)

        each_part(turn)
        return carry

    lax.fori_loop(1, STEPS - 1, step, 0)

    end = STEPS - 1

    def final(p):
        finish(p, (end - 1) % 2, end)
        move(p, end, end % 2, last=True)

    each_part(final)

    def gather(f, ref, k):
        for z in range(8):
            middle, first_tile, second_tile = (ref[p, k, level(z), :] for p in (MIDDLE, LEFT, RIGHT))
            out[f, z, :, cut(0)] = jnp.where(lane < FIRST_CUT, first_tile, middle)
            out[f, z, :, cut(1)] = jnp.where(lane < SECOND_CUT, middle, second_tile)

    for f in range(3):
        gather(f, V, f)
    each_part(lambda p: finish(p, end % 2))
    for f in range(6):
        gather(3 + f, S, f)

    for i in range(2):
        arrived(OZ.at[i], z_send.at[i])

        @functools.partial(reach, i)
        def _(i=i):
            arrived(OX.at[i], x_send.at[i])
            arrived(OE.at[i], e_send.at[i])


def solution(mesh):
    sizes = (mesh.shape["dom"], mesh.shape["gx"], mesh.shape["gy"])

    def on_device(state, source, floor, region, lame, shear, buoy):
        hbm = pl.BlockSpec(memory_space=pltpu.HBM)

        def tiles(*shape):
            return pltpu.VMEM(shape + (8, 128), f32)

        return pl.pallas_call(
            functools.partial(kernel, sizes),
            out_shape=jax.ShapeDtypeStruct(state.shape, f32),
            in_specs=[hbm] * 7,
            out_specs=pl.BlockSpec(memory_space=pltpu.VMEM),
            scratch_shapes=[
                pltpu.VMEM(state.shape, f32),
                pltpu.VMEM(source.shape, f32),
                pltpu.VMEM(floor.shape, jnp.int32),
                pltpu.VMEM(region.shape, jnp.int32),
                pltpu.SMEM(lame.shape, f32),
                pltpu.SMEM(shear.shape, f32),
                pltpu.SMEM(buoy.shape, f32),
                pltpu.VMEM((3, 6, 10 * BLOCK, 128), f32),
                pltpu.VMEM((3, 3, 10 * BLOCK, 128), f32),
                pltpu.VMEM((3, 64, 128), f32),
                pltpu.VMEM((3, 64, 128), f32),
                pltpu.VMEM((3, 64, 128), f32),
                pltpu.VMEM((3, 8 * STEPS, 128), f32),
                tiles(2, 3),
                tiles(2, 3),
                tiles(2, 3),
                tiles(2, 3),
                tiles(2, 3),
                tiles(2, 113),
                tiles(2, 120),
                pltpu.VMEM((2, 3 * STEPS - 3, 2, 2, 128), f32),
                tiles(2, 14),
                tiles(2, 12),
                tiles(2, 9),
                tiles(2, 3, 2, 6),
                tiles(2, 3, 2, 6),
                pltpu.VMEM((2, 3, 2, 2, 2, 128), f32),
                pltpu.SemaphoreType.DMA((7,)),
                pltpu.SemaphoreType.DMA((2,)),
                pltpu.SemaphoreType.DMA((2,)),
                pltpu.SemaphoreType.DMA((2,)),
                pltpu.SemaphoreType.DMA((3, 2)),
                pltpu.SemaphoreType.DMA((3,)),
                pltpu.SemaphoreType.DMA((1,)),
                pltpu.SemaphoreType.DMA((2, 3, 2)),
                pltpu.SemaphoreType.DMA((2, 3)),
                pltpu.SemaphoreType.DMA((2, 3, 2)),
            ],
            compiler_params=pltpu.CompilerParams(
                collective_id=0, has_side_effects=True, vmem_limit_bytes=32 * 1024 * 1024
            ),
        )(*(
            pltpu.with_memory_space_constraint(v, pltpu.HBM)
            for v in (state, source, floor, region, lame, shear, buoy)
        ))

    return jax.shard_map(
        on_device,
        mesh=mesh,
        in_specs=(
            P(None, "dom", "gx", "gy"),
            P(None, "gx", "gy"),
            P("gx", "gy"),
            P("dom", "gx", "gy"),
            P(),
            P(),
            P(),
        ),
        out_specs=P(None, "dom", "gx", "gy"),
        check_vma=False,
    )
```

```python
import functools

import jax
import jax.numpy as jnp
from jax import lax
from jax.experimental import pallas as pl
from jax.experimental.pallas import tpu as pltpu
from jax.sharding import PartitionSpec as P

STEPS = 6
COURANT = 0.25
REGIONS = 16
BLOCK = 16
WIDE = 12
MIDDLE, LEFT, RIGHT = 0, 1, 2
FIRST_CUT, SECOND_CUT, SEAM = 86, 171 - 128, 64
MESH = pl.DeviceIdType.MESH

f32 = jnp.float32


def rows(z, x=0):
    return (z + 1) * BLOCK + 8 + x


def level(z):
    return pl.ds(rows(z), 8)


def column(x):
    return pl.ds(rows(0, x), 8, stride=BLOCK)


def dy(v):
    return pltpu.roll(v, 127, 1) - pltpu.roll(v, 1, 1)


def pick(bits, table):
    values = list(table)
    for bit in bits:
        values = [jnp.where(bit, values[2 * i + 1], values[2 * i]) for i in range(len(values) // 2)]
    return values[0]


def kernel(
    sizes, state_in, source_in, floor_in, region_in, lame_in, shear_in, buoy_in, out,
    state, source, floor, region, lame, shear, buoy,
    S, V, L, M, B, SRC, LX, MX, SX, LZ, MZ, OX, OZ, OE, XR0, ZR0, YR, XR, ZR, ER,
    in_sem, x_send, z_send, e_send, x_first_recv, z_first_recv, y_recv, x_recv, z_recv, e_recv,
):
    n_dom, n_gx, n_gy = sizes
    dom, gx, gy = lax.axis_index("dom"), lax.axis_index("gx"), lax.axis_index("gy")
    lane = lax.broadcasted_iota(jnp.int32, (8, 128), 1)
    sub = lax.broadcasted_iota(jnp.int32, (8, 128), 0)
    zero = jnp.zeros((8, 128), f32)

    loads = [
        pltpu.make_async_copy(src, dst, in_sem.at[i])
        for i, (src, dst) in enumerate((
            (region_in, region), (floor_in, floor), (source_in, source), (state_in, state),
            (lame_in, lame), (shear_in, shear), (buoy_in, buoy)))
    ]
    for load in loads:
        load.start()

    sides = (-1, 1)
    there = [gx > 0, gx < n_gx - 1]
    z_there = [dom > 0, dom < n_dom - 1]

    doms = [dom, jnp.where(dom == n_dom - 1, 0, dom + 1), jnp.where(dom == 0, n_dom - 1, dom - 1)]
    gxs = [gx, gx + 1, gx - 1]
    gys = [gy, jnp.where(gy == n_gy - 1, 0, gy + 1), jnp.where(gy == 0, n_gy - 1, gy - 1)]

    def at(dz, dx, dyy):
        return (doms[dz], gxs[dx], gys[dyy])

    def reach(i, then):
        pl.when(there[i])(then)

    barrier = pltpu.get_barrier_semaphore()

    def greet(*way):
        pl.semaphore_signal(barrier, inc=1, device_id=at(*way), device_id_type=MESH)

    for i, dx in enumerate(sides):
        @functools.partial(reach, i)
        def _(dx=dx):
            for way in ((0, dx, 0), (-1, dx, 0), (1, dx, 0), (0, dx, -1), (0, dx, 1)):
                greet(*way)
    for way in [(a, 0, b) for a in (-1, 0, 1) for b in (-1, 0, 1) if a or b]:
        greet(*way)

    for i in range(2):
        @pl.when(jnp.logical_not(there[i]))
        def _(i=i):
            XR0[i] = jnp.zeros(XR0.shape[1:], f32)
            for slot in range(2):
                for p in range(3):
                    XR[slot, p, i] = jnp.zeros(XR.shape[3:], f32)
                    ER[slot, p, i] = jnp.zeros(ER.shape[3:], f32)

    for p in range(3):
        for f in range(3):
            for z in range(-1, 9):
                V[p, f, pl.ds(rows(z, -8), 8), :] = zero
            for z in (-1, 8):
                V[p, f, level(z), :] = zero

    for load in loads[:4]:
        load.wait()

    def side_by_side(parts, t):
        tile = zero
        for k, v in enumerate(parts):
            shift = (WIDE * k + (WIDE if t else 0)) % 128
            v = pltpu.roll(v, shift, 1) if shift else v
            tile = jnp.where((lane >= WIDE * k) & (lane < WIDE * (k + 1)), v, tile)
        return tile

    def cut(t):
        return slice(128 * t, 128 * t + 128)

    def remote(src, dst, send, recv, way):
        return pltpu.make_async_remote_copy(
            src_ref=src, dst_ref=dst, send_sem=send, recv_sem=recv, device_id=at(*way), device_id_type=MESH)

    def xa_first(i):
        return remote(OX.at[i, 0:6], XR0.at[1 - i, 0:6], x_send.at[i], x_first_recv.at[0, 1 - i], (0, sides[i], 0))

    def xy_first(i, j):
        return remote(
            OX.at[i, 6 + j], XR0.at[1 - i, 7 - j], x_send.at[i], x_first_recv.at[2, 1 - i], (0, sides[i], sides[j]))

    def xb_first(i):
        return remote(OX.at[i, 8:14], XR0.at[1 - i, 8:14], x_send.at[i], x_first_recv.at[1, 1 - i], (0, sides[i], 0))

    def za_first(i):
        return remote(OZ.at[i, 0:6], ZR0.at[1 - i, 0:6], z_send.at[i], z_first_recv.at[0], (sides[i], 0, 0))

    def zy_first(i, j):
        return remote(
            OZ.at[i, 6 + j], ZR0.at[1 - i, 7 - j], z_send.at[i], z_first_recv.at[2], (sides[i], 0, sides[j]))

    def zb_first(i):
        return remote(OZ.at[i, 8:12], ZR0.at[1 - i, 8:12], z_send.at[i], z_first_recv.at[1], (sides[i], 0, 0))

    def y_first(i):
        return remote(OZ.at[i, 111:120], YR.at[1 - i], z_send.at[i], y_recv.at[0], (0, 0, sides[i]))

    def arrived(ref, sem):
        pltpu.make_async_copy(ref, ref, sem).wait()

    def put(ref, index, pair):
        ref[(MIDDLE, *index)] = jnp.where(lane < SEAM, pair[1], pair[0])
        ref[(LEFT, *index)] = pair[0]
        ref[(RIGHT, *index)] = pair[1]

    def put_margin(ref, index, v):
        ref[(LEFT, *index)] = jnp.where(lane >= 128 - WIDE, v, ref[(LEFT, *index)])
        ref[(RIGHT, *index)] = jnp.where(lane < WIDE, v, ref[(RIGHT, *index)])

    everywhere = slice(None)
    for z in range(8):
        solid = [(dom * 8 + z) >= floor[:, cut(t)] for t in range(2)]
        for f in range(6):
            v = [state[3 + f, z, :, cut(t)] for t in range(2)]
            if f >= 3:
                v = [jnp.where(m, w, 0.0) for m, w in zip(solid, v)]
            elif z == 0:
                v = [w + jnp.where(dom == 0, source[0, :, cut(t)], 0.0) for t, w in enumerate(v)]
            put(S, (f, level(z), everywhere), v)
    x_fields, z_fields = (0, 3, 4), (2, 4, 5)
    pair = (LEFT, RIGHT)
    for i, at_edge in enumerate((0, 7)):
        for k in range(3):
            for t in range(2):
                OX[i, 2 * k + t] = S[pair[t], x_fields[k], column(at_edge), :]
                OZ[i, 2 * k + t] = S[pair[t], z_fields[k], level(at_edge), :]
    for i in range(2):
        for z in range(8):
            OZ[i, 111 + z] = side_by_side(
                [state[f, z, :, cut(i)] for f in range(9)] + [region[z, :, cut(i)].astype(f32)], i)
        OZ[i, 119] = side_by_side([source[s, :, cut(i)] for s in range(STEPS)] + [floor[:, cut(i)].astype(f32)], i)

    pl.semaphore_wait(barrier, 8 + 5 * (there[0].astype(jnp.int32) + there[1].astype(jnp.int32)))
    for i in range(2):
        @functools.partial(reach, i)
        def _(i=i):
            xa_first(i).start()
    for i in range(2):
        za_first(i).start()
        y_first(i).start()

    for load in loads[4:]:
        load.wait()
    scale = 0.5 * COURANT
    tables = [[t[k] * scale for k in range(REGIONS)] for t in (lame, shear, buoy)]

    def materials(number, seafloor, z):
        bits = [(number & (1 << k)) != 0 for k in range(4)]
        solid = (dom * 8 + z) >= seafloor
        lam, mu, b = (pick(bits, t) for t in tables)
        return lam, jnp.where(solid, mu, 0.0), b, solid

    for s in range(STEPS):
        put(SRC, (pl.ds(8 * s, 8), everywhere),
            [jnp.where(dom == 0, source[s, :, cut(t)], 0.0) for t in range(2)])
    for z in range(8):
        made = [materials(region[z, :, cut(t)], floor[:, cut(t)], z) for t in range(2)]
        for k, ref in enumerate((L, M, B)):
            put(ref, (pl.ds(8 * z, 8), everywhere), [m[k] for m in made])
        for f in range(3):
            put(V, (f, level(z), everywhere), [state[f, z, :, cut(t)] for t in range(2)])

    for i, x in ((0, 0), (1, 7)):
        parts = [[OX[i, 2 * k + t] for t in range(2)] for k in range(3)]
        parts += [[m[p, pl.ds(x, 8, stride=8), :] for p in pair] for m in (L, M)]
        parts += [[
            jnp.concatenate([SRC[p, pl.ds(x, STEPS, stride=8), :], jnp.zeros((8 - STEPS, 128), f32)], 0) for p in pair]]
        for k in range(3, 6):
            for t in range(2):
                OX[i, 2 * k + t + 2] = parts[k][t]
        for j in range(2):
            OX[i, 6 + j] = side_by_side([v[j] for v in parts], j)

        @functools.partial(reach, i)
        def _(i=i):
            for j in range(2):
                xy_first(i, j).start()
            xb_first(i).start()
    for i, z in ((0, 0), (1, 7)):
        parts = [[OZ[i, 2 * k + t] for t in range(2)] for k in range(3)]
        parts += [[m[p, pl.ds(8 * z, 8), :] for p in pair] for m in (L, M)]
        for k in range(3, 5):
            for t in range(2):
                OZ[i, 2 * k + t + 2] = parts[k][t]
        for j in range(2):
            OZ[i, 6 + j] = side_by_side([v[j] for v in parts], j)
            zy_first(i, j).start()
        zb_first(i).start()

    left = (lane >= 128 - WIDE) & (gy > 0)
    right = (lane < WIDE) & (gy < n_gy - 1)
    inside = left | right

    def margin(low, high, f):
        shift_r = (128 - WIDE * f) % 128
        shift_l = (256 - WIDE - WIDE * f) % 128
        a = pltpu.roll(high, shift_r, 1) if shift_r else high
        c = pltpu.roll(low, shift_l, 1) if shift_l else low
        return jnp.where(left, c, jnp.where(right, a, 0.0))

    arrived(ZR0.at[:, 0:6], z_first_recv.at[0])
    for i in range(2):
        @functools.partial(reach, i)
        def _(i=i):
            arrived(XR0.at[i, 0:6], x_first_recv.at[0, i])

    def three(first_tile, second_tile, edge):
        return (
            jnp.where(lane < SEAM, second_tile, first_tile),
            jnp.where(lane >= 128 - WIDE, edge, first_tile),
            jnp.where(lane < WIDE, edge, second_tile),
        )

    def border(parts):
        for i, x in ((0, -1), (1, 8)):
            for k, f in enumerate(x_fields):
                edge = zero if parts == (MIDDLE,) else margin(XR0[i, 6], XR0[i, 7], k)
                tiles = three(XR0[i, 2 * k], XR0[i, 2 * k + 1], edge)
                for p in parts:
                    S[p, f, column(x), :] = tiles[p]
        for i, z in ((0, -1), (1, 8)):
            for k, f in enumerate(z_fields):
                edge = zero if parts == (MIDDLE,) else margin(ZR0[i, 6], ZR0[i, 7], k)
                tiles = three(ZR0[i, 2 * k], ZR0[i, 2 * k + 1], edge)
                for p in parts:
                    S[p, f, level(z), :] = jnp.where(z_there[i], tiles[p], 0.0)

    border((MIDDLE,))
    def x_base(p, s, last):
        return 14 + 18 * s + (3 * p if last else 6 * p)

    def z_base(p, s, last):
        return 12 + 18 * s + (3 * p if last else 6 * p)

    def x_copy(p, i, s, slot, last):
        n = 3 if last else 6
        return remote(
            OX.at[i, pl.ds(x_base(p, s, last), n)], XR.at[slot, p, 1 - i, 0:n], x_send.at[i], x_recv.at[slot, p, 1 - i],
            (0, sides[i], 0))

    def e_copy(p, i, j, s, slot):
        return remote(
            OE.at[i, 3 * s + p, j], ER.at[slot, p, 1 - i, 1 - j], e_send.at[i],
            e_recv.at[slot, p, 1 - i], (sides[j], sides[i], 0))

    def z_copy(p, i, s, slot, last):
        n = 3 if last else 6
        return remote(
            OZ.at[i, pl.ds(z_base(p, s, last), n)], ZR.at[slot, p, 1 - i, 0:n], z_send.at[i], z_recv.at[slot, p],
            (sides[i], 0, 0))

    def move(p, s, slot, last=False):
        def accelerate(levels):
            moved = []
            for z in levels:
                own = level(z)
                after, before = pl.ds(rows(z, 1), 8), pl.ds(rows(z, -1), 8)
                above, below = level(z + 1), level(z - 1)

                def dx(f):
                    return S[p, f, after, :] - S[p, f, before, :]

                def dz(f):
                    return S[p, f, above, :] - S[p, f, below, :]

                b = B[p, pl.ds(8 * z, 8), :]
                moved.append((0, own, V[p, 0, own, :] - b * (dx(0) + dy(S[p, 3, own, :]) + dz(4))))
                moved.append((1, own, V[p, 1, own, :] - b * (dx(3) + dy(S[p, 1, own, :]) + dz(5))))
                moved.append((2, own, V[p, 2, own, :] - b * (dx(4) + dy(S[p, 5, own, :]) + dz(2))))
            for f, own, v in moved:
                V[p, f, own, :] = v

        accelerate((0, 7))
        if not last:
            for i, x in ((0, 0), (1, 7)):
                for j in range(2):
                    for k, f in enumerate((0, 2)):
                        OE[i, 3 * s + p, j, k : k + 1, :] = V[p, f, pl.ds(rows(7 * j, x), 1), :]

                @functools.partial(reach, i)
                def _(i=i):
                    for j in range(2):
                        e_copy(p, i, j, s, slot).start()
        accelerate((1, 2, 3))
        accelerate((4, 5, 6))
        base = x_base(p, s, last)
        for i, (x, inner) in enumerate(((0, 1), (7, 6))):
            for k, v in enumerate([V[p, f, column(c), :] for c in ((x,) if last else (x, inner)) for f in range(3)]):
                OX[i, base + k] = v

            @functools.partial(reach, i)
            def _(i=i):
                x_copy(p, i, s, slot, last).start()
        base = z_base(p, s, last)
        for i, (z, inner) in enumerate(((0, 1), (7, 6))):
            for f in range(3):
                OZ[i, base + f] = V[p, f, level(z), :]
                if not last:
                    OZ[i, base + 3 + f] = V[p, f, level(inner), :]
            z_copy(p, i, s, slot, last).start()

    def settle(p):
        later = []
        for z in range(8):
            own = level(z)
            after, before = pl.ds(rows(z, 1), 8), pl.ds(rows(z, -1), 8)
            above, below = level(z + 1), level(z - 1)
            dxs = [V[p, f, after, :] - V[p, f, before, :] for f in range(3)]
            dzs = [V[p, f, above, :] - V[p, f, below, :] for f in range(3)]
            dys = [dy(V[p, f, own, :]) for f in range(3)]
            lam, mu = L[p, pl.ds(8 * z, 8), :], M[p, pl.ds(8 * z, 8), :]
            spread = lam * (dxs[0] + dys[1] + dzs[2])
            mu2 = mu + mu
            change = (
                spread + mu2 * dxs[0], spread + mu2 * dys[1], spread + mu2 * dzs[2],
                mu * (dys[0] + dxs[1]), mu * (dzs[0] + dxs[2]), mu * (dzs[1] + dys[2]))
            later += [(f, own, S[p, f, own, :] - change[f]) for f in range(6)]
            if z % 2:
                write(p, later)
                later = []

    def write(p, results):
        for f, at_rows, v in results:
            S[p, f, at_rows, :] = v

    def finish(p, slot, then=None):
        last = then is None
        if not last:
            added = SRC[p, pl.ds(8 * then if isinstance(then, int) else pl.multiple_of(8 * then, 8), 8), :]
            results = [(f, level(0), S[p, f, level(0), :] + added) for f in range(3)]
            for i, x in ((0, -1), (1, 8)):
                outer = pl.ds(rows(0, x), 1)
                results.append((0, outer, S[p, 0, outer, :] + SX[i, p, pl.ds(then, 1), :]))
            write(p, results)
        arrived(ZR.at[slot, p, :, 0:3] if last else ZR.at[slot, p], z_recv.at[slot, p])
        results = []
        for i, z in ((0, 0), (1, 7)):
            near = [ZR[slot, p, i, f] for f in range(3)]
            own = level(z)
            lam, mu = L[p, pl.ds(8 * z, 8), :], M[p, pl.ds(8 * z, 8), :]
            sign = jnp.where(z_there[i], (-1.0, 1.0)[i], 0.0)
            slope = [sign * v for v in near]
            spread = lam * slope[2]
            results.append((0, own, S[p, 0, own, :] - (spread)))
            results.append((1, own, S[p, 1, own, :] - (spread)))
            results.append((2, own, S[p, 2, own, :] - (spread + (mu + mu) * slope[2])))
            results.append((4, own, S[p, 4, own, :] - (mu * slope[0])))
            results.append((5, own, S[p, 5, own, :] - (mu * slope[1])))
        write(p, results)

        for i in range(2):
            @functools.partial(reach, i)
            def _(i=i):
                arrived(XR.at[slot, p, i, 0:3] if last else XR.at[slot, p, i], x_recv.at[slot, p, i])

        results = []
        for i, x, sign in ((0, 0, -1.0), (1, 7, 1.0)):
            near = [XR[slot, p, i, f] for f in range(3)]
            lam, mu = L[p, pl.ds(x, 8, stride=8), :], M[p, pl.ds(x, 8, stride=8), :]
            slope = [sign * v for v in near]
            spread = lam * slope[0]
            results.append((0, column(x), S[p, 0, column(x), :] - (spread + (mu + mu) * slope[0])))
            results.append((1, column(x), S[p, 1, column(x), :] - (spread)))
            results.append((2, column(x), S[p, 2, column(x), :] - (spread)))
            results.append((3, column(x), S[p, 3, column(x), :] - (mu * slope[1])))
            results.append((4, column(x), S[p, 4, column(x), :] - (mu * slope[2])))

        if last:
            write(p, results)
            return
        for i, x, sign in ((0, 0, -1.0), (1, 7, 1.0)):
            near, far = [XR[slot, p, i, f] for f in range(3)], [XR[slot, p, i, 3 + f] for f in range(3)]
            lam, mu = LX[i, p], MX[i, p]
            dxs = [sign * (far[f] - V[p, f, column(x), :]) for f in range(3)]
            dzs = {}
            for f in (0, 2):
                up, down = pltpu.roll(near[f], 7, 0), pltpu.roll(near[f], 1, 0)
                dzs[f] = jnp.where(sub == 7, 0.0, up) - jnp.where(sub == 0, 0.0, down)
            trace = dxs[0] + dy(near[1]) + dzs[2]
            beyond = column((-1, 8)[i])
            results.append((0, beyond, S[p, 0, beyond, :] - (lam * trace + (mu + mu) * dxs[0])))
            results.append((3, beyond, S[p, 3, beyond, :] - (mu * (dy(near[0]) + dxs[1]))))
            results.append((4, beyond, S[p, 4, beyond, :] - (mu * (dzs[0] + dxs[2]))))
        for i, z, sign in ((0, 0, -1.0), (1, 7, 1.0)):
            near, far = [ZR[slot, p, i, f] for f in range(3)], [ZR[slot, p, i, 3 + f] for f in range(3)]
            lam, mu = LZ[i, p], MZ[i, p]
            dzs = [sign * (far[f] - V[p, f, level(z), :]) for f in range(3)]
            dxs = {}
            for f in (0, 2):
                ahead, behind = pltpu.roll(near[f], 7, 0), pltpu.roll(near[f], 1, 0)
                dxs[f] = jnp.where(sub == 7, 0.0, ahead) - jnp.where(sub == 0, 0.0, behind)
            trace = dxs[0] + dy(near[1]) + dzs[2]
            beyond = level((-1, 8)[i])
            results.append((2, beyond, S[p, 2, beyond, :] - (lam * trace + (mu + mu) * dzs[2])))
            results.append((4, beyond, S[p, 4, beyond, :] - (mu * (dzs[0] + dxs[2]))))
            results.append((5, beyond, S[p, 5, beyond, :] - (mu * (dzs[1] + dy(near[2])))))

        write(p, results)

        for i in range(2):
            @functools.partial(reach, i)
            def _(i=i):
                arrived(ER.at[slot, p, i], e_recv.at[slot, p, i])
        results = []
        for i, x in ((0, 0), (1, 7)):
            for j, z in ((0, 0), (1, 7)):
                edge_x, edge_z = (ER[slot, p, i, j, k : k + 1, :] for k in range(2))
                sign = jnp.where(z_there[j], (-1.0, 1.0)[j], 0.0)
                outer = pl.ds(rows(z, (-1, 8)[i]), 1)
                at_z, at_x = slice(z, z + 1), slice(x, x + 1)
                results.append((0, outer, S[p, 0, outer, :] - (LX[i, p, at_z, :] * (sign * edge_z))))
                results.append((4, outer, S[p, 4, outer, :] - (MX[i, p, at_z, :] * (sign * edge_x))))
                outer = pl.ds(rows((-1, 8)[j], x), 1)
                results.append((2, outer, S[p, 2, outer, :] - (LZ[j, p, at_x, :] * (sides[i] * edge_x))))
                results.append((4, outer, S[p, 4, outer, :] - (MZ[j, p, at_x, :] * (sides[i] * edge_z))))
        write(p, results)

    def each_part(then):
        for p in range(3):
            then(p)

    move(MIDDLE, 0, 0)
    settle(MIDDLE)

    arrived(YR, y_recv.at[0])
    low, high = YR[0, 8], YR[1, 8]
    seafloor = margin(low, high, STEPS).astype(jnp.int32)
    first_source = None
    for s in range(STEPS):
        v = jnp.where(dom == 0, margin(low, high, s), 0.0)
        first_source = v if s == 0 else first_source
        put_margin(SRC, (pl.ds(8 * s, 8), everywhere), v)
    for z in range(8):
        low, high = YR[0, z], YR[1, z]
        lam, mu, b, solid = materials(margin(low, high, 9).astype(jnp.int32), seafloor, z)
        for ref, v in ((L, lam), (M, mu), (B, b)):
            put_margin(ref, (pl.ds(8 * z, 8), everywhere), jnp.where(inside, v, 0.0))
        for f in range(9):
            v = margin(low, high, f)
            if f < 3:
                put_margin(V, (f, level(z), everywhere), v)
            else:
                if f >= 6:
                    v = jnp.where(solid, v, 0.0)
                elif z == 0:
                    v = v + first_source
                put_margin(S, (f - 3, level(z), everywhere), v)

    arrived(ZR0.at[:, 6:8], z_first_recv.at[2])
    for i in range(2):
        @functools.partial(reach, i)
        def _(i=i):
            arrived(XR0.at[i, 6:8], x_first_recv.at[2, i])
    border((LEFT, RIGHT))

    for p in (LEFT, RIGHT):
        move(p, 0, 0)
    for p in (LEFT, RIGHT):
        settle(p)

    arrived(ZR0.at[:, 8:12], z_first_recv.at[1])
    for i in range(2):
        @functools.partial(reach, i)
        def _(i=i):
            arrived(XR0.at[i, 8:14], x_first_recv.at[1, i])
    for i in range(2):
        for k, ref in enumerate((LX, MX, SX)):
            tiles = three(XR0[i, 8 + 2 * k], XR0[i, 9 + 2 * k], margin(XR0[i, 6], XR0[i, 7], 3 + k))
            for p in range(3):
                ref[i, p] = tiles[p]
        for k, ref in enumerate((LZ, MZ)):
            tiles = three(ZR0[i, 8 + 2 * k], ZR0[i, 9 + 2 * k], margin(ZR0[i, 6], ZR0[i, 7], 3 + k))
            for p in range(3):
                ref[i, p] = jnp.where(z_there[i], tiles[p], 0.0)

    def step(s, carry):
        slot = lax.rem(s, 2)

        def turn(p):
            finish(p, 1 - slot, s)
            move(p, s, slot)

        each_part(turn)
        each_part(settle)
        return carry

    lax.fori_loop(1, STEPS - 1, step, 0)

    end = STEPS - 1

    def final(p):
        finish(p, (end - 1) % 2, end)
        move(p, end, end % 2, last=True)

    each_part(final)
    each_part(settle)

    def gather(f, ref, k):
        for z in range(8):
            middle, first_tile, second_tile = (ref[p, k, level(z), :] for p in (MIDDLE, LEFT, RIGHT))
            out[f, z, :, cut(0)] = jnp.where(lane < FIRST_CUT, first_tile, middle)
            out[f, z, :, cut(1)] = jnp.where(lane < SECOND_CUT, middle, second_tile)

    for f in range(3):
        gather(f, V, f)
    each_part(lambda p: finish(p, end % 2))
    for f in range(6):
        gather(3 + f, S, f)

    for i in range(2):
        arrived(OZ.at[i], z_send.at[i])

        @functools.partial(reach, i)
        def _(i=i):
            arrived(OX.at[i], x_send.at[i])
            arrived(OE.at[i], e_send.at[i])


def solution(mesh):
    sizes = (mesh.shape["dom"], mesh.shape["gx"], mesh.shape["gy"])

    def on_device(state, source, floor, region, lame, shear, buoy):
        hbm = pl.BlockSpec(memory_space=pltpu.HBM)

        def tiles(*shape):
            return pltpu.VMEM(shape + (8, 128), f32)

        return pl.pallas_call(
            functools.partial(kernel, sizes),
            out_shape=jax.ShapeDtypeStruct(state.shape, f32),
            in_specs=[hbm] * 7,
            out_specs=pl.BlockSpec(memory_space=pltpu.VMEM),
            scratch_shapes=[
                pltpu.VMEM(state.shape, f32),
                pltpu.VMEM(source.shape, f32),
                pltpu.VMEM(floor.shape, jnp.int32),
                pltpu.VMEM(region.shape, jnp.int32),
                pltpu.SMEM(lame.shape, f32),
                pltpu.SMEM(shear.shape, f32),
                pltpu.SMEM(buoy.shape, f32),
                pltpu.VMEM((3, 6, 10 * BLOCK, 128), f32),
                pltpu.VMEM((3, 3, 10 * BLOCK, 128), f32),
                pltpu.VMEM((3, 64, 128), f32),
                pltpu.VMEM((3, 64, 128), f32),
                pltpu.VMEM((3, 64, 128), f32),
                pltpu.VMEM((3, 8 * STEPS, 128), f32),
                tiles(2, 3),
                tiles(2, 3),
                tiles(2, 3),
                tiles(2, 3),
                tiles(2, 3),
                tiles(2, 113),
                tiles(2, 120),
                pltpu.VMEM((2, 3 * STEPS - 3, 2, 2, 128), f32),
                tiles(2, 14),
                tiles(2, 12),
                tiles(2, 9),
                tiles(2, 3, 2, 6),
                tiles(2, 3, 2, 6),
                pltpu.VMEM((2, 3, 2, 2, 2, 128), f32),
                pltpu.SemaphoreType.DMA((7,)),
                pltpu.SemaphoreType.DMA((2,)),
                pltpu.SemaphoreType.DMA((2,)),
                pltpu.SemaphoreType.DMA((2,)),
                pltpu.SemaphoreType.DMA((3, 2)),
                pltpu.SemaphoreType.DMA((3,)),
                pltpu.SemaphoreType.DMA((1,)),
                pltpu.SemaphoreType.DMA((2, 3, 2)),
                pltpu.SemaphoreType.DMA((2, 3)),
                pltpu.SemaphoreType.DMA((2, 3, 2)),
            ],
            compiler_params=pltpu.CompilerParams(
                collective_id=0, has_side_effects=True, vmem_limit_bytes=32 * 1024 * 1024
            ),
        )(*(
            pltpu.with_memory_space_constraint(v, pltpu.HBM)
            for v in (state, source, floor, region, lame, shear, buoy)
        ))

    return jax.shard_map(
        on_device,
        mesh=mesh,
        in_specs=(
            P(None, "dom", "gx", "gy"),
            P(None, "gx", "gy"),
            P("gx", "gy"),
            P("dom", "gx", "gy"),
            P(),
            P(),
            P(),
        ),
        out_specs=P(None, "dom", "gx", "gy"),
        check_vma=False,
    )
```

```python
import functools

import jax
import jax.numpy as jnp
from jax import lax
from jax.experimental import pallas as pl
from jax.experimental.pallas import tpu as pltpu
from jax.sharding import PartitionSpec as P

STEPS = 6
COURANT = 0.25
REGIONS = 16
NEED = 106
SPARE = 128 - NEED
BLOCK = 16
WIDE = 12
MIDDLE, LEFT, RIGHT = 0, 1, 2
FIRST_CUT, SECOND_CUT, SEAM = 86, 171 - 128, 64
MESH = pl.DeviceIdType.MESH

f32 = jnp.float32


def rows(z, x=0):
    return (z + 1) * BLOCK + 8 + x


def level(z):
    return pl.ds(rows(z), 8)


def column(x):
    return pl.ds(rows(0, x), 8, stride=BLOCK)


def dy(v):
    return pltpu.roll(v, 127, 1) - pltpu.roll(v, 1, 1)


def pick(bits, table):
    values = list(table)
    for bit in bits:
        values = [jnp.where(bit, values[2 * i + 1], values[2 * i]) for i in range(len(values) // 2)]
    return values[0]


def kernel(
    sizes, state_in, source_in, floor_in, region_in, lame_in, shear_in, buoy_in, out,
    state, source, floor, region, lame, shear, buoy,
    S, V, L, M, B, SRC, LX, MX, SX, LZ, MZ, OX, OZ, OE, XR0, ZR0, YR, XR, ZR, ER,
    in_sem, x_send, z_send, e_send, x_first_recv, z_first_recv, y_recv, x_recv, z_recv, e_recv,
):
    n_dom, n_gx, n_gy = sizes
    dom, gx, gy = lax.axis_index("dom"), lax.axis_index("gx"), lax.axis_index("gy")
    lane = lax.broadcasted_iota(jnp.int32, (8, 128), 1)
    sub = lax.broadcasted_iota(jnp.int32, (8, 128), 0)
    zero = jnp.zeros((8, 128), f32)

    loads = [
        pltpu.make_async_copy(src, dst, in_sem.at[i])
        for i, (src, dst) in enumerate((
            (region_in, region), (floor_in, floor), (source_in, source), (state_in, state),
            (lame_in, lame), (shear_in, shear), (buoy_in, buoy)))
    ]
    for load in loads:
        load.start()

    sides = (-1, 1)
    there = [gx > 0, gx < n_gx - 1]
    z_there = [dom > 0, dom < n_dom - 1]

    doms = [dom, jnp.where(dom == n_dom - 1, 0, dom + 1), jnp.where(dom == 0, n_dom - 1, dom - 1)]
    gxs = [gx, gx + 1, gx - 1]
    gys = [gy, jnp.where(gy == n_gy - 1, 0, gy + 1), jnp.where(gy == 0, n_gy - 1, gy - 1)]

    def at(dz, dx, dyy):
        return (doms[dz], gxs[dx], gys[dyy])

    def reach(i, then):
        pl.when(there[i])(then)

    barrier = pltpu.get_barrier_semaphore()

    def greet(*way):
        pl.semaphore_signal(barrier, inc=1, device_id=at(*way), device_id_type=MESH)

    for i, dx in enumerate(sides):
        @functools.partial(reach, i)
        def _(dx=dx):
            for way in ((0, dx, 0), (-1, dx, 0), (1, dx, 0), (0, dx, -1), (0, dx, 1)):
                greet(*way)
    for way in [(a, 0, b) for a in (-1, 0, 1) for b in (-1, 0, 1) if a or b]:
        greet(*way)

    for i in range(2):
        @pl.when(jnp.logical_not(there[i]))
        def _(i=i):
            XR0[i] = jnp.zeros(XR0.shape[1:], f32)
            for slot in range(2):
                for p in range(3):
                    XR[slot, p, i] = jnp.zeros(XR.shape[3:], f32)
                    ER[slot, p, i] = jnp.zeros(ER.shape[3:], f32)

    for p in range(3):
        for f in range(3):
            for z in range(-1, 9):
                V[p, f, pl.ds(rows(z, -8), 8), :] = zero
            for z in (-1, 8):
                V[p, f, level(z), :] = zero

    for load in loads[:4]:
        load.wait()

    def side_by_side(parts, t):
        tile = zero
        for k, v in enumerate(parts):
            shift = (WIDE * k + (WIDE if t else 0)) % 128
            v = pltpu.roll(v, shift, 1) if shift else v
            tile = jnp.where((lane >= WIDE * k) & (lane < WIDE * (k + 1)), v, tile)
        return tile

    def cut(t):
        return slice(128 * t, 128 * t + 128)

    def remote(src, dst, send, recv, way):
        return pltpu.make_async_remote_copy(
            src_ref=src, dst_ref=dst, send_sem=send, recv_sem=recv, device_id=at(*way), device_id_type=MESH)

    def xa_first(i):
        return remote(OX.at[i, 0:6], XR0.at[1 - i, 0:6], x_send.at[i], x_first_recv.at[0, 1 - i], (0, sides[i], 0))

    def xy_first(i, j):
        return remote(
            OX.at[i, 6 + j], XR0.at[1 - i, 7 - j], x_send.at[i], x_first_recv.at[2, 1 - i], (0, sides[i], sides[j]))

    def xb_first(i):
        return remote(OX.at[i, 8:14], XR0.at[1 - i, 8:14], x_send.at[i], x_first_recv.at[1, 1 - i], (0, sides[i], 0))

    def za_first(i):
        return remote(OZ.at[i, 0:6], ZR0.at[1 - i, 0:6], z_send.at[i], z_first_recv.at[0], (sides[i], 0, 0))

    def zy_first(i, j):
        return remote(
            OZ.at[i, 6 + j], ZR0.at[1 - i, 7 - j], z_send.at[i], z_first_recv.at[2], (sides[i], 0, sides[j]))

    def zb_first(i):
        return remote(OZ.at[i, 8:12], ZR0.at[1 - i, 8:12], z_send.at[i], z_first_recv.at[1], (sides[i], 0, 0))

    def y_first(i):
        return remote(OZ.at[i, 111:120], YR.at[1 - i], z_send.at[i], y_recv.at[0], (0, 0, sides[i]))

    def arrived(ref, sem):
        pltpu.make_async_copy(ref, ref, sem).wait()

    def put(ref, index, pair):
        ref[(MIDDLE, *index)] = jnp.where(lane < SEAM, pair[1], pair[0])
        ref[(LEFT, *index)] = pair[0]
        ref[(RIGHT, *index)] = pair[1]

    def put_margin(ref, index, v):
        ref[(LEFT, *index)] = jnp.where(lane >= 128 - WIDE, v, ref[(LEFT, *index)])
        ref[(RIGHT, *index)] = jnp.where(lane < WIDE, v, ref[(RIGHT, *index)])

    everywhere = slice(None)
    for z in range(8):
        solid = [(dom * 8 + z) >= floor[:, cut(t)] for t in range(2)]
        for f in range(6):
            v = [state[3 + f, z, :, cut(t)] for t in range(2)]
            if f >= 3:
                v = [jnp.where(m, w, 0.0) for m, w in zip(solid, v)]
            elif z == 0:
                v = [w + jnp.where(dom == 0, source[0, :, cut(t)], 0.0) for t, w in enumerate(v)]
            put(S, (f, level(z), everywhere), v)
    x_fields, z_fields = (0, 3, 4), (2, 4, 5)
    pair = (LEFT, RIGHT)
    for i, at_edge in enumerate((0, 7)):
        for k in range(3):
            for t in range(2):
                OX[i, 2 * k + t] = S[pair[t], x_fields[k], column(at_edge), :]
                OZ[i, 2 * k + t] = S[pair[t], z_fields[k], level(at_edge), :]
    for i in range(2):
        for z in range(8):
            OZ[i, 111 + z] = side_by_side(
                [state[f, z, :, cut(i)] for f in range(9)] + [region[z, :, cut(i)].astype(f32)], i)
        OZ[i, 119] = side_by_side([source[s, :, cut(i)] for s in range(STEPS)] + [floor[:, cut(i)].astype(f32)], i)

    pl.semaphore_wait(barrier, 8 + 5 * (there[0].astype(jnp.int32) + there[1].astype(jnp.int32)))
    for i in range(2):
        @functools.partial(reach, i)
        def _(i=i):
            xa_first(i).start()
    for i in range(2):
        za_first(i).start()
        y_first(i).start()

    for load in loads[4:]:
        load.wait()
    scale = 0.5 * COURANT
    tables = [[t[k] * scale for k in range(REGIONS)] for t in (lame, shear, buoy)]

    def materials(number, seafloor, z):
        bits = [(number & (1 << k)) != 0 for k in range(4)]
        solid = (dom * 8 + z) >= seafloor
        lam, mu, b = (pick(bits, t) for t in tables)
        return lam, jnp.where(solid, mu, 0.0), b, solid

    for s in range(STEPS):
        put(SRC, (pl.ds(8 * s, 8), everywhere),
            [jnp.where(dom == 0, source[s, :, cut(t)], 0.0) for t in range(2)])
    for z in range(8):
        made = [materials(region[z, :, cut(t)], floor[:, cut(t)], z) for t in range(2)]
        for k, ref in enumerate((L, M, B)):
            put(ref, (pl.ds(8 * z, 8), everywhere), [m[k] for m in made])
        for f in range(3):
            put(V, (f, level(z), everywhere), [state[f, z, :, cut(t)] for t in range(2)])

    for i, x in ((0, 0), (1, 7)):
        parts = [[OX[i, 2 * k + t] for t in range(2)] for k in range(3)]
        parts += [[m[p, pl.ds(x, 8, stride=8), :] for p in pair] for m in (L, M)]
        parts += [[
            jnp.concatenate([SRC[p, pl.ds(x, STEPS, stride=8), :], jnp.zeros((8 - STEPS, 128), f32)], 0) for p in pair]]
        for k in range(3, 6):
            for t in range(2):
                OX[i, 2 * k + t + 2] = parts[k][t]
        for j in range(2):
            OX[i, 6 + j] = side_by_side([v[j] for v in parts], j)

        @functools.partial(reach, i)
        def _(i=i):
            for j in range(2):
                xy_first(i, j).start()
            xb_first(i).start()
    for i, z in ((0, 0), (1, 7)):
        parts = [[OZ[i, 2 * k + t] for t in range(2)] for k in range(3)]
        parts += [[m[p, pl.ds(8 * z, 8), :] for p in pair] for m in (L, M)]
        for k in range(3, 5):
            for t in range(2):
                OZ[i, 2 * k + t + 2] = parts[k][t]
        for j in range(2):
            OZ[i, 6 + j] = side_by_side([v[j] for v in parts], j)
            zy_first(i, j).start()
        zb_first(i).start()

    left = (lane >= 128 - WIDE) & (gy > 0)
    right = (lane < WIDE) & (gy < n_gy - 1)
    inside = left | right

    def margin(low, high, f):
        shift_r = (128 - WIDE * f) % 128
        shift_l = (256 - WIDE - WIDE * f) % 128
        a = pltpu.roll(high, shift_r, 1) if shift_r else high
        c = pltpu.roll(low, shift_l, 1) if shift_l else low
        return jnp.where(left, c, jnp.where(right, a, 0.0))

    arrived(ZR0.at[:, 0:6], z_first_recv.at[0])
    for i in range(2):
        @functools.partial(reach, i)
        def _(i=i):
            arrived(XR0.at[i, 0:6], x_first_recv.at[0, i])

    def three(first_tile, second_tile, edge):
        return (
            jnp.where(lane < SEAM, second_tile, first_tile),
            jnp.where(lane >= 128 - WIDE, edge, first_tile),
            jnp.where(lane < WIDE, edge, second_tile),
        )

    def border(parts):
        for i, x in ((0, -1), (1, 8)):
            for k, f in enumerate(x_fields):
                edge = zero if parts == (MIDDLE,) else margin(XR0[i, 6], XR0[i, 7], k)
                tiles = three(XR0[i, 2 * k], XR0[i, 2 * k + 1], edge)
                for p in parts:
                    S[p, f, column(x), :] = tiles[p]
        for i, z in ((0, -1), (1, 8)):
            for k, f in enumerate(z_fields):
                edge = zero if parts == (MIDDLE,) else margin(ZR0[i, 6], ZR0[i, 7], k)
                tiles = three(ZR0[i, 2 * k], ZR0[i, 2 * k + 1], edge)
                for p in parts:
                    S[p, f, level(z), :] = jnp.where(z_there[i], tiles[p], 0.0)

    border((MIDDLE,))
    def place(p):
        return (lane + (52 - 42 * p)) & 127

    def squeeze(where, row, k, sixth):
        return jnp.where(where < NEED, row, pltpu.roll(sixth, NEED - SPARE * k, 1))

    def restore(where, tiles):
        sixth = pltpu.roll(tiles[4], 5 * SPARE, 1)
        for k in range(4):
            sixth = jnp.where((where >= SPARE * k) & (where < SPARE * (k + 1)), pltpu.roll(tiles[k], SPARE * (k + 1), 1), sixth)
        return sixth

    def x_base(p, s, last):
        return 14 + 15 * s + (3 * p if last else 5 * p)

    def z_base(p, s, last):
        return 12 + 18 * s + (3 * p if last else 6 * p)

    def x_copy(p, i, s, slot, last):
        n = 3 if last else 5
        return remote(
            OX.at[i, pl.ds(x_base(p, s, last), n)], XR.at[slot, p, 1 - i, 0:n], x_send.at[i], x_recv.at[slot, p, 1 - i],
            (0, sides[i], 0))

    def e_copy(p, i, j, s, slot):
        return remote(
            OE.at[i, 3 * s + p, j], ER.at[slot, p, 1 - i, 1 - j], e_send.at[i],
            e_recv.at[slot, p, 1 - i], (sides[j], sides[i], 0))

    def z_copy(p, i, s, slot, last):
        n = 3 if last else 6
        return remote(
            OZ.at[i, pl.ds(z_base(p, s, last), n)], ZR.at[slot, p, 1 - i, 0:n], z_send.at[i], z_recv.at[slot, p],
            (sides[i], 0, 0))

    def move(p, s, slot, last=False):
        def accelerate(levels):
            moved = []
            for z in levels:
                own = level(z)
                after, before = pl.ds(rows(z, 1), 8), pl.ds(rows(z, -1), 8)
                above, below = level(z + 1), level(z - 1)

                def dx(f):
                    return S[p, f, after, :] - S[p, f, before, :]

                def dz(f):
                    return S[p, f, above, :] - S[p, f, below, :]

                b = B[p, pl.ds(8 * z, 8), :]
                moved.append((0, own, V[p, 0, own, :] - b * (dx(0) + dy(S[p, 3, own, :]) + dz(4))))
                moved.append((1, own, V[p, 1, own, :] - b * (dx(3) + dy(S[p, 1, own, :]) + dz(5))))
                moved.append((2, own, V[p, 2, own, :] - b * (dx(4) + dy(S[p, 5, own, :]) + dz(2))))
            for f, own, v in moved:
                V[p, f, own, :] = v

        accelerate((0, 7))
        if not last:
            for i, x in ((0, 0), (1, 7)):
                for j in range(2):
                    for k, f in enumerate((0, 2)):
                        OE[i, 3 * s + p, j, k : k + 1, :] = V[p, f, pl.ds(rows(7 * j, x), 1), :]

                @functools.partial(reach, i)
                def _(i=i):
                    for j in range(2):
                        e_copy(p, i, j, s, slot).start()
        accelerate((1, 2, 3))
        accelerate((4, 5, 6))
        base = x_base(p, s, last)
        for i, (x, inner) in enumerate(((0, 1), (7, 6))):
            near = [V[p, f, column(x), :] for f in range(3)]
            if last:
                tiles_out = near
            else:
                far = [V[p, f, column(inner), :] for f in range(3)]
                where = place(p)
                tiles_out = [squeeze(where, v, k, far[1]) for k, v in enumerate(near + [far[0], far[2]])]
            for k, v in enumerate(tiles_out):
                OX[i, base + k] = v

            @functools.partial(reach, i)
            def _(i=i):
                x_copy(p, i, s, slot, last).start()
        base = z_base(p, s, last)
        for i, (z, inner) in enumerate(((0, 1), (7, 6))):
            for f in range(3):
                OZ[i, base + f] = V[p, f, level(z), :]
                if not last:
                    OZ[i, base + 3 + f] = V[p, f, level(inner), :]
            z_copy(p, i, s, slot, last).start()

        later = []
        for z in range(8):
            own = level(z)
            after, before = pl.ds(rows(z, 1), 8), pl.ds(rows(z, -1), 8)
            above, below = level(z + 1), level(z - 1)
            dxs = [V[p, f, after, :] - V[p, f, before, :] for f in range(3)]
            dzs = [V[p, f, above, :] - V[p, f, below, :] for f in range(3)]
            dys = [dy(V[p, f, own, :]) for f in range(3)]
            lam, mu = L[p, pl.ds(8 * z, 8), :], M[p, pl.ds(8 * z, 8), :]
            spread = lam * (dxs[0] + dys[1] + dzs[2])
            mu2 = mu + mu
            change = (
                spread + mu2 * dxs[0], spread + mu2 * dys[1], spread + mu2 * dzs[2],
                mu * (dys[0] + dxs[1]), mu * (dzs[0] + dxs[2]), mu * (dzs[1] + dys[2]))
            later += [(f, own, S[p, f, own, :] - change[f]) for f in range(6)]
            if z % 2:
                write(p, later)
                later = []

    def write(p, results):
        for f, at_rows, v in results:
            S[p, f, at_rows, :] = v

    def finish(p, slot, then=None):
        last = then is None
        if not last:
            added = SRC[p, pl.ds(8 * then if isinstance(then, int) else pl.multiple_of(8 * then, 8), 8), :]
            results = [(f, level(0), S[p, f, level(0), :] + added) for f in range(3)]
            for i, x in ((0, -1), (1, 8)):
                outer = pl.ds(rows(0, x), 1)
                results.append((0, outer, S[p, 0, outer, :] + SX[i, p, pl.ds(then, 1), :]))
            write(p, results)
        arrived(ZR.at[slot, p, :, 0:3] if last else ZR.at[slot, p], z_recv.at[slot, p])
        results = []
        for i, z in ((0, 0), (1, 7)):
            near = [ZR[slot, p, i, f] for f in range(3)]
            own = level(z)
            lam, mu = L[p, pl.ds(8 * z, 8), :], M[p, pl.ds(8 * z, 8), :]
            sign = jnp.where(z_there[i], (-1.0, 1.0)[i], 0.0)
            slope = [sign * v for v in near]
            spread = lam * slope[2]
            results.append((0, own, S[p, 0, own, :] - (spread)))
            results.append((1, own, S[p, 1, own, :] - (spread)))
            results.append((2, own, S[p, 2, own, :] - (spread + (mu + mu) * slope[2])))
            results.append((4, own, S[p, 4, own, :] - (mu * slope[0])))
            results.append((5, own, S[p, 5, own, :] - (mu * slope[1])))
        write(p, results)

        for i in range(2):
            @functools.partial(reach, i)
            def _(i=i):
                arrived(XR.at[slot, p, i, 0:3] if last else XR.at[slot, p, i], x_recv.at[slot, p, i])

        results = []
        for i, x, sign in ((0, 0, -1.0), (1, 7, 1.0)):
            near = [XR[slot, p, i, f] for f in range(3)]
            lam, mu = L[p, pl.ds(x, 8, stride=8), :], M[p, pl.ds(x, 8, stride=8), :]
            slope = [sign * v for v in near]
            spread = lam * slope[0]
            results.append((0, column(x), S[p, 0, column(x), :] - (spread + (mu + mu) * slope[0])))
            results.append((1, column(x), S[p, 1, column(x), :] - (spread)))
            results.append((2, column(x), S[p, 2, column(x), :] - (spread)))
            results.append((3, column(x), S[p, 3, column(x), :] - (mu * slope[1])))
            results.append((4, column(x), S[p, 4, column(x), :] - (mu * slope[2])))

        if last:
            write(p, results)
            return
        for i, x, sign in ((0, 0, -1.0), (1, 7, 1.0)):
            got = [XR[slot, p, i, k] for k in range(5)]
            near, far = got[0:3], (got[3], restore(place(p), got), got[4])
            lam, mu = LX[i, p], MX[i, p]
            dxs = [sign * (far[f] - V[p, f, column(x), :]) for f in range(3)]
            dzs = {}
            for f in (0, 2):
                up, down = pltpu.roll(near[f], 7, 0), pltpu.roll(near[f], 1, 0)
                dzs[f] = jnp.where(sub == 7, 0.0, up) - jnp.where(sub == 0, 0.0, down)
            trace = dxs[0] + dy(near[1]) + dzs[2]
            beyond = column((-1, 8)[i])
            results.append((0, beyond, S[p, 0, beyond, :] - (lam * trace + (mu + mu) * dxs[0])))
            results.append((3, beyond, S[p, 3, beyond, :] - (mu * (dy(near[0]) + dxs[1]))))
            results.append((4, beyond, S[p, 4, beyond, :] - (mu * (dzs[0] + dxs[2]))))
        for i, z, sign in ((0, 0, -1.0), (1, 7, 1.0)):
            near, far = [ZR[slot, p, i, f] for f in range(3)], [ZR[slot, p, i, 3 + f] for f in range(3)]
            lam, mu = LZ[i, p], MZ[i, p]
            dzs = [sign * (far[f] - V[p, f, level(z), :]) for f in range(3)]
            dxs = {}
            for f in (0, 2):
                ahead, behind = pltpu.roll(near[f], 7, 0), pltpu.roll(near[f], 1, 0)
                dxs[f] = jnp.where(sub == 7, 0.0, ahead) - jnp.where(sub == 0, 0.0, behind)
            trace = dxs[0] + dy(near[1]) + dzs[2]
            beyond = level((-1, 8)[i])
            results.append((2, beyond, S[p, 2, beyond, :] - (lam * trace + (mu + mu) * dzs[2])))
            results.append((4, beyond, S[p, 4, beyond, :] - (mu * (dzs[0] + dxs[2]))))
            results.append((5, beyond, S[p, 5, beyond, :] - (mu * (dzs[1] + dy(near[2])))))

        write(p, results)

        for i in range(2):
            @functools.partial(reach, i)
            def _(i=i):
                arrived(ER.at[slot, p, i], e_recv.at[slot, p, i])
        results = []
        for i, x in ((0, 0), (1, 7)):
            for j, z in ((0, 0), (1, 7)):
                edge_x, edge_z = (ER[slot, p, i, j, k : k + 1, :] for k in range(2))
                sign = jnp.where(z_there[j], (-1.0, 1.0)[j], 0.0)
                outer = pl.ds(rows(z, (-1, 8)[i]), 1)
                at_z, at_x = slice(z, z + 1), slice(x, x + 1)
                results.append((0, outer, S[p, 0, outer, :] - (LX[i, p, at_z, :] * (sign * edge_z))))
                results.append((4, outer, S[p, 4, outer, :] - (MX[i, p, at_z, :] * (sign * edge_x))))
                outer = pl.ds(rows((-1, 8)[j], x), 1)
                results.append((2, outer, S[p, 2, outer, :] - (LZ[j, p, at_x, :] * (sides[i] * edge_x))))
                results.append((4, outer, S[p, 4, outer, :] - (MZ[j, p, at_x, :] * (sides[i] * edge_z))))
        write(p, results)

    def each_part(then):
        for p in range(3):
            then(p)

    move(MIDDLE, 0, 0)

    arrived(YR, y_recv.at[0])
    low, high = YR[0, 8], YR[1, 8]
    seafloor = margin(low, high, STEPS).astype(jnp.int32)
    first_source = None
    for s in range(STEPS):
        v = jnp.where(dom == 0, margin(low, high, s), 0.0)
        first_source = v if s == 0 else first_source
        put_margin(SRC, (pl.ds(8 * s, 8), everywhere), v)
    for z in range(8):
        low, high = YR[0, z], YR[1, z]
        lam, mu, b, solid = materials(margin(low, high, 9).astype(jnp.int32), seafloor, z)
        for ref, v in ((L, lam), (M, mu), (B, b)):
            put_margin(ref, (pl.ds(8 * z, 8), everywhere), jnp.where(inside, v, 0.0))
        for f in range(9):
            v = margin(low, high, f)
            if f < 3:
                put_margin(V, (f, level(z), everywhere), v)
            else:
                if f >= 6:
                    v = jnp.where(solid, v, 0.0)
                elif z == 0:
                    v = v + first_source
                put_margin(S, (f - 3, level(z), everywhere), v)

    arrived(ZR0.at[:, 6:8], z_first_recv.at[2])
    for i in range(2):
        @functools.partial(reach, i)
        def _(i=i):
            arrived(XR0.at[i, 6:8], x_first_recv.at[2, i])
    border((LEFT, RIGHT))

    move(LEFT, 0, 0)
    move(RIGHT, 0, 0)

    arrived(ZR0.at[:, 8:12], z_first_recv.at[1])
    for i in range(2):
        @functools.partial(reach, i)
        def _(i=i):
            arrived(XR0.at[i, 8:14], x_first_recv.at[1, i])
    for i in range(2):
        for k, ref in enumerate((LX, MX, SX)):
            tiles = three(XR0[i, 8 + 2 * k], XR0[i, 9 + 2 * k], margin(XR0[i, 6], XR0[i, 7], 3 + k))
            for p in range(3):
                ref[i, p] = tiles[p]
        for k, ref in enumerate((LZ, MZ)):
            tiles = three(ZR0[i, 8 + 2 * k], ZR0[i, 9 + 2 * k], margin(ZR0[i, 6], ZR0[i, 7], 3 + k))
            for p in range(3):
                ref[i, p] = jnp.where(z_there[i], tiles[p], 0.0)

    def step(s, carry):
        slot = lax.rem(s, 2)

        def turn(p):
            finish(p, 1 - slot, s)
            move(p, s, slot)

        each_part(turn)
        return carry

    lax.fori_loop(1, STEPS - 1, step, 0)

    end = STEPS - 1

    def final(p):
        finish(p, (end - 1) % 2, end)
        move(p, end, end % 2, last=True)

    each_part(final)

    def gather(f, ref, k):
        for z in range(8):
            middle, first_tile, second_tile = (ref[p, k, level(z), :] for p in (MIDDLE, LEFT, RIGHT))
            out[f, z, :, cut(0)] = jnp.where(lane < FIRST_CUT, first_tile, middle)
            out[f, z, :, cut(1)] = jnp.where(lane < SECOND_CUT, middle, second_tile)

    for f in range(3):
        gather(f, V, f)
    each_part(lambda p: finish(p, end % 2))
    for f in range(6):
        gather(3 + f, S, f)

    for i in range(2):
        arrived(OZ.at[i], z_send.at[i])

        @functools.partial(reach, i)
        def _(i=i):
            arrived(OX.at[i], x_send.at[i])
            arrived(OE.at[i], e_send.at[i])


def solution(mesh):
    sizes = (mesh.shape["dom"], mesh.shape["gx"], mesh.shape["gy"])

    def on_device(state, source, floor, region, lame, shear, buoy):
        hbm = pl.BlockSpec(memory_space=pltpu.HBM)

        def tiles(*shape):
            return pltpu.VMEM(shape + (8, 128), f32)

        return pl.pallas_call(
            functools.partial(kernel, sizes),
            out_shape=jax.ShapeDtypeStruct(state.shape, f32),
            in_specs=[hbm] * 7,
            out_specs=pl.BlockSpec(memory_space=pltpu.VMEM),
            scratch_shapes=[
                pltpu.VMEM(state.shape, f32),
                pltpu.VMEM(source.shape, f32),
                pltpu.VMEM(floor.shape, jnp.int32),
                pltpu.VMEM(region.shape, jnp.int32),
                pltpu.SMEM(lame.shape, f32),
                pltpu.SMEM(shear.shape, f32),
                pltpu.SMEM(buoy.shape, f32),
                pltpu.VMEM((3, 6, 10 * BLOCK, 128), f32),
                pltpu.VMEM((3, 3, 10 * BLOCK, 128), f32),
                pltpu.VMEM((3, 64, 128), f32),
                pltpu.VMEM((3, 64, 128), f32),
                pltpu.VMEM((3, 64, 128), f32),
                pltpu.VMEM((3, 8 * STEPS, 128), f32),
                tiles(2, 3),
                tiles(2, 3),
                tiles(2, 3),
                tiles(2, 3),
                tiles(2, 3),
                tiles(2, 98),
                tiles(2, 120),
                pltpu.VMEM((2, 3 * STEPS - 3, 2, 2, 128), f32),
                tiles(2, 14),
                tiles(2, 12),
                tiles(2, 9),
                tiles(2, 3, 2, 5),
                tiles(2, 3, 2, 6),
                pltpu.VMEM((2, 3, 2, 2, 2, 128), f32),
                pltpu.SemaphoreType.DMA((7,)),
                pltpu.SemaphoreType.DMA((2,)),
                pltpu.SemaphoreType.DMA((2,)),
                pltpu.SemaphoreType.DMA((2,)),
                pltpu.SemaphoreType.DMA((3, 2)),
                pltpu.SemaphoreType.DMA((3,)),
                pltpu.SemaphoreType.DMA((1,)),
                pltpu.SemaphoreType.DMA((2, 3, 2)),
                pltpu.SemaphoreType.DMA((2, 3)),
                pltpu.SemaphoreType.DMA((2, 3, 2)),
            ],
            compiler_params=pltpu.CompilerParams(
                collective_id=0, has_side_effects=True, vmem_limit_bytes=32 * 1024 * 1024
            ),
        )(*(
            pltpu.with_memory_space_constraint(v, pltpu.HBM)
            for v in (state, source, floor, region, lame, shear, buoy)
        ))

    return jax.shard_map(
        on_device,
        mesh=mesh,
        in_specs=(
            P(None, "dom", "gx", "gy"),
            P(None, "gx", "gy"),
            P("gx", "gy"),
            P("dom", "gx", "gy"),
            P(),
            P(),
            P(),
        ),
        out_specs=P(None, "dom", "gx", "gy"),
        check_vma=False,
    )
```

```python
import functools

import jax
import jax.numpy as jnp
from jax import lax
from jax.experimental import pallas as pl
from jax.experimental.pallas import tpu as pltpu
from jax.sharding import PartitionSpec as P

STEPS = 6
COURANT = 0.25
REGIONS = 16
BLOCK = 16
WIDE = 12
MIDDLE, LEFT, RIGHT = 0, 1, 2
FIRST_CUT, SECOND_CUT, SEAM = 86, 171 - 128, 64
MESH = pl.DeviceIdType.MESH

f32 = jnp.float32


def rows(z, x=0):
    return (z + 1) * BLOCK + 8 + x


def level(z):
    return pl.ds(rows(z), 8)


def column(x):
    return pl.ds(rows(0, x), 8, stride=BLOCK)


def dy(v):
    return pltpu.roll(v, 127, 1) - pltpu.roll(v, 1, 1)


def pick(bits, table):
    values = list(table)
    for bit in bits:
        values = [jnp.where(bit, values[2 * i + 1], values[2 * i]) for i in range(len(values) // 2)]
    return values[0]


def kernel(
    sizes, state_in, source_in, floor_in, region_in, lame_in, shear_in, buoy_in, out,
    state, source, floor, region, lame, shear, buoy,
    S, V, L, M, B, SRC, LX, MX, SX, LZ, MZ, OX, OZ, OE, XR0, ZR0, YR, XR, ZR, ER,
    in_sem, x_send, z_send, e_send, x_first_recv, z_first_recv, y_recv, x_recv, z_recv, e_recv,
):
    n_dom, n_gx, n_gy = sizes
    dom, gx, gy = lax.axis_index("dom"), lax.axis_index("gx"), lax.axis_index("gy")
    lane = lax.broadcasted_iota(jnp.int32, (8, 128), 1)
    sub = lax.broadcasted_iota(jnp.int32, (8, 128), 0)
    zero = jnp.zeros((8, 128), f32)

    loads = [
        pltpu.make_async_copy(src, dst, in_sem.at[i])
        for i, (src, dst) in enumerate((
            (floor_in, floor), (state_in.at[3:6], state.at[3:6]), (state_in.at[6:9], state.at[6:9]),
            (state_in.at[0:3], state.at[0:3]), (region_in, region), (source_in, source),
            (lame_in, lame), (shear_in, shear), (buoy_in, buoy)))
    ]
    for load in loads:
        load.start()

    sides = (-1, 1)
    there = [gx > 0, gx < n_gx - 1]
    z_there = [dom > 0, dom < n_dom - 1]

    doms = [dom, jnp.where(dom == n_dom - 1, 0, dom + 1), jnp.where(dom == 0, n_dom - 1, dom - 1)]
    gxs = [gx, gx + 1, gx - 1]
    gys = [gy, jnp.where(gy == n_gy - 1, 0, gy + 1), jnp.where(gy == 0, n_gy - 1, gy - 1)]

    def at(dz, dx, dyy):
        return (doms[dz], gxs[dx], gys[dyy])

    def reach(i, then):
        pl.when(there[i])(then)

    barrier = pltpu.get_barrier_semaphore()

    def greet(*way):
        pl.semaphore_signal(barrier, inc=1, device_id=at(*way), device_id_type=MESH)

    for i, dx in enumerate(sides):
        @functools.partial(reach, i)
        def _(dx=dx):
            for way in ((0, dx, 0), (-1, dx, 0), (1, dx, 0), (0, dx, -1), (0, dx, 1)):
                greet(*way)
    for way in [(a, 0, b) for a in (-1, 0, 1) for b in (-1, 0, 1) if a or b]:
        greet(*way)

    for i in range(2):
        @pl.when(jnp.logical_not(there[i]))
        def _(i=i):
            XR0[i] = jnp.zeros(XR0.shape[1:], f32)
            for slot in range(2):
                for p in range(3):
                    XR[slot, p, i] = jnp.zeros(XR.shape[3:], f32)
                    ER[slot, p, i] = jnp.zeros(ER.shape[3:], f32)

    for p in range(3):
        for f in range(3):
            for z in range(-1, 9):
                V[p, f, pl.ds(rows(z, -8), 8), :] = zero
            for z in (-1, 8):
                V[p, f, level(z), :] = zero

    for load in loads[:6]:
        load.wait()

    def side_by_side(parts, t):
        tile = zero
        for k, v in enumerate(parts):
            shift = (WIDE * k + (WIDE if t else 0)) % 128
            v = pltpu.roll(v, shift, 1) if shift else v
            tile = jnp.where((lane >= WIDE * k) & (lane < WIDE * (k + 1)), v, tile)
        return tile

    def cut(t):
        return slice(128 * t, 128 * t + 128)

    def remote(src, dst, send, recv, way):
        return pltpu.make_async_remote_copy(
            src_ref=src, dst_ref=dst, send_sem=send, recv_sem=recv, device_id=at(*way), device_id_type=MESH)

    def xa_first(i):
        return remote(OX.at[i, 0:6], XR0.at[1 - i, 0:6], x_send.at[i], x_first_recv.at[0, 1 - i], (0, sides[i], 0))

    def xy_first(i, j):
        return remote(
            OX.at[i, 6 + j], XR0.at[1 - i, 7 - j], x_send.at[i], x_first_recv.at[2, 1 - i], (0, sides[i], sides[j]))

    def xb_first(i):
        return remote(OX.at[i, 8:14], XR0.at[1 - i, 8:14], x_send.at[i], x_first_recv.at[1, 1 - i], (0, sides[i], 0))

    def za_first(i):
        return remote(OZ.at[i, 0:6], ZR0.at[1 - i, 0:6], z_send.at[i], z_first_recv.at[0], (sides[i], 0, 0))

    def zy_first(i, j):
        return remote(
            OZ.at[i, 6 + j], ZR0.at[1 - i, 7 - j], z_send.at[i], z_first_recv.at[2], (sides[i], 0, sides[j]))

    def zb_first(i):
        return remote(OZ.at[i, 8:12], ZR0.at[1 - i, 8:12], z_send.at[i], z_first_recv.at[1], (sides[i], 0, 0))

    def y_first(i):
        return remote(OZ.at[i, 111:120], YR.at[1 - i], z_send.at[i], y_recv.at[0], (0, 0, sides[i]))

    def arrived(ref, sem):
        pltpu.make_async_copy(ref, ref, sem).wait()

    def put(ref, index, pair):
        ref[(MIDDLE, *index)] = jnp.where(lane < SEAM, pair[1], pair[0])
        ref[(LEFT, *index)] = pair[0]
        ref[(RIGHT, *index)] = pair[1]

    def put_margin(ref, index, v):
        ref[(LEFT, *index)] = jnp.where(lane >= 128 - WIDE, v, ref[(LEFT, *index)])
        ref[(RIGHT, *index)] = jnp.where(lane < WIDE, v, ref[(RIGHT, *index)])

    everywhere = slice(None)
    for z in range(8):
        solid = [(dom * 8 + z) >= floor[:, cut(t)] for t in range(2)]
        for f in range(6):
            v = [state[3 + f, z, :, cut(t)] for t in range(2)]
            if f >= 3:
                v = [jnp.where(m, w, 0.0) for m, w in zip(solid, v)]
            elif z == 0:
                v = [w + jnp.where(dom == 0, source[0, :, cut(t)], 0.0) for t, w in enumerate(v)]
            put(S, (f, level(z), everywhere), v)
    x_fields, z_fields = (0, 3, 4), (2, 4, 5)
    pair = (LEFT, RIGHT)
    for i, at_edge in enumerate((0, 7)):
        for k in range(3):
            for t in range(2):
                OX[i, 2 * k + t] = S[pair[t], x_fields[k], column(at_edge), :]
                OZ[i, 2 * k + t] = S[pair[t], z_fields[k], level(at_edge), :]
    for i in range(2):
        for z in range(8):
            OZ[i, 111 + z] = side_by_side(
                [state[f, z, :, cut(i)] for f in range(9)] + [region[z, :, cut(i)].astype(f32)], i)
        OZ[i, 119] = side_by_side([source[s, :, cut(i)] for s in range(STEPS)] + [floor[:, cut(i)].astype(f32)], i)

    for load in loads[6:]:
        load.wait()
    scale = 0.5 * COURANT
    tables = [[t[k] * scale for k in range(REGIONS)] for t in (lame, shear, buoy)]

    def materials(number, seafloor, z):
        bits = [(number & (1 << k)) != 0 for k in range(4)]
        solid = (dom * 8 + z) >= seafloor
        lam, mu, b = (pick(bits, t) for t in tables)
        return lam, jnp.where(solid, mu, 0.0), b, solid

    for s in range(STEPS):
        put(SRC, (pl.ds(8 * s, 8), everywhere),
            [jnp.where(dom == 0, source[s, :, cut(t)], 0.0) for t in range(2)])
    for z in range(8):
        made = [materials(region[z, :, cut(t)], floor[:, cut(t)], z) for t in range(2)]
        for k, ref in enumerate((L, M, B)):
            put(ref, (pl.ds(8 * z, 8), everywhere), [m[k] for m in made])

    for i, x in ((0, 0), (1, 7)):
        parts = [[OX[i, 2 * k + t] for t in range(2)] for k in range(3)]
        parts += [[m[p, pl.ds(x, 8, stride=8), :] for p in pair] for m in (L, M)]
        parts += [[
            jnp.concatenate([SRC[p, pl.ds(x, STEPS, stride=8), :], jnp.zeros((8 - STEPS, 128), f32)], 0) for p in pair]]
        for k in range(3, 6):
            for t in range(2):
                OX[i, 2 * k + t + 2] = parts[k][t]
        for j in range(2):
            OX[i, 6 + j] = side_by_side([v[j] for v in parts], j)
    for i, z in ((0, 0), (1, 7)):
        parts = [[OZ[i, 2 * k + t] for t in range(2)] for k in range(3)]
        parts += [[m[p, pl.ds(8 * z, 8), :] for p in pair] for m in (L, M)]
        for k in range(3, 5):
            for t in range(2):
                OZ[i, 2 * k + t + 2] = parts[k][t]
        for j in range(2):
            OZ[i, 6 + j] = side_by_side([v[j] for v in parts], j)

    pl.semaphore_wait(barrier, 8 + 5 * (there[0].astype(jnp.int32) + there[1].astype(jnp.int32)))
    for i in range(2):
        @functools.partial(reach, i)
        def _(i=i):
            for j in range(2):
                xy_first(i, j).start()
            xa_first(i).start()
    for i in range(2):
        for j in range(2):
            zy_first(i, j).start()
        za_first(i).start()
        y_first(i).start()
    for i in range(2):
        @functools.partial(reach, i)
        def _(i=i):
            xb_first(i).start()
        zb_first(i).start()
    for z in range(8):
        for f in range(3):
            put(V, (f, level(z), everywhere), [state[f, z, :, cut(t)] for t in range(2)])

    left = (lane >= 128 - WIDE) & (gy > 0)
    right = (lane < WIDE) & (gy < n_gy - 1)
    inside = left | right

    def margin(low, high, f):
        shift_r = (128 - WIDE * f) % 128
        shift_l = (256 - WIDE - WIDE * f) % 128
        a = pltpu.roll(high, shift_r, 1) if shift_r else high
        c = pltpu.roll(low, shift_l, 1) if shift_l else low
        return jnp.where(left, c, jnp.where(right, a, 0.0))

    arrived(ZR0.at[:, 0:6], z_first_recv.at[0])
    for i in range(2):
        @functools.partial(reach, i)
        def _(i=i):
            arrived(XR0.at[i, 0:6], x_first_recv.at[0, i])

    def three(first_tile, second_tile, edge):
        return (
            jnp.where(lane < SEAM, second_tile, first_tile),
            jnp.where(lane >= 128 - WIDE, edge, first_tile),
            jnp.where(lane < WIDE, edge, second_tile),
        )

    def border(parts):
        for i, x in ((0, -1), (1, 8)):
            for k, f in enumerate(x_fields):
                edge = zero if parts == (MIDDLE,) else margin(XR0[i, 6], XR0[i, 7], k)
                tiles = three(XR0[i, 2 * k], XR0[i, 2 * k + 1], edge)
                for p in parts:
                    S[p, f, column(x), :] = tiles[p]
        for i, z in ((0, -1), (1, 8)):
            for k, f in enumerate(z_fields):
                edge = zero if parts == (MIDDLE,) else margin(ZR0[i, 6], ZR0[i, 7], k)
                tiles = three(ZR0[i, 2 * k], ZR0[i, 2 * k + 1], edge)
                for p in parts:
                    S[p, f, level(z), :] = jnp.where(z_there[i], tiles[p], 0.0)

    border((MIDDLE,))
    def x_base(p, s, last):
        return 14 + 18 * s + (3 * p if last else 6 * p)

    def z_base(p, s, last):
        return 12 + 18 * s + (3 * p if last else 6 * p)

    def x_copy(p, i, s, slot, last):
        n = 3 if last else 6
        return remote(
            OX.at[i, pl.ds(x_base(p, s, last), n)], XR.at[slot, p, 1 - i, 0:n], x_send.at[i], x_recv.at[slot, p, 1 - i],
            (0, sides[i], 0))

    def e_copy(p, i, j, s, slot):
        return remote(
            OE.at[i, 3 * s + p, j], ER.at[slot, p, 1 - i, 1 - j], e_send.at[i],
            e_recv.at[slot, p, 1 - i], (sides[j], sides[i], 0))

    def z_copy(p, i, s, slot, last):
        n = 3 if last else 6
        return remote(
            OZ.at[i, pl.ds(z_base(p, s, last), n)], ZR.at[slot, p, 1 - i, 0:n], z_send.at[i], z_recv.at[slot, p],
            (sides[i], 0, 0))

    def move(p, s, slot, last=False):
        def accelerate(levels):
            moved = []
            for z in levels:
                own = level(z)
                after, before = pl.ds(rows(z, 1), 8), pl.ds(rows(z, -1), 8)
                above, below = level(z + 1), level(z - 1)

                def dx(f):
                    return S[p, f, after, :] - S[p, f, before, :]

                def dz(f):
                    return S[p, f, above, :] - S[p, f, below, :]

                b = B[p, pl.ds(8 * z, 8), :]
                moved.append((0, own, V[p, 0, own, :] - b * (dx(0) + dy(S[p, 3, own, :]) + dz(4))))
                moved.append((1, own, V[p, 1, own, :] - b * (dx(3) + dy(S[p, 1, own, :]) + dz(5))))
                moved.append((2, own, V[p, 2, own, :] - b * (dx(4) + dy(S[p, 5, own, :]) + dz(2))))
            for f, own, v in moved:
                V[p, f, own, :] = v

        accelerate((0, 7))
        if not last:
            for i, x in ((0, 0), (1, 7)):
                for j in range(2):
                    for k, f in enumerate((0, 2)):
                        OE[i, 3 * s + p, j, k : k + 1, :] = V[p, f, pl.ds(rows(7 * j, x), 1), :]

                @functools.partial(reach, i)
                def _(i=i):
                    for j in range(2):
                        e_copy(p, i, j, s, slot).start()
        accelerate((1, 2, 3))
        accelerate((4, 5, 6))
        base = x_base(p, s, last)
        for i, (x, inner) in enumerate(((0, 1), (7, 6))):
            for k, v in enumerate([V[p, f, column(c), :] for c in ((x,) if last else (x, inner)) for f in range(3)]):
                OX[i, base + k] = v

            @functools.partial(reach, i)
            def _(i=i):
                x_copy(p, i, s, slot, last).start()
        base = z_base(p, s, last)
        for i, (z, inner) in enumerate(((0, 1), (7, 6))):
            for f in range(3):
                OZ[i, base + f] = V[p, f, level(z), :]
                if not last:
                    OZ[i, base + 3 + f] = V[p, f, level(inner), :]
            z_copy(p, i, s, slot, last).start()

        later = []
        for z in range(8):
            own = level(z)
            after, before = pl.ds(rows(z, 1), 8), pl.ds(rows(z, -1), 8)
            above, below = level(z + 1), level(z - 1)
            dxs = [V[p, f, after, :] - V[p, f, before, :] for f in range(3)]
            dzs = [V[p, f, above, :] - V[p, f, below, :] for f in range(3)]
            dys = [dy(V[p, f, own, :]) for f in range(3)]
            lam, mu = L[p, pl.ds(8 * z, 8), :], M[p, pl.ds(8 * z, 8), :]
            spread = lam * (dxs[0] + dys[1] + dzs[2])
            mu2 = mu + mu
            change = (
                spread + mu2 * dxs[0], spread + mu2 * dys[1], spread + mu2 * dzs[2],
                mu * (dys[0] + dxs[1]), mu * (dzs[0] + dxs[2]), mu * (dzs[1] + dys[2]))
            later += [(f, own, S[p, f, own, :] - change[f]) for f in range(6)]
            if z % 2:
                write(p, later)
                later = []

    def write(p, results):
        for f, at_rows, v in results:
            S[p, f, at_rows, :] = v

    def finish(p, slot, then=None):
        last = then is None
        if not last:
            added = SRC[p, pl.ds(8 * then if isinstance(then, int) else pl.multiple_of(8 * then, 8), 8), :]
            results = [(f, level(0), S[p, f, level(0), :] + added) for f in range(3)]
            for i, x in ((0, -1), (1, 8)):
                outer = pl.ds(rows(0, x), 1)
                results.append((0, outer, S[p, 0, outer, :] + SX[i, p, pl.ds(then, 1), :]))
            write(p, results)
        arrived(ZR.at[slot, p, :, 0:3] if last else ZR.at[slot, p], z_recv.at[slot, p])
        results = []
        for i, z in ((0, 0), (1, 7)):
            near = [ZR[slot, p, i, f] for f in range(3)]
            own = level(z)
            lam, mu = L[p, pl.ds(8 * z, 8), :], M[p, pl.ds(8 * z, 8), :]
            sign = jnp.where(z_there[i], (-1.0, 1.0)[i], 0.0)
            slope = [sign * v for v in near]
            spread = lam * slope[2]
            results.append((0, own, S[p, 0, own, :] - (spread)))
            results.append((1, own, S[p, 1, own, :] - (spread)))
            results.append((2, own, S[p, 2, own, :] - (spread + (mu + mu) * slope[2])))
            results.append((4, own, S[p, 4, own, :] - (mu * slope[0])))
            results.append((5, own, S[p, 5, own, :] - (mu * slope[1])))
        write(p, results)

        for i in range(2):
            @functools.partial(reach, i)
            def _(i=i):
                arrived(XR.at[slot, p, i, 0:3] if last else XR.at[slot, p, i], x_recv.at[slot, p, i])

        results = []
        for i, x, sign in ((0, 0, -1.0), (1, 7, 1.0)):
            near = [XR[slot, p, i, f] for f in range(3)]
            lam, mu = L[p, pl.ds(x, 8, stride=8), :], M[p, pl.ds(x, 8, stride=8), :]
            slope = [sign * v for v in near]
            spread = lam * slope[0]
            results.append((0, column(x), S[p, 0, column(x), :] - (spread + (mu + mu) * slope[0])))
            results.append((1, column(x), S[p, 1, column(x), :] - (spread)))
            results.append((2, column(x), S[p, 2, column(x), :] - (spread)))
            results.append((3, column(x), S[p, 3, column(x), :] - (mu * slope[1])))
            results.append((4, column(x), S[p, 4, column(x), :] - (mu * slope[2])))

        if last:
            write(p, results)
            return
        for i, x, sign in ((0, 0, -1.0), (1, 7, 1.0)):
            near, far = [XR[slot, p, i, f] for f in range(3)], [XR[slot, p, i, 3 + f] for f in range(3)]
            lam, mu = LX[i, p], MX[i, p]
            dxs = [sign * (far[f] - V[p, f, column(x), :]) for f in range(3)]
            dzs = {}
            for f in (0, 2):
                up, down = pltpu.roll(near[f], 7, 0), pltpu.roll(near[f], 1, 0)
                dzs[f] = jnp.where(sub == 7, 0.0, up) - jnp.where(sub == 0, 0.0, down)
            trace = dxs[0] + dy(near[1]) + dzs[2]
            beyond = column((-1, 8)[i])
            results.append((0, beyond, S[p, 0, beyond, :] - (lam * trace + (mu + mu) * dxs[0])))
            results.append((3, beyond, S[p, 3, beyond, :] - (mu * (dy(near[0]) + dxs[1]))))
            results.append((4, beyond, S[p, 4, beyond, :] - (mu * (dzs[0] + dxs[2]))))
        for i, z, sign in ((0, 0, -1.0), (1, 7, 1.0)):
            near, far = [ZR[slot, p, i, f] for f in range(3)], [ZR[slot, p, i, 3 + f] for f in range(3)]
            lam, mu = LZ[i, p], MZ[i, p]
            dzs = [sign * (far[f] - V[p, f, level(z), :]) for f in range(3)]
            dxs = {}
            for f in (0, 2):
                ahead, behind = pltpu.roll(near[f], 7, 0), pltpu.roll(near[f], 1, 0)
                dxs[f] = jnp.where(sub == 7, 0.0, ahead) - jnp.where(sub == 0, 0.0, behind)
            trace = dxs[0] + dy(near[1]) + dzs[2]
            beyond = level((-1, 8)[i])
            results.append((2, beyond, S[p, 2, beyond, :] - (lam * trace + (mu + mu) * dzs[2])))
            results.append((4, beyond, S[p, 4, beyond, :] - (mu * (dzs[0] + dxs[2]))))
            results.append((5, beyond, S[p, 5, beyond, :] - (mu * (dzs[1] + dy(near[2])))))

        write(p, results)

        for i in range(2):
            @functools.partial(reach, i)
            def _(i=i):
                arrived(ER.at[slot, p, i], e_recv.at[slot, p, i])
        results = []
        for i, x in ((0, 0), (1, 7)):
            for j, z in ((0, 0), (1, 7)):
                edge_x, edge_z = (ER[slot, p, i, j, k : k + 1, :] for k in range(2))
                sign = jnp.where(z_there[j], (-1.0, 1.0)[j], 0.0)
                outer = pl.ds(rows(z, (-1, 8)[i]), 1)
                at_z, at_x = slice(z, z + 1), slice(x, x + 1)
                results.append((0, outer, S[p, 0, outer, :] - (LX[i, p, at_z, :] * (sign * edge_z))))
                results.append((4, outer, S[p, 4, outer, :] - (MX[i, p, at_z, :] * (sign * edge_x))))
                outer = pl.ds(rows((-1, 8)[j], x), 1)
                results.append((2, outer, S[p, 2, outer, :] - (LZ[j, p, at_x, :] * (sides[i] * edge_x))))
                results.append((4, outer, S[p, 4, outer, :] - (MZ[j, p, at_x, :] * (sides[i] * edge_z))))
        write(p, results)

    def each_part(then):
        for p in range(3):
            then(p)

    move(MIDDLE, 0, 0)

    arrived(YR, y_recv.at[0])
    low, high = YR[0, 8], YR[1, 8]
    seafloor = margin(low, high, STEPS).astype(jnp.int32)
    first_source = None
    for s in range(STEPS):
        v = jnp.where(dom == 0, margin(low, high, s), 0.0)
        first_source = v if s == 0 else first_source
        put_margin(SRC, (pl.ds(8 * s, 8), everywhere), v)
    for z in range(8):
        low, high = YR[0, z], YR[1, z]
        lam, mu, b, solid = materials(margin(low, high, 9).astype(jnp.int32), seafloor, z)
        for ref, v in ((L, lam), (M, mu), (B, b)):
            put_margin(ref, (pl.ds(8 * z, 8), everywhere), jnp.where(inside, v, 0.0))
        for f in range(9):
            v = margin(low, high, f)
            if f < 3:
                put_margin(V, (f, level(z), everywhere), v)
            else:
                if f >= 6:
                    v = jnp.where(solid, v, 0.0)
                elif z == 0:
                    v = v + first_source
                put_margin(S, (f - 3, level(z), everywhere), v)

    arrived(ZR0.at[:, 6:8], z_first_recv.at[2])
    for i in range(2):
        @functools.partial(reach, i)
        def _(i=i):
            arrived(XR0.at[i, 6:8], x_first_recv.at[2, i])
    border((LEFT, RIGHT))

    move(LEFT, 0, 0)
    move(RIGHT, 0, 0)

    arrived(ZR0.at[:, 8:12], z_first_recv.at[1])
    for i in range(2):
        @functools.partial(reach, i)
        def _(i=i):
            arrived(XR0.at[i, 8:14], x_first_recv.at[1, i])
    for i in range(2):
        for k, ref in enumerate((LX, MX, SX)):
            tiles = three(XR0[i, 8 + 2 * k], XR0[i, 9 + 2 * k], margin(XR0[i, 6], XR0[i, 7], 3 + k))
            for p in range(3):
                ref[i, p] = tiles[p]
        for k, ref in enumerate((LZ, MZ)):
            tiles = three(ZR0[i, 8 + 2 * k], ZR0[i, 9 + 2 * k], margin(ZR0[i, 6], ZR0[i, 7], 3 + k))
            for p in range(3):
                ref[i, p] = jnp.where(z_there[i], tiles[p], 0.0)

    def step(s, carry):
        slot = lax.rem(s, 2)

        def turn(p):
            finish(p, 1 - slot, s)
            move(p, s, slot)

        each_part(turn)
        return carry

    lax.fori_loop(1, STEPS - 1, step, 0)

    end = STEPS - 1

    def final(p):
        finish(p, (end - 1) % 2, end)
        move(p, end, end % 2, last=True)

    each_part(final)

    def gather(f, ref, k):
        for z in range(8):
            middle, first_tile, second_tile = (ref[p, k, level(z), :] for p in (MIDDLE, LEFT, RIGHT))
            out[f, z, :, cut(0)] = jnp.where(lane < FIRST_CUT, first_tile, middle)
            out[f, z, :, cut(1)] = jnp.where(lane < SECOND_CUT, middle, second_tile)

    for f in range(3):
        gather(f, V, f)
    each_part(lambda p: finish(p, end % 2))
    for f in range(6):
        gather(3 + f, S, f)

    for i in range(2):
        arrived(OZ.at[i], z_send.at[i])

        @functools.partial(reach, i)
        def _(i=i):
            arrived(OX.at[i], x_send.at[i])
            arrived(OE.at[i], e_send.at[i])


def solution(mesh):
    sizes = (mesh.shape["dom"], mesh.shape["gx"], mesh.shape["gy"])

    def on_device(state, source, floor, region, lame, shear, buoy):
        hbm = pl.BlockSpec(memory_space=pltpu.HBM)

        def tiles(*shape):
            return pltpu.VMEM(shape + (8, 128), f32)

        return pl.pallas_call(
            functools.partial(kernel, sizes),
            out_shape=jax.ShapeDtypeStruct(state.shape, f32),
            in_specs=[hbm] * 7,
            out_specs=pl.BlockSpec(memory_space=pltpu.VMEM),
            scratch_shapes=[
                pltpu.VMEM(state.shape, f32),
                pltpu.VMEM(source.shape, f32),
                pltpu.VMEM(floor.shape, jnp.int32),
                pltpu.VMEM(region.shape, jnp.int32),
                pltpu.SMEM(lame.shape, f32),
                pltpu.SMEM(shear.shape, f32),
                pltpu.SMEM(buoy.shape, f32),
                pltpu.VMEM((3, 6, 10 * BLOCK, 128), f32),
                pltpu.VMEM((3, 3, 10 * BLOCK, 128), f32),
                pltpu.VMEM((3, 64, 128), f32),
                pltpu.VMEM((3, 64, 128), f32),
                pltpu.VMEM((3, 64, 128), f32),
                pltpu.VMEM((3, 8 * STEPS, 128), f32),
                tiles(2, 3),
                tiles(2, 3),
                tiles(2, 3),
                tiles(2, 3),
                tiles(2, 3),
                tiles(2, 113),
                tiles(2, 120),
                pltpu.VMEM((2, 3 * STEPS - 3, 2, 2, 128), f32),
                tiles(2, 14),
                tiles(2, 12),
                tiles(2, 9),
                tiles(2, 3, 2, 6),
                tiles(2, 3, 2, 6),
                pltpu.VMEM((2, 3, 2, 2, 2, 128), f32),
                pltpu.SemaphoreType.DMA((9,)),
                pltpu.SemaphoreType.DMA((2,)),
                pltpu.SemaphoreType.DMA((2,)),
                pltpu.SemaphoreType.DMA((2,)),
                pltpu.SemaphoreType.DMA((3, 2)),
                pltpu.SemaphoreType.DMA((3,)),
                pltpu.SemaphoreType.DMA((1,)),
                pltpu.SemaphoreType.DMA((2, 3, 2)),
                pltpu.SemaphoreType.DMA((2, 3)),
                pltpu.SemaphoreType.DMA((2, 3, 2)),
            ],
            compiler_params=pltpu.CompilerParams(
                collective_id=0, has_side_effects=True, vmem_limit_bytes=32 * 1024 * 1024
            ),
        )(*(
            pltpu.with_memory_space_constraint(v, pltpu.HBM)
            for v in (state, source, floor, region, lame, shear, buoy)
        ))

    return jax.shard_map(
        on_device,
        mesh=mesh,
        in_specs=(
            P(None, "dom", "gx", "gy"),
            P(None, "gx", "gy"),
            P("gx", "gy"),
            P("dom", "gx", "gy"),
            P(),
            P(),
            P(),
        ),
        out_specs=P(None, "dom", "gx", "gy"),
        check_vma=False,
    )
```

```python
import functools

import jax
import jax.numpy as jnp
from jax import lax
from jax.experimental import pallas as pl
from jax.experimental.pallas import tpu as pltpu
from jax.sharding import PartitionSpec as P

STEPS = 6
COURANT = 0.25
REGIONS = 16
BLOCK = 16
WIDE = 12
MIDDLE, LEFT, RIGHT = 0, 1, 2
FIRST_CUT, SECOND_CUT, SEAM = 86, 171 - 128, 64
MESH = pl.DeviceIdType.MESH

f32 = jnp.float32


def rows(z, x=0):
    return (z + 1) * BLOCK + 8 + x


def level(z):
    return pl.ds(rows(z), 8)


def column(x):
    return pl.ds(rows(0, x), 8, stride=BLOCK)


def dy(v):
    return pltpu.roll(v, 127, 1) - pltpu.roll(v, 1, 1)


def pick(bits, table):
    values = list(table)
    for bit in bits:
        values = [jnp.where(bit, values[2 * i + 1], values[2 * i]) for i in range(len(values) // 2)]
    return values[0]


def kernel(
    sizes, state_in, source_in, floor_in, region_in, lame_in, shear_in, buoy_in, out,
    state, source, floor, region, lame, shear, buoy,
    S, V, L, M, B, SRC, LX, MX, SX, LZ, MZ, OX, OZ, OE, XR0, ZR0, YR, XR, ZR, ER,
    in_sem, x_send, z_send, e_send, x_first_recv, z_first_recv, y_recv, x_recv, z_recv, e_recv,
):
    n_dom, n_gx, n_gy = sizes
    dom, gx, gy = lax.axis_index("dom"), lax.axis_index("gx"), lax.axis_index("gy")
    lane = lax.broadcasted_iota(jnp.int32, (8, 128), 1)
    sub = lax.broadcasted_iota(jnp.int32, (8, 128), 0)
    zero = jnp.zeros((8, 128), f32)

    loads = [
        pltpu.make_async_copy(src, dst, in_sem.at[i])
        for i, (src, dst) in enumerate((
            (floor_in, floor), (source_in, source), (state_in.at[3:9], state.at[3:9]),
            (state_in.at[0:3], state.at[0:3]), (region_in, region),
            (lame_in, lame), (shear_in, shear), (buoy_in, buoy)))
    ]
    for load in loads:
        load.start()

    sides = (-1, 1)
    there = [gx > 0, gx < n_gx - 1]
    z_there = [dom > 0, dom < n_dom - 1]

    doms = [dom, jnp.where(dom == n_dom - 1, 0, dom + 1), jnp.where(dom == 0, n_dom - 1, dom - 1)]
    gxs = [gx, gx + 1, gx - 1]
    gys = [gy, jnp.where(gy == n_gy - 1, 0, gy + 1), jnp.where(gy == 0, n_gy - 1, gy - 1)]

    def at(dz, dx, dyy):
        return (doms[dz], gxs[dx], gys[dyy])

    def reach(i, then):
        pl.when(there[i])(then)

    barrier = pltpu.get_barrier_semaphore()

    def greet(*way):
        pl.semaphore_signal(barrier, inc=1, device_id=at(*way), device_id_type=MESH)

    for i, dx in enumerate(sides):
        @functools.partial(reach, i)
        def _(dx=dx):
            for way in ((0, dx, 0), (-1, dx, 0), (1, dx, 0), (0, dx, -1), (0, dx, 1)):
                greet(*way)
    for way in [(a, 0, b) for a in (-1, 0, 1) for b in (-1, 0, 1) if a or b]:
        greet(*way)

    for i in range(2):
        @pl.when(jnp.logical_not(there[i]))
        def _(i=i):
            XR0[i] = jnp.zeros(XR0.shape[1:], f32)
            for slot in range(2):
                for p in range(3):
                    XR[slot, p, i] = jnp.zeros(XR.shape[3:], f32)
                    ER[slot, p, i] = jnp.zeros(ER.shape[3:], f32)

    for p in range(3):
        for f in range(3):
            for z in range(-1, 9):
                V[p, f, pl.ds(rows(z, -8), 8), :] = zero
            for z in (-1, 8):
                V[p, f, level(z), :] = zero

    for load in loads[:3]:
        load.wait()

    def side_by_side(parts, t):
        tile = zero
        for k, v in enumerate(parts):
            shift = (WIDE * k + (WIDE if t else 0)) % 128
            v = pltpu.roll(v, shift, 1) if shift else v
            tile = jnp.where((lane >= WIDE * k) & (lane < WIDE * (k + 1)), v, tile)
        return tile

    def cut(t):
        return slice(128 * t, 128 * t + 128)

    def remote(src, dst, send, recv, way):
        return pltpu.make_async_remote_copy(
            src_ref=src, dst_ref=dst, send_sem=send, recv_sem=recv, device_id=at(*way), device_id_type=MESH)

    def xa_first(i):
        return remote(OX.at[i, 0:6], XR0.at[1 - i, 0:6], x_send.at[i], x_first_recv.at[0, 1 - i], (0, sides[i], 0))

    def xy_first(i, j):
        return remote(
            OX.at[i, 6 + j], XR0.at[1 - i, 7 - j], x_send.at[i], x_first_recv.at[2, 1 - i], (0, sides[i], sides[j]))

    def xb_first(i):
        return remote(OX.at[i, 8:14], XR0.at[1 - i, 8:14], x_send.at[i], x_first_recv.at[1, 1 - i], (0, sides[i], 0))

    def za_first(i):
        return remote(OZ.at[i, 0:6], ZR0.at[1 - i, 0:6], z_send.at[i], z_first_recv.at[0], (sides[i], 0, 0))

    def zy_first(i, j):
        return remote(
            OZ.at[i, 6 + j], ZR0.at[1 - i, 7 - j], z_send.at[i], z_first_recv.at[2], (sides[i], 0, sides[j]))

    def zb_first(i):
        return remote(OZ.at[i, 8:12], ZR0.at[1 - i, 8:12], z_send.at[i], z_first_recv.at[1], (sides[i], 0, 0))

    def y_first(i):
        return remote(OZ.at[i, 111:120], YR.at[1 - i], z_send.at[i], y_recv.at[0], (0, 0, sides[i]))

    def arrived(ref, sem):
        pltpu.make_async_copy(ref, ref, sem).wait()

    def put(ref, index, pair):
        ref[(MIDDLE, *index)] = jnp.where(lane < SEAM, pair[1], pair[0])
        ref[(LEFT, *index)] = pair[0]
        ref[(RIGHT, *index)] = pair[1]

    def put_margin(ref, index, v):
        ref[(LEFT, *index)] = jnp.where(lane >= 128 - WIDE, v, ref[(LEFT, *index)])
        ref[(RIGHT, *index)] = jnp.where(lane < WIDE, v, ref[(RIGHT, *index)])

    everywhere = slice(None)
    for z in range(8):
        solid = [(dom * 8 + z) >= floor[:, cut(t)] for t in range(2)]
        for f in range(6):
            v = [state[3 + f, z, :, cut(t)] for t in range(2)]
            if f >= 3:
                v = [jnp.where(m, w, 0.0) for m, w in zip(solid, v)]
            elif z == 0:
                v = [w + jnp.where(dom == 0, source[0, :, cut(t)], 0.0) for t, w in enumerate(v)]
            put(S, (f, level(z), everywhere), v)
    x_fields, z_fields = (0, 3, 4), (2, 4, 5)
    pair = (LEFT, RIGHT)
    for i, at_edge in enumerate((0, 7)):
        for k in range(3):
            for t in range(2):
                OX[i, 2 * k + t] = S[pair[t], x_fields[k], column(at_edge), :]
                OZ[i, 2 * k + t] = S[pair[t], z_fields[k], level(at_edge), :]
    pl.semaphore_wait(barrier, 8 + 5 * (there[0].astype(jnp.int32) + there[1].astype(jnp.int32)))
    for i in range(2):
        @functools.partial(reach, i)
        def _(i=i):
            xa_first(i).start()
        za_first(i).start()
    for load in loads[3:]:
        load.wait()
    for i in range(2):
        for z in range(8):
            OZ[i, 111 + z] = side_by_side(
                [state[f, z, :, cut(i)] for f in range(9)] + [region[z, :, cut(i)].astype(f32)], i)
        OZ[i, 119] = side_by_side([source[s, :, cut(i)] for s in range(STEPS)] + [floor[:, cut(i)].astype(f32)], i)

    for i in range(2):
        y_first(i).start()

    scale = 0.5 * COURANT
    tables = [[t[k] * scale for k in range(REGIONS)] for t in (lame, shear, buoy)]

    def materials(number, seafloor, z):
        bits = [(number & (1 << k)) != 0 for k in range(4)]
        solid = (dom * 8 + z) >= seafloor
        lam, mu, b = (pick(bits, t) for t in tables)
        return lam, jnp.where(solid, mu, 0.0), b, solid

    for s in range(STEPS):
        put(SRC, (pl.ds(8 * s, 8), everywhere),
            [jnp.where(dom == 0, source[s, :, cut(t)], 0.0) for t in range(2)])
    for z in range(8):
        made = [materials(region[z, :, cut(t)], floor[:, cut(t)], z) for t in range(2)]
        for k, ref in enumerate((L, M, B)):
            put(ref, (pl.ds(8 * z, 8), everywhere), [m[k] for m in made])
        for f in range(3):
            put(V, (f, level(z), everywhere), [state[f, z, :, cut(t)] for t in range(2)])

    for i, x in ((0, 0), (1, 7)):
        parts = [[OX[i, 2 * k + t] for t in range(2)] for k in range(3)]
        parts += [[m[p, pl.ds(x, 8, stride=8), :] for p in pair] for m in (L, M)]
        parts += [[
            jnp.concatenate([SRC[p, pl.ds(x, STEPS, stride=8), :], jnp.zeros((8 - STEPS, 128), f32)], 0) for p in pair]]
        for k in range(3, 6):
            for t in range(2):
                OX[i, 2 * k + t + 2] = parts[k][t]
        for j in range(2):
            OX[i, 6 + j] = side_by_side([v[j] for v in parts], j)

        @functools.partial(reach, i)
        def _(i=i):
            for j in range(2):
                xy_first(i, j).start()
            xb_first(i).start()
    for i, z in ((0, 0), (1, 7)):
        parts = [[OZ[i, 2 * k + t] for t in range(2)] for k in range(3)]
        parts += [[m[p, pl.ds(8 * z, 8), :] for p in pair] for m in (L, M)]
        for k in range(3, 5):
            for t in range(2):
                OZ[i, 2 * k + t + 2] = parts[k][t]
        for j in range(2):
            OZ[i, 6 + j] = side_by_side([v[j] for v in parts], j)
            zy_first(i, j).start()
        zb_first(i).start()

    left = (lane >= 128 - WIDE) & (gy > 0)
    right = (lane < WIDE) & (gy < n_gy - 1)
    inside = left | right

    def margin(low, high, f):
        shift_r = (128 - WIDE * f) % 128
        shift_l = (256 - WIDE - WIDE * f) % 128
        a = pltpu.roll(high, shift_r, 1) if shift_r else high
        c = pltpu.roll(low, shift_l, 1) if shift_l else low
        return jnp.where(left, c, jnp.where(right, a, 0.0))

    arrived(ZR0.at[:, 0:6], z_first_recv.at[0])
    for i in range(2):
        @functools.partial(reach, i)
        def _(i=i):
            arrived(XR0.at[i, 0:6], x_first_recv.at[0, i])

    def three(first_tile, second_tile, edge):
        return (
            jnp.where(lane < SEAM, second_tile, first_tile),
            jnp.where(lane >= 128 - WIDE, edge, first_tile),
            jnp.where(lane < WIDE, edge, second_tile),
        )

    def border(parts):
        for i, x in ((0, -1), (1, 8)):
            for k, f in enumerate(x_fields):
                edge = zero if parts == (MIDDLE,) else margin(XR0[i, 6], XR0[i, 7], k)
                tiles = three(XR0[i, 2 * k], XR0[i, 2 * k + 1], edge)
                for p in parts:
                    S[p, f, column(x), :] = tiles[p]
        for i, z in ((0, -1), (1, 8)):
            for k, f in enumerate(z_fields):
                edge = zero if parts == (MIDDLE,) else margin(ZR0[i, 6], ZR0[i, 7], k)
                tiles = three(ZR0[i, 2 * k], ZR0[i, 2 * k + 1], edge)
                for p in parts:
                    S[p, f, level(z), :] = jnp.where(z_there[i], tiles[p], 0.0)

    border((MIDDLE,))
    def x_base(p, s, last):
        return 14 + 18 * s + (3 * p if last else 6 * p)

    def z_base(p, s, last):
        return 12 + 18 * s + (3 * p if last else 6 * p)

    def x_copy(p, i, s, slot, last):
        n = 3 if last else 6
        return remote(
            OX.at[i, pl.ds(x_base(p, s, last), n)], XR.at[slot, p, 1 - i, 0:n], x_send.at[i], x_recv.at[slot, p, 1 - i],
            (0, sides[i], 0))

    def e_copy(p, i, j, s, slot):
        return remote(
            OE.at[i, 3 * s + p, j], ER.at[slot, p, 1 - i, 1 - j], e_send.at[i],
            e_recv.at[slot, p, 1 - i], (sides[j], sides[i], 0))

    def z_copy(p, i, s, slot, last):
        n = 3 if last else 6
        return remote(
            OZ.at[i, pl.ds(z_base(p, s, last), n)], ZR.at[slot, p, 1 - i, 0:n], z_send.at[i], z_recv.at[slot, p],
            (sides[i], 0, 0))

    def move(p, s, slot, last=False):
        def accelerate(levels):
            moved = []
            for z in levels:
                own = level(z)
                after, before = pl.ds(rows(z, 1), 8), pl.ds(rows(z, -1), 8)
                above, below = level(z + 1), level(z - 1)

                def dx(f):
                    return S[p, f, after, :] - S[p, f, before, :]

                def dz(f):
                    return S[p, f, above, :] - S[p, f, below, :]

                b = B[p, pl.ds(8 * z, 8), :]
                moved.append((0, own, V[p, 0, own, :] - b * (dx(0) + dy(S[p, 3, own, :]) + dz(4))))
                moved.append((1, own, V[p, 1, own, :] - b * (dx(3) + dy(S[p, 1, own, :]) + dz(5))))
                moved.append((2, own, V[p, 2, own, :] - b * (dx(4) + dy(S[p, 5, own, :]) + dz(2))))
            for f, own, v in moved:
                V[p, f, own, :] = v

        accelerate((0, 7))
        if not last:
            for i, x in ((0, 0), (1, 7)):
                for j in range(2):
                    for k, f in enumerate((0, 2)):
                        OE[i, 3 * s + p, j, k : k + 1, :] = V[p, f, pl.ds(rows(7 * j, x), 1), :]

                @functools.partial(reach, i)
                def _(i=i):
                    for j in range(2):
                        e_copy(p, i, j, s, slot).start()
        accelerate((1, 2, 3))
        accelerate((4, 5, 6))
        base = x_base(p, s, last)
        for i, (x, inner) in enumerate(((0, 1), (7, 6))):
            for k, v in enumerate([V[p, f, column(c), :] for c in ((x,) if last else (x, inner)) for f in range(3)]):
                OX[i, base + k] = v

            @functools.partial(reach, i)
            def _(i=i):
                x_copy(p, i, s, slot, last).start()
        base = z_base(p, s, last)
        for i, (z, inner) in enumerate(((0, 1), (7, 6))):
            for f in range(3):
                OZ[i, base + f] = V[p, f, level(z), :]
                if not last:
                    OZ[i, base + 3 + f] = V[p, f, level(inner), :]
            z_copy(p, i, s, slot, last).start()

        later = []
        for z in range(8):
            own = level(z)
            after, before = pl.ds(rows(z, 1), 8), pl.ds(rows(z, -1), 8)
            above, below = level(z + 1), level(z - 1)
            dxs = [V[p, f, after, :] - V[p, f, before, :] for f in range(3)]
            dzs = [V[p, f, above, :] - V[p, f, below, :] for f in range(3)]
            dys = [dy(V[p, f, own, :]) for f in range(3)]
            lam, mu = L[p, pl.ds(8 * z, 8), :], M[p, pl.ds(8 * z, 8), :]
            spread = lam * (dxs[0] + dys[1] + dzs[2])
            mu2 = mu + mu
            change = (
                spread + mu2 * dxs[0], spread + mu2 * dys[1], spread + mu2 * dzs[2],
                mu * (dys[0] + dxs[1]), mu * (dzs[0] + dxs[2]), mu * (dzs[1] + dys[2]))
            later += [(f, own, S[p, f, own, :] - change[f]) for f in range(6)]
            if z % 2:
                write(p, later)
                later = []

    def write(p, results):
        for f, at_rows, v in results:
            S[p, f, at_rows, :] = v

    def finish(p, slot, then=None):
        last = then is None
        if not last:
            added = SRC[p, pl.ds(8 * then if isinstance(then, int) else pl.multiple_of(8 * then, 8), 8), :]
            results = [(f, level(0), S[p, f, level(0), :] + added) for f in range(3)]
            for i, x in ((0, -1), (1, 8)):
                outer = pl.ds(rows(0, x), 1)
                results.append((0, outer, S[p, 0, outer, :] + SX[i, p, pl.ds(then, 1), :]))
            write(p, results)
        arrived(ZR.at[slot, p, :, 0:3] if last else ZR.at[slot, p], z_recv.at[slot, p])
        results = []
        for i, z in ((0, 0), (1, 7)):
            near = [ZR[slot, p, i, f] for f in range(3)]
            own = level(z)
            lam, mu = L[p, pl.ds(8 * z, 8), :], M[p, pl.ds(8 * z, 8), :]
            sign = jnp.where(z_there[i], (-1.0, 1.0)[i], 0.0)
            slope = [sign * v for v in near]
            spread = lam * slope[2]
            results.append((0, own, S[p, 0, own, :] - (spread)))
            results.append((1, own, S[p, 1, own, :] - (spread)))
            results.append((2, own, S[p, 2, own, :] - (spread + (mu + mu) * slope[2])))
            results.append((4, own, S[p, 4, own, :] - (mu * slope[0])))
            results.append((5, own, S[p, 5, own, :] - (mu * slope[1])))
        write(p, results)

        for i in range(2):
            @functools.partial(reach, i)
            def _(i=i):
                arrived(XR.at[slot, p, i, 0:3] if last else XR.at[slot, p, i], x_recv.at[slot, p, i])

        results = []
        for i, x, sign in ((0, 0, -1.0), (1, 7, 1.0)):
            near = [XR[slot, p, i, f] for f in range(3)]
            lam, mu = L[p, pl.ds(x, 8, stride=8), :], M[p, pl.ds(x, 8, stride=8), :]
            slope = [sign * v for v in near]
            spread = lam * slope[0]
            results.append((0, column(x), S[p, 0, column(x), :] - (spread + (mu + mu) * slope[0])))
            results.append((1, column(x), S[p, 1, column(x), :] - (spread)))
            results.append((2, column(x), S[p, 2, column(x), :] - (spread)))
            results.append((3, column(x), S[p, 3, column(x), :] - (mu * slope[1])))
            results.append((4, column(x), S[p, 4, column(x), :] - (mu * slope[2])))

        if last:
            write(p, results)
            return
        for i, x, sign in ((0, 0, -1.0), (1, 7, 1.0)):
            near, far = [XR[slot, p, i, f] for f in range(3)], [XR[slot, p, i, 3 + f] for f in range(3)]
            lam, mu = LX[i, p], MX[i, p]
            dxs = [sign * (far[f] - V[p, f, column(x), :]) for f in range(3)]
            dzs = {}
            for f in (0, 2):
                up, down = pltpu.roll(near[f], 7, 0), pltpu.roll(near[f], 1, 0)
                dzs[f] = jnp.where(sub == 7, 0.0, up) - jnp.where(sub == 0, 0.0, down)
            trace = dxs[0] + dy(near[1]) + dzs[2]
            beyond = column((-1, 8)[i])
            results.append((0, beyond, S[p, 0, beyond, :] - (lam * trace + (mu + mu) * dxs[0])))
            results.append((3, beyond, S[p, 3, beyond, :] - (mu * (dy(near[0]) + dxs[1]))))
            results.append((4, beyond, S[p, 4, beyond, :] - (mu * (dzs[0] + dxs[2]))))
        for i, z, sign in ((0, 0, -1.0), (1, 7, 1.0)):
            near, far = [ZR[slot, p, i, f] for f in range(3)], [ZR[slot, p, i, 3 + f] for f in range(3)]
            lam, mu = LZ[i, p], MZ[i, p]
            dzs = [sign * (far[f] - V[p, f, level(z), :]) for f in range(3)]
            dxs = {}
            for f in (0, 2):
                ahead, behind = pltpu.roll(near[f], 7, 0), pltpu.roll(near[f], 1, 0)
                dxs[f] = jnp.where(sub == 7, 0.0, ahead) - jnp.where(sub == 0, 0.0, behind)
            trace = dxs[0] + dy(near[1]) + dzs[2]
            beyond = level((-1, 8)[i])
            results.append((2, beyond, S[p, 2, beyond, :] - (lam * trace + (mu + mu) * dzs[2])))
            results.append((4, beyond, S[p, 4, beyond, :] - (mu * (dzs[0] + dxs[2]))))
            results.append((5, beyond, S[p, 5, beyond, :] - (mu * (dzs[1] + dy(near[2])))))

        write(p, results)

        for i in range(2):
            @functools.partial(reach, i)
            def _(i=i):
                arrived(ER.at[slot, p, i], e_recv.at[slot, p, i])
        results = []
        for i, x in ((0, 0), (1, 7)):
            for j, z in ((0, 0), (1, 7)):
                edge_x, edge_z = (ER[slot, p, i, j, k : k + 1, :] for k in range(2))
                sign = jnp.where(z_there[j], (-1.0, 1.0)[j], 0.0)
                outer = pl.ds(rows(z, (-1, 8)[i]), 1)
                at_z, at_x = slice(z, z + 1), slice(x, x + 1)
                results.append((0, outer, S[p, 0, outer, :] - (LX[i, p, at_z, :] * (sign * edge_z))))
                results.append((4, outer, S[p, 4, outer, :] - (MX[i, p, at_z, :] * (sign * edge_x))))
                outer = pl.ds(rows((-1, 8)[j], x), 1)
                results.append((2, outer, S[p, 2, outer, :] - (LZ[j, p, at_x, :] * (sides[i] * edge_x))))
                results.append((4, outer, S[p, 4, outer, :] - (MZ[j, p, at_x, :] * (sides[i] * edge_z))))
        write(p, results)

    def each_part(then):
        for p in range(3):
            then(p)

    move(MIDDLE, 0, 0)

    arrived(YR, y_recv.at[0])
    low, high = YR[0, 8], YR[1, 8]
    seafloor = margin(low, high, STEPS).astype(jnp.int32)
    first_source = None
    for s in range(STEPS):
        v = jnp.where(dom == 0, margin(low, high, s), 0.0)
        first_source = v if s == 0 else first_source
        put_margin(SRC, (pl.ds(8 * s, 8), everywhere), v)
    for z in range(8):
        low, high = YR[0, z], YR[1, z]
        lam, mu, b, solid = materials(margin(low, high, 9).astype(jnp.int32), seafloor, z)
        for ref, v in ((L, lam), (M, mu), (B, b)):
            put_margin(ref, (pl.ds(8 * z, 8), everywhere), jnp.where(inside, v, 0.0))
        for f in range(9):
            v = margin(low, high, f)
            if f < 3:
                put_margin(V, (f, level(z), everywhere), v)
            else:
                if f >= 6:
                    v = jnp.where(solid, v, 0.0)
                elif z == 0:
                    v = v + first_source
                put_margin(S, (f - 3, level(z), everywhere), v)

    arrived(ZR0.at[:, 6:8], z_first_recv.at[2])
    for i in range(2):
        @functools.partial(reach, i)
        def _(i=i):
            arrived(XR0.at[i, 6:8], x_first_recv.at[2, i])
    border((LEFT, RIGHT))

    move(LEFT, 0, 0)
    move(RIGHT, 0, 0)

    arrived(ZR0.at[:, 8:12], z_first_recv.at[1])
    for i in range(2):
        @functools.partial(reach, i)
        def _(i=i):
            arrived(XR0.at[i, 8:14], x_first_recv.at[1, i])
    for i in range(2):
        for k, ref in enumerate((LX, MX, SX)):
            tiles = three(XR0[i, 8 + 2 * k], XR0[i, 9 + 2 * k], margin(XR0[i, 6], XR0[i, 7], 3 + k))
            for p in range(3):
                ref[i, p] = tiles[p]
        for k, ref in enumerate((LZ, MZ)):
            tiles = three(ZR0[i, 8 + 2 * k], ZR0[i, 9 + 2 * k], margin(ZR0[i, 6], ZR0[i, 7], 3 + k))
            for p in range(3):
                ref[i, p] = jnp.where(z_there[i], tiles[p], 0.0)

    def step(s, carry):
        slot = lax.rem(s, 2)

        def turn(p):
            finish(p, 1 - slot, s)
            move(p, s, slot)

        each_part(turn)
        return carry

    lax.fori_loop(1, STEPS - 1, step, 0)

    end = STEPS - 1

    def final(p):
        finish(p, (end - 1) % 2, end)
        move(p, end, end % 2, last=True)

    each_part(final)

    def gather(f, ref, k):
        for z in range(8):
            middle, first_tile, second_tile = (ref[p, k, level(z), :] for p in (MIDDLE, LEFT, RIGHT))
            out[f, z, :, cut(0)] = jnp.where(lane < FIRST_CUT, first_tile, middle)
            out[f, z, :, cut(1)] = jnp.where(lane < SECOND_CUT, middle, second_tile)

    for f in range(3):
        gather(f, V, f)
    each_part(lambda p: finish(p, end % 2))
    for f in range(6):
        gather(3 + f, S, f)

    for i in range(2):
        arrived(OZ.at[i], z_send.at[i])

        @functools.partial(reach, i)
        def _(i=i):
            arrived(OX.at[i], x_send.at[i])
            arrived(OE.at[i], e_send.at[i])


def solution(mesh):
    sizes = (mesh.shape["dom"], mesh.shape["gx"], mesh.shape["gy"])

    def on_device(state, source, floor, region, lame, shear, buoy):
        hbm = pl.BlockSpec(memory_space=pltpu.HBM)

        def tiles(*shape):
            return pltpu.VMEM(shape + (8, 128), f32)

        return pl.pallas_call(
            functools.partial(kernel, sizes),
            out_shape=jax.ShapeDtypeStruct(state.shape, f32),
            in_specs=[hbm] * 7,
            out_specs=pl.BlockSpec(memory_space=pltpu.VMEM),
            scratch_shapes=[
                pltpu.VMEM(state.shape, f32),
                pltpu.VMEM(source.shape, f32),
                pltpu.VMEM(floor.shape, jnp.int32),
                pltpu.VMEM(region.shape, jnp.int32),
                pltpu.SMEM(lame.shape, f32),
                pltpu.SMEM(shear.shape, f32),
                pltpu.SMEM(buoy.shape, f32),
                pltpu.VMEM((3, 6, 10 * BLOCK, 128), f32),
                pltpu.VMEM((3, 3, 10 * BLOCK, 128), f32),
                pltpu.VMEM((3, 64, 128), f32),
                pltpu.VMEM((3, 64, 128), f32),
                pltpu.VMEM((3, 64, 128), f32),
                pltpu.VMEM((3, 8 * STEPS, 128), f32),
                tiles(2, 3),
                tiles(2, 3),
                tiles(2, 3),
                tiles(2, 3),
                tiles(2, 3),
                tiles(2, 113),
                tiles(2, 120),
                pltpu.VMEM((2, 3 * STEPS - 3, 2, 2, 128), f32),
                tiles(2, 14),
                tiles(2, 12),
                tiles(2, 9),
                tiles(2, 3, 2, 6),
                tiles(2, 3, 2, 6),
                pltpu.VMEM((2, 3, 2, 2, 2, 128), f32),
                pltpu.SemaphoreType.DMA((8,)),
                pltpu.SemaphoreType.DMA((2,)),
                pltpu.SemaphoreType.DMA((2,)),
                pltpu.SemaphoreType.DMA((2,)),
                pltpu.SemaphoreType.DMA((3, 2)),
                pltpu.SemaphoreType.DMA((3,)),
                pltpu.SemaphoreType.DMA((1,)),
                pltpu.SemaphoreType.DMA((2, 3, 2)),
                pltpu.SemaphoreType.DMA((2, 3)),
                pltpu.SemaphoreType.DMA((2, 3, 2)),
            ],
            compiler_params=pltpu.CompilerParams(
                collective_id=0, has_side_effects=True, vmem_limit_bytes=32 * 1024 * 1024
            ),
        )(*(
            pltpu.with_memory_space_constraint(v, pltpu.HBM)
            for v in (state, source, floor, region, lame, shear, buoy)
        ))

    return jax.shard_map(
        on_device,
        mesh=mesh,
        in_specs=(
            P(None, "dom", "gx", "gy"),
            P(None, "gx", "gy"),
            P("gx", "gy"),
            P("dom", "gx", "gy"),
            P(),
            P(),
            P(),
        ),
        out_specs=P(None, "dom", "gx", "gy"),
        check_vma=False,
    )
```

```python
import functools

import jax
import jax.numpy as jnp
from jax import lax
from jax.experimental import pallas as pl
from jax.experimental.pallas import tpu as pltpu
from jax.sharding import PartitionSpec as P

STEPS = 6
COURANT = 0.25
REGIONS = 16
BLOCK = 16
WIDE = 12
MIDDLE, LEFT, RIGHT = 0, 1, 2
FIRST_CUT, SECOND_CUT, SEAM = 86, 171 - 128, 64
MESH = pl.DeviceIdType.MESH

f32 = jnp.float32


def rows(z, x=0):
    return (z + 1) * BLOCK + 8 + x


def level(z):
    return pl.ds(rows(z), 8)


def column(x):
    return pl.ds(rows(0, x), 8, stride=BLOCK)


def dy(v):
    return pltpu.roll(v, 127, 1) - pltpu.roll(v, 1, 1)


def pick(bits, table):
    values = list(table)
    for bit in bits:
        values = [jnp.where(bit, values[2 * i + 1], values[2 * i]) for i in range(len(values) // 2)]
    return values[0]


def kernel(
    sizes, state_in, source_in, floor_in, region_in, lame_in, shear_in, buoy_in, out,
    state, source, floor, region, lame, shear, buoy,
    S, V, L, M, B, SRC, LX, MX, SX, LZ, MZ, OX, OZ, OE, XR0, ZR0, YR, XR, ZR, ER,
    in_sem, x_send, z_send, e_send, x_first_recv, z_first_recv, y_recv, x_recv, z_recv, e_recv,
):
    n_dom, n_gx, n_gy = sizes
    dom, gx, gy = lax.axis_index("dom"), lax.axis_index("gx"), lax.axis_index("gy")
    lane = lax.broadcasted_iota(jnp.int32, (8, 128), 1)
    sub = lax.broadcasted_iota(jnp.int32, (8, 128), 0)
    zero = jnp.zeros((8, 128), f32)

    loads = [
        pltpu.make_async_copy(src, dst, in_sem.at[i])
        for i, (src, dst) in enumerate((
            (region_in, region), (floor_in, floor), (source_in, source),
            (state_in.at[0:3], state.at[0:3]), (state_in.at[3:6], state.at[3:6]), (state_in.at[6:9], state.at[6:9]),
            (lame_in, lame), (shear_in, shear), (buoy_in, buoy)))
    ]
    for load in loads:
        load.start()

    sides = (-1, 1)
    there = [gx > 0, gx < n_gx - 1]
    z_there = [dom > 0, dom < n_dom - 1]

    doms = [dom, jnp.where(dom == n_dom - 1, 0, dom + 1), jnp.where(dom == 0, n_dom - 1, dom - 1)]
    gxs = [gx, gx + 1, gx - 1]
    gys = [gy, jnp.where(gy == n_gy - 1, 0, gy + 1), jnp.where(gy == 0, n_gy - 1, gy - 1)]

    def at(dz, dx, dyy):
        return (doms[dz], gxs[dx], gys[dyy])

    def reach(i, then):
        pl.when(there[i])(then)

    barrier = pltpu.get_barrier_semaphore()

    def greet(*way):
        pl.semaphore_signal(barrier, inc=1, device_id=at(*way), device_id_type=MESH)

    for i, dx in enumerate(sides):
        @functools.partial(reach, i)
        def _(dx=dx):
            for way in ((0, dx, 0), (-1, dx, 0), (1, dx, 0), (0, dx, -1), (0, dx, 1)):
                greet(*way)
    for way in [(a, 0, b) for a in (-1, 0, 1) for b in (-1, 0, 1) if a or b]:
        greet(*way)

    for i in range(2):
        @pl.when(jnp.logical_not(there[i]))
        def _(i=i):
            XR0[i] = jnp.zeros(XR0.shape[1:], f32)
            for slot in range(2):
                for p in range(3):
                    XR[slot, p, i] = jnp.zeros(XR.shape[3:], f32)
                    ER[slot, p, i] = jnp.zeros(ER.shape[3:], f32)

    for p in range(3):
        for f in range(3):
            for z in range(-1, 9):
                V[p, f, pl.ds(rows(z, -8), 8), :] = zero
            for z in (-1, 8):
                V[p, f, level(z), :] = zero

    for load in loads[:6]:
        load.wait()

    def side_by_side(parts, t):
        tile = zero
        for k, v in enumerate(parts):
            shift = (WIDE * k + (WIDE if t else 0)) % 128
            v = pltpu.roll(v, shift, 1) if shift else v
            tile = jnp.where((lane >= WIDE * k) & (lane < WIDE * (k + 1)), v, tile)
        return tile

    def cut(t):
        return slice(128 * t, 128 * t + 128)

    def remote(src, dst, send, recv, way):
        return pltpu.make_async_remote_copy(
            src_ref=src, dst_ref=dst, send_sem=send, recv_sem=recv, device_id=at(*way), device_id_type=MESH)

    def xa_first(i):
        return remote(OX.at[i, 0:6], XR0.at[1 - i, 0:6], x_send.at[i], x_first_recv.at[0, 1 - i], (0, sides[i], 0))

    def xy_first(i, j):
        return remote(
            OX.at[i, 6 + j], XR0.at[1 - i, 7 - j], x_send.at[i], x_first_recv.at[2, 1 - i], (0, sides[i], sides[j]))

    def xb_first(i):
        return remote(OX.at[i, 8:14], XR0.at[1 - i, 8:14], x_send.at[i], x_first_recv.at[1, 1 - i], (0, sides[i], 0))

    def za_first(i):
        return remote(OZ.at[i, 0:6], ZR0.at[1 - i, 0:6], z_send.at[i], z_first_recv.at[0], (sides[i], 0, 0))

    def zy_first(i, j):
        return remote(
            OZ.at[i, 6 + j], ZR0.at[1 - i, 7 - j], z_send.at[i], z_first_recv.at[2], (sides[i], 0, sides[j]))

    def zb_first(i):
        return remote(OZ.at[i, 8:12], ZR0.at[1 - i, 8:12], z_send.at[i], z_first_recv.at[1], (sides[i], 0, 0))

    def y_first(i):
        return remote(OZ.at[i, 111:120], YR.at[1 - i], z_send.at[i], y_recv.at[0], (0, 0, sides[i]))

    def arrived(ref, sem):
        pltpu.make_async_copy(ref, ref, sem).wait()

    def put(ref, index, pair):
        ref[(MIDDLE, *index)] = jnp.where(lane < SEAM, pair[1], pair[0])
        ref[(LEFT, *index)] = pair[0]
        ref[(RIGHT, *index)] = pair[1]

    def put_margin(ref, index, v):
        ref[(LEFT, *index)] = jnp.where(lane >= 128 - WIDE, v, ref[(LEFT, *index)])
        ref[(RIGHT, *index)] = jnp.where(lane < WIDE, v, ref[(RIGHT, *index)])

    everywhere = slice(None)
    for z in range(8):
        solid = [(dom * 8 + z) >= floor[:, cut(t)] for t in range(2)]
        for f in range(6):
            v = [state[3 + f, z, :, cut(t)] for t in range(2)]
            if f >= 3:
                v = [jnp.where(m, w, 0.0) for m, w in zip(solid, v)]
            elif z == 0:
                v = [w + jnp.where(dom == 0, source[0, :, cut(t)], 0.0) for t, w in enumerate(v)]
            put(S, (f, level(z), everywhere), v)
    x_fields, z_fields = (0, 3, 4), (2, 4, 5)
    pair = (LEFT, RIGHT)
    for i, at_edge in enumerate((0, 7)):
        for k in range(3):
            for t in range(2):
                OX[i, 2 * k + t] = S[pair[t], x_fields[k], column(at_edge), :]
                OZ[i, 2 * k + t] = S[pair[t], z_fields[k], level(at_edge), :]
    for i in range(2):
        for z in range(8):
            OZ[i, 111 + z] = side_by_side(
                [state[f, z, :, cut(i)] for f in range(9)] + [region[z, :, cut(i)].astype(f32)], i)
        OZ[i, 119] = side_by_side([source[s, :, cut(i)] for s in range(STEPS)] + [floor[:, cut(i)].astype(f32)], i)

    pl.semaphore_wait(barrier, 8 + 5 * (there[0].astype(jnp.int32) + there[1].astype(jnp.int32)))
    for i in range(2):
        @functools.partial(reach, i)
        def _(i=i):
            xa_first(i).start()
    for i in range(2):
        za_first(i).start()
        y_first(i).start()

    for load in loads[6:]:
        load.wait()
    scale = 0.5 * COURANT
    tables = [[t[k] * scale for k in range(REGIONS)] for t in (lame, shear, buoy)]

    def materials(number, seafloor, z):
        bits = [(number & (1 << k)) != 0 for k in range(4)]
        solid = (dom * 8 + z) >= seafloor
        lam, mu, b = (pick(bits, t) for t in tables)
        return lam, jnp.where(solid, mu, 0.0), b, solid

    for s in range(STEPS):
        put(SRC, (pl.ds(8 * s, 8), everywhere),
            [jnp.where(dom == 0, source[s, :, cut(t)], 0.0) for t in range(2)])
    for z in range(8):
        made = [materials(region[z, :, cut(t)], floor[:, cut(t)], z) for t in range(2)]
        for k, ref in enumerate((L, M, B)):
            put(ref, (pl.ds(8 * z, 8), everywhere), [m[k] for m in made])
        for f in range(3):
            put(V, (f, level(z), everywhere), [state[f, z, :, cut(t)] for t in range(2)])

    for i, x in ((0, 0), (1, 7)):
        parts = [[OX[i, 2 * k + t] for t in range(2)] for k in range(3)]
        parts += [[m[p, pl.ds(x, 8, stride=8), :] for p in pair] for m in (L, M)]
        parts += [[
            jnp.concatenate([SRC[p, pl.ds(x, STEPS, stride=8), :], jnp.zeros((8 - STEPS, 128), f32)], 0) for p in pair]]
        for k in range(3, 6):
            for t in range(2):
                OX[i, 2 * k + t + 2] = parts[k][t]
        for j in range(2):
            OX[i, 6 + j] = side_by_side([v[j] for v in parts], j)

        @functools.partial(reach, i)
        def _(i=i):
            for j in range(2):
                xy_first(i, j).start()
            xb_first(i).start()
    for i, z in ((0, 0), (1, 7)):
        parts = [[OZ[i, 2 * k + t] for t in range(2)] for k in range(3)]
        parts += [[m[p, pl.ds(8 * z, 8), :] for p in pair] for m in (L, M)]
        for k in range(3, 5):
            for t in range(2):
                OZ[i, 2 * k + t + 2] = parts[k][t]
        for j in range(2):
            OZ[i, 6 + j] = side_by_side([v[j] for v in parts], j)
            zy_first(i, j).start()
        zb_first(i).start()

    left = (lane >= 128 - WIDE) & (gy > 0)
    right = (lane < WIDE) & (gy < n_gy - 1)
    inside = left | right

    def margin(low, high, f):
        shift_r = (128 - WIDE * f) % 128
        shift_l = (256 - WIDE - WIDE * f) % 128
        a = pltpu.roll(high, shift_r, 1) if shift_r else high
        c = pltpu.roll(low, shift_l, 1) if shift_l else low
        return jnp.where(left, c, jnp.where(right, a, 0.0))

    arrived(ZR0.at[:, 0:6], z_first_recv.at[0])
    for i in range(2):
        @functools.partial(reach, i)
        def _(i=i):
            arrived(XR0.at[i, 0:6], x_first_recv.at[0, i])

    def three(first_tile, second_tile, edge):
        return (
            jnp.where(lane < SEAM, second_tile, first_tile),
            jnp.where(lane >= 128 - WIDE, edge, first_tile),
            jnp.where(lane < WIDE, edge, second_tile),
        )

    def border(parts):
        for i, x in ((0, -1), (1, 8)):
            for k, f in enumerate(x_fields):
                edge = zero if parts == (MIDDLE,) else margin(XR0[i, 6], XR0[i, 7], k)
                tiles = three(XR0[i, 2 * k], XR0[i, 2 * k + 1], edge)
                for p in parts:
                    S[p, f, column(x), :] = tiles[p]
        for i, z in ((0, -1), (1, 8)):
            for k, f in enumerate(z_fields):
                edge = zero if parts == (MIDDLE,) else margin(ZR0[i, 6], ZR0[i, 7], k)
                tiles = three(ZR0[i, 2 * k], ZR0[i, 2 * k + 1], edge)
                for p in parts:
                    S[p, f, level(z), :] = jnp.where(z_there[i], tiles[p], 0.0)

    border((MIDDLE,))
    def x_base(p, s, last):
        return 14 + 18 * s + (3 * p if last else 6 * p)

    def z_base(p, s, last):
        return 12 + 18 * s + (3 * p if last else 6 * p)

    def x_copy(p, i, s, slot, last):
        n = 3 if last else 6
        return remote(
            OX.at[i, pl.ds(x_base(p, s, last), n)], XR.at[slot, p, 1 - i, 0:n], x_send.at[i], x_recv.at[slot, p, 1 - i],
            (0, sides[i], 0))

    def e_copy(p, i, j, s, slot):
        return remote(
            OE.at[i, 3 * s + p, j], ER.at[slot, p, 1 - i, 1 - j], e_send.at[i],
            e_recv.at[slot, p, 1 - i], (sides[j], sides[i], 0))

    def z_copy(p, i, s, slot, last):
        n = 3 if last else 6
        return remote(
            OZ.at[i, pl.ds(z_base(p, s, last), n)], ZR.at[slot, p, 1 - i, 0:n], z_send.at[i], z_recv.at[slot, p],
            (sides[i], 0, 0))

    def move(p, s, slot, last=False):
        def accelerate(levels):
            moved = []
            for z in levels:
                own = level(z)
                after, before = pl.ds(rows(z, 1), 8), pl.ds(rows(z, -1), 8)
                above, below = level(z + 1), level(z - 1)

                def dx(f):
                    return S[p, f, after, :] - S[p, f, before, :]

                def dz(f):
                    return S[p, f, above, :] - S[p, f, below, :]

                b = B[p, pl.ds(8 * z, 8), :]
                moved.append((0, own, V[p, 0, own, :] - b * (dx(0) + dy(S[p, 3, own, :]) + dz(4))))
                moved.append((1, own, V[p, 1, own, :] - b * (dx(3) + dy(S[p, 1, own, :]) + dz(5))))
                moved.append((2, own, V[p, 2, own, :] - b * (dx(4) + dy(S[p, 5, own, :]) + dz(2))))
            for f, own, v in moved:
                V[p, f, own, :] = v

        accelerate((0, 7))
        if not last:
            for i, x in ((0, 0), (1, 7)):
                for j in range(2):
                    for k, f in enumerate((0, 2)):
                        OE[i, 3 * s + p, j, k : k + 1, :] = V[p, f, pl.ds(rows(7 * j, x), 1), :]

                @functools.partial(reach, i)
                def _(i=i):
                    for j in range(2):
                        e_copy(p, i, j, s, slot).start()
        accelerate((1, 2, 3))
        accelerate((4, 5, 6))
        base = x_base(p, s, last)
        for i, (x, inner) in enumerate(((0, 1), (7, 6))):
            for k, v in enumerate([V[p, f, column(c), :] for c in ((x,) if last else (x, inner)) for f in range(3)]):
                OX[i, base + k] = v

            @functools.partial(reach, i)
            def _(i=i):
                x_copy(p, i, s, slot, last).start()
        base = z_base(p, s, last)
        for i, (z, inner) in enumerate(((0, 1), (7, 6))):
            for f in range(3):
                OZ[i, base + f] = V[p, f, level(z), :]
                if not last:
                    OZ[i, base + 3 + f] = V[p, f, level(inner), :]
            z_copy(p, i, s, slot, last).start()

        later = []
        for z in range(8):
            own = level(z)
            after, before = pl.ds(rows(z, 1), 8), pl.ds(rows(z, -1), 8)
            above, below = level(z + 1), level(z - 1)
            dxs = [V[p, f, after, :] - V[p, f, before, :] for f in range(3)]
            dzs = [V[p, f, above, :] - V[p, f, below, :] for f in range(3)]
            dys = [dy(V[p, f, own, :]) for f in range(3)]
            lam, mu = L[p, pl.ds(8 * z, 8), :], M[p, pl.ds(8 * z, 8), :]
            spread = lam * (dxs[0] + dys[1] + dzs[2])
            mu2 = mu + mu
            change = (
                spread + mu2 * dxs[0], spread + mu2 * dys[1], spread + mu2 * dzs[2],
                mu * (dys[0] + dxs[1]), mu * (dzs[0] + dxs[2]), mu * (dzs[1] + dys[2]))
            later += [(f, own, S[p, f, own, :] - change[f]) for f in range(6)]
            if z % 2:
                write(p, later)
                later = []

    def write(p, results):
        for f, at_rows, v in results:
            S[p, f, at_rows, :] = v

    def finish(p, slot, then=None):
        last = then is None
        if not last:
            added = SRC[p, pl.ds(8 * then if isinstance(then, int) else pl.multiple_of(8 * then, 8), 8), :]
            results = [(f, level(0), S[p, f, level(0), :] + added) for f in range(3)]
            for i, x in ((0, -1), (1, 8)):
                outer = pl.ds(rows(0, x), 1)
                results.append((0, outer, S[p, 0, outer, :] + SX[i, p, pl.ds(then, 1), :]))
            write(p, results)
        arrived(ZR.at[slot, p, :, 0:3] if last else ZR.at[slot, p], z_recv.at[slot, p])
        results = []
        for i, z in ((0, 0), (1, 7)):
            near = [ZR[slot, p, i, f] for f in range(3)]
            own = level(z)
            lam, mu = L[p, pl.ds(8 * z, 8), :], M[p, pl.ds(8 * z, 8), :]
            sign = jnp.where(z_there[i], (-1.0, 1.0)[i], 0.0)
            slope = [sign * v for v in near]
            spread = lam * slope[2]
            results.append((0, own, S[p, 0, own, :] - (spread)))
            results.append((1, own, S[p, 1, own, :] - (spread)))
            results.append((2, own, S[p, 2, own, :] - (spread + (mu + mu) * slope[2])))
            results.append((4, own, S[p, 4, own, :] - (mu * slope[0])))
            results.append((5, own, S[p, 5, own, :] - (mu * slope[1])))
        write(p, results)

        for i in range(2):
            @functools.partial(reach, i)
            def _(i=i):
                arrived(XR.at[slot, p, i, 0:3] if last else XR.at[slot, p, i], x_recv.at[slot, p, i])

        results = []
        for i, x, sign in ((0, 0, -1.0), (1, 7, 1.0)):
            near = [XR[slot, p, i, f] for f in range(3)]
            lam, mu = L[p, pl.ds(x, 8, stride=8), :], M[p, pl.ds(x, 8, stride=8), :]
            slope = [sign * v for v in near]
            spread = lam * slope[0]
            results.append((0, column(x), S[p, 0, column(x), :] - (spread + (mu + mu) * slope[0])))
            results.append((1, column(x), S[p, 1, column(x), :] - (spread)))
            results.append((2, column(x), S[p, 2, column(x), :] - (spread)))
            results.append((3, column(x), S[p, 3, column(x), :] - (mu * slope[1])))
            results.append((4, column(x), S[p, 4, column(x), :] - (mu * slope[2])))

        if last:
            write(p, results)
            return
        for i, x, sign in ((0, 0, -1.0), (1, 7, 1.0)):
            near, far = [XR[slot, p, i, f] for f in range(3)], [XR[slot, p, i, 3 + f] for f in range(3)]
            lam, mu = LX[i, p], MX[i, p]
            dxs = [sign * (far[f] - V[p, f, column(x), :]) for f in range(3)]
            dzs = {}
            for f in (0, 2):
                up, down = pltpu.roll(near[f], 7, 0), pltpu.roll(near[f], 1, 0)
                dzs[f] = jnp.where(sub == 7, 0.0, up) - jnp.where(sub == 0, 0.0, down)
            trace = dxs[0] + dy(near[1]) + dzs[2]
            beyond = column((-1, 8)[i])
            results.append((0, beyond, S[p, 0, beyond, :] - (lam * trace + (mu + mu) * dxs[0])))
            results.append((3, beyond, S[p, 3, beyond, :] - (mu * (dy(near[0]) + dxs[1]))))
            results.append((4, beyond, S[p, 4, beyond, :] - (mu * (dzs[0] + dxs[2]))))
        for i, z, sign in ((0, 0, -1.0), (1, 7, 1.0)):
            near, far = [ZR[slot, p, i, f] for f in range(3)], [ZR[slot, p, i, 3 + f] for f in range(3)]
            lam, mu = LZ[i, p], MZ[i, p]
            dzs = [sign * (far[f] - V[p, f, level(z), :]) for f in range(3)]
            dxs = {}
            for f in (0, 2):
                ahead, behind = pltpu.roll(near[f], 7, 0), pltpu.roll(near[f], 1, 0)
                dxs[f] = jnp.where(sub == 7, 0.0, ahead) - jnp.where(sub == 0, 0.0, behind)
            trace = dxs[0] + dy(near[1]) + dzs[2]
            beyond = level((-1, 8)[i])
            results.append((2, beyond, S[p, 2, beyond, :] - (lam * trace + (mu + mu) * dzs[2])))
            results.append((4, beyond, S[p, 4, beyond, :] - (mu * (dzs[0] + dxs[2]))))
            results.append((5, beyond, S[p, 5, beyond, :] - (mu * (dzs[1] + dy(near[2])))))

        write(p, results)

        for i in range(2):
            @functools.partial(reach, i)
            def _(i=i):
                arrived(ER.at[slot, p, i], e_recv.at[slot, p, i])
        results = []
        for i, x in ((0, 0), (1, 7)):
            for j, z in ((0, 0), (1, 7)):
                edge_x, edge_z = (ER[slot, p, i, j, k : k + 1, :] for k in range(2))
                sign = jnp.where(z_there[j], (-1.0, 1.0)[j], 0.0)
                outer = pl.ds(rows(z, (-1, 8)[i]), 1)
                at_z, at_x = slice(z, z + 1), slice(x, x + 1)
                results.append((0, outer, S[p, 0, outer, :] - (LX[i, p, at_z, :] * (sign * edge_z))))
                results.append((4, outer, S[p, 4, outer, :] - (MX[i, p, at_z, :] * (sign * edge_x))))
                outer = pl.ds(rows((-1, 8)[j], x), 1)
                results.append((2, outer, S[p, 2, outer, :] - (LZ[j, p, at_x, :] * (sides[i] * edge_x))))
                results.append((4, outer, S[p, 4, outer, :] - (MZ[j, p, at_x, :] * (sides[i] * edge_z))))
        write(p, results)

    def each_part(then):
        for p in range(3):
            then(p)

    move(MIDDLE, 0, 0)

    arrived(YR, y_recv.at[0])
    low, high = YR[0, 8], YR[1, 8]
    seafloor = margin(low, high, STEPS).astype(jnp.int32)
    first_source = None
    for s in range(STEPS):
        v = jnp.where(dom == 0, margin(low, high, s), 0.0)
        first_source = v if s == 0 else first_source
        put_margin(SRC, (pl.ds(8 * s, 8), everywhere), v)
    for z in range(8):
        low, high = YR[0, z], YR[1, z]
        lam, mu, b, solid = materials(margin(low, high, 9).astype(jnp.int32), seafloor, z)
        for ref, v in ((L, lam), (M, mu), (B, b)):
            put_margin(ref, (pl.ds(8 * z, 8), everywhere), jnp.where(inside, v, 0.0))
        for f in range(9):
            v = margin(low, high, f)
            if f < 3:
                put_margin(V, (f, level(z), everywhere), v)
            else:
                if f >= 6:
                    v = jnp.where(solid, v, 0.0)
                elif z == 0:
                    v = v + first_source
                put_margin(S, (f - 3, level(z), everywhere), v)

    arrived(ZR0.at[:, 6:8], z_first_recv.at[2])
    for i in range(2):
        @functools.partial(reach, i)
        def _(i=i):
            arrived(XR0.at[i, 6:8], x_first_recv.at[2, i])
    border((LEFT, RIGHT))

    move(LEFT, 0, 0)
    move(RIGHT, 0, 0)

    arrived(ZR0.at[:, 8:12], z_first_recv.at[1])
    for i in range(2):
        @functools.partial(reach, i)
        def _(i=i):
            arrived(XR0.at[i, 8:14], x_first_recv.at[1, i])
    for i in range(2):
        for k, ref in enumerate((LX, MX, SX)):
            tiles = three(XR0[i, 8 + 2 * k], XR0[i, 9 + 2 * k], margin(XR0[i, 6], XR0[i, 7], 3 + k))
            for p in range(3):
                ref[i, p] = tiles[p]
        for k, ref in enumerate((LZ, MZ)):
            tiles = three(ZR0[i, 8 + 2 * k], ZR0[i, 9 + 2 * k], margin(ZR0[i, 6], ZR0[i, 7], 3 + k))
            for p in range(3):
                ref[i, p] = jnp.where(z_there[i], tiles[p], 0.0)

    def step(s, carry):
        slot = lax.rem(s, 2)

        def turn(p):
            finish(p, 1 - slot, s)
            move(p, s, slot)

        each_part(turn)
        return carry

    lax.fori_loop(1, STEPS - 1, step, 0)

    end = STEPS - 1

    def final(p):
        finish(p, (end - 1) % 2, end)
        move(p, end, end % 2, last=True)

    each_part(final)

    def gather(f, ref, k):
        for z in range(8):
            middle, first_tile, second_tile = (ref[p, k, level(z), :] for p in (MIDDLE, LEFT, RIGHT))
            out[f, z, :, cut(0)] = jnp.where(lane < FIRST_CUT, first_tile, middle)
            out[f, z, :, cut(1)] = jnp.where(lane < SECOND_CUT, middle, second_tile)

    for f in range(3):
        gather(f, V, f)
    each_part(lambda p: finish(p, end % 2))
    for f in range(6):
        gather(3 + f, S, f)

    for i in range(2):
        arrived(OZ.at[i], z_send.at[i])

        @functools.partial(reach, i)
        def _(i=i):
            arrived(OX.at[i], x_send.at[i])
            arrived(OE.at[i], e_send.at[i])


def solution(mesh):
    sizes = (mesh.shape["dom"], mesh.shape["gx"], mesh.shape["gy"])

    def on_device(state, source, floor, region, lame, shear, buoy):
        hbm = pl.BlockSpec(memory_space=pltpu.HBM)

        def tiles(*shape):
            return pltpu.VMEM(shape + (8, 128), f32)

        return pl.pallas_call(
            functools.partial(kernel, sizes),
            out_shape=jax.ShapeDtypeStruct(state.shape, f32),
            in_specs=[hbm] * 7,
            out_specs=pl.BlockSpec(memory_space=pltpu.VMEM),
            scratch_shapes=[
                pltpu.VMEM(state.shape, f32),
                pltpu.VMEM(source.shape, f32),
                pltpu.VMEM(floor.shape, jnp.int32),
                pltpu.VMEM(region.shape, jnp.int32),
                pltpu.SMEM(lame.shape, f32),
                pltpu.SMEM(shear.shape, f32),
                pltpu.SMEM(buoy.shape, f32),
                pltpu.VMEM((3, 6, 10 * BLOCK, 128), f32),
                pltpu.VMEM((3, 3, 10 * BLOCK, 128), f32),
                pltpu.VMEM((3, 64, 128), f32),
                pltpu.VMEM((3, 64, 128), f32),
                pltpu.VMEM((3, 64, 128), f32),
                pltpu.VMEM((3, 8 * STEPS, 128), f32),
                tiles(2, 3),
                tiles(2, 3),
                tiles(2, 3),
                tiles(2, 3),
                tiles(2, 3),
                tiles(2, 113),
                tiles(2, 120),
                pltpu.VMEM((2, 3 * STEPS - 3, 2, 2, 128), f32),
                tiles(2, 14),
                tiles(2, 12),
                tiles(2, 9),
                tiles(2, 3, 2, 6),
                tiles(2, 3, 2, 6),
                pltpu.VMEM((2, 3, 2, 2, 2, 128), f32),
                pltpu.SemaphoreType.DMA((9,)),
                pltpu.SemaphoreType.DMA((2,)),
                pltpu.SemaphoreType.DMA((2,)),
                pltpu.SemaphoreType.DMA((2,)),
                pltpu.SemaphoreType.DMA((3, 2)),
                pltpu.SemaphoreType.DMA((3,)),
                pltpu.SemaphoreType.DMA((1,)),
                pltpu.SemaphoreType.DMA((2, 3, 2)),
                pltpu.SemaphoreType.DMA((2, 3)),
                pltpu.SemaphoreType.DMA((2, 3, 2)),
            ],
            compiler_params=pltpu.CompilerParams(
                collective_id=0, has_side_effects=True, vmem_limit_bytes=32 * 1024 * 1024
            ),
        )(*(
            pltpu.with_memory_space_constraint(v, pltpu.HBM)
            for v in (state, source, floor, region, lame, shear, buoy)
        ))

    return jax.shard_map(
        on_device,
        mesh=mesh,
        in_specs=(
            P(None, "dom", "gx", "gy"),
            P(None, "gx", "gy"),
            P("gx", "gy"),
            P("dom", "gx", "gy"),
            P(),
            P(),
            P(),
        ),
        out_specs=P(None, "dom", "gx", "gy"),
        check_vma=False,
    )
```
